32 devices in a mesh: runs: 2 (over y), box: 4 (over z), slab: 2 (over x), fld: 2 (over core).
Axes of the slice: x: 2, y: 2, z: 4, core: 2. Of those that a mesh axis runs over, the one named last changes fastest.
Arguments:
- boxes: float32 [3, 32, 24, 16, 256], P(None, ('runs', 'box'), 'fld', 'slab'), parts along dimension 1, may hold values from -6 to 6
- move_dest: int32 [32], P('runs'), parts along dimension 0, may hold values from 0 to 3, as said below
- parent: int32 [32], P('runs'), parts along dimension 0, may hold values from 0 to 31, as said below
- coarse: float32 [64, 24, 1000], P(('runs', 'box'), 'fld'), parts along dimension 0, may hold values from -6 to 6
- lap_mix: float32 [24, 24], replicated, may hold values from -0.3125 to 0.3125
- grad_mix: float32 [24, 24], replicated, may hold values from -1.25 to 1.25
- damp_mix: float32 [24, 24], replicated, may hold values from -1.25 to 1.25
Outputs:
- moved_levels: float32 [3, 64, 24, 16, 256], P(None, ('runs', 'box'), 'fld', 'slab'), parts along dimension 1
- slope: float32 [64, 24, 16, 256], P(('runs', 'box'), 'fld', 'slab'), parts along dimension 0
The draws below stay inside these ranges and needn't reach their ends.
There are 2 independent parts, one for each index of `runs`. The reference program is written for one: setup_inputs(seed, part) draws one part's arguments, and reference() takes and returns one part's arrays. A program takes and returns all parts, laid end to end along the dimension named above; an argument that names none is the same for every part. Nothing has to cross between parts.
Inputs may be any that keep to these rules, and one draw needn't show every extreme that they name: `move_dest`: of the 4 boxes of one index of box, at most 2 share a destination; in every draw some destination receives exactly 2 boxes from every index of box, and every index of box is the destination of some box. `parent`: the boxes that one destination receives from one source have parents held by one index of box, and different sources give different such indices; so at most 2 boxes of one destination have parents on one index of box, and some destination reaches 2 from every index.
All inputs are finite; a program needn't handle non-finite values.
Results may differ from the reference program's by a relative error of at most 0.00007.
Values sent between devices are 32-bit elements; how exact they have to be, the bound alone decides.
No kernel may reach another device: no remote copies, remote signals or barrier semaphores. Data moves between devices by JAX's collectives and lax.ppermute only.
A program may use at most 128 MiB of HBM per device.

```python
import jax
import jax.numpy as jnp
from jax import lax

FIELDS = 24
EDGE = 16
LEVELS = 3
COARSE_DEV = 8
BOXES = 16
SLOTS = 32
COARSE = 32
N_BOX = 4


def plan_moves(key):
    count = N_BOX
    key_hot, key_turn, key_pick, key_owner, key_local = jax.random.split(key, 5)
    hottest = jax.random.randint(key_hot, (), 0, count).astype(jnp.int32)
    rotation = jax.random.randint(key_turn, (), 0, count - 1).astype(jnp.int32)

    def one_sender(sender, sender_key):
        offsets = (sender + rotation + jnp.arange(count // 2 - 1, dtype=jnp.int32)) % (count - 1)
        picked = (hottest + 1 + offsets) % count
        targets = jnp.concatenate([jnp.full((2,), hottest, dtype=jnp.int32), jnp.repeat(picked, 2)])
        return jax.random.permutation(sender_key, targets).astype(jnp.int32)
    senders = jnp.arange(count, dtype=jnp.int32)
    dest_grid = jax.vmap(one_sender)(senders, jax.random.split(key_pick, count))
    owner_table = jax.vmap(lambda owner_key: jax.random.permutation(owner_key, count))(jax.random.split(key_owner, count)).astype(jnp.int32)
    sources = jnp.broadcast_to(senders[:, None], dest_grid.shape)
    owners = owner_table[dest_grid, sources]
    local_index = jax.random.randint(key_local, dest_grid.shape, 0, COARSE_DEV).astype(jnp.int32)
    parents = owners * COARSE_DEV + local_index
    return (dest_grid.reshape(-1).astype(jnp.int32), parents.reshape(-1).astype(jnp.int32))


def draw_move_dest(key, part):
    return plan_moves(key)[0]


def draw_parent(key, part):
    return plan_moves(key)[1]


def shard_levels(own_key, dims, cuts, least, top_value):
    loudness, own = 1.0, jax.random.fold_in(own_key, 6)
    for dim, shards_of in cuts:
        steps = jnp.exp(jax.random.uniform(jax.random.fold_in(own, dim), (shards_of,), jnp.float32, least / len(cuts), top_value / len(cuts)))
        loudness = loudness * jnp.repeat(steps, dims[dim] // shards_of).reshape([-1 if axis == dim else 1 for axis in range(len(dims))])
    return loudness


def gaussian(stream_key, dims, scale, most, cuts=(), held_as=jnp.bfloat16):
    factor_of = shard_levels(stream_key, dims, cuts, -0.22, 0.18) if cuts else 1.0
    result = jax.random.normal(stream_key, dims, jnp.float32) * scale * factor_of
    return jnp.minimum(jnp.maximum(result, -most), most).astype(held_as)


def setup_inputs(seed: int = 0, part: int = 0) -> dict:
    arg_keys = jax.random.split(jax.random.key(seed), 8)
    own_keys = jax.random.split(jax.random.fold_in(arg_keys[7], part), 8)
    boxes = gaussian(own_keys[0], (LEVELS, BOXES, FIELDS, EDGE, EDGE * EDGE), 1.0, 6.0, ((1, 4), (2, 2), (3, 2)), jnp.float32)
    move_dest = draw_move_dest(jax.random.fold_in(jax.random.fold_in(arg_keys[7], part), 71), part)
    parent = draw_parent(jax.random.fold_in(jax.random.fold_in(arg_keys[7], part), 71), part)
    coarse = gaussian(own_keys[3], (COARSE, FIELDS, (EDGE // 2 + 2) ** 3), 1.0, 6.0, ((0, 4), (1, 2)), jnp.float32)
    lap_mix = gaussian(arg_keys[4], (FIELDS, FIELDS), (16 * FIELDS) ** -0.5, 0.3125, (), jnp.float32)
    grad_mix = gaussian(arg_keys[5], (FIELDS, FIELDS), FIELDS ** -0.5, 1.25, (), jnp.float32)
    damp_mix = gaussian(arg_keys[6], (FIELDS, FIELDS), FIELDS ** -0.5, 1.25, (), jnp.float32)
    return dict(boxes=boxes, move_dest=move_dest, parent=parent, coarse=coarse, lap_mix=lap_mix, grad_mix=grad_mix, damp_mix=damp_mix)


def prolong_block(values):
    for axis_pos in (-3, -2, -1):
        values = jnp.repeat(values, 2, axis=axis_pos)
    return values[..., 1:-1, 1:-1, 1:-1]


def stencil_terms(padded):
    centre = padded[..., 1:-1, 1:-1, 1:-1]
    x_after = padded[..., 2:, 1:-1, 1:-1]
    x_before = padded[..., :-2, 1:-1, 1:-1]
    y_after = padded[..., 1:-1, 2:, 1:-1]
    y_before = padded[..., 1:-1, :-2, 1:-1]
    z_after = padded[..., 1:-1, 1:-1, 2:]
    z_before = padded[..., 1:-1, 1:-1, :-2]
    laplace = x_after + x_before + y_after + y_before + z_after + z_before - 6.0 * centre
    slopes = 0.5 * ((x_after - x_before) + (y_after - y_before) + (z_after - z_before))
    return laplace, slopes, centre


def reference(boxes, move_dest, parent, coarse, lap_mix, grad_mix, damp_mix):
    fields = boxes.shape[2]
    box_edge = boxes.shape[3]
    coarse_side = box_edge // 2 + 2
    per_device = BOXES // N_BOX
    dest_grid = move_dest.reshape(N_BOX, per_device)
    earlier = jnp.arange(per_device)[None, :] < jnp.arange(per_device)[:, None]
    matching = dest_grid[:, :, None] == dest_grid[:, None, :]
    box_rank = jnp.sum(matching & earlier[None], axis=2, dtype=jnp.int32)
    source = jnp.broadcast_to(jnp.arange(N_BOX, dtype=jnp.int32)[:, None], dest_grid.shape)
    new_slot = ((dest_grid * N_BOX + source) * 2 + box_rank).reshape(-1).astype(jnp.int32)
    moved_levels = jnp.zeros((LEVELS, SLOTS) + boxes.shape[2:], jnp.float32).at[:, new_slot].set(boxes)
    mixing = jnp.concatenate([lap_mix, grad_mix, damp_mix], axis=1)

    def one_box(box_items):
        field_now, parent_id = box_items
        coarse_shell = lax.dynamic_index_in_dim(coarse, parent_id, 0, keepdims=False)
        coarse_shell = coarse_shell.reshape(fields, coarse_side, coarse_side, coarse_side)
        padded = prolong_block(coarse_shell)
        padded = padded.at[:, 1:-1, 1:-1, 1:-1].set(field_now.reshape(fields, box_edge, box_edge, box_edge))
        stencil_all = jnp.concatenate(stencil_terms(padded), axis=-4)
        mixed_terms = jnp.einsum("fg,gxyz->fxyz", mixing, stencil_all, precision=lax.Precision.HIGHEST)
        return mixed_terms.reshape(fields, box_edge, box_edge * box_edge)

    slopes_all = lax.map(one_box, (boxes[0], parent))
    slope_out = jnp.zeros((SLOTS,) + boxes.shape[2:], jnp.float32).at[new_slot].set(slopes_all)
    return moved_levels, slope_out
```

```python
import functools

import jax
import jax.numpy as jnp
import numpy as np
from jax import lax
from jax.experimental import pallas as pl
from jax.experimental.pallas import tpu as pltpu
from jax.sharding import PartitionSpec as P

HIGHEST = lax.Precision.HIGHEST
ROWS = 16


def round_up(value, unit):
    return -(-value // unit) * unit


def split_three(values):
    high = values.astype(jnp.bfloat16)
    rest = values - high.astype(jnp.float32)
    middle = rest.astype(jnp.bfloat16)
    low = (rest - middle.astype(jnp.float32)).astype(jnp.bfloat16)
    return high, middle, low


def pack_kernel(levels, per_device, slots, dest_ref, boxes_ref, *refs):
    outs, (table, zeros, sems) = refs[: len(levels)], refs[len(levels) :]
    own = lax.axis_index("box")
    zeros[...] = jnp.zeros_like(zeros)
    for slot in range(slots):
        table[slot] = -1

    def place(b, carry):
        slot = 2 * dest_ref[own * per_device + b]
        slot = jnp.where(table[slot] >= 0, slot + 1, slot)
        table[slot] = b
        return carry

    lax.fori_loop(0, per_device, place, 0)
    for n, level in enumerate(levels):
        for slot in range(slots):
            b = table[slot]

            @pl.when(b >= 0)
            def _():
                pltpu.make_async_copy(boxes_ref.at[level, b], outs[n].at[slot], sems.at[n, slot]).start()

            @pl.when(b < 0)
            def _():
                pltpu.make_async_copy(zeros, outs[n].at[slot], sems.at[n, slot]).start()

    for n in range(len(levels)):
        for slot in range(slots):
            pltpu.make_async_copy(zeros, outs[n].at[slot], sems.at[n, slot]).wait()


def pack_levels(levels, boxes, move_dest, slots):
    per_device = boxes.shape[1]
    item = boxes.shape[2:]
    size = int(np.prod(item)) * 4
    return pl.pallas_call(
        functools.partial(pack_kernel, levels, per_device, slots),
        out_shape=[jax.ShapeDtypeStruct((slots,) + item, jnp.float32)] * len(levels),
        in_specs=[pl.BlockSpec(memory_space=pltpu.SMEM), pl.BlockSpec(memory_space=pl.ANY)],
        out_specs=[pl.BlockSpec(memory_space=pl.ANY)] * len(levels),
        scratch_shapes=[
            pltpu.SMEM((slots,), jnp.int32),
            pltpu.VMEM(item, jnp.float32),
            pltpu.SemaphoreType.DMA((len(levels), slots)),
        ],
        cost_estimate=pl.CostEstimate(
            flops=0, bytes_accessed=2 * len(levels) * slots * size, transcendentals=0
        ),
    )(move_dest, boxes)


def face_tables(coarse_side, coarse_planes, slabs):
    half = coarse_side - 2
    square = coarse_side * coarse_side
    inner = np.arange(half) + 1
    sides = []
    for c in range(coarse_planes):
        base = (c + 1) * square
        sides += [base + inner, base + (coarse_side - 1) * coarse_side + inner]
        sides += [base + inner * coarse_side, base + inner * coarse_side + coarse_side - 1]
    yz = np.concatenate(sides)
    x = (inner[:, None] * coarse_side + inner[None, :]).reshape(-1)
    lanes = round_up(yz.size + x.size, 128)
    table = np.zeros((8, lanes), np.int32)
    table[0] = -(10 ** 6)
    table[0, : yz.size] = yz
    table[1, : yz.size] = coarse_planes * square
    table[0, yz.size : yz.size + x.size] = x
    table[2, yz.size : yz.size + x.size] = (coarse_side - 1) * square
    return table


def expand_table(coarse_planes, edge, lanes):
    half = edge // 2
    cross = edge * edge
    spread = np.zeros((lanes, (2 * coarse_planes + 1) * cross), np.float32)
    for c in range(coarse_planes):
        base = c * 4 * half
        forward, backward = 2 * c * cross, (2 * c + 1) * cross
        for m in range(edge):
            spread[base + m // 2, backward + m] += 1
            spread[base + half + m // 2, forward + (edge - 1) * edge + m] += 1
            spread[base + 2 * half + m // 2, backward + m * edge] += 1
            spread[base + 3 * half + m // 2, forward + m * edge + edge - 1] += 1
    base, to = coarse_planes * 4 * half, 2 * coarse_planes * cross
    for y in range(edge):
        for z in range(edge):
            spread[base + (y // 2) * half + z // 2, to + y * edge + z] = 1
    return spread


def faces_kernel(slots, total, dest_ref, parent_ref, coarse_ref, table_ref, out_ref, picked, table):
    coarse_count, fields, cells = coarse_ref.shape
    own, slab = lax.axis_index("box"), lax.axis_index("slab")
    picked[...] = jnp.zeros_like(picked)
    for slot in range(slots):
        table[slot] = -1

    def place(b, carry):
        slot = 2 * dest_ref[b]
        local = parent_ref[b] - own * coarse_count

        @pl.when(jnp.logical_and(local >= 0, local < coarse_count))
        def _():
            table[jnp.where(table[slot] >= 0, slot + 1, slot)] = local

        return carry

    lax.fori_loop(0, total, place, 0)
    for slot in range(slots):
        local = table[slot]

        @pl.when(local >= 0)
        def _():
            picked[slot * ROWS : slot * ROWS + fields, :cells] = coarse_ref[local]

    index = table_ref[0:1] + slab * table_ref[1:2] + jnp.where(slab > 0, table_ref[2:3], 0)
    cell = lax.broadcasted_iota(jnp.int32, (picked.shape[1], index.shape[1]), 0)
    chosen = (cell == index).astype(jnp.float32).astype(jnp.bfloat16)
    high, middle, low = (
        jnp.dot(part, chosen, preferred_element_type=jnp.float32) for part in split_three(picked[...])
    )
    out_ref[...] = (high + (middle + low)).reshape(out_ref.shape)


def pack_faces(coarse, move_dest, parent, slots, slabs, coarse_side, coarse_planes):
    table = face_tables(coarse_side, coarse_planes, slabs)
    lanes = table.shape[1]
    depth = round_up(coarse.shape[2], 128)
    smem, vmem = pl.BlockSpec(memory_space=pltpu.SMEM), pl.BlockSpec(memory_space=pltpu.VMEM)
    return pl.pallas_call(
        functools.partial(faces_kernel, slots, move_dest.shape[0]),
        out_shape=jax.ShapeDtypeStruct((slots, ROWS, lanes), jnp.float32),
        in_specs=[smem, smem, vmem, vmem],
        out_specs=vmem,
        scratch_shapes=[pltpu.VMEM((slots * ROWS, depth), jnp.float32), pltpu.SMEM((slots,), jnp.int32)],
        compiler_params=pltpu.CompilerParams(vmem_limit_bytes=32 * 2 ** 20),
        cost_estimate=pl.CostEstimate(
            flops=6 * slots * ROWS * depth * lanes, bytes_accessed=4 * coarse.size, transcendentals=0
        ),
    )(move_dest, parent, coarse, jnp.asarray(table))


def slope_columns(fields, planes, coarse_planes):
    column_field, forward, backward, centre = [], [], [], []
    p = np.arange(planes)

    def add(field, f, b, c):
        column_field.append(field)
        forward.append(f * np.ones(planes))
        backward.append(b * np.ones(planes))
        centre.append(c * np.ones(planes))

    for f, b, c in ((1, 0, 0), (0, 1, 0), (0, 0, 1)):
        for g in range(2 * fields):
            for q in range(planes):
                here = p == q
                add(g, f * here + c * (p + 1 == q), b * here + c * (p - 1 == q), c * here)
    rows = [g if g < fields else -1 for g in range(ROWS)]
    rows += [fields + g if g < fields else -1 for g in range(ROWS)]
    for g in rows:
        add(g, 0, p == 0, 0)
    for g in rows:
        add(g, p == planes - 1, 0, 0)
    for c in range(coarse_planes):
        for g in rows:
            add(g, p // 2 == c, 0, 0)
        for g in rows:
            add(g, 0, p // 2 == c, 0)
    width = round_up(len(column_field), 128)
    select = np.zeros((2 * fields, width), np.float32)
    masks = np.zeros((3, planes, width), np.float32)
    for k, g in enumerate(column_field):
        if g >= 0:
            select[g, k] = 1
        masks[0, :, k], masks[1, :, k], masks[2, :, k] = forward[k], backward[k], centre[k]
    return select, masks


def slope_kernel(
    edge, planes, fields, coarse_planes, per_device, total, coarse_count, slots, slabs,
    dest_ref, parent_ref, own_ref, other_ref, own_low, other_low, own_high, other_high,
    own_faces, other_faces, spread_ref, weight_ref, out_ref, stack, table, count,
):
    step = pl.program_id(0)
    cross = edge * edge
    rows = fields * planes
    own, slab = lax.axis_index("box"), lax.axis_index("slab")

    @pl.when(step == 0)
    def _():
        stack[...] = jnp.zeros_like(stack)
        for slot in range(slots):
            table[slot] = -1
            count[slot] = 0

        def place(b, carry):
            @pl.when(dest_ref[b] == own)
            def _():
                slot = 2 * (b // per_device)
                owner = parent_ref[b] // coarse_count
                table[jnp.where(table[slot] >= 0, slot + 1, slot)] = 2 * owner + count[owner]
                count[owner] = count[owner] + 1

            return carry

        lax.fori_loop(0, total, place, 0)

    face = table[step]

    @pl.when(face < 0)
    def _():
        out_ref[...] = jnp.zeros_like(out_ref)

    @pl.when(face >= 0)
    def _():
        lane = lax.broadcasted_iota(jnp.int32, (1, cross), 1)
        y, z = lane // edge, lane % edge
        if planes % 8:
            for n, ref in enumerate((own_ref, other_ref)):
                for f in range(fields):
                    at = 4 * rows + n * rows + f * planes
                    stack[at : at + planes] = ref[0, f]
        else:
            stack[4 * rows : 5 * rows] = own_ref[0].reshape(rows, cross)
            stack[5 * rows : 6 * rows] = other_ref[0].reshape(rows, cross)
        cells = stack[4 * rows : 6 * rows]
        stack[0 : 2 * rows] = jnp.where(y < edge - 1, pltpu.roll(cells, cross - edge, 1), 0.0) + jnp.where(
            z < edge - 1, pltpu.roll(cells, cross - 1, 1), 0.0
        )
        stack[2 * rows : 4 * rows] = jnp.where(y > 0, pltpu.roll(cells, edge, 1), 0.0) + jnp.where(
            z > 0, pltpu.roll(cells, 1, 1), 0.0
        )
        rim = jnp.concatenate([own_faces[face], other_faces[face]], axis=0)
        high, middle, low = (
            jnp.dot(part, spread_ref[...], preferred_element_type=jnp.float32) for part in split_three(rim)
        )
        ghosts = high + (middle + low)
        base = 6 * rows
        x_face = ghosts[:, 2 * coarse_planes * cross :]
        stack[base : base + 2 * ROWS] = x_face
        stack[base + 2 * ROWS : base + 4 * ROWS] = x_face

        @pl.when(slab > 0)
        def _():
            stack[base : base + fields] = own_low[0]
            stack[base + ROWS : base + ROWS + fields] = other_low[0]

        @pl.when(slab < slabs - 1)
        def _():
            stack[base + 2 * ROWS : base + 2 * ROWS + fields] = own_high[0]
            stack[base + 3 * ROWS : base + 3 * ROWS + fields] = other_high[0]

        base += 4 * ROWS
        for n in range(2 * coarse_planes):
            stack[base + 2 * ROWS * n : base + 2 * ROWS * (n + 1)] = ghosts[:, n * cross : (n + 1) * cross]
        mixed = jnp.dot(weight_ref[...], stack[...], precision=HIGHEST, preferred_element_type=jnp.float32)
        if planes % 8:
            for f in range(fields):
                out_ref[0, f] = mixed[f * planes : (f + 1) * planes]
        else:
            out_ref[0] = mixed.reshape(fields, planes, cross)


def body(boxes, move_dest, parent, coarse, lap_mix, grad_mix, damp_mix):
    box_count = lax.axis_size("box")
    slabs = lax.axis_size("slab")
    slab = lax.axis_index("slab")
    group = lax.axis_index("fld")
    levels, per_device, fields, planes, cross = boxes.shape
    edge = planes * slabs
    coarse_side = edge // 2 + 2
    coarse_planes = planes // 2
    slots = 2 * box_count
    total = move_dest.shape[0]
    coarse_count = coarse.shape[0]

    def exchange(values):
        return lax.all_to_all(values, "box", split_axis=0, concat_axis=0, tiled=True)

    (now,) = pack_levels((0,), boxes, move_dest, slots)
    now = exchange(now)
    faces = pack_faces(coarse, move_dest, parent, slots, slabs, coarse_side, coarse_planes)
    faces = exchange(faces)
    later = pack_levels(tuple(range(1, levels)), boxes, move_dest, slots)
    later = [exchange(values) for values in later]

    swap = [(0, 1), (1, 0)]
    now_other = lax.ppermute(now, "fld", swap)
    faces_other = lax.ppermute(faces, "fld", swap)

    def shifted(values, up):
        pairs = [(s, s + 1) if up else (s + 1, s) for s in range(slabs - 1)]
        crossed = [(2 * a + f, 2 * b + 1 - f) for a, b in pairs for f in range(2)]
        return lax.ppermute(values, "slab", pairs), lax.ppermute(values, ("slab", "fld"), crossed)

    first, last = now[:, :, 0], now[:, :, planes - 1]
    if slabs == 2:
        facing = jnp.where(slab == 0, last, first)
        pairs = [(0, 1), (1, 0)]
        crossed = [(0, 3), (3, 0), (1, 2), (2, 1)]
        low = high = (lax.ppermute(facing, "slab", pairs), lax.ppermute(facing, ("slab", "fld"), crossed))
    else:
        low, high = shifted(last, True), shifted(first, False)

    select, masks = slope_columns(fields, planes, coarse_planes)
    terms = jnp.stack([lap_mix + 0.5 * grad_mix, lap_mix - 0.5 * grad_mix, damp_mix - 6.0 * lap_mix])
    terms = lax.dynamic_slice_in_dim(terms, group * fields, fields, 1)
    terms = jnp.where(group == 0, terms, jnp.roll(terms, fields, axis=2))
    terms = jnp.einsum("tfg,gk->tfk", terms, jnp.asarray(select), precision=HIGHEST)
    width = select.shape[1]
    weight = jnp.sum(terms[:, :, None, :] * jnp.asarray(masks)[:, None], axis=0).reshape(fields * planes, width)
    spread = expand_table(coarse_planes, edge, faces.shape[2])
    spread = jnp.asarray(spread).astype(jnp.bfloat16)

    smem = pl.BlockSpec(memory_space=pltpu.SMEM)
    by_slot = pl.BlockSpec((1, fields, planes, cross), lambda n: (n, 0, 0, 0))
    rim_slot = pl.BlockSpec((1, fields, cross), lambda n: (n, 0, 0))
    whole_faces = pl.BlockSpec(faces.shape, lambda n: (0, 0, 0))
    slope = pl.pallas_call(
        functools.partial(
            slope_kernel, edge, planes, fields, coarse_planes, per_device, total, coarse_count, slots, slabs
        ),
        grid=(slots,),
        out_shape=jax.ShapeDtypeStruct(now.shape, jnp.float32),
        in_specs=[smem, smem, by_slot, by_slot, rim_slot, rim_slot, rim_slot, rim_slot, whole_faces, whole_faces]
        + [pl.BlockSpec(spread.shape, lambda n: (0, 0)), pl.BlockSpec(weight.shape, lambda n: (0, 0))],
        out_specs=by_slot,
        scratch_shapes=[
            pltpu.VMEM((width, cross), jnp.float32),
            pltpu.SMEM((slots,), jnp.int32),
            pltpu.SMEM((slots,), jnp.int32),
        ],
        compiler_params=pltpu.CompilerParams(vmem_limit_bytes=32 * 2 ** 20),
        cost_estimate=pl.CostEstimate(
            flops=12 * slots * weight.shape[0] * width * cross, bytes_accessed=12 * now.size, transcendentals=0
        ),
    )(move_dest, parent, now, now_other, low[0], low[1], high[0], high[1], faces, faces_other, spread, weight)
    return jnp.stack([now] + later), slope


def solution(mesh):
    placed = (
        P(None, ("runs", "box"), "fld", "slab", None),
        P("runs"),
        P("runs"),
        P(("runs", "box"), "fld", None),
        P(),
        P(),
        P(),
    )
    return jax.shard_map(
        body,
        mesh=mesh,
        in_specs=placed,
        out_specs=(
            P(None, ("runs", "box"), "fld", "slab", None),
            P(("runs", "box"), "fld", "slab", None),
        ),
        check_vma=False,
    )
```

```python
import functools

import jax
import jax.numpy as jnp
import numpy as np
from jax import lax
from jax.experimental import pallas as pl
from jax.experimental.pallas import tpu as pltpu
from jax.sharding import PartitionSpec as P

HIGHEST = lax.Precision.HIGHEST
ROWS = 16


def round_up(value, unit):
    return -(-value // unit) * unit


def split_three(values):
    high = values.astype(jnp.bfloat16)
    rest = values - high.astype(jnp.float32)
    middle = rest.astype(jnp.bfloat16)
    low = (rest - middle.astype(jnp.float32)).astype(jnp.bfloat16)
    return high, middle, low


def pack_kernel(per_device, box_count, dest_ref, boxes_ref, *refs):
    outs, table = refs[:box_count], refs[box_count]
    own = lax.axis_index("box")
    for slot in range(2 * box_count):
        table[slot] = -1

    def place(b, carry):
        slot = 2 * dest_ref[own * per_device + b]
        slot = jnp.where(table[slot] >= 0, slot + 1, slot)
        table[slot] = b
        return carry

    lax.fori_loop(0, per_device, place, 0)
    for shift in range(box_count):
        target = lax.rem(own + shift, box_count)
        for k in range(2):
            b = table[2 * target + k]
            values = boxes_ref[0, jnp.maximum(b, 0)]
            outs[shift][k] = jnp.where(b >= 0, values, 0.0)


def pack_level(level, boxes, move_dest, box_count):
    per_device = boxes.shape[1]
    item = boxes.shape[2:]
    size = int(np.prod(item)) * 4
    zero = (0,) * 4
    return pl.pallas_call(
        functools.partial(pack_kernel, per_device, box_count),
        grid=(1,),
        out_shape=[jax.ShapeDtypeStruct((2,) + item, jnp.float32)] * box_count,
        in_specs=[
            pl.BlockSpec(memory_space=pltpu.SMEM),
            pl.BlockSpec((1,) + boxes.shape[1:], lambda n: (level,) + zero),
        ],
        out_specs=[pl.BlockSpec((2,) + item, lambda n: zero)] * box_count,
        scratch_shapes=[pltpu.SMEM((2 * box_count,), jnp.int32)],
        compiler_params=pltpu.CompilerParams(vmem_limit_bytes=32 * 2 ** 20),
        cost_estimate=pl.CostEstimate(
            flops=0, bytes_accessed=(per_device + 2 * box_count) * size, transcendentals=0
        ),
    )(move_dest, boxes)


def settle_kernel(level, box_count, *refs):
    pieces, out_ref, sems = refs[:box_count], refs[-2], refs[-1]
    own = lax.axis_index("box")

    def copy(shift):
        source = lax.rem(own - shift + box_count, box_count)
        return pltpu.make_async_copy(pieces[shift], out_ref.at[level, pl.ds(2 * source, 2)], sems.at[shift])

    for shift in range(box_count):
        copy(shift).start()
    for shift in range(box_count):
        copy(shift).wait()


def settle(level, pieces, moved):
    box_count = len(pieces)
    vmem, anywhere = pl.BlockSpec(memory_space=pltpu.VMEM), pl.BlockSpec(memory_space=pl.ANY)
    return pl.pallas_call(
        functools.partial(settle_kernel, level, box_count),
        out_shape=jax.ShapeDtypeStruct(moved.shape, jnp.float32),
        in_specs=[vmem] * box_count + [anywhere],
        out_specs=anywhere,
        scratch_shapes=[pltpu.SemaphoreType.DMA((box_count,))],
        input_output_aliases={box_count: 0},
        compiler_params=pltpu.CompilerParams(vmem_limit_bytes=32 * 2 ** 20),
        cost_estimate=pl.CostEstimate(
            flops=0, bytes_accessed=8 * box_count * pieces[0].size, transcendentals=0
        ),
    )(*pieces, moved)


def arrive_kernel(box_count, slabs, *refs):
    pieces, edges, sems = refs[:box_count], refs[box_count + 2 : -1], refs[-1]
    now_ref, moved_ref = refs[box_count : box_count + 2]
    own, slab = lax.axis_index("box"), lax.axis_index("slab")
    _, fields, planes, _ = now_ref.shape

    def copy(shift):
        source = lax.rem(own - shift + box_count, box_count)
        return pltpu.make_async_copy(pieces[shift], moved_ref.at[0, pl.ds(2 * source, 2)], sems.at[shift])

    for shift in range(box_count):
        copy(shift).start()
    faced = [jnp.where(slab == 0, planes - 1, 0)] if slabs == 2 else [0, planes - 1]
    for shift in range(box_count):
        source = lax.rem(own - shift + box_count, box_count)
        for k in range(2):
            now_ref[2 * source + k] = pieces[shift][k]
            for edge_ref, plane in zip(edges, faced):
                for f in range(fields):
                    edge_ref[2 * source + k, f : f + 1] = pieces[shift][k, f, pl.ds(plane, 1)]
    for shift in range(box_count):
        copy(shift).wait()


def arrive(pieces, levels, slabs):
    box_count = len(pieces)
    _, fields, planes, cross = pieces[0].shape
    slots = 2 * box_count
    sides = 1 if slabs == 2 else 2
    vmem, anywhere = pl.BlockSpec(memory_space=pltpu.VMEM), pl.BlockSpec(memory_space=pl.ANY)
    shapes = [(slots, fields, planes, cross), (levels, slots, fields, planes, cross)] + [(slots, fields, cross)] * sides
    return pl.pallas_call(
        functools.partial(arrive_kernel, box_count, slabs),
        out_shape=[jax.ShapeDtypeStruct(shape, jnp.float32) for shape in shapes],
        in_specs=[vmem] * box_count,
        out_specs=[vmem, anywhere] + [vmem] * sides,
        scratch_shapes=[pltpu.SemaphoreType.DMA((box_count,))],
        compiler_params=pltpu.CompilerParams(vmem_limit_bytes=32 * 2 ** 20),
        cost_estimate=pl.CostEstimate(
            flops=0, bytes_accessed=12 * box_count * pieces[0].size, transcendentals=0
        ),
    )(*pieces)


def face_tables(coarse_side, coarse_planes, slabs):
    half = coarse_side - 2
    square = coarse_side * coarse_side
    inner = np.arange(half) + 1
    sides = []
    for c in range(coarse_planes):
        base = (c + 1) * square
        sides += [base + inner, base + (coarse_side - 1) * coarse_side + inner]
        sides += [base + inner * coarse_side, base + inner * coarse_side + coarse_side - 1]
    yz = np.concatenate(sides)
    x = (inner[:, None] * coarse_side + inner[None, :]).reshape(-1)
    lanes = round_up(yz.size + x.size, 128)
    table = np.zeros((8, lanes), np.int32)
    table[0] = -(10 ** 6)
    table[0, : yz.size] = yz
    table[1, : yz.size] = coarse_planes * square
    table[0, yz.size : yz.size + x.size] = x
    table[2, yz.size : yz.size + x.size] = (coarse_side - 1) * square
    return table


def expand_table(coarse_planes, edge, lanes):
    half = edge // 2
    cross = edge * edge
    spread = np.zeros((lanes, (2 * coarse_planes + 1) * cross), np.float32)
    for c in range(coarse_planes):
        base = c * 4 * half
        forward, backward = 2 * c * cross, (2 * c + 1) * cross
        for m in range(edge):
            spread[base + m // 2, backward + m] += 1
            spread[base + half + m // 2, forward + (edge - 1) * edge + m] += 1
            spread[base + 2 * half + m // 2, backward + m * edge] += 1
            spread[base + 3 * half + m // 2, forward + m * edge + edge - 1] += 1
    base, to = coarse_planes * 4 * half, 2 * coarse_planes * cross
    for y in range(edge):
        for z in range(edge):
            spread[base + (y // 2) * half + z // 2, to + y * edge + z] = 1
    return spread


def faces_kernel(box_count, total, dest_ref, parent_ref, coarse_ref, table_ref, *refs):
    outs, picked, table = refs[:box_count], refs[-2], refs[-1]
    slots = 2 * box_count
    coarse_count, fields, cells = coarse_ref.shape
    own, slab = lax.axis_index("box"), lax.axis_index("slab")
    picked[...] = jnp.zeros_like(picked)
    for slot in range(slots):
        table[slot] = -1

    def place(b, carry):
        slot = 2 * dest_ref[b]
        local = parent_ref[b] - own * coarse_count

        @pl.when(jnp.logical_and(local >= 0, local < coarse_count))
        def _():
            table[jnp.where(table[slot] >= 0, slot + 1, slot)] = local

        return carry

    lax.fori_loop(0, total, place, 0)
    for slot in range(slots):
        local = table[2 * lax.rem(own + slot // 2, box_count) + slot % 2]

        @pl.when(local >= 0)
        def _():
            picked[slot * ROWS : slot * ROWS + fields, :cells] = coarse_ref[local]

    index = table_ref[0:1] + slab * table_ref[1:2] + jnp.where(slab > 0, table_ref[2:3], 0)
    cell = lax.broadcasted_iota(jnp.int32, (picked.shape[1], index.shape[1]), 0)
    chosen = (cell == index).astype(jnp.float32).astype(jnp.bfloat16)
    high, middle, low = (
        jnp.dot(part, chosen, preferred_element_type=jnp.float32) for part in split_three(picked[...])
    )
    chosen_cells = high + (middle + low)
    for shift in range(box_count):
        for k in range(2):
            at = (2 * shift + k) * ROWS
            outs[shift][k] = chosen_cells[at : at + ROWS]


def pack_faces(coarse, move_dest, parent, slots, slabs, coarse_side, coarse_planes):
    table = face_tables(coarse_side, coarse_planes, slabs)
    lanes = table.shape[1]
    depth = round_up(coarse.shape[2], 128)
    smem, vmem = pl.BlockSpec(memory_space=pltpu.SMEM), pl.BlockSpec(memory_space=pltpu.VMEM)
    return pl.pallas_call(
        functools.partial(faces_kernel, slots // 2, move_dest.shape[0]),
        out_shape=[jax.ShapeDtypeStruct((2, ROWS, lanes), jnp.float32)] * (slots // 2),
        in_specs=[smem, smem, vmem, vmem],
        out_specs=[vmem] * (slots // 2),
        scratch_shapes=[pltpu.VMEM((slots * ROWS, depth), jnp.float32), pltpu.SMEM((slots,), jnp.int32)],
        compiler_params=pltpu.CompilerParams(vmem_limit_bytes=32 * 2 ** 20),
        cost_estimate=pl.CostEstimate(
            flops=6 * slots * ROWS * depth * lanes, bytes_accessed=4 * coarse.size, transcendentals=0
        ),
    )(move_dest, parent, coarse, jnp.asarray(table))


def slope_columns(fields, planes, coarse_planes):
    column_field, forward, backward, centre = [], [], [], []
    p = np.arange(planes)

    def add(field, f, b, c):
        column_field.append(field)
        forward.append(f * np.ones(planes))
        backward.append(b * np.ones(planes))
        centre.append(c * np.ones(planes))

    for f, b, c in ((1, 0, 0), (0, 1, 0), (0, 0, 1)):
        for g in range(2 * fields):
            for q in range(planes):
                here = p == q
                add(g, f * here + c * (p + 1 == q), b * here + c * (p - 1 == q), c * here)
    rows = [g if g < fields else -1 for g in range(ROWS)]
    rows += [fields + g if g < fields else -1 for g in range(ROWS)]
    for g in rows:
        add(g, 0, p == 0, 0)
    for g in rows:
        add(g, p == planes - 1, 0, 0)
    for c in range(coarse_planes):
        for g in rows:
            add(g, p // 2 == c, 0, 0)
        for g in rows:
            add(g, 0, p // 2 == c, 0)
    width = round_up(len(column_field), 128)
    select = np.zeros((2 * fields, width), np.float32)
    masks = np.zeros((3, planes, width), np.float32)
    for k, g in enumerate(column_field):
        if g >= 0:
            select[g, k] = 1
        masks[0, :, k], masks[1, :, k], masks[2, :, k] = forward[k], backward[k], centre[k]
    return select, masks


def slope_kernel(
    edge, planes, fields, coarse_planes, per_device, total, coarse_count, slots, slabs,
    dest_ref, parent_ref, own_ref, other_ref, own_low, other_low, own_high, other_high,
    own_faces, other_faces, spread_ref, weight_ref, out_ref, stack, table, count,
):
    step = pl.program_id(0)
    cross = edge * edge
    rows = fields * planes
    own, slab = lax.axis_index("box"), lax.axis_index("slab")

    @pl.when(step == 0)
    def _():
        stack[...] = jnp.zeros_like(stack)
        for slot in range(slots):
            table[slot] = -1
            count[slot] = 0

        def place(b, carry):
            @pl.when(dest_ref[b] == own)
            def _():
                slot = 2 * (b // per_device)
                owner = parent_ref[b] // coarse_count
                table[jnp.where(table[slot] >= 0, slot + 1, slot)] = 2 * owner + count[owner]
                count[owner] = count[owner] + 1

            return carry

        lax.fori_loop(0, total, place, 0)

    face = table[step]

    @pl.when(face < 0)
    def _():
        out_ref[...] = jnp.zeros_like(out_ref)

    @pl.when(face >= 0)
    def _():
        lane = lax.broadcasted_iota(jnp.int32, (1, cross), 1)
        y, z = lane // edge, lane % edge
        if planes % 8:
            for n, ref in enumerate((own_ref, other_ref)):
                for f in range(fields):
                    at = 4 * rows + n * rows + f * planes
                    stack[at : at + planes] = ref[0, f]
        else:
            stack[4 * rows : 5 * rows] = own_ref[0].reshape(rows, cross)
            stack[5 * rows : 6 * rows] = other_ref[0].reshape(rows, cross)
        cells = stack[4 * rows : 6 * rows]
        stack[0 : 2 * rows] = jnp.where(y < edge - 1, pltpu.roll(cells, cross - edge, 1), 0.0) + jnp.where(
            z < edge - 1, pltpu.roll(cells, cross - 1, 1), 0.0
        )
        stack[2 * rows : 4 * rows] = jnp.where(y > 0, pltpu.roll(cells, edge, 1), 0.0) + jnp.where(
            z > 0, pltpu.roll(cells, 1, 1), 0.0
        )
        shift = lax.rem(own - face // 2 + slots // 2, slots // 2)
        rim = jnp.concatenate([own_faces[shift, face % 2], other_faces[shift, face % 2]], axis=0)
        high, middle, low = (
            jnp.dot(part, spread_ref[...], preferred_element_type=jnp.float32) for part in split_three(rim)
        )
        ghosts = high + (middle + low)
        base = 6 * rows
        x_face = ghosts[:, 2 * coarse_planes * cross :]
        stack[base : base + 2 * ROWS] = x_face
        stack[base + 2 * ROWS : base + 4 * ROWS] = x_face

        @pl.when(slab > 0)
        def _():
            stack[base : base + fields] = own_low[0]
            stack[base + ROWS : base + ROWS + fields] = other_low[0]

        @pl.when(slab < slabs - 1)
        def _():
            stack[base + 2 * ROWS : base + 2 * ROWS + fields] = own_high[0]
            stack[base + 3 * ROWS : base + 3 * ROWS + fields] = other_high[0]

        base += 4 * ROWS
        for n in range(2 * coarse_planes):
            stack[base + 2 * ROWS * n : base + 2 * ROWS * (n + 1)] = ghosts[:, n * cross : (n + 1) * cross]
        mixed = jnp.dot(weight_ref[...], stack[...], precision=HIGHEST, preferred_element_type=jnp.float32)
        if planes % 8:
            for f in range(fields):
                out_ref[0, f] = mixed[f * planes : (f + 1) * planes]
        else:
            out_ref[0] = mixed.reshape(fields, planes, cross)


def body(boxes, move_dest, parent, coarse, lap_mix, grad_mix, damp_mix):
    box_count = lax.axis_size("box")
    slabs = lax.axis_size("slab")
    group = lax.axis_index("fld")
    levels, per_device, fields, planes, cross = boxes.shape
    edge = planes * slabs
    coarse_side = edge // 2 + 2
    coarse_planes = planes // 2
    slots = 2 * box_count
    total = move_dest.shape[0]
    coarse_count = coarse.shape[0]

    def exchange(pieces):
        around = [[(s, (s + shift) % box_count) for s in range(box_count)] for shift in range(box_count)]
        return [pieces[0]] + [lax.ppermute(pieces[n], "box", around[n]) for n in range(1, box_count)]

    arrived = exchange(pack_level(0, boxes, move_dest, box_count))
    faces = exchange(pack_faces(coarse, move_dest, parent, slots, slabs, coarse_side, coarse_planes))
    later = [exchange(pack_level(level, boxes, move_dest, box_count)) for level in range(1, levels)]
    now, moved, *facing = arrive(arrived, levels, slabs)
    faces = jnp.stack(faces)

    swap = [(0, 1), (1, 0)]
    now_other = lax.ppermute(now, "fld", swap)
    faces_other = lax.ppermute(faces, "fld", swap)

    def shifted(values, up):
        pairs = [(s, s + 1) if up else (s + 1, s) for s in range(slabs - 1)]
        crossed = [(2 * a + f, 2 * b + 1 - f) for a, b in pairs for f in range(2)]
        return lax.ppermute(values, "slab", pairs), lax.ppermute(values, ("slab", "fld"), crossed)

    if slabs == 2:
        crossed = [(0, 3), (3, 0), (1, 2), (2, 1)]
        low = high = (lax.ppermute(facing[0], "slab", swap), lax.ppermute(facing[0], ("slab", "fld"), crossed))
    else:
        low, high = shifted(facing[1], True), shifted(facing[0], False)

    select, masks = slope_columns(fields, planes, coarse_planes)
    terms = jnp.stack([lap_mix + 0.5 * grad_mix, lap_mix - 0.5 * grad_mix, damp_mix - 6.0 * lap_mix])
    terms = lax.dynamic_slice_in_dim(terms, group * fields, fields, 1)
    terms = jnp.where(group == 0, terms, jnp.roll(terms, fields, axis=2))
    terms = jnp.einsum("tfg,gk->tfk", terms, jnp.asarray(select), precision=HIGHEST)
    width = select.shape[1]
    weight = jnp.sum(terms[:, :, None, :] * jnp.asarray(masks)[:, None], axis=0).reshape(fields * planes, width)
    spread = expand_table(coarse_planes, edge, faces.shape[3])
    spread = jnp.asarray(spread).astype(jnp.bfloat16)

    smem = pl.BlockSpec(memory_space=pltpu.SMEM)
    by_slot = pl.BlockSpec((1, fields, planes, cross), lambda n: (n, 0, 0, 0))
    rim_slot = pl.BlockSpec((1, fields, cross), lambda n: (n, 0, 0))
    whole_faces = pl.BlockSpec(faces.shape, lambda n: (0, 0, 0, 0))
    slope = pl.pallas_call(
        functools.partial(
            slope_kernel, edge, planes, fields, coarse_planes, per_device, total, coarse_count, slots, slabs
        ),
        grid=(slots,),
        out_shape=jax.ShapeDtypeStruct(now.shape, jnp.float32),
        in_specs=[smem, smem, by_slot, by_slot, rim_slot, rim_slot, rim_slot, rim_slot, whole_faces, whole_faces]
        + [pl.BlockSpec(spread.shape, lambda n: (0, 0)), pl.BlockSpec(weight.shape, lambda n: (0, 0))],
        out_specs=by_slot,
        scratch_shapes=[
            pltpu.VMEM((width, cross), jnp.float32),
            pltpu.SMEM((slots,), jnp.int32),
            pltpu.SMEM((slots,), jnp.int32),
        ],
        compiler_params=pltpu.CompilerParams(vmem_limit_bytes=32 * 2 ** 20),
        cost_estimate=pl.CostEstimate(
            flops=12 * slots * weight.shape[0] * width * cross, bytes_accessed=12 * now.size, transcendentals=0
        ),
    )(move_dest, parent, now, now_other, low[0], low[1], high[0], high[1], faces, faces_other, spread, weight)
    for n, pieces in enumerate(later):
        moved = settle(n + 1, pieces, moved)
    return moved, slope


def solution(mesh):
    placed = (
        P(None, ("runs", "box"), "fld", "slab", None),
        P("runs"),
        P("runs"),
        P(("runs", "box"), "fld", None),
        P(),
        P(),
        P(),
    )
    return jax.shard_map(
        body,
        mesh=mesh,
        in_specs=placed,
        out_specs=(
            P(None, ("runs", "box"), "fld", "slab", None),
            P(("runs", "box"), "fld", "slab", None),
        ),
        check_vma=False,
    )
```

```python
import functools

import jax
import jax.numpy as jnp
import numpy as np
from jax import lax
from jax.experimental import pallas as pl
from jax.experimental.pallas import tpu as pltpu
from jax.sharding import PartitionSpec as P

HIGHEST = lax.Precision.HIGHEST
ROWS = 16


def round_up(value, unit):
    return -(-value // unit) * unit


def split_three(values):
    high = values.astype(jnp.bfloat16)
    rest = values - high.astype(jnp.float32)
    middle = rest.astype(jnp.bfloat16)
    low = (rest - middle.astype(jnp.float32)).astype(jnp.bfloat16)
    return high, middle, low


def place_boxes(per_device, box_count, dest_ref, table):
    own = lax.axis_index("box")
    for slot in range(2 * box_count):
        table[slot] = -1

    def place(b, carry):
        slot = 2 * dest_ref[own * per_device + b]
        table[jnp.where(table[slot] >= 0, slot + 1, slot)] = b
        return carry

    lax.fori_loop(0, per_device, place, 0)


def each_slot(box_count):
    own = lax.axis_index("box")
    for shift in range(box_count):
        for k in range(2):
            yield shift, k, 2 * lax.rem(own + shift, box_count) + k


def first_kernel(per_device, box_count, total, dest_ref, parent_ref, boxes_ref, coarse_ref, table_ref, *refs):
    outs, (chosen, box_table, face_table, sems) = refs[:box_count], refs[box_count:]
    fields, coarse_count, cells = coarse_ref.shape
    own, slab = lax.axis_index("box"), lax.axis_index("slab")
    place_boxes(per_device, box_count, dest_ref, box_table)

    def copy(shift, k, b):
        return pltpu.make_async_copy(
            boxes_ref.at[0, b], outs[shift].at[k, pl.ds(0, fields)], sems.at[shift, k]
        )

    for shift, k, slot in each_slot(box_count):
        b = box_table[slot]

        @pl.when(b >= 0)
        def _():
            copy(shift, k, b).start()

        @pl.when(b < 0)
        def _():
            outs[shift][k, :fields] = jnp.zeros((fields,) + outs[shift].shape[2:], jnp.float32)

    for slot in range(2 * box_count):
        face_table[slot] = -1

    def place(b, carry):
        slot = 2 * dest_ref[b]
        local = parent_ref[b] - own * coarse_count

        @pl.when(jnp.logical_and(local >= 0, local < coarse_count))
        def _():
            face_table[jnp.where(face_table[slot] >= 0, slot + 1, slot)] = local

        return carry

    lax.fori_loop(0, total, place, 0)
    index = table_ref[0:1] + slab * table_ref[1:2] + jnp.where(slab > 0, table_ref[2:3], 0)
    cell = lax.broadcasted_iota(jnp.int32, (cells, index.shape[1]), 0)
    one_hot = (cell == index).astype(jnp.float32).astype(jnp.bfloat16)
    high, middle, low = (
        jnp.dot(part, one_hot, preferred_element_type=jnp.float32)
        for part in split_three(coarse_ref[...].reshape(fields * coarse_count, cells))
    )
    chosen[...] = (high + (middle + low)).reshape(chosen.shape)
    planes = outs[0].shape[2]
    for shift, k, slot in each_slot(box_count):
        local = face_table[slot]
        for row in range(ROWS):
            to = fields + row // planes
            if row < fields:
                values = chosen[row, pl.ds(jnp.maximum(local, 0), 1)]
                values = jnp.where(local >= 0, values, 0.0)
            else:
                values = jnp.zeros((1, chosen.shape[2]), jnp.float32)
            outs[shift][k, to, row % planes : row % planes + 1] = values
    for shift, k, slot in each_slot(box_count):
        b = box_table[slot]

        @pl.when(b >= 0)
        def _():
            copy(shift, k, b).wait()


def pack_first(boxes, coarse, move_dest, parent, table, box_count):
    per_device, fields, planes, cross = boxes.shape[1:]
    coarse = jnp.transpose(coarse, (1, 0, 2))
    smem, vmem = pl.BlockSpec(memory_space=pltpu.SMEM), pl.BlockSpec(memory_space=pltpu.VMEM)
    item = (2, fields + ROWS // planes, planes, cross)
    return pl.pallas_call(
        functools.partial(first_kernel, per_device, box_count, move_dest.shape[0]),
        out_shape=[jax.ShapeDtypeStruct(item, jnp.float32)] * box_count,
        in_specs=[smem, smem, pl.BlockSpec(memory_space=pl.ANY), vmem, vmem],
        out_specs=[vmem] * box_count,
        scratch_shapes=[
            pltpu.VMEM(coarse.shape[:2] + (cross,), jnp.float32),
            pltpu.SMEM((2 * box_count,), jnp.int32),
            pltpu.SMEM((2 * box_count,), jnp.int32),
            pltpu.SemaphoreType.DMA((box_count, 2)),
        ],
        compiler_params=pltpu.CompilerParams(vmem_limit_bytes=48 * 2 ** 20),
        cost_estimate=pl.CostEstimate(
            flops=6 * coarse.size * cross, bytes_accessed=4 * (coarse.size + 2 * boxes.size), transcendentals=0
        ),
    )(move_dest, parent, boxes, coarse, table)


def later_kernel(per_device, box_count, levels, dest_ref, boxes_ref, *refs):
    outs, (table, sems) = refs[:box_count], refs[box_count:]
    place_boxes(per_device, box_count, dest_ref, table)

    def copy(shift, k, b, n):
        return pltpu.make_async_copy(boxes_ref.at[n + 1, b], outs[shift].at[n, k], sems.at[n, shift, k])

    for shift, k, slot in each_slot(box_count):
        b = table[slot]

        @pl.when(b >= 0)
        def _():
            for n in range(levels):
                copy(shift, k, b, n).start()

        @pl.when(b < 0)
        def _():
            for n in range(levels):
                outs[shift][n, k] = jnp.zeros(outs[shift].shape[2:], jnp.float32)

    for shift, k, slot in each_slot(box_count):
        b = table[slot]

        @pl.when(b >= 0)
        def _():
            for n in range(levels):
                copy(shift, k, b, n).wait()


def pack_later(boxes, move_dest, box_count):
    levels, per_device = boxes.shape[0] - 1, boxes.shape[1]
    return pl.pallas_call(
        functools.partial(later_kernel, per_device, box_count, levels),
        out_shape=[jax.ShapeDtypeStruct((levels, 2) + boxes.shape[2:], jnp.float32)] * box_count,
        in_specs=[pl.BlockSpec(memory_space=pltpu.SMEM), pl.BlockSpec(memory_space=pl.ANY)],
        out_specs=[pl.BlockSpec(memory_space=pltpu.VMEM)] * box_count,
        scratch_shapes=[
            pltpu.SMEM((2 * box_count,), jnp.int32),
            pltpu.SemaphoreType.DMA((levels, box_count, 2)),
        ],
        compiler_params=pltpu.CompilerParams(vmem_limit_bytes=48 * 2 ** 20),
        cost_estimate=pl.CostEstimate(flops=0, bytes_accessed=12 * boxes.size, transcendentals=0),
    )(move_dest, boxes)


def source_of(shift, box_count):
    return lax.rem(lax.axis_index("box") - shift + box_count, box_count)


def settle_kernel(levels, box_count, *refs):
    pieces, out_ref, sems = refs[: box_count - 1], refs[-2], refs[-1]

    def copy(shift):
        to = out_ref.at[pl.ds(1, levels), pl.ds(2 * source_of(shift, box_count), 2)]
        return pltpu.make_async_copy(pieces[shift - 1], to, sems.at[shift])

    for shift in range(1, box_count):
        copy(shift).start()
    for shift in range(1, box_count):
        copy(shift).wait()


def settle(pieces, moved, after):
    box_count = len(pieces) + 1
    levels = moved.shape[0] - 1
    vmem, anywhere = pl.BlockSpec(memory_space=pltpu.VMEM), pl.BlockSpec(memory_space=pl.ANY)
    return pl.pallas_call(
        functools.partial(settle_kernel, levels, box_count),
        out_shape=jax.ShapeDtypeStruct(moved.shape, jnp.float32),
        in_specs=[vmem] * (box_count - 1) + [anywhere] * 2,
        out_specs=anywhere,
        scratch_shapes=[pltpu.SemaphoreType.DMA((box_count,))],
        input_output_aliases={box_count - 1: 0},
        compiler_params=pltpu.CompilerParams(vmem_limit_bytes=48 * 2 ** 20),
        cost_estimate=pl.CostEstimate(
            flops=0, bytes_accessed=8 * (box_count - 1) * pieces[0].size, transcendentals=0
        ),
    )(*pieces, moved, after)


def arrive_kernel(box_count, slabs, levels, fields, *refs):
    pieces, own_later, (now_ref, moved_ref) = refs[:box_count], refs[box_count], refs[box_count + 1 : box_count + 3]
    edges, sems = refs[box_count + 3 : -1], refs[-1]
    slab = lax.axis_index("slab")
    planes = now_ref.shape[2]
    copies = []
    for shift in range(box_count):
        to = moved_ref.at[0, pl.ds(2 * source_of(shift, box_count), 2)]
        copies.append(pltpu.make_async_copy(pieces[shift].at[:, pl.ds(0, fields)], to, sems.at[shift]))
    to = moved_ref.at[pl.ds(1, levels - 1), pl.ds(2 * source_of(0, box_count), 2)]
    copies.append(pltpu.make_async_copy(own_later, to, sems.at[box_count]))
    for copy in copies:
        copy.start()
    faced = [jnp.where(slab == 0, planes - 1, 0)] if slabs == 2 else [0, planes - 1]
    for shift in range(box_count):
        source = source_of(shift, box_count)
        for k in range(2):
            now_ref[2 * source + k] = pieces[shift][k]
            for edge_ref, plane in zip(edges, faced):
                for f in range(fields):
                    edge_ref[2 * source + k, f : f + 1] = pieces[shift][k, f, pl.ds(plane, 1)]
    for copy in copies:
        copy.wait()


def arrive(pieces, own_later, slabs):
    box_count = len(pieces)
    _, blocks, planes, cross = pieces[0].shape
    levels, fields = own_later.shape[0] + 1, own_later.shape[2]
    slots = 2 * box_count
    sides = 1 if slabs == 2 else 2
    vmem, anywhere = pl.BlockSpec(memory_space=pltpu.VMEM), pl.BlockSpec(memory_space=pl.ANY)
    shapes = [(slots, blocks, planes, cross), (levels, slots, fields, planes, cross)]
    shapes += [(slots, fields, cross)] * sides
    return pl.pallas_call(
        functools.partial(arrive_kernel, box_count, slabs, levels, fields),
        out_shape=[jax.ShapeDtypeStruct(shape, jnp.float32) for shape in shapes],
        in_specs=[vmem] * (box_count + 1),
        out_specs=[vmem, anywhere] + [vmem] * sides,
        scratch_shapes=[pltpu.SemaphoreType.DMA((box_count + 1,))],
        compiler_params=pltpu.CompilerParams(vmem_limit_bytes=48 * 2 ** 20),
        cost_estimate=pl.CostEstimate(
            flops=0, bytes_accessed=12 * box_count * pieces[0].size, transcendentals=0
        ),
    )(*pieces, own_later)


def face_tables(coarse_side, coarse_planes, lanes):
    half = coarse_side - 2
    square = coarse_side * coarse_side
    inner = np.arange(half) + 1
    sides = []
    for c in range(coarse_planes):
        base = (c + 1) * square
        sides += [base + inner, base + (coarse_side - 1) * coarse_side + inner]
        sides += [base + inner * coarse_side, base + inner * coarse_side + coarse_side - 1]
    yz = np.concatenate(sides)
    x = (inner[:, None] * coarse_side + inner[None, :]).reshape(-1)
    table = np.zeros((8, lanes), np.int32)
    table[0] = -(10 ** 6)
    table[0, : yz.size] = yz
    table[1, : yz.size] = coarse_planes * square
    table[0, yz.size : yz.size + x.size] = x
    table[2, yz.size : yz.size + x.size] = (coarse_side - 1) * square
    return table


def expand_table(coarse_planes, edge, lanes):
    half = edge // 2
    cross = edge * edge
    spread = np.zeros((lanes, (2 * coarse_planes + 1) * cross), np.float32)
    for c in range(coarse_planes):
        base = c * 4 * half
        forward, backward = 2 * c * cross, (2 * c + 1) * cross
        for m in range(edge):
            spread[base + m // 2, backward + m] += 1
            spread[base + half + m // 2, forward + (edge - 1) * edge + m] += 1
            spread[base + 2 * half + m // 2, backward + m * edge] += 1
            spread[base + 3 * half + m // 2, forward + m * edge + edge - 1] += 1
    base, to = coarse_planes * 4 * half, 2 * coarse_planes * cross
    for y in range(edge):
        for z in range(edge):
            spread[base + (y // 2) * half + z // 2, to + y * edge + z] = 1
    return spread


def slope_columns(fields, planes, coarse_planes):
    column_field, forward, backward, centre = [], [], [], []
    p = np.arange(planes)

    def add(field, f, b, c):
        column_field.append(field)
        forward.append(f * np.ones(planes))
        backward.append(b * np.ones(planes))
        centre.append(c * np.ones(planes))

    for f, b, c in ((1, 0, 0), (0, 1, 0), (0, 0, 1)):
        for g in range(2 * fields):
            for q in range(planes):
                here = p == q
                add(g, f * here + c * (p + 1 == q), b * here + c * (p - 1 == q), c * here)
    rows = [g if g < fields else -1 for g in range(ROWS)]
    rows += [fields + g if g < fields else -1 for g in range(ROWS)]
    for g in rows:
        add(g, 0, p == 0, 0)
    for g in rows:
        add(g, p == planes - 1, 0, 0)
    for c in range(coarse_planes):
        for g in rows:
            add(g, p // 2 == c, 0, 0)
        for g in rows:
            add(g, 0, p // 2 == c, 0)
    width = round_up(len(column_field), 128)
    select = np.zeros((2 * fields, width), np.float32)
    masks = np.zeros((3, planes, width), np.float32)
    for k, g in enumerate(column_field):
        if g >= 0:
            select[g, k] = 1
        masks[0, :, k], masks[1, :, k], masks[2, :, k] = forward[k], backward[k], centre[k]
    return select, masks


def slope_kernel(
    edge, planes, fields, coarse_planes, per_device, total, coarse_count, slots, slabs,
    dest_ref, parent_ref, own_ref, other_ref, own_low, other_low, own_high, other_high,
    spread_ref, weight_ref, out_ref, stack, ghosts, table, count,
):
    step = pl.program_id(0)
    cross = edge * edge
    rows = fields * planes
    own, slab = lax.axis_index("box"), lax.axis_index("slab")

    @pl.when(step == 0)
    def _():
        stack[...] = jnp.zeros_like(stack)
        for slot in range(slots):
            table[slot] = -1
            count[slot] = 0

        def place(b, carry):
            @pl.when(dest_ref[b] == own)
            def _():
                slot = 2 * (b // per_device)
                owner = parent_ref[b] // coarse_count
                table[jnp.where(table[slot] >= 0, slot + 1, slot)] = 2 * owner + count[owner]
                count[owner] = count[owner] + 1

            return carry

        lax.fori_loop(0, total, place, 0)
        for slot in range(slots):
            for n, ref in enumerate((own_ref, other_ref)):
                at = (2 * slot + n) * ROWS
                for block in range(ROWS // planes):
                    ghosts[at + block * planes : at + (block + 1) * planes, :cross] = ref[slot, fields + block]
        high, middle, low = (
            jnp.dot(part, spread_ref[...], preferred_element_type=jnp.float32)
            for part in split_three(ghosts[:, :cross])
        )
        ghosts[...] = high + (middle + low)

    face = table[step]

    @pl.when(face < 0)
    def _():
        out_ref[...] = jnp.zeros_like(out_ref)

    @pl.when(face >= 0)
    def _():
        lane = lax.broadcasted_iota(jnp.int32, (1, cross), 1)
        y, z = lane // edge, lane % edge
        for n, ref in enumerate((own_ref, other_ref)):
            at = (4 + n) * rows
            if planes % 8:
                for f in range(fields):
                    stack[at + f * planes : at + (f + 1) * planes] = ref[step, f]
            else:
                stack[at : at + rows] = ref[step, :fields].reshape(rows, cross)
        cells = stack[4 * rows : 6 * rows]
        stack[0 : 2 * rows] = jnp.where(y < edge - 1, pltpu.roll(cells, cross - edge, 1), 0.0) + jnp.where(
            z < edge - 1, pltpu.roll(cells, cross - 1, 1), 0.0
        )
        stack[2 * rows : 4 * rows] = jnp.where(y > 0, pltpu.roll(cells, edge, 1), 0.0) + jnp.where(
            z > 0, pltpu.roll(cells, 1, 1), 0.0
        )
        rim = ghosts[pl.ds(pl.multiple_of(2 * ROWS * face, 2 * ROWS), 2 * ROWS)]
        base = 6 * rows
        x_face = rim[:, 2 * coarse_planes * cross :]
        stack[base : base + 2 * ROWS] = x_face
        stack[base + 2 * ROWS : base + 4 * ROWS] = x_face

        @pl.when(slab > 0)
        def _():
            stack[base : base + fields] = own_low[step]
            stack[base + ROWS : base + ROWS + fields] = other_low[step]

        @pl.when(slab < slabs - 1)
        def _():
            stack[base + 2 * ROWS : base + 2 * ROWS + fields] = own_high[step]
            stack[base + 3 * ROWS : base + 3 * ROWS + fields] = other_high[step]

        base += 4 * ROWS
        for n in range(2 * coarse_planes):
            stack[base + 2 * ROWS * n : base + 2 * ROWS * (n + 1)] = rim[:, n * cross : (n + 1) * cross]
        mixed = jnp.dot(weight_ref[...], stack[...], precision=HIGHEST, preferred_element_type=jnp.float32)
        if planes % 8:
            for f in range(fields):
                out_ref[0, f] = mixed[f * planes : (f + 1) * planes]
        else:
            out_ref[0] = mixed.reshape(fields, planes, cross)


def mixing_weights(mixes, group, fields, planes, coarse_planes):
    lap_mix, grad_mix, damp_mix = mixes
    select, masks = slope_columns(fields, planes, coarse_planes)
    terms = jnp.stack([lap_mix + 0.5 * grad_mix, lap_mix - 0.5 * grad_mix, damp_mix - 6.0 * lap_mix])
    terms = lax.dynamic_slice_in_dim(terms, group * fields, fields, 1)
    terms = jnp.where(group == 0, terms, jnp.roll(terms, fields, axis=2))
    terms = jnp.einsum("tfg,gk->tfk", terms, jnp.asarray(select), precision=HIGHEST)
    return jnp.sum(terms[:, :, None, :] * jnp.asarray(masks)[:, None], axis=0).reshape(fields * planes, -1)


def body(boxes, move_dest, parent, coarse, lap_mix, grad_mix, damp_mix):
    box_count = lax.axis_size("box")
    slabs = lax.axis_size("slab")
    group = lax.axis_index("fld")
    levels, per_device, fields, planes, cross = boxes.shape
    edge = planes * slabs
    coarse_side = edge // 2 + 2
    coarse_planes = planes // 2
    slots = 2 * box_count
    total = move_dest.shape[0]
    coarse_count = coarse.shape[0]

    def exchange(pieces):
        around = [[(s, (s + shift) % box_count) for s in range(box_count)] for shift in range(box_count)]
        return [lax.ppermute(pieces[n], "box", around[n]) for n in range(1, box_count)]

    table = jnp.asarray(face_tables(coarse_side, coarse_planes, cross))
    first = pack_first(boxes, coarse, move_dest, parent, table, box_count)
    later = pack_later(boxes, move_dest, box_count)
    arrived = [first[0]] + exchange(first)
    later_arrived = exchange(later)
    now, moved, *facing = arrive(arrived, later[0], slabs)

    swap = [(0, 1), (1, 0)]
    now_other = lax.ppermute(now, "fld", swap)

    def shifted(values, up):
        pairs = [(s, s + 1) if up else (s + 1, s) for s in range(slabs - 1)]
        crossed = [(2 * a + f, 2 * b + 1 - f) for a, b in pairs for f in range(2)]
        return lax.ppermute(values, "slab", pairs), lax.ppermute(values, ("slab", "fld"), crossed)

    if slabs == 2:
        crossed = [(0, 3), (3, 0), (1, 2), (2, 1)]
        low = high = (lax.ppermute(facing[0], "slab", swap), lax.ppermute(facing[0], ("slab", "fld"), crossed))
    else:
        low, high = shifted(facing[1], True), shifted(facing[0], False)

    weight = mixing_weights((lap_mix, grad_mix, damp_mix), group, fields, planes, coarse_planes)
    spread = jnp.asarray(expand_table(coarse_planes, edge, cross)).astype(jnp.bfloat16)
    smem, vmem = pl.BlockSpec(memory_space=pltpu.SMEM), pl.BlockSpec(memory_space=pltpu.VMEM)
    slope = pl.pallas_call(
        functools.partial(
            slope_kernel, edge, planes, fields, coarse_planes, per_device, total, coarse_count, slots, slabs
        ),
        grid=(slots,),
        out_shape=jax.ShapeDtypeStruct((slots, fields, planes, cross), jnp.float32),
        in_specs=[smem, smem] + [vmem] * 8,
        out_specs=pl.BlockSpec((1, fields, planes, cross), lambda n: (n, 0, 0, 0)),
        scratch_shapes=[
            pltpu.VMEM((weight.shape[1], cross), jnp.float32),
            pltpu.VMEM((2 * ROWS * slots, spread.shape[1]), jnp.float32),
            pltpu.SMEM((slots,), jnp.int32),
            pltpu.SMEM((slots,), jnp.int32),
        ],
        compiler_params=pltpu.CompilerParams(vmem_limit_bytes=48 * 2 ** 20),
        cost_estimate=pl.CostEstimate(
            flops=12 * slots * weight.size * cross, bytes_accessed=12 * now.size, transcendentals=0
        ),
    )(move_dest, parent, now, now_other, low[0], low[1], high[0], high[1], spread, weight)
    return settle(later_arrived, moved, slope), slope


def solution(mesh):
    placed = (
        P(None, ("runs", "box"), "fld", "slab", None),
        P("runs"),
        P("runs"),
        P(("runs", "box"), "fld", None),
        P(),
        P(),
        P(),
    )
    return jax.shard_map(
        body,
        mesh=mesh,
        in_specs=placed,
        out_specs=(
            P(None, ("runs", "box"), "fld", "slab", None),
            P(("runs", "box"), "fld", "slab", None),
        ),
        check_vma=False,
    )
```

```python
import functools

import jax
import jax.numpy as jnp
import numpy as np
from jax import lax
from jax.experimental import pallas as pl
from jax.experimental.pallas import tpu as pltpu
from jax.sharding import PartitionSpec as P

HIGHEST = lax.Precision.HIGHEST
ROWS = 16


def round_up(value, unit):
    return -(-value // unit) * unit


def split_three(values):
    high = values.astype(jnp.bfloat16)
    rest = values - high.astype(jnp.float32)
    middle = rest.astype(jnp.bfloat16)
    low = (rest - middle.astype(jnp.float32)).astype(jnp.bfloat16)
    return high, middle, low


def place_boxes(per_device, box_count, dest_ref, table):
    own = lax.axis_index("box")
    for slot in range(2 * box_count):
        table[slot] = -1

    def place(b, carry):
        slot = 2 * dest_ref[own * per_device + b]
        table[jnp.where(table[slot] >= 0, slot + 1, slot)] = b
        return carry

    lax.fori_loop(0, per_device, place, 0)


def each_slot(box_count):
    own = lax.axis_index("box")
    for shift in range(box_count):
        for k in range(2):
            yield shift, k, 2 * lax.rem(own + shift, box_count) + k


def first_kernel(per_device, box_count, edge, dest_ref, parent_ref, boxes_ref, coarse_ref, *refs):
    outs, (shells, chosen, dest, parent, box_table, face_table, sems, in_sems) = refs[:box_count], refs[box_count:]
    fields, coarse_count, cells = coarse_ref.shape
    planes, cross = outs[0].shape[2:]
    own, slab = lax.axis_index("box"), lax.axis_index("slab")
    fetches = [
        pltpu.make_async_copy(coarse_ref, shells, in_sems.at[0]),
        pltpu.make_async_copy(dest_ref, dest, in_sems.at[1]),
        pltpu.make_async_copy(parent_ref, parent, in_sems.at[2]),
    ]
    for fetch in fetches:
        fetch.start()
    index = face_cells(lax.broadcasted_iota(jnp.int32, (1, cross), 1), edge, planes // 2, slab)
    cell = lax.broadcasted_iota(jnp.int32, (cells, cross), 0)
    one_hot = (cell == index).astype(jnp.float32).astype(jnp.bfloat16)
    fetches[1].wait()
    place_boxes(per_device, box_count, dest, box_table)

    def copy(shift, k, b):
        return pltpu.make_async_copy(
            boxes_ref.at[0, b], outs[shift].at[k, pl.ds(0, fields)], sems.at[shift, k]
        )

    for shift, k, slot in each_slot(box_count):
        b = box_table[slot]

        @pl.when(b >= 0)
        def _():
            copy(shift, k, b).start()

        @pl.when(b < 0)
        def _():
            outs[shift][k, :fields] = jnp.zeros((fields, planes, cross), jnp.float32)

    for slot in range(2 * box_count):
        face_table[slot] = -1
    fetches[2].wait()

    def place(b, carry):
        slot = 2 * dest[b]
        local = parent[b] - own * coarse_count

        @pl.when(jnp.logical_and(local >= 0, local < coarse_count))
        def _():
            face_table[jnp.where(face_table[slot] >= 0, slot + 1, slot)] = local

        return carry

    lax.fori_loop(0, dest.shape[0], place, 0)
    fetches[0].wait()
    high, middle, low = (
        jnp.dot(part, one_hot, preferred_element_type=jnp.float32)
        for part in split_three(shells[...].reshape(fields * coarse_count, cells))
    )
    chosen[...] = (high + (middle + low)).reshape(chosen.shape)
    for shift, k, slot in each_slot(box_count):
        local = face_table[slot]
        for row in range(ROWS):
            to = fields + row // planes
            if row < fields:
                values = chosen[row, pl.ds(jnp.maximum(local, 0), 1)]
                values = jnp.where(local >= 0, values, 0.0)
            else:
                values = jnp.zeros((1, cross), jnp.float32)
            outs[shift][k, to, row % planes : row % planes + 1] = values
    for shift, k, slot in each_slot(box_count):
        b = box_table[slot]

        @pl.when(b >= 0)
        def _():
            copy(shift, k, b).wait()


def pack_first(boxes, coarse, move_dest, parent, edge, box_count):
    per_device, fields, planes, cross = boxes.shape[1:]
    coarse = jnp.transpose(coarse, (1, 0, 2))
    hbm, vmem = pl.BlockSpec(memory_space=pltpu.HBM), pl.BlockSpec(memory_space=pltpu.VMEM)
    item = (2, fields + ROWS // planes, planes, cross)
    return pl.pallas_call(
        functools.partial(first_kernel, per_device, box_count, edge),
        out_shape=[jax.ShapeDtypeStruct(item, jnp.float32)] * box_count,
        in_specs=[hbm] * 4,
        out_specs=[vmem] * box_count,
        scratch_shapes=[
            pltpu.VMEM(coarse.shape, jnp.float32),
            pltpu.VMEM(coarse.shape[:2] + (cross,), jnp.float32),
            pltpu.SMEM(move_dest.shape, jnp.int32),
            pltpu.SMEM(parent.shape, jnp.int32),
            pltpu.SMEM((2 * box_count,), jnp.int32),
            pltpu.SMEM((2 * box_count,), jnp.int32),
            pltpu.SemaphoreType.DMA((box_count, 2)),
            pltpu.SemaphoreType.DMA((3,)),
        ],
        compiler_params=pltpu.CompilerParams(vmem_limit_bytes=48 * 2 ** 20),
        cost_estimate=pl.CostEstimate(
            flops=6 * coarse.size * cross, bytes_accessed=4 * (coarse.size + 2 * boxes.size), transcendentals=0
        ),
    )(move_dest, parent, boxes, coarse)


def later_kernel(per_device, box_count, levels, dest_ref, boxes_ref, *refs):
    outs, (table, sems) = refs[:box_count], refs[box_count:]
    place_boxes(per_device, box_count, dest_ref, table)

    def copy(shift, k, b, n):
        return pltpu.make_async_copy(boxes_ref.at[n + 1, b], outs[shift].at[n, k], sems.at[n, shift, k])

    for shift, k, slot in each_slot(box_count):
        b = table[slot]

        @pl.when(b >= 0)
        def _():
            for n in range(levels):
                copy(shift, k, b, n).start()

        @pl.when(b < 0)
        def _():
            for n in range(levels):
                outs[shift][n, k] = jnp.zeros(outs[shift].shape[2:], jnp.float32)

    for shift, k, slot in each_slot(box_count):
        b = table[slot]

        @pl.when(b >= 0)
        def _():
            for n in range(levels):
                copy(shift, k, b, n).wait()


def pack_later(boxes, move_dest, box_count):
    levels, per_device = boxes.shape[0] - 1, boxes.shape[1]
    return pl.pallas_call(
        functools.partial(later_kernel, per_device, box_count, levels),
        out_shape=[jax.ShapeDtypeStruct((levels, 2) + boxes.shape[2:], jnp.float32)] * box_count,
        in_specs=[pl.BlockSpec(memory_space=pltpu.SMEM), pl.BlockSpec(memory_space=pltpu.HBM)],
        out_specs=[pl.BlockSpec(memory_space=pltpu.VMEM)] * box_count,
        scratch_shapes=[
            pltpu.SMEM((2 * box_count,), jnp.int32),
            pltpu.SemaphoreType.DMA((levels, box_count, 2)),
        ],
        compiler_params=pltpu.CompilerParams(vmem_limit_bytes=48 * 2 ** 20),
        cost_estimate=pl.CostEstimate(flops=0, bytes_accessed=12 * boxes.size, transcendentals=0),
    )(move_dest, boxes)


def source_of(shift, box_count):
    return lax.rem(lax.axis_index("box") - shift + box_count, box_count)


def settle_kernel(levels, box_count, *refs):
    pieces, out_ref, sems = refs[: box_count - 1], refs[-2], refs[-1]

    def copy(shift):
        to = out_ref.at[pl.ds(1, levels), pl.ds(2 * source_of(shift, box_count), 2)]
        return pltpu.make_async_copy(pieces[shift - 1], to, sems.at[shift])

    for shift in range(1, box_count):
        copy(shift).start()
    for shift in range(1, box_count):
        copy(shift).wait()


def settle(pieces, moved, after):
    box_count = len(pieces) + 1
    levels = moved.shape[0] - 1
    vmem, anywhere = pl.BlockSpec(memory_space=pltpu.VMEM), pl.BlockSpec(memory_space=pl.ANY)
    return pl.pallas_call(
        functools.partial(settle_kernel, levels, box_count),
        out_shape=jax.ShapeDtypeStruct(moved.shape, jnp.float32),
        in_specs=[vmem] * (box_count - 1) + [anywhere, vmem],
        out_specs=anywhere,
        scratch_shapes=[pltpu.SemaphoreType.DMA((box_count,))],
        input_output_aliases={box_count - 1: 0},
        compiler_params=pltpu.CompilerParams(vmem_limit_bytes=48 * 2 ** 20),
        cost_estimate=pl.CostEstimate(
            flops=0, bytes_accessed=8 * (box_count - 1) * pieces[0].size, transcendentals=0
        ),
    )(*pieces, moved, after)


def arrive_kernel(box_count, slabs, levels, fields, *refs):
    pieces, own_later, (now_ref, moved_ref) = refs[:box_count], refs[box_count], refs[box_count + 1 : box_count + 3]
    edges, sems = refs[box_count + 3 : -1], refs[-1]
    slab = lax.axis_index("slab")
    planes = now_ref.shape[2]
    copies = []
    for shift in range(box_count):
        to = moved_ref.at[0, pl.ds(2 * source_of(shift, box_count), 2)]
        copies.append(pltpu.make_async_copy(pieces[shift].at[:, pl.ds(0, fields)], to, sems.at[shift]))
    to = moved_ref.at[pl.ds(1, levels - 1), pl.ds(2 * source_of(0, box_count), 2)]
    copies.append(pltpu.make_async_copy(own_later, to, sems.at[box_count]))
    for copy in copies:
        copy.start()
    faced = [jnp.where(slab == 0, planes - 1, 0)] if slabs == 2 else [0, planes - 1]
    for shift in range(box_count):
        source = source_of(shift, box_count)
        for k in range(2):
            now_ref[2 * source + k] = pieces[shift][k]
            for edge_ref, plane in zip(edges, faced):
                for f in range(fields):
                    edge_ref[2 * source + k, f : f + 1] = pieces[shift][k, f, pl.ds(plane, 1)]
    for copy in copies:
        copy.wait()


def arrive(pieces, own_later, slabs):
    box_count = len(pieces)
    _, blocks, planes, cross = pieces[0].shape
    levels, fields = own_later.shape[0] + 1, own_later.shape[2]
    slots = 2 * box_count
    sides = 1 if slabs == 2 else 2
    vmem, anywhere = pl.BlockSpec(memory_space=pltpu.VMEM), pl.BlockSpec(memory_space=pl.ANY)
    shapes = [(slots, blocks, planes, cross), (levels, slots, fields, planes, cross)]
    shapes += [(slots, fields, cross)] * sides
    return pl.pallas_call(
        functools.partial(arrive_kernel, box_count, slabs, levels, fields),
        out_shape=[jax.ShapeDtypeStruct(shape, jnp.float32) for shape in shapes],
        in_specs=[vmem] * (box_count + 1),
        out_specs=[vmem, anywhere] + [vmem] * sides,
        scratch_shapes=[pltpu.SemaphoreType.DMA((box_count + 1,))],
        compiler_params=pltpu.CompilerParams(vmem_limit_bytes=48 * 2 ** 20),
        cost_estimate=pl.CostEstimate(
            flops=0, bytes_accessed=12 * box_count * pieces[0].size, transcendentals=0
        ),
    )(*pieces, own_later)


def face_cells(lane, edge, coarse_planes, slab):
    half, side = edge // 2, edge // 2 + 2
    plane, m = lane // (4 * half), lane % half + 1
    which = (lane // half) % 4
    rim = jnp.where(which == 0, m, jnp.where(which == 1, (side - 1) * side + m, m * side))
    rim = jnp.where(which == 3, rim + side - 1, rim) + (slab * coarse_planes + plane + 1) * side * side
    t = lane - 4 * half * coarse_planes
    x_rim = jnp.where(slab > 0, (side - 1) * side * side, 0) + (t // half + 1) * side + m
    return jnp.where(t < 0, rim, jnp.where(t < half * half, x_rim, -1))


def expand_table(coarse_planes, edge, lanes):
    half = edge // 2
    cross = edge * edge
    spread = np.zeros((lanes, (2 * coarse_planes + 1) * cross), np.float32)
    for c in range(coarse_planes):
        base = c * 4 * half
        forward, backward = 2 * c * cross, (2 * c + 1) * cross
        for m in range(edge):
            spread[base + m // 2, backward + m] += 1
            spread[base + half + m // 2, forward + (edge - 1) * edge + m] += 1
            spread[base + 2 * half + m // 2, backward + m * edge] += 1
            spread[base + 3 * half + m // 2, forward + m * edge + edge - 1] += 1
    base, to = coarse_planes * 4 * half, 2 * coarse_planes * cross
    for y in range(edge):
        for z in range(edge):
            spread[base + (y // 2) * half + z // 2, to + y * edge + z] = 1
    return spread


def slope_columns(fields, planes, coarse_planes):
    column_field, forward, backward, centre = [], [], [], []
    p = np.arange(planes)

    def add(field, f, b, c):
        column_field.append(field)
        forward.append(f * np.ones(planes))
        backward.append(b * np.ones(planes))
        centre.append(c * np.ones(planes))

    for f, b, c in ((1, 0, 0), (0, 1, 0), (0, 0, 1)):
        for g in range(2 * fields):
            for q in range(planes):
                here = p == q
                add(g, f * here + c * (p + 1 == q), b * here + c * (p - 1 == q), c * here)
    rows = [g if g < fields else -1 for g in range(ROWS)]
    rows += [fields + g if g < fields else -1 for g in range(ROWS)]
    for g in rows:
        add(g, 0, p == 0, 0)
    for g in rows:
        add(g, p == planes - 1, 0, 0)
    for c in range(coarse_planes):
        for g in rows:
            add(g, p // 2 == c, 0, 0)
        for g in rows:
            add(g, 0, p // 2 == c, 0)
    width = round_up(len(column_field), 128)
    select = np.zeros((2 * fields, width), np.float32)
    masks = np.zeros((3, planes, width), np.float32)
    for k, g in enumerate(column_field):
        if g >= 0:
            select[g, k] = 1
        masks[0, :, k], masks[1, :, k], masks[2, :, k] = forward[k], backward[k], centre[k]
    return select, masks


def slope_kernel(
    edge, planes, fields, coarse_planes, per_device, total, coarse_count, slots, slabs,
    dest_ref, parent_ref, own_ref, other_ref, own_low, other_low, own_high, other_high,
    spread_ref, weight_ref, out_ref, token_ref, stack, ghosts, table, count,
):
    step = pl.program_id(0)
    cross = edge * edge
    rows = fields * planes
    own, slab = lax.axis_index("box"), lax.axis_index("slab")

    @pl.when(step == 0)
    def _():
        token_ref[...] = jnp.zeros_like(token_ref)
        stack[...] = jnp.zeros_like(stack)
        for slot in range(slots):
            table[slot] = -1
            count[slot] = 0

        def place(b, carry):
            @pl.when(dest_ref[b] == own)
            def _():
                slot = 2 * (b // per_device)
                owner = parent_ref[b] // coarse_count
                table[jnp.where(table[slot] >= 0, slot + 1, slot)] = 2 * owner + count[owner]
                count[owner] = count[owner] + 1

            return carry

        lax.fori_loop(0, total, place, 0)
        for slot in range(slots):
            for n, ref in enumerate((own_ref, other_ref)):
                at = (2 * slot + n) * ROWS
                for block in range(ROWS // planes):
                    ghosts[at + block * planes : at + (block + 1) * planes, :cross] = ref[slot, fields + block]
        high, middle, low = (
            jnp.dot(part, spread_ref[...], preferred_element_type=jnp.float32)
            for part in split_three(ghosts[:, :cross])
        )
        ghosts[...] = high + (middle + low)

    face = table[step]

    @pl.when(face < 0)
    def _():
        out_ref[...] = jnp.zeros_like(out_ref)

    @pl.when(face >= 0)
    def _():
        lane = lax.broadcasted_iota(jnp.int32, (1, cross), 1)
        y, z = lane // edge, lane % edge
        for n, ref in enumerate((own_ref, other_ref)):
            at = (4 + n) * rows
            if planes % 8:
                for f in range(fields):
                    stack[at + f * planes : at + (f + 1) * planes] = ref[step, f]
            else:
                stack[at : at + rows] = ref[step, :fields].reshape(rows, cross)
        cells = stack[4 * rows : 6 * rows]
        stack[0 : 2 * rows] = jnp.where(y < edge - 1, pltpu.roll(cells, cross - edge, 1), 0.0) + jnp.where(
            z < edge - 1, pltpu.roll(cells, cross - 1, 1), 0.0
        )
        stack[2 * rows : 4 * rows] = jnp.where(y > 0, pltpu.roll(cells, edge, 1), 0.0) + jnp.where(
            z > 0, pltpu.roll(cells, 1, 1), 0.0
        )
        rim = ghosts[pl.ds(pl.multiple_of(2 * ROWS * face, 2 * ROWS), 2 * ROWS)]
        base = 6 * rows
        x_face = rim[:, 2 * coarse_planes * cross :]
        stack[base : base + 2 * ROWS] = x_face
        stack[base + 2 * ROWS : base + 4 * ROWS] = x_face

        @pl.when(slab > 0)
        def _():
            stack[base : base + fields] = own_low[step]
            stack[base + ROWS : base + ROWS + fields] = other_low[step]

        @pl.when(slab < slabs - 1)
        def _():
            stack[base + 2 * ROWS : base + 2 * ROWS + fields] = own_high[step]
            stack[base + 3 * ROWS : base + 3 * ROWS + fields] = other_high[step]

        base += 4 * ROWS
        for n in range(2 * coarse_planes):
            stack[base + 2 * ROWS * n : base + 2 * ROWS * (n + 1)] = rim[:, n * cross : (n + 1) * cross]
        mixed = jnp.dot(weight_ref[...], stack[...], precision=HIGHEST, preferred_element_type=jnp.float32)
        if planes % 8:
            for f in range(fields):
                out_ref[0, f] = mixed[f * planes : (f + 1) * planes]
        else:
            out_ref[0] = mixed.reshape(fields, planes, cross)


def mixing_weights(mixes, group, fields, planes, coarse_planes):
    lap_mix, grad_mix, damp_mix = mixes
    select, masks = slope_columns(fields, planes, coarse_planes)
    terms = jnp.stack([lap_mix + 0.5 * grad_mix, lap_mix - 0.5 * grad_mix, damp_mix - 6.0 * lap_mix])
    terms = lax.dynamic_slice_in_dim(terms, group * fields, fields, 1)
    terms = jnp.where(group == 0, terms, jnp.roll(terms, fields, axis=2))
    terms = jnp.einsum("tfg,gk->tfk", terms, jnp.asarray(select), precision=HIGHEST)
    return jnp.sum(terms[:, :, None, :] * jnp.asarray(masks)[:, None], axis=0).reshape(fields * planes, -1)


def body(boxes, move_dest, parent, coarse, lap_mix, grad_mix, damp_mix):
    box_count = lax.axis_size("box")
    slabs = lax.axis_size("slab")
    group = lax.axis_index("fld")
    levels, per_device, fields, planes, cross = boxes.shape
    edge = planes * slabs
    coarse_planes = planes // 2
    slots = 2 * box_count
    total = move_dest.shape[0]
    coarse_count = coarse.shape[0]

    def send(piece, shift):
        return lax.ppermute(piece, "box", [(s, (s + shift) % box_count) for s in range(box_count)])

    first = pack_first(boxes, coarse, move_dest, parent, edge, box_count)
    later = pack_later(boxes, move_dest, box_count)
    arrived, later_arrived = [first[0]], []
    for shift in range(1, box_count):
        arrived.append(send(first[shift], shift))
    for shift in range(1, box_count):
        held, arrived[shift] = lax.optimization_barrier((later[shift], arrived[shift]))
        later_arrived.append(send(held, shift))
    now, moved, *facing = arrive(arrived, later[0], slabs)

    swap = [(0, 1), (1, 0)]
    now_other = lax.ppermute(now, "fld", swap)

    def shifted(values, up):
        pairs = [(s, s + 1) if up else (s + 1, s) for s in range(slabs - 1)]
        crossed = [(2 * a + f, 2 * b + 1 - f) for a, b in pairs for f in range(2)]
        return lax.ppermute(values, "slab", pairs), lax.ppermute(values, ("slab", "fld"), crossed)

    if slabs == 2:
        crossed = [(0, 3), (3, 0), (1, 2), (2, 1)]
        low = high = (lax.ppermute(facing[0], "slab", swap), lax.ppermute(facing[0], ("slab", "fld"), crossed))
    else:
        low, high = shifted(facing[1], True), shifted(facing[0], False)

    weight = mixing_weights((lap_mix, grad_mix, damp_mix), group, fields, planes, coarse_planes)
    spread = jnp.asarray(expand_table(coarse_planes, edge, cross)).astype(jnp.bfloat16)
    smem, vmem = pl.BlockSpec(memory_space=pltpu.SMEM), pl.BlockSpec(memory_space=pltpu.VMEM)
    slope, token = pl.pallas_call(
        functools.partial(
            slope_kernel, edge, planes, fields, coarse_planes, per_device, total, coarse_count, slots, slabs
        ),
        grid=(slots,),
        out_shape=[
            jax.ShapeDtypeStruct((slots, fields, planes, cross), jnp.float32),
            jax.ShapeDtypeStruct((8, 128), jnp.float32),
        ],
        in_specs=[smem, smem] + [vmem] * 8,
        out_specs=[pl.BlockSpec((1, fields, planes, cross), lambda n: (n, 0, 0, 0)), vmem],
        scratch_shapes=[
            pltpu.VMEM((weight.shape[1], cross), jnp.float32),
            pltpu.VMEM((2 * ROWS * slots, spread.shape[1]), jnp.float32),
            pltpu.SMEM((slots,), jnp.int32),
            pltpu.SMEM((slots,), jnp.int32),
        ],
        compiler_params=pltpu.CompilerParams(vmem_limit_bytes=48 * 2 ** 20),
        cost_estimate=pl.CostEstimate(
            flops=12 * slots * weight.size * cross, bytes_accessed=12 * now.size, transcendentals=0
        ),
    )(move_dest, parent, now, now_other, low[0], low[1], high[0], high[1], spread, weight)
    return settle(later_arrived, moved, token), slope


def solution(mesh):
    placed = (
        P(None, ("runs", "box"), "fld", "slab", None),
        P("runs"),
        P("runs"),
        P(("runs", "box"), "fld", None),
        P(),
        P(),
        P(),
    )
    return jax.shard_map(
        body,
        mesh=mesh,
        in_specs=placed,
        out_specs=(
            P(None, ("runs", "box"), "fld", "slab", None),
            P(("runs", "box"), "fld", "slab", None),
        ),
        check_vma=False,
    )
```

```python
import functools

import jax
import jax.numpy as jnp
import numpy as np
from jax import lax
from jax.experimental import pallas as pl
from jax.experimental.pallas import tpu as pltpu
from jax.sharding import PartitionSpec as P

HIGHEST = lax.Precision.HIGHEST
ROWS = 16


def round_up(value, unit):
    return -(-value // unit) * unit


def split_three(values):
    high = values.astype(jnp.bfloat16)
    rest = values - high.astype(jnp.float32)
    middle = rest.astype(jnp.bfloat16)
    low = (rest - middle.astype(jnp.float32)).astype(jnp.bfloat16)
    return high, middle, low


def place_boxes(per_device, box_count, dest_ref, table):
    own = lax.axis_index("box")
    for slot in range(2 * box_count):
        table[slot] = -1

    def place(b, carry):
        slot = 2 * dest_ref[own * per_device + b]
        table[jnp.where(table[slot] >= 0, slot + 1, slot)] = b
        return carry

    lax.fori_loop(0, per_device, place, 0)


def each_slot(box_count):
    own = lax.axis_index("box")
    for shift in range(box_count):
        for k in range(2):
            yield shift, k, 2 * lax.rem(own + shift, box_count) + k


def first_kernel(per_device, box_count, edge, dest_ref, parent_ref, boxes_ref, coarse_ref, *refs):
    outs, (shells, chosen, dest, parent, box_table, face_table, sems, in_sems) = refs[:box_count], refs[box_count:]
    fields, coarse_count, cells = coarse_ref.shape
    planes, cross = outs[0].shape[2:]
    own, slab = lax.axis_index("box"), lax.axis_index("slab")
    fetches = [
        pltpu.make_async_copy(coarse_ref, shells, in_sems.at[0]),
        pltpu.make_async_copy(dest_ref, dest, in_sems.at[1]),
        pltpu.make_async_copy(parent_ref, parent, in_sems.at[2]),
    ]
    for fetch in fetches:
        fetch.start()
    index = face_cells(lax.broadcasted_iota(jnp.int32, (1, cross), 1), edge, planes // 2, slab)
    cell = lax.broadcasted_iota(jnp.int32, (cells, cross), 0)
    one_hot = (cell == index).astype(jnp.float32).astype(jnp.bfloat16)
    fetches[1].wait()
    place_boxes(per_device, box_count, dest, box_table)

    def copy(shift, k, b):
        return pltpu.make_async_copy(
            boxes_ref.at[0, b], outs[shift].at[k, pl.ds(0, fields)], sems.at[shift, k]
        )

    for shift, k, slot in each_slot(box_count):
        b = box_table[slot]

        @pl.when(b >= 0)
        def _():
            copy(shift, k, b).start()

        @pl.when(b < 0)
        def _():
            outs[shift][k, :fields] = jnp.zeros((fields, planes, cross), jnp.float32)

    for slot in range(2 * box_count):
        face_table[slot] = -1
    fetches[2].wait()

    def place(b, carry):
        slot = 2 * dest[b]
        local = parent[b] - own * coarse_count

        @pl.when(jnp.logical_and(local >= 0, local < coarse_count))
        def _():
            face_table[jnp.where(face_table[slot] >= 0, slot + 1, slot)] = local

        return carry

    lax.fori_loop(0, dest.shape[0], place, 0)
    fetches[0].wait()
    high, middle, low = (
        jnp.dot(part, one_hot, preferred_element_type=jnp.float32)
        for part in split_three(shells[...].reshape(fields * coarse_count, cells))
    )
    chosen[...] = (high + (middle + low)).reshape(chosen.shape)
    for shift, k, slot in each_slot(box_count):
        local = face_table[slot]
        for row in range(ROWS):
            to = fields + row // planes
            if row < fields:
                values = chosen[row, pl.ds(jnp.maximum(local, 0), 1)]
                values = jnp.where(local >= 0, values, 0.0)
            else:
                values = jnp.zeros((1, cross), jnp.float32)
            outs[shift][k, to, row % planes : row % planes + 1] = values
    for shift, k, slot in each_slot(box_count):
        b = box_table[slot]

        @pl.when(b >= 0)
        def _():
            copy(shift, k, b).wait()


def pack_first(boxes, coarse, move_dest, parent, edge, box_count):
    per_device, fields, planes, cross = boxes.shape[1:]
    coarse = jnp.transpose(coarse, (1, 0, 2))
    hbm, vmem = pl.BlockSpec(memory_space=pltpu.HBM), pl.BlockSpec(memory_space=pltpu.VMEM)
    item = (2, fields + ROWS // planes, planes, cross)
    return pl.pallas_call(
        functools.partial(first_kernel, per_device, box_count, edge),
        out_shape=[jax.ShapeDtypeStruct(item, jnp.float32)] * box_count,
        in_specs=[hbm] * 4,
        out_specs=[vmem] * box_count,
        scratch_shapes=[
            pltpu.VMEM(coarse.shape, jnp.float32),
            pltpu.VMEM(coarse.shape[:2] + (cross,), jnp.float32),
            pltpu.SMEM(move_dest.shape, jnp.int32),
            pltpu.SMEM(parent.shape, jnp.int32),
            pltpu.SMEM((2 * box_count,), jnp.int32),
            pltpu.SMEM((2 * box_count,), jnp.int32),
            pltpu.SemaphoreType.DMA((box_count, 2)),
            pltpu.SemaphoreType.DMA((3,)),
        ],
        cost_estimate=pl.CostEstimate(
            flops=6 * coarse.size * cross, bytes_accessed=4 * (coarse.size + 2 * boxes.size), transcendentals=0
        ),
    )(move_dest, parent, boxes, coarse)


def later_kernel(per_device, box_count, levels, dest_ref, boxes_ref, *refs):
    outs, (dest, table, sems, in_sem) = refs[:box_count], refs[box_count:]
    fetch = pltpu.make_async_copy(dest_ref, dest, in_sem)
    fetch.start()
    fetch.wait()
    place_boxes(per_device, box_count, dest, table)

    def copy(shift, k, b, n):
        return pltpu.make_async_copy(boxes_ref.at[n + 1, b], outs[shift].at[n, k], sems.at[n, shift, k])

    for shift, k, slot in each_slot(box_count):
        b = table[slot]

        @pl.when(b >= 0)
        def _():
            for n in range(levels):
                copy(shift, k, b, n).start()

        @pl.when(b < 0)
        def _():
            for n in range(levels):
                outs[shift][n, k] = jnp.zeros(outs[shift].shape[2:], jnp.float32)

    for shift, k, slot in each_slot(box_count):
        b = table[slot]

        @pl.when(b >= 0)
        def _():
            for n in range(levels):
                copy(shift, k, b, n).wait()


def pack_later(boxes, move_dest, box_count):
    levels, per_device = boxes.shape[0] - 1, boxes.shape[1]
    return pl.pallas_call(
        functools.partial(later_kernel, per_device, box_count, levels),
        out_shape=[jax.ShapeDtypeStruct((levels, 2) + boxes.shape[2:], jnp.float32)] * box_count,
        in_specs=[pl.BlockSpec(memory_space=pltpu.HBM)] * 2,
        out_specs=[pl.BlockSpec(memory_space=pltpu.VMEM)] * box_count,
        scratch_shapes=[
            pltpu.SMEM(move_dest.shape, jnp.int32),
            pltpu.SMEM((2 * box_count,), jnp.int32),
            pltpu.SemaphoreType.DMA((levels, box_count, 2)),
            pltpu.SemaphoreType.DMA,
        ],
        cost_estimate=pl.CostEstimate(flops=0, bytes_accessed=12 * boxes.size, transcendentals=0),
    )(move_dest, boxes)


def source_of(shift, box_count):
    return lax.rem(lax.axis_index("box") - shift + box_count, box_count)


def settle_kernel(levels, box_count, *refs):
    pieces, out_ref, sems = refs[: box_count - 1], refs[-2], refs[-1]

    def copy(shift):
        to = out_ref.at[pl.ds(1, levels), pl.ds(2 * source_of(shift, box_count), 2)]
        return pltpu.make_async_copy(pieces[shift - 1], to, sems.at[shift])

    for shift in range(1, box_count):
        copy(shift).start()
    for shift in range(1, box_count):
        copy(shift).wait()


def settle(pieces, moved, after):
    box_count = len(pieces) + 1
    levels = moved.shape[0] - 1
    vmem, anywhere = pl.BlockSpec(memory_space=pltpu.VMEM), pl.BlockSpec(memory_space=pl.ANY)
    return pl.pallas_call(
        functools.partial(settle_kernel, levels, box_count),
        out_shape=jax.ShapeDtypeStruct(moved.shape, jnp.float32),
        in_specs=[vmem] * (box_count - 1) + [anywhere, vmem],
        out_specs=anywhere,
        scratch_shapes=[pltpu.SemaphoreType.DMA((box_count,))],
        input_output_aliases={box_count - 1: 0},
        compiler_params=pltpu.CompilerParams(vmem_limit_bytes=48 * 2 ** 20),
        cost_estimate=pl.CostEstimate(
            flops=0, bytes_accessed=8 * (box_count - 1) * pieces[0].size, transcendentals=0
        ),
    )(*pieces, moved, after)


def arrive_kernel(box_count, slabs, levels, fields, *refs):
    pieces, own_later, (now_ref, moved_ref) = refs[:box_count], refs[box_count], refs[box_count + 1 : box_count + 3]
    edges, sems = refs[box_count + 3 : -1], refs[-1]
    slab = lax.axis_index("slab")
    planes = now_ref.shape[2]
    copies = []
    for shift in range(box_count):
        to = moved_ref.at[0, pl.ds(2 * source_of(shift, box_count), 2)]
        copies.append(pltpu.make_async_copy(pieces[shift].at[:, pl.ds(0, fields)], to, sems.at[shift]))
    to = moved_ref.at[pl.ds(1, levels - 1), pl.ds(2 * source_of(0, box_count), 2)]
    copies.append(pltpu.make_async_copy(own_later, to, sems.at[box_count]))
    for copy in copies:
        copy.start()
    faced = [jnp.where(slab == 0, planes - 1, 0)] if slabs == 2 else [0, planes - 1]
    for shift in range(box_count):
        source = source_of(shift, box_count)
        for k in range(2):
            now_ref[2 * source + k] = pieces[shift][k]
            for edge_ref, plane in zip(edges, faced):
                for f in range(fields):
                    edge_ref[2 * source + k, f : f + 1] = pieces[shift][k, f, pl.ds(plane, 1)]
    for copy in copies:
        copy.wait()


def arrive(pieces, own_later, slabs):
    box_count = len(pieces)
    _, blocks, planes, cross = pieces[0].shape
    levels, fields = own_later.shape[0] + 1, own_later.shape[2]
    slots = 2 * box_count
    sides = 1 if slabs == 2 else 2
    vmem, anywhere = pl.BlockSpec(memory_space=pltpu.VMEM), pl.BlockSpec(memory_space=pl.ANY)
    shapes = [(slots, blocks, planes, cross), (levels, slots, fields, planes, cross)]
    shapes += [(slots, fields, cross)] * sides
    return pl.pallas_call(
        functools.partial(arrive_kernel, box_count, slabs, levels, fields),
        out_shape=[jax.ShapeDtypeStruct(shape, jnp.float32) for shape in shapes],
        in_specs=[vmem] * (box_count + 1),
        out_specs=[vmem, anywhere] + [vmem] * sides,
        scratch_shapes=[pltpu.SemaphoreType.DMA((box_count + 1,))],
        compiler_params=pltpu.CompilerParams(vmem_limit_bytes=48 * 2 ** 20),
        cost_estimate=pl.CostEstimate(
            flops=0, bytes_accessed=12 * box_count * pieces[0].size, transcendentals=0
        ),
    )(*pieces, own_later)


def face_cells(lane, edge, coarse_planes, slab):
    half, side = edge // 2, edge // 2 + 2
    plane, m = lane // (4 * half), lane % half + 1
    which = (lane // half) % 4
    rim = jnp.where(which == 0, m, jnp.where(which == 1, (side - 1) * side + m, m * side))
    rim = jnp.where(which == 3, rim + side - 1, rim) + (slab * coarse_planes + plane + 1) * side * side
    t = lane - 4 * half * coarse_planes
    x_rim = jnp.where(slab > 0, (side - 1) * side * side, 0) + (t // half + 1) * side + m
    return jnp.where(t < 0, rim, jnp.where(t < half * half, x_rim, -1))


def expand_table(coarse_planes, edge, lanes):
    half = edge // 2
    cross = edge * edge
    spread = np.zeros((lanes, (2 * coarse_planes + 1) * cross), np.float32)
    for c in range(coarse_planes):
        base = c * 4 * half
        forward, backward = 2 * c * cross, (2 * c + 1) * cross
        for m in range(edge):
            spread[base + m // 2, backward + m] += 1
            spread[base + half + m // 2, forward + (edge - 1) * edge + m] += 1
            spread[base + 2 * half + m // 2, backward + m * edge] += 1
            spread[base + 3 * half + m // 2, forward + m * edge + edge - 1] += 1
    base, to = coarse_planes * 4 * half, 2 * coarse_planes * cross
    for y in range(edge):
        for z in range(edge):
            spread[base + (y // 2) * half + z // 2, to + y * edge + z] = 1
    return spread


def slope_columns(fields, planes, coarse_planes):
    column_field, forward, backward, centre = [], [], [], []
    p = np.arange(planes)

    def add(field, f, b, c):
        column_field.append(field)
        forward.append(f * np.ones(planes))
        backward.append(b * np.ones(planes))
        centre.append(c * np.ones(planes))

    for f, b, c in ((1, 0, 0), (0, 1, 0), (0, 0, 1)):
        for g in range(2 * fields):
            for q in range(planes):
                here = p == q
                add(g, f * here + c * (p + 1 == q), b * here + c * (p - 1 == q), c * here)
    rows = [g if g < fields else -1 for g in range(ROWS)]
    rows += [fields + g if g < fields else -1 for g in range(ROWS)]
    for g in rows:
        add(g, 0, p == 0, 0)
    for g in rows:
        add(g, p == planes - 1, 0, 0)
    for c in range(coarse_planes):
        for g in rows:
            add(g, p // 2 == c, 0, 0)
        for g in rows:
            add(g, 0, p // 2 == c, 0)
    width = round_up(len(column_field), 128)
    select = np.zeros((2 * fields, width), np.float32)
    masks = np.zeros((3, planes, width), np.float32)
    for k, g in enumerate(column_field):
        if g >= 0:
            select[g, k] = 1
        masks[0, :, k], masks[1, :, k], masks[2, :, k] = forward[k], backward[k], centre[k]
    return select, masks


def slope_kernel(
    edge, planes, fields, coarse_planes, per_device, total, coarse_count, slots, slabs,
    dest_ref, parent_ref, own_ref, other_ref, own_low, other_low, own_high, other_high,
    spread_ref, weight_ref, out_ref, token_ref, stack, ghosts, table, count,
):
    step = pl.program_id(0)
    cross = edge * edge
    rows = fields * planes
    own, slab = lax.axis_index("box"), lax.axis_index("slab")

    @pl.when(step == 0)
    def _():
        token_ref[...] = jnp.zeros_like(token_ref)
        stack[...] = jnp.zeros_like(stack)
        for slot in range(slots):
            table[slot] = -1
            count[slot] = 0

        def place(b, carry):
            @pl.when(dest_ref[b] == own)
            def _():
                slot = 2 * (b // per_device)
                owner = parent_ref[b] // coarse_count
                table[jnp.where(table[slot] >= 0, slot + 1, slot)] = 2 * owner + count[owner]
                count[owner] = count[owner] + 1

            return carry

        lax.fori_loop(0, total, place, 0)
        for slot in range(slots):
            for n, ref in enumerate((own_ref, other_ref)):
                at = (2 * slot + n) * ROWS
                for block in range(ROWS // planes):
                    ghosts[at + block * planes : at + (block + 1) * planes, :cross] = ref[slot, fields + block]
        high, middle, low = (
            jnp.dot(part, spread_ref[...], preferred_element_type=jnp.float32)
            for part in split_three(ghosts[:, :cross])
        )
        ghosts[...] = high + (middle + low)

    face = table[step]

    @pl.when(face < 0)
    def _():
        out_ref[...] = jnp.zeros_like(out_ref)

    @pl.when(face >= 0)
    def _():
        lane = lax.broadcasted_iota(jnp.int32, (1, cross), 1)
        y, z = lane // edge, lane % edge
        for n, ref in enumerate((own_ref, other_ref)):
            at = (4 + n) * rows
            if planes % 8:
                for f in range(fields):
                    stack[at + f * planes : at + (f + 1) * planes] = ref[step, f]
            else:
                stack[at : at + rows] = ref[step, :fields].reshape(rows, cross)
        cells = stack[4 * rows : 6 * rows]
        stack[0 : 2 * rows] = jnp.where(y < edge - 1, pltpu.roll(cells, cross - edge, 1), 0.0) + jnp.where(
            z < edge - 1, pltpu.roll(cells, cross - 1, 1), 0.0
        )
        stack[2 * rows : 4 * rows] = jnp.where(y > 0, pltpu.roll(cells, edge, 1), 0.0) + jnp.where(
            z > 0, pltpu.roll(cells, 1, 1), 0.0
        )
        rim = ghosts[pl.ds(pl.multiple_of(2 * ROWS * face, 2 * ROWS), 2 * ROWS)]
        base = 6 * rows
        x_face = rim[:, 2 * coarse_planes * cross :]
        stack[base : base + 2 * ROWS] = x_face
        stack[base + 2 * ROWS : base + 4 * ROWS] = x_face

        @pl.when(slab > 0)
        def _():
            stack[base : base + fields] = own_low[step]
            stack[base + ROWS : base + ROWS + fields] = other_low[step]

        @pl.when(slab < slabs - 1)
        def _():
            stack[base + 2 * ROWS : base + 2 * ROWS + fields] = own_high[step]
            stack[base + 3 * ROWS : base + 3 * ROWS + fields] = other_high[step]

        base += 4 * ROWS
        for n in range(2 * coarse_planes):
            stack[base + 2 * ROWS * n : base + 2 * ROWS * (n + 1)] = rim[:, n * cross : (n + 1) * cross]
        mixed = jnp.dot(weight_ref[...], stack[...], precision=HIGHEST, preferred_element_type=jnp.float32)
        if planes % 8:
            for f in range(fields):
                out_ref[0, f] = mixed[f * planes : (f + 1) * planes]
        else:
            out_ref[0] = mixed.reshape(fields, planes, cross)


def mixing_weights(mixes, group, fields, planes, coarse_planes):
    lap_mix, grad_mix, damp_mix = mixes
    select, masks = slope_columns(fields, planes, coarse_planes)
    terms = jnp.stack([lap_mix + 0.5 * grad_mix, lap_mix - 0.5 * grad_mix, damp_mix - 6.0 * lap_mix])
    terms = lax.dynamic_slice_in_dim(terms, group * fields, fields, 1)
    terms = jnp.where(group == 0, terms, jnp.roll(terms, fields, axis=2))
    terms = jnp.einsum("tfg,gk->tfk", terms, jnp.asarray(select), precision=HIGHEST)
    return jnp.sum(terms[:, :, None, :] * jnp.asarray(masks)[:, None], axis=0).reshape(fields * planes, -1)


def body(boxes, move_dest, parent, coarse, lap_mix, grad_mix, damp_mix):
    box_count = lax.axis_size("box")
    slabs = lax.axis_size("slab")
    group = lax.axis_index("fld")
    levels, per_device, fields, planes, cross = boxes.shape
    edge = planes * slabs
    coarse_planes = planes // 2
    slots = 2 * box_count
    total = move_dest.shape[0]
    coarse_count = coarse.shape[0]

    def send(piece, shift):
        return lax.ppermute(piece, "box", [(s, (s + shift) % box_count) for s in range(box_count)])

    first = pack_first(boxes, coarse, move_dest, parent, edge, box_count)
    arrived = [first[0]] + [send(first[shift], shift) for shift in range(1, box_count)]
    later = pack_later(boxes, move_dest, box_count)
    later_arrived = [send(later[1], 1)]
    for shift in range(2, box_count):
        held, arrived[shift - 1] = lax.optimization_barrier((later[shift], arrived[shift - 1]))
        later_arrived.append(send(held, shift))
    now, moved, *facing = arrive(arrived, later[0], slabs)

    swap = [(0, 1), (1, 0)]
    now_other = lax.ppermute(now, "fld", swap)

    def shifted(values, up):
        pairs = [(s, s + 1) if up else (s + 1, s) for s in range(slabs - 1)]
        crossed = [(2 * a + f, 2 * b + 1 - f) for a, b in pairs for f in range(2)]
        return lax.ppermute(values, "slab", pairs), lax.ppermute(values, ("slab", "fld"), crossed)

    if slabs == 2:
        crossed = [(0, 3), (3, 0), (1, 2), (2, 1)]
        low = high = (lax.ppermute(facing[0], "slab", swap), lax.ppermute(facing[0], ("slab", "fld"), crossed))
    else:
        low, high = shifted(facing[1], True), shifted(facing[0], False)

    weight = mixing_weights((lap_mix, grad_mix, damp_mix), group, fields, planes, coarse_planes)
    spread = jnp.asarray(expand_table(coarse_planes, edge, cross)).astype(jnp.bfloat16)
    smem, vmem = pl.BlockSpec(memory_space=pltpu.SMEM), pl.BlockSpec(memory_space=pltpu.VMEM)
    slope, token = pl.pallas_call(
        functools.partial(
            slope_kernel, edge, planes, fields, coarse_planes, per_device, total, coarse_count, slots, slabs
        ),
        grid=(slots,),
        out_shape=[
            jax.ShapeDtypeStruct((slots, fields, planes, cross), jnp.float32),
            jax.ShapeDtypeStruct((8, 128), jnp.float32),
        ],
        in_specs=[smem, smem] + [vmem] * 8,
        out_specs=[pl.BlockSpec((1, fields, planes, cross), lambda n: (n, 0, 0, 0)), vmem],
        scratch_shapes=[
            pltpu.VMEM((weight.shape[1], cross), jnp.float32),
            pltpu.VMEM((2 * ROWS * slots, spread.shape[1]), jnp.float32),
            pltpu.SMEM((slots,), jnp.int32),
            pltpu.SMEM((slots,), jnp.int32),
        ],
        compiler_params=pltpu.CompilerParams(vmem_limit_bytes=48 * 2 ** 20),
        cost_estimate=pl.CostEstimate(
            flops=12 * slots * weight.size * cross, bytes_accessed=12 * now.size, transcendentals=0
        ),
    )(move_dest, parent, now, now_other, low[0], low[1], high[0], high[1], spread, weight)
    return settle(later_arrived, moved, token), slope


def solution(mesh):
    placed = (
        P(None, ("runs", "box"), "fld", "slab", None),
        P("runs"),
        P("runs"),
        P(("runs", "box"), "fld", None),
        P(),
        P(),
        P(),
    )
    return jax.shard_map(
        body,
        mesh=mesh,
        in_specs=placed,
        out_specs=(
            P(None, ("runs", "box"), "fld", "slab", None),
            P(("runs", "box"), "fld", "slab", None),
        ),
        check_vma=False,
    )
```

```python
import functools

import jax
import jax.numpy as jnp
import numpy as np
from jax import lax
from jax.experimental import pallas as pl
from jax.experimental.pallas import tpu as pltpu
from jax.sharding import PartitionSpec as P

HIGHEST = lax.Precision.HIGHEST
ROWS = 16


def round_up(value, unit):
    return -(-value // unit) * unit


def split_three(values):
    high = values.astype(jnp.bfloat16)
    rest = values - high.astype(jnp.float32)
    middle = rest.astype(jnp.bfloat16)
    low = (rest - middle.astype(jnp.float32)).astype(jnp.bfloat16)
    return high, middle, low


def place_boxes(per_device, box_count, dest_ref, table):
    own = lax.axis_index("box")
    for slot in range(2 * box_count):
        table[slot] = -1

    def place(b, carry):
        slot = 2 * dest_ref[own * per_device + b]
        table[jnp.where(table[slot] >= 0, slot + 1, slot)] = b
        return carry

    lax.fori_loop(0, per_device, place, 0)


def partner(own, turn, box_count):
    return own ^ turn


def each_slot(box_count):
    own = lax.axis_index("box")
    for turn in range(box_count):
        for k in range(2):
            yield turn, k, 2 * partner(own, turn, box_count) + k


def first_kernel(per_device, box_count, edge, dest_ref, parent_ref, boxes_ref, coarse_ref, *refs):
    outs, (shells, chosen, dest, parent, box_table, face_table, sems, in_sems) = refs[:box_count], refs[box_count:]
    fields, coarse_count, cells = coarse_ref.shape
    planes, cross = outs[0].shape[2:]
    own, slab = lax.axis_index("box"), lax.axis_index("slab")
    fetches = [
        pltpu.make_async_copy(coarse_ref, shells, in_sems.at[0]),
        pltpu.make_async_copy(dest_ref, dest, in_sems.at[1]),
        pltpu.make_async_copy(parent_ref, parent, in_sems.at[2]),
    ]
    for fetch in fetches:
        fetch.start()
    index = face_cells(lax.broadcasted_iota(jnp.int32, (1, cross), 1), edge, planes // 2, slab)
    cell = lax.broadcasted_iota(jnp.int32, (cells, cross), 0)
    one_hot = (cell == index).astype(jnp.float32).astype(jnp.bfloat16)
    fetches[1].wait()
    place_boxes(per_device, box_count, dest, box_table)

    def copy(shift, k, b):
        return pltpu.make_async_copy(
            boxes_ref.at[0, b], outs[shift].at[k, pl.ds(0, fields)], sems.at[shift, k]
        )

    for shift, k, slot in each_slot(box_count):
        b = box_table[slot]

        @pl.when(b >= 0)
        def _():
            copy(shift, k, b).start()

        @pl.when(b < 0)
        def _():
            outs[shift][k, :fields] = jnp.zeros((fields, planes, cross), jnp.float32)

    for slot in range(2 * box_count):
        face_table[slot] = -1
    fetches[2].wait()

    def place(b, carry):
        slot = 2 * dest[b]
        local = parent[b] - own * coarse_count

        @pl.when(jnp.logical_and(local >= 0, local < coarse_count))
        def _():
            face_table[jnp.where(face_table[slot] >= 0, slot + 1, slot)] = local

        return carry

    lax.fori_loop(0, dest.shape[0], place, 0)
    fetches[0].wait()
    high, middle, low = (
        jnp.dot(part, one_hot, preferred_element_type=jnp.float32)
        for part in split_three(shells[...].reshape(fields * coarse_count, cells))
    )
    chosen[...] = (high + (middle + low)).reshape(chosen.shape)
    for shift, k, slot in each_slot(box_count):
        local = face_table[slot]
        for row in range(ROWS):
            to = fields + row // planes
            if row < fields:
                values = chosen[row, pl.ds(jnp.maximum(local, 0), 1)]
                values = jnp.where(local >= 0, values, 0.0)
            else:
                values = jnp.zeros((1, cross), jnp.float32)
            outs[shift][k, to, row % planes : row % planes + 1] = values
    for shift, k, slot in each_slot(box_count):
        b = box_table[slot]

        @pl.when(b >= 0)
        def _():
            copy(shift, k, b).wait()


def pack_first(boxes, coarse, move_dest, parent, edge, box_count):
    per_device, fields, planes, cross = boxes.shape[1:]
    coarse = jnp.transpose(coarse, (1, 0, 2))
    hbm, vmem = pl.BlockSpec(memory_space=pltpu.HBM), pl.BlockSpec(memory_space=pltpu.VMEM)
    item = (2, fields + ROWS // planes, planes, cross)
    return pl.pallas_call(
        functools.partial(first_kernel, per_device, box_count, edge),
        out_shape=[jax.ShapeDtypeStruct(item, jnp.float32)] * box_count,
        in_specs=[hbm] * 4,
        out_specs=[vmem] * box_count,
        scratch_shapes=[
            pltpu.VMEM(coarse.shape, jnp.float32),
            pltpu.VMEM(coarse.shape[:2] + (cross,), jnp.float32),
            pltpu.SMEM(move_dest.shape, jnp.int32),
            pltpu.SMEM(parent.shape, jnp.int32),
            pltpu.SMEM((2 * box_count,), jnp.int32),
            pltpu.SMEM((2 * box_count,), jnp.int32),
            pltpu.SemaphoreType.DMA((box_count, 2)),
            pltpu.SemaphoreType.DMA((3,)),
        ],
        cost_estimate=pl.CostEstimate(
            flops=6 * coarse.size * cross, bytes_accessed=4 * (coarse.size + 2 * boxes.size), transcendentals=0
        ),
    )(move_dest, parent, boxes, coarse)


def later_kernel(per_device, box_count, levels, dest_ref, boxes_ref, after_ref, *refs):
    outs, moved_ref = refs[: box_count - 1], refs[box_count - 1]
    stay, dest, table, sems, in_sem, out_sem = refs[box_count:]
    own = lax.axis_index("box")
    fetch = pltpu.make_async_copy(dest_ref, dest, in_sem)
    fetch.start()
    fetch.wait()
    place_boxes(per_device, box_count, dest, table)

    def copies(turn, k, b):
        for n in range(0 if turn == 0 else 1, levels):
            to = stay.at[n, k] if turn == 0 else outs[turn - 1].at[n - 1, k]
            yield pltpu.make_async_copy(boxes_ref.at[n, b], to, sems.at[n, turn, k])

    for turn, k, slot in each_slot(box_count):
        b = table[slot]

        @pl.when(b >= 0)
        def _():
            for copy in copies(turn, k, b):
                copy.start()

        @pl.when(b < 0)
        def _():
            to = stay if turn == 0 else outs[turn - 1]
            for n in range(to.shape[0]):
                to[n, k] = jnp.zeros(to.shape[2:], jnp.float32)

    for turn, k, slot in each_slot(box_count):
        b = table[slot]

        @pl.when(b >= 0)
        def _():
            for copy in copies(turn, k, b):
                copy.wait()

        if (turn, k) == (0, 1):
            settled = pltpu.make_async_copy(stay, moved_ref.at[:, pl.ds(2 * own, 2)], out_sem)
            settled.start()
    settled.wait()


def pack_later(boxes, move_dest, after, box_count):
    levels, per_device = boxes.shape[:2]
    item = boxes.shape[2:]
    hbm, vmem = pl.BlockSpec(memory_space=pltpu.HBM), pl.BlockSpec(memory_space=pltpu.VMEM)
    return pl.pallas_call(
        functools.partial(later_kernel, per_device, box_count, levels),
        out_shape=[jax.ShapeDtypeStruct((levels - 1, 2) + item, jnp.float32)] * (box_count - 1)
        + [jax.ShapeDtypeStruct((levels, 2 * box_count) + item, jnp.float32)],
        in_specs=[hbm] * 3,
        out_specs=[vmem] * (box_count - 1) + [hbm],
        scratch_shapes=[
            pltpu.VMEM((levels, 2) + item, jnp.float32),
            pltpu.SMEM(move_dest.shape, jnp.int32),
            pltpu.SMEM((2 * box_count,), jnp.int32),
            pltpu.SemaphoreType.DMA((levels, box_count, 2)),
            pltpu.SemaphoreType.DMA,
            pltpu.SemaphoreType.DMA,
        ],
        cost_estimate=pl.CostEstimate(flops=0, bytes_accessed=12 * boxes.size, transcendentals=0),
    )(move_dest, boxes, after)


def settle_later(piece, turn, moved_ref, sem):
    source = partner(lax.axis_index("box"), turn, moved_ref.shape[1] // 2)
    to = moved_ref.at[pl.ds(1, moved_ref.shape[0] - 1), pl.ds(2 * source, 2)]
    return pltpu.make_async_copy(piece, to, sem)


def settle_kernel(turns, *refs):
    out_ref, sems = refs[-2:]
    copies = [settle_later(refs[n], turn, out_ref, sems.at[n]) for n, turn in enumerate(turns)]
    for copy in copies:
        copy.start()
    for copy in copies:
        copy.wait()


def settle(turns, pieces, moved, after):
    count = len(pieces)
    vmem, hbm = pl.BlockSpec(memory_space=pltpu.VMEM), pl.BlockSpec(memory_space=pltpu.HBM)
    return pl.pallas_call(
        functools.partial(settle_kernel, turns),
        out_shape=jax.ShapeDtypeStruct(moved.shape, jnp.float32),
        in_specs=[vmem] * count + [hbm, vmem],
        out_specs=hbm,
        scratch_shapes=[pltpu.SemaphoreType.DMA((count,))],
        input_output_aliases={count: 0},
        compiler_params=pltpu.CompilerParams(vmem_limit_bytes=48 * 2 ** 20),
        cost_estimate=pl.CostEstimate(
            flops=0, bytes_accessed=8 * count * pieces[0].size, transcendentals=0
        ),
    )(*pieces, moved, after)


def arrive_kernel(box_count, slabs, early, fields, *refs):
    pieces, later = refs[:box_count], refs[box_count : box_count + len(early)]
    now_ref, moved_ref, *edges, sems = refs[box_count + len(early) + 1 :]
    own, slab = lax.axis_index("box"), lax.axis_index("slab")
    planes = now_ref.shape[2]
    mine = pltpu.make_async_copy(pieces[0], now_ref.at[pl.ds(2 * own, 2)], sems.at[0])
    mine.start()
    copies = []
    for turn in range(1, box_count):
        to = moved_ref.at[0, pl.ds(2 * partner(own, turn, box_count), 2)]
        copies.append(pltpu.make_async_copy(pieces[turn].at[:, pl.ds(0, fields)], to, sems.at[turn]))
    for n, turn in enumerate(early):
        copies.append(settle_later(later[n], turn, moved_ref, sems.at[box_count + n]))
    for copy in copies:
        copy.start()
    faced = [jnp.where(slab == 0, planes - 1, 0)] if slabs == 2 else [0, planes - 1]

    def cut(source):
        for k in range(2):
            for edge_ref, plane in zip(edges, faced):
                for f in range(fields):
                    edge_ref[2 * source + k, f : f + 1] = now_ref[2 * source + k, f, pl.ds(plane, 1)]

    for turn in range(1, box_count):
        source = partner(own, turn, box_count)
        for k in range(2):
            now_ref[2 * source + k] = pieces[turn][k]
        cut(source)
    mine.wait()
    cut(own)
    for copy in copies:
        copy.wait()


def arrive(pieces, early, later, moved, slabs):
    box_count = len(pieces)
    _, blocks, planes, cross = pieces[0].shape
    fields = moved.shape[2]
    slots = 2 * box_count
    sides = 1 if slabs == 2 else 2
    vmem, hbm = pl.BlockSpec(memory_space=pltpu.VMEM), pl.BlockSpec(memory_space=pltpu.HBM)
    shapes = [(slots, blocks, planes, cross), moved.shape] + [(slots, fields, cross)] * sides
    count = box_count + len(later)
    return pl.pallas_call(
        functools.partial(arrive_kernel, box_count, slabs, early, fields),
        out_shape=[jax.ShapeDtypeStruct(shape, jnp.float32) for shape in shapes],
        in_specs=[hbm] + [vmem] * (count - 1) + [hbm],
        out_specs=[vmem, hbm] + [vmem] * sides,
        scratch_shapes=[pltpu.SemaphoreType.DMA((count,))],
        input_output_aliases={count: 1},
        compiler_params=pltpu.CompilerParams(vmem_limit_bytes=48 * 2 ** 20),
        cost_estimate=pl.CostEstimate(
            flops=0, bytes_accessed=12 * box_count * pieces[0].size, transcendentals=0
        ),
    )(*pieces, *later, moved)


def face_cells(lane, edge, coarse_planes, slab):
    half, side = edge // 2, edge // 2 + 2
    plane, m = lane // (4 * half), lane % half + 1
    which = (lane // half) % 4
    rim = jnp.where(which == 0, m, jnp.where(which == 1, (side - 1) * side + m, m * side))
    rim = jnp.where(which == 3, rim + side - 1, rim) + (slab * coarse_planes + plane + 1) * side * side
    t = lane - 4 * half * coarse_planes
    x_rim = jnp.where(slab > 0, (side - 1) * side * side, 0) + (t // half + 1) * side + m
    return jnp.where(t < 0, rim, jnp.where(t < half * half, x_rim, -1))


def expand_table(coarse_planes, edge, lanes):
    half = edge // 2
    cross = edge * edge
    spread = np.zeros((lanes, (2 * coarse_planes + 1) * cross), np.float32)
    for c in range(coarse_planes):
        base = c * 4 * half
        forward, backward = 2 * c * cross, (2 * c + 1) * cross
        for m in range(edge):
            spread[base + m // 2, backward + m] += 1
            spread[base + half + m // 2, forward + (edge - 1) * edge + m] += 1
            spread[base + 2 * half + m // 2, backward + m * edge] += 1
            spread[base + 3 * half + m // 2, forward + m * edge + edge - 1] += 1
    base, to = coarse_planes * 4 * half, 2 * coarse_planes * cross
    for y in range(edge):
        for z in range(edge):
            spread[base + (y // 2) * half + z // 2, to + y * edge + z] = 1
    return spread


def slope_columns(fields, planes, coarse_planes):
    column_field, forward, backward, centre = [], [], [], []
    p = np.arange(planes)

    def add(field, f, b, c):
        column_field.append(field)
        forward.append(f * np.ones(planes))
        backward.append(b * np.ones(planes))
        centre.append(c * np.ones(planes))

    for f, b, c in ((1, 0, 0), (0, 1, 0), (0, 0, 1)):
        for g in range(2 * fields):
            for q in range(planes):
                here = p == q
                add(g, f * here + c * (p + 1 == q), b * here + c * (p - 1 == q), c * here)
    rows = [g if g < fields else -1 for g in range(ROWS)]
    rows += [fields + g if g < fields else -1 for g in range(ROWS)]
    for g in rows:
        add(g, 0, p == 0, 0)
    for g in rows:
        add(g, p == planes - 1, 0, 0)
    for c in range(coarse_planes):
        for g in rows:
            add(g, p // 2 == c, 0, 0)
        for g in rows:
            add(g, 0, p // 2 == c, 0)
    width = round_up(len(column_field), 128)
    select = np.zeros((2 * fields, width), np.float32)
    masks = np.zeros((3, planes, width), np.float32)
    for k, g in enumerate(column_field):
        if g >= 0:
            select[g, k] = 1
        masks[0, :, k], masks[1, :, k], masks[2, :, k] = forward[k], backward[k], centre[k]
    return select, masks


def slope_kernel(
    edge, planes, fields, coarse_planes, per_device, total, coarse_count, slots, slabs,
    dest_ref, parent_ref, own_ref, other_ref, own_low, other_low, own_high, other_high,
    spread_ref, weight_ref, out_ref, token_ref, stack, ghosts, table, count,
):
    step = pl.program_id(0)
    cross = edge * edge
    rows = fields * planes
    own, slab = lax.axis_index("box"), lax.axis_index("slab")

    @pl.when(step == 0)
    def _():
        token_ref[...] = jnp.zeros_like(token_ref)
        stack[...] = jnp.zeros_like(stack)
        for slot in range(slots):
            table[slot] = -1
            count[slot] = 0

        def place(b, carry):
            @pl.when(dest_ref[b] == own)
            def _():
                slot = 2 * (b // per_device)
                owner = parent_ref[b] // coarse_count
                table[jnp.where(table[slot] >= 0, slot + 1, slot)] = 2 * owner + count[owner]
                count[owner] = count[owner] + 1

            return carry

        lax.fori_loop(0, total, place, 0)
        for slot in range(slots):
            for n, ref in enumerate((own_ref, other_ref)):
                at = (2 * slot + n) * ROWS
                for block in range(ROWS // planes):
                    ghosts[at + block * planes : at + (block + 1) * planes, :cross] = ref[slot, fields + block]
        high, middle, low = (
            jnp.dot(part, spread_ref[...], preferred_element_type=jnp.float32)
            for part in split_three(ghosts[:, :cross])
        )
        ghosts[...] = high + (middle + low)

    face = table[step]

    @pl.when(face < 0)
    def _():
        out_ref[...] = jnp.zeros_like(out_ref)

    @pl.when(face >= 0)
    def _():
        lane = lax.broadcasted_iota(jnp.int32, (1, cross), 1)
        y, z = lane // edge, lane % edge
        for n, ref in enumerate((own_ref, other_ref)):
            at = (4 + n) * rows
            if planes % 8:
                for f in range(fields):
                    stack[at + f * planes : at + (f + 1) * planes] = ref[step, f]
            else:
                stack[at : at + rows] = ref[step, :fields].reshape(rows, cross)
        cells = stack[4 * rows : 6 * rows]
        stack[0 : 2 * rows] = jnp.where(y < edge - 1, pltpu.roll(cells, cross - edge, 1), 0.0) + jnp.where(
            z < edge - 1, pltpu.roll(cells, cross - 1, 1), 0.0
        )
        stack[2 * rows : 4 * rows] = jnp.where(y > 0, pltpu.roll(cells, edge, 1), 0.0) + jnp.where(
            z > 0, pltpu.roll(cells, 1, 1), 0.0
        )
        rim = ghosts[pl.ds(pl.multiple_of(2 * ROWS * face, 2 * ROWS), 2 * ROWS)]
        base = 6 * rows
        x_face = rim[:, 2 * coarse_planes * cross :]
        stack[base : base + 2 * ROWS] = x_face
        stack[base + 2 * ROWS : base + 4 * ROWS] = x_face

        @pl.when(slab > 0)
        def _():
            stack[base : base + fields] = own_low[step]
            stack[base + ROWS : base + ROWS + fields] = other_low[step]

        @pl.when(slab < slabs - 1)
        def _():
            stack[base + 2 * ROWS : base + 2 * ROWS + fields] = own_high[step]
            stack[base + 3 * ROWS : base + 3 * ROWS + fields] = other_high[step]

        base += 4 * ROWS
        for n in range(2 * coarse_planes):
            stack[base + 2 * ROWS * n : base + 2 * ROWS * (n + 1)] = rim[:, n * cross : (n + 1) * cross]
        mixed = jnp.dot(weight_ref[...], stack[...], precision=HIGHEST, preferred_element_type=jnp.float32)
        if planes % 8:
            for f in range(fields):
                out_ref[0, f] = mixed[f * planes : (f + 1) * planes]
        else:
            out_ref[0] = mixed.reshape(fields, planes, cross)


def mixing_weights(mixes, group, fields, planes, coarse_planes):
    lap_mix, grad_mix, damp_mix = mixes
    select, masks = slope_columns(fields, planes, coarse_planes)
    terms = jnp.stack([lap_mix + 0.5 * grad_mix, lap_mix - 0.5 * grad_mix, damp_mix - 6.0 * lap_mix])
    terms = lax.dynamic_slice_in_dim(terms, group * fields, fields, 1)
    terms = jnp.where(group == 0, terms, jnp.roll(terms, fields, axis=2))
    terms = jnp.einsum("tfg,gk->tfk", terms, jnp.asarray(select), precision=HIGHEST)
    return jnp.sum(terms[:, :, None, :] * jnp.asarray(masks)[:, None], axis=0).reshape(fields * planes, -1)


def body(boxes, move_dest, parent, coarse, lap_mix, grad_mix, damp_mix):
    box_count = lax.axis_size("box")
    slabs = lax.axis_size("slab")
    group = lax.axis_index("fld")
    levels, per_device, fields, planes, cross = boxes.shape
    edge = planes * slabs
    coarse_planes = planes // 2
    slots = 2 * box_count
    total = move_dest.shape[0]
    coarse_count = coarse.shape[0]

    def send(piece, turn):
        return lax.ppermute(piece, "box", [(s, partner(s, turn, box_count)) for s in range(box_count)])

    first = pack_first(boxes, coarse, move_dest, parent, edge, box_count)
    arrived = [first[0]] + [send(first[turn], turn) for turn in range(1, box_count)]
    *later, moved = pack_later(boxes, move_dest, first[0], box_count)
    later = [send(piece, n + 1) for n, piece in enumerate(later)]
    now, moved, *facing = arrive(arrived, (1,), later[:1], moved, slabs)

    swap = [(0, 1), (1, 0)]
    now_other = lax.ppermute(now, "fld", swap)

    def shifted(values, up):
        pairs = [(s, s + 1) if up else (s + 1, s) for s in range(slabs - 1)]
        crossed = [(2 * a + f, 2 * b + 1 - f) for a, b in pairs for f in range(2)]
        return lax.ppermute(values, "slab", pairs), lax.ppermute(values, ("slab", "fld"), crossed)

    if slabs == 2:
        crossed = [(0, 3), (3, 0), (1, 2), (2, 1)]
        low = high = (lax.ppermute(facing[0], "slab", swap), lax.ppermute(facing[0], ("slab", "fld"), crossed))
    else:
        low, high = shifted(facing[1], True), shifted(facing[0], False)

    weight = mixing_weights((lap_mix, grad_mix, damp_mix), group, fields, planes, coarse_planes)
    spread = jnp.asarray(expand_table(coarse_planes, edge, cross)).astype(jnp.bfloat16)
    smem, vmem = pl.BlockSpec(memory_space=pltpu.SMEM), pl.BlockSpec(memory_space=pltpu.VMEM)
    slope, token = pl.pallas_call(
        functools.partial(
            slope_kernel, edge, planes, fields, coarse_planes, per_device, total, coarse_count, slots, slabs
        ),
        grid=(slots,),
        out_shape=[
            jax.ShapeDtypeStruct((slots, fields, planes, cross), jnp.float32),
            jax.ShapeDtypeStruct((8, 128), jnp.float32),
        ],
        in_specs=[smem, smem] + [vmem] * 8,
        out_specs=[pl.BlockSpec((1, fields, planes, cross), lambda n: (n, 0, 0, 0)), vmem],
        scratch_shapes=[
            pltpu.VMEM((weight.shape[1], cross), jnp.float32),
            pltpu.VMEM((2 * ROWS * slots, spread.shape[1]), jnp.float32),
            pltpu.SMEM((slots,), jnp.int32),
            pltpu.SMEM((slots,), jnp.int32),
        ],
        compiler_params=pltpu.CompilerParams(vmem_limit_bytes=48 * 2 ** 20),
        cost_estimate=pl.CostEstimate(
            flops=12 * slots * weight.size * cross, bytes_accessed=12 * now.size, transcendentals=0
        ),
    )(move_dest, parent, now, now_other, low[0], low[1], high[0], high[1], spread, weight)
    return settle(tuple(range(2, box_count)), later[1:], moved, token), slope


def solution(mesh):
    placed = (
        P(None, ("runs", "box"), "fld", "slab", None),
        P("runs"),
        P("runs"),
        P(("runs", "box"), "fld", None),
        P(),
        P(),
        P(),
    )
    return jax.shard_map(
        body,
        mesh=mesh,
        in_specs=placed,
        out_specs=(
            P(None, ("runs", "box"), "fld", "slab", None),
            P(("runs", "box"), "fld", "slab", None),
        ),
        check_vma=False,
    )
```

```python
import functools

import jax
import jax.numpy as jnp
import numpy as np
from jax import lax
from jax.experimental import pallas as pl
from jax.experimental.pallas import tpu as pltpu
from jax.sharding import PartitionSpec as P

HIGHEST = lax.Precision.HIGHEST
ROWS = 16


def round_up(value, unit):
    return -(-value // unit) * unit


def split_three(values):
    high = values.astype(jnp.bfloat16)
    rest = values - high.astype(jnp.float32)
    middle = rest.astype(jnp.bfloat16)
    low = (rest - middle.astype(jnp.float32)).astype(jnp.bfloat16)
    return high, middle, low


def place_boxes(per_device, box_count, dest_ref, table):
    own = lax.axis_index("box")
    for slot in range(2 * box_count):
        table[slot] = -1

    def place(b, carry):
        slot = 2 * dest_ref[own * per_device + b]
        table[jnp.where(table[slot] >= 0, slot + 1, slot)] = b
        return carry

    lax.fori_loop(0, per_device, place, 0)


def partner(own, turn, box_count):
    return own ^ turn


def each_slot(box_count):
    own = lax.axis_index("box")
    for turn in range(box_count):
        for k in range(2):
            yield turn, k, 2 * partner(own, turn, box_count) + k


def first_kernel(per_device, box_count, edge, dest_ref, parent_ref, boxes_ref, coarse_ref, *refs):
    outs, (shells, chosen, dest, parent, box_table, face_table, sems, in_sems) = refs[:box_count], refs[box_count:]
    fields, coarse_count, cells = coarse_ref.shape
    planes, cross = outs[0].shape[2:]
    own, slab = lax.axis_index("box"), lax.axis_index("slab")
    fetches = [
        pltpu.make_async_copy(coarse_ref, shells, in_sems.at[0]),
        pltpu.make_async_copy(dest_ref, dest, in_sems.at[1]),
        pltpu.make_async_copy(parent_ref, parent, in_sems.at[2]),
    ]
    for fetch in fetches:
        fetch.start()
    index = face_cells(lax.broadcasted_iota(jnp.int32, (1, cross), 1), edge, planes // 2, slab)
    cell = lax.broadcasted_iota(jnp.int32, (cells, cross), 0)
    one_hot = (cell == index).astype(jnp.float32).astype(jnp.bfloat16)
    fetches[1].wait()
    place_boxes(per_device, box_count, dest, box_table)

    def copy(shift, k, b):
        return pltpu.make_async_copy(
            boxes_ref.at[0, b], outs[shift].at[k, pl.ds(0, fields)], sems.at[shift, k]
        )

    for shift, k, slot in each_slot(box_count):
        b = box_table[slot]

        @pl.when(b >= 0)
        def _():
            copy(shift, k, b).start()

        @pl.when(b < 0)
        def _():
            outs[shift][k, :fields] = jnp.zeros((fields, planes, cross), jnp.float32)

    for slot in range(2 * box_count):
        face_table[slot] = -1
    fetches[2].wait()

    def place(b, carry):
        slot = 2 * dest[b]
        local = parent[b] - own * coarse_count

        @pl.when(jnp.logical_and(local >= 0, local < coarse_count))
        def _():
            face_table[jnp.where(face_table[slot] >= 0, slot + 1, slot)] = local

        return carry

    lax.fori_loop(0, dest.shape[0], place, 0)
    fetches[0].wait()
    high, middle, low = (
        jnp.dot(part, one_hot, preferred_element_type=jnp.float32)
        for part in split_three(shells[...].reshape(fields * coarse_count, cells))
    )
    chosen[...] = (high + (middle + low)).reshape(chosen.shape)
    for shift, k, slot in each_slot(box_count):
        local = face_table[slot]
        for row in range(ROWS):
            to = fields + row // planes
            if row < fields:
                values = chosen[row, pl.ds(jnp.maximum(local, 0), 1)]
                values = jnp.where(local >= 0, values, 0.0)
            else:
                values = jnp.zeros((1, cross), jnp.float32)
            outs[shift][k, to, row % planes : row % planes + 1] = values
    for shift, k, slot in each_slot(box_count):
        b = box_table[slot]

        @pl.when(b >= 0)
        def _():
            copy(shift, k, b).wait()


def pack_first(boxes, coarse, move_dest, parent, edge, box_count):
    per_device, fields, planes, cross = boxes.shape[1:]
    coarse = jnp.transpose(coarse, (1, 0, 2))
    hbm, vmem = pl.BlockSpec(memory_space=pltpu.HBM), pl.BlockSpec(memory_space=pltpu.VMEM)
    item = (2, fields + ROWS // planes, planes, cross)
    return pl.pallas_call(
        functools.partial(first_kernel, per_device, box_count, edge),
        out_shape=[jax.ShapeDtypeStruct(item, jnp.float32)] * box_count,
        in_specs=[hbm] * 4,
        out_specs=[vmem] * box_count,
        scratch_shapes=[
            pltpu.VMEM(coarse.shape, jnp.float32),
            pltpu.VMEM(coarse.shape[:2] + (cross,), jnp.float32),
            pltpu.SMEM(move_dest.shape, jnp.int32),
            pltpu.SMEM(parent.shape, jnp.int32),
            pltpu.SMEM((2 * box_count,), jnp.int32),
            pltpu.SMEM((2 * box_count,), jnp.int32),
            pltpu.SemaphoreType.DMA((box_count, 2)),
            pltpu.SemaphoreType.DMA((3,)),
        ],
        cost_estimate=pl.CostEstimate(
            flops=6 * coarse.size * cross, bytes_accessed=4 * (coarse.size + 2 * boxes.size), transcendentals=0
        ),
    )(move_dest, parent, boxes, coarse)


def later_kernel(turns, per_device, box_count, levels, dest_ref, boxes_ref, *refs):
    outs, (dest, table, sems, in_sem) = refs[: len(turns)], refs[len(turns) :]
    own = lax.axis_index("box")
    fetch = pltpu.make_async_copy(dest_ref, dest, in_sem)
    fetch.start()
    fetch.wait()
    place_boxes(per_device, box_count, dest, table)
    places = [(n, turn, k, 2 * partner(own, turn, box_count) + k) for n, turn in enumerate(turns) for k in range(2)]

    def copies(n, turn, k, b):
        skip = min(turn, 1)
        for level in range(skip, levels):
            yield pltpu.make_async_copy(boxes_ref.at[level, b], outs[n].at[level - skip, k], sems.at[n, level, k])

    for n, turn, k, slot in places:
        b = table[slot]

        @pl.when(b >= 0)
        def _():
            for copy in copies(n, turn, k, b):
                copy.start()

        @pl.when(b < 0)
        def _():
            for level in range(outs[n].shape[0]):
                outs[n][level, k] = jnp.zeros(outs[n].shape[2:], jnp.float32)

    for n, turn, k, slot in places:
        b = table[slot]

        @pl.when(b >= 0)
        def _():
            for copy in copies(n, turn, k, b):
                copy.wait()


def pack_later(turns, boxes, move_dest, box_count):
    levels, per_device = boxes.shape[:2]
    item = boxes.shape[2:]
    hbm, vmem = pl.BlockSpec(memory_space=pltpu.HBM), pl.BlockSpec(memory_space=pltpu.VMEM)
    size = int(np.prod(item)) * 4
    return pl.pallas_call(
        functools.partial(later_kernel, turns, per_device, box_count, levels),
        out_shape=[jax.ShapeDtypeStruct((levels - min(turn, 1), 2) + item, jnp.float32) for turn in turns],
        in_specs=[hbm] * 2,
        out_specs=[vmem] * len(turns),
        scratch_shapes=[
            pltpu.SMEM(move_dest.shape, jnp.int32),
            pltpu.SMEM((2 * box_count,), jnp.int32),
            pltpu.SemaphoreType.DMA((len(turns), levels, 2)),
            pltpu.SemaphoreType.DMA,
        ],
        cost_estimate=pl.CostEstimate(
            flops=0, bytes_accessed=4 * len(turns) * levels * size, transcendentals=0
        ),
    )(move_dest, boxes)


def settle_kernel(box_count, *refs):
    out_ref, sems = refs[-2:]
    own = lax.axis_index("box")
    levels = out_ref.shape[0]
    middle = jnp.logical_or(own == box_count // 2, own == box_count // 2 - 1)

    def copy(turn, piece):
        to = out_ref.at[pl.ds(1, levels - 1), pl.ds(2 * partner(own, turn, box_count), 2)]
        return pltpu.make_async_copy(piece, to, sems.at[turn])

    last = box_count - 1

    @pl.when(middle)
    def _():
        copy(last, refs[last]).start()

    @pl.when(jnp.logical_not(middle))
    def _():
        copy(last, refs[last - 1]).start()

    for turn in range(1, last):
        copy(turn, refs[turn - 1]).start()
    for turn in range(1, box_count):
        copy(turn, refs[turn - 1]).wait()


def settle(pieces, moved, after):
    count = len(pieces)
    vmem, hbm = pl.BlockSpec(memory_space=pltpu.VMEM), pl.BlockSpec(memory_space=pltpu.HBM)
    return pl.pallas_call(
        functools.partial(settle_kernel, count),
        out_shape=jax.ShapeDtypeStruct(moved.shape, jnp.float32),
        in_specs=[vmem] * count + [hbm, vmem],
        out_specs=hbm,
        scratch_shapes=[pltpu.SemaphoreType.DMA((count,))],
        input_output_aliases={count: 0},
        compiler_params=pltpu.CompilerParams(vmem_limit_bytes=48 * 2 ** 20),
        cost_estimate=pl.CostEstimate(
            flops=0, bytes_accessed=8 * count * pieces[0].size, transcendentals=0
        ),
    )(*pieces, moved, after)


def arrive_kernel(box_count, slabs, fields, *refs):
    pieces, stay = refs[:box_count], refs[box_count]
    now_ref, moved_ref, *edges, sems = refs[box_count + 1 :]
    own, slab = lax.axis_index("box"), lax.axis_index("slab")
    planes = now_ref.shape[2]
    mine = pltpu.make_async_copy(pieces[0], now_ref.at[pl.ds(2 * own, 2)], sems.at[0])
    mine.start()
    copies = [pltpu.make_async_copy(stay, moved_ref.at[:, pl.ds(2 * own, 2)], sems.at[box_count])]
    for turn in range(1, box_count):
        to = moved_ref.at[0, pl.ds(2 * partner(own, turn, box_count), 2)]
        copies.append(pltpu.make_async_copy(pieces[turn].at[:, pl.ds(0, fields)], to, sems.at[turn]))
    for copy in copies:
        copy.start()
    faced = [jnp.where(slab == 0, planes - 1, 0)] if slabs == 2 else [0, planes - 1]

    def cut(source):
        for k in range(2):
            for edge_ref, plane in zip(edges, faced):
                for f in range(fields):
                    edge_ref[2 * source + k, f : f + 1] = now_ref[2 * source + k, f, pl.ds(plane, 1)]

    for turn in range(1, box_count):
        source = partner(own, turn, box_count)
        for k in range(2):
            now_ref[2 * source + k] = pieces[turn][k]
        cut(source)
    mine.wait()
    cut(own)
    for copy in copies:
        copy.wait()


def arrive(pieces, stay, slabs):
    box_count = len(pieces)
    _, blocks, planes, cross = pieces[0].shape
    levels, _, fields = stay.shape[:3]
    slots = 2 * box_count
    sides = 1 if slabs == 2 else 2
    vmem, hbm = pl.BlockSpec(memory_space=pltpu.VMEM), pl.BlockSpec(memory_space=pltpu.HBM)
    shapes = [(slots, blocks, planes, cross), (levels, slots, fields, planes, cross)] + [(slots, fields, cross)] * sides
    return pl.pallas_call(
        functools.partial(arrive_kernel, box_count, slabs, fields),
        out_shape=[jax.ShapeDtypeStruct(shape, jnp.float32) for shape in shapes],
        in_specs=[hbm] + [vmem] * box_count,
        out_specs=[vmem, hbm] + [vmem] * sides,
        scratch_shapes=[pltpu.SemaphoreType.DMA((box_count + 1,))],
        compiler_params=pltpu.CompilerParams(vmem_limit_bytes=48 * 2 ** 20),
        cost_estimate=pl.CostEstimate(
            flops=0, bytes_accessed=12 * box_count * pieces[0].size, transcendentals=0
        ),
    )(*pieces, stay)


def face_cells(lane, edge, coarse_planes, slab):
    half, side = edge // 2, edge // 2 + 2
    plane, m = lane // (4 * half), lane % half + 1
    which = (lane // half) % 4
    rim = jnp.where(which == 0, m, jnp.where(which == 1, (side - 1) * side + m, m * side))
    rim = jnp.where(which == 3, rim + side - 1, rim) + (slab * coarse_planes + plane + 1) * side * side
    t = lane - 4 * half * coarse_planes
    x_rim = jnp.where(slab > 0, (side - 1) * side * side, 0) + (t // half + 1) * side + m
    return jnp.where(t < 0, rim, jnp.where(t < half * half, x_rim, -1))


def expand_table(coarse_planes, edge, lanes):
    half = edge // 2
    cross = edge * edge
    spread = np.zeros((lanes, (2 * coarse_planes + 1) * cross), np.float32)
    for c in range(coarse_planes):
        base = c * 4 * half
        forward, backward = 2 * c * cross, (2 * c + 1) * cross
        for m in range(edge):
            spread[base + m // 2, backward + m] += 1
            spread[base + half + m // 2, forward + (edge - 1) * edge + m] += 1
            spread[base + 2 * half + m // 2, backward + m * edge] += 1
            spread[base + 3 * half + m // 2, forward + m * edge + edge - 1] += 1
    base, to = coarse_planes * 4 * half, 2 * coarse_planes * cross
    for y in range(edge):
        for z in range(edge):
            spread[base + (y // 2) * half + z // 2, to + y * edge + z] = 1
    return spread


def slope_columns(fields, planes, coarse_planes):
    column_field, forward, backward, centre = [], [], [], []
    p = np.arange(planes)

    def add(field, f, b, c):
        column_field.append(field)
        forward.append(f * np.ones(planes))
        backward.append(b * np.ones(planes))
        centre.append(c * np.ones(planes))

    for f, b, c in ((1, 0, 0), (0, 1, 0), (0, 0, 1)):
        for g in range(2 * fields):
            for q in range(planes):
                here = p == q
                add(g, f * here + c * (p + 1 == q), b * here + c * (p - 1 == q), c * here)
    rows = [g if g < fields else -1 for g in range(ROWS)]
    rows += [fields + g if g < fields else -1 for g in range(ROWS)]
    for g in rows:
        add(g, 0, p == 0, 0)
    for g in rows:
        add(g, p == planes - 1, 0, 0)
    for c in range(coarse_planes):
        for g in rows:
            add(g, p // 2 == c, 0, 0)
        for g in rows:
            add(g, 0, p // 2 == c, 0)
    width = round_up(len(column_field), 128)
    select = np.zeros((2 * fields, width), np.float32)
    masks = np.zeros((3, planes, width), np.float32)
    for k, g in enumerate(column_field):
        if g >= 0:
            select[g, k] = 1
        masks[0, :, k], masks[1, :, k], masks[2, :, k] = forward[k], backward[k], centre[k]
    return select, masks


def slope_kernel(
    edge, planes, fields, coarse_planes, per_device, total, coarse_count, slots, slabs,
    dest_ref, parent_ref, own_ref, other_ref, own_low, other_low, own_high, other_high,
    spread_ref, weight_ref, out_ref, token_ref, stack, ghosts, table, count,
):
    step = pl.program_id(0)
    cross = edge * edge
    rows = fields * planes
    own, slab = lax.axis_index("box"), lax.axis_index("slab")

    @pl.when(step == 0)
    def _():
        token_ref[...] = jnp.zeros_like(token_ref)
        stack[...] = jnp.zeros_like(stack)
        for slot in range(slots):
            table[slot] = -1
            count[slot] = 0

        def place(b, carry):
            @pl.when(dest_ref[b] == own)
            def _():
                slot = 2 * (b // per_device)
                owner = parent_ref[b] // coarse_count
                table[jnp.where(table[slot] >= 0, slot + 1, slot)] = 2 * owner + count[owner]
                count[owner] = count[owner] + 1

            return carry

        lax.fori_loop(0, total, place, 0)
        for slot in range(slots):
            for n, ref in enumerate((own_ref, other_ref)):
                at = (2 * slot + n) * ROWS
                for block in range(ROWS // planes):
                    ghosts[at + block * planes : at + (block + 1) * planes, :cross] = ref[slot, fields + block]
        high, middle, low = (
            jnp.dot(part, spread_ref[...], preferred_element_type=jnp.float32)
            for part in split_three(ghosts[:, :cross])
        )
        ghosts[...] = high + (middle + low)

    face = table[step]

    @pl.when(face < 0)
    def _():
        out_ref[...] = jnp.zeros_like(out_ref)

    @pl.when(face >= 0)
    def _():
        lane = lax.broadcasted_iota(jnp.int32, (1, cross), 1)
        y, z = lane // edge, lane % edge
        for n, ref in enumerate((own_ref, other_ref)):
            at = (4 + n) * rows
            if planes % 8:
                for f in range(fields):
                    stack[at + f * planes : at + (f + 1) * planes] = ref[step, f]
            else:
                stack[at : at + rows] = ref[step, :fields].reshape(rows, cross)
        cells = stack[4 * rows : 6 * rows]
        stack[0 : 2 * rows] = jnp.where(y < edge - 1, pltpu.roll(cells, cross - edge, 1), 0.0) + jnp.where(
            z < edge - 1, pltpu.roll(cells, cross - 1, 1), 0.0
        )
        stack[2 * rows : 4 * rows] = jnp.where(y > 0, pltpu.roll(cells, edge, 1), 0.0) + jnp.where(
            z > 0, pltpu.roll(cells, 1, 1), 0.0
        )
        rim = ghosts[pl.ds(pl.multiple_of(2 * ROWS * face, 2 * ROWS), 2 * ROWS)]
        base = 6 * rows
        x_face = rim[:, 2 * coarse_planes * cross :]
        stack[base : base + 2 * ROWS] = x_face
        stack[base + 2 * ROWS : base + 4 * ROWS] = x_face

        @pl.when(slab > 0)
        def _():
            stack[base : base + fields] = own_low[step]
            stack[base + ROWS : base + ROWS + fields] = other_low[step]

        @pl.when(slab < slabs - 1)
        def _():
            stack[base + 2 * ROWS : base + 2 * ROWS + fields] = own_high[step]
            stack[base + 3 * ROWS : base + 3 * ROWS + fields] = other_high[step]

        base += 4 * ROWS
        for n in range(2 * coarse_planes):
            stack[base + 2 * ROWS * n : base + 2 * ROWS * (n + 1)] = rim[:, n * cross : (n + 1) * cross]
        mixed = jnp.dot(weight_ref[...], stack[...], precision=HIGHEST, preferred_element_type=jnp.float32)
        if planes % 8:
            for f in range(fields):
                out_ref[0, f] = mixed[f * planes : (f + 1) * planes]
        else:
            out_ref[0] = mixed.reshape(fields, planes, cross)


def mixing_weights(mixes, group, fields, planes, coarse_planes):
    lap_mix, grad_mix, damp_mix = mixes
    select, masks = slope_columns(fields, planes, coarse_planes)
    terms = jnp.stack([lap_mix + 0.5 * grad_mix, lap_mix - 0.5 * grad_mix, damp_mix - 6.0 * lap_mix])
    terms = lax.dynamic_slice_in_dim(terms, group * fields, fields, 1)
    terms = jnp.where(group == 0, terms, jnp.roll(terms, fields, axis=2))
    terms = jnp.einsum("tfg,gk->tfk", terms, jnp.asarray(select), precision=HIGHEST)
    return jnp.sum(terms[:, :, None, :] * jnp.asarray(masks)[:, None], axis=0).reshape(fields * planes, -1)


def body(boxes, move_dest, parent, coarse, lap_mix, grad_mix, damp_mix):
    box_count = lax.axis_size("box")
    slabs = lax.axis_size("slab")
    group = lax.axis_index("fld")
    levels, per_device, fields, planes, cross = boxes.shape
    edge = planes * slabs
    coarse_planes = planes // 2
    slots = 2 * box_count
    total = move_dest.shape[0]
    coarse_count = coarse.shape[0]

    def send(piece, turn, members=range(box_count)):
        return lax.ppermute(piece, "box", [(s, partner(s, turn, box_count)) for s in members])

    last = box_count - 1
    middle = (box_count // 2 - 1, box_count // 2)
    outer = [s for s in range(box_count) if s not in middle]
    fill = pack_later((1, last), boxes, move_dest, box_count)
    fillers = [send(fill[0], 1), send(fill[1], last, middle)]
    first = pack_first(boxes, coarse, move_dest, parent, edge, box_count)
    arrived = [first[0]] + [send(first[turn], turn) for turn in range(1, box_count)]
    stay, *rest = pack_later((0,) + tuple(range(2, last)), boxes, move_dest, box_count)
    held, arrived[last] = lax.optimization_barrier((tuple(rest), arrived[last]))
    rest = list(held)
    rest = [send(piece, n + 2) for n, piece in enumerate(rest)] + [send(fill[1], last, outer)]
    now, moved, *facing = arrive(arrived, stay, slabs)
    now, *fillers = lax.optimization_barrier((now, *fillers))

    swap = [(0, 1), (1, 0)]
    now_other = lax.ppermute(now, "fld", swap)

    def shifted(values, up):
        pairs = [(s, s + 1) if up else (s + 1, s) for s in range(slabs - 1)]
        crossed = [(2 * a + f, 2 * b + 1 - f) for a, b in pairs for f in range(2)]
        return lax.ppermute(values, "slab", pairs), lax.ppermute(values, ("slab", "fld"), crossed)

    if slabs == 2:
        crossed = [(0, 3), (3, 0), (1, 2), (2, 1)]
        low = high = (lax.ppermute(facing[0], "slab", swap), lax.ppermute(facing[0], ("slab", "fld"), crossed))
    else:
        low, high = shifted(facing[1], True), shifted(facing[0], False)

    weight = mixing_weights((lap_mix, grad_mix, damp_mix), group, fields, planes, coarse_planes)
    spread = jnp.asarray(expand_table(coarse_planes, edge, cross)).astype(jnp.bfloat16)
    smem, vmem = pl.BlockSpec(memory_space=pltpu.SMEM), pl.BlockSpec(memory_space=pltpu.VMEM)
    slope, token = pl.pallas_call(
        functools.partial(
            slope_kernel, edge, planes, fields, coarse_planes, per_device, total, coarse_count, slots, slabs
        ),
        grid=(slots,),
        out_shape=[
            jax.ShapeDtypeStruct((slots, fields, planes, cross), jnp.float32),
            jax.ShapeDtypeStruct((8, 128), jnp.float32),
        ],
        in_specs=[smem, smem] + [vmem] * 8,
        out_specs=[pl.BlockSpec((1, fields, planes, cross), lambda n: (n, 0, 0, 0)), vmem],
        scratch_shapes=[
            pltpu.VMEM((weight.shape[1], cross), jnp.float32),
            pltpu.VMEM((2 * ROWS * slots, spread.shape[1]), jnp.float32),
            pltpu.SMEM((slots,), jnp.int32),
            pltpu.SMEM((slots,), jnp.int32),
        ],
        compiler_params=pltpu.CompilerParams(vmem_limit_bytes=48 * 2 ** 20),
        cost_estimate=pl.CostEstimate(
            flops=12 * slots * weight.size * cross, bytes_accessed=12 * now.size, transcendentals=0
        ),
    )(move_dest, parent, now, now_other, low[0], low[1], high[0], high[1], spread, weight)
    return settle([fillers[0]] + rest + [fillers[1]], moved, token), slope


def solution(mesh):
    placed = (
        P(None, ("runs", "box"), "fld", "slab", None),
        P("runs"),
        P("runs"),
        P(("runs", "box"), "fld", None),
        P(),
        P(),
        P(),
    )
    return jax.shard_map(
        body,
        mesh=mesh,
        in_specs=placed,
        out_specs=(
            P(None, ("runs", "box"), "fld", "slab", None),
            P(("runs", "box"), "fld", "slab", None),
        ),
        check_vma=False,
    )
```

```python
import functools

import jax
import jax.numpy as jnp
import numpy as np
from jax import lax
from jax.experimental import pallas as pl
from jax.experimental.pallas import tpu as pltpu
from jax.sharding import PartitionSpec as P

HIGHEST = lax.Precision.HIGHEST
ROWS = 16


def round_up(value, unit):
    return -(-value // unit) * unit


def split_three(values):
    high = values.astype(jnp.bfloat16)
    rest = values - high.astype(jnp.float32)
    middle = rest.astype(jnp.bfloat16)
    low = (rest - middle.astype(jnp.float32)).astype(jnp.bfloat16)
    return high, middle, low


def place_boxes(per_device, box_count, dest_ref, table):
    own = lax.axis_index("box")
    for slot in range(2 * box_count):
        table[slot] = -1

    def place(b, carry):
        slot = 2 * dest_ref[own * per_device + b]
        table[jnp.where(table[slot] >= 0, slot + 1, slot)] = b
        return carry

    lax.fori_loop(0, per_device, place, 0)


def partner(own, turn, box_count):
    return own ^ turn


def each_slot(box_count):
    own = lax.axis_index("box")
    for turn in range(box_count):
        for k in range(2):
            yield turn, k, 2 * partner(own, turn, box_count) + k


def first_kernel(per_device, box_count, edge, dest_ref, parent_ref, boxes_ref, coarse_ref, *refs):
    outs, (shells, chosen, dest, parent, box_table, face_table, sems, in_sems) = refs[:box_count], refs[box_count:]
    fields, coarse_count, cells = coarse_ref.shape
    planes, cross = outs[0].shape[2:]
    own, slab = lax.axis_index("box"), lax.axis_index("slab")
    fetches = [
        pltpu.make_async_copy(coarse_ref, shells, in_sems.at[0]),
        pltpu.make_async_copy(dest_ref, dest, in_sems.at[1]),
        pltpu.make_async_copy(parent_ref, parent, in_sems.at[2]),
    ]
    for fetch in fetches:
        fetch.start()
    index = face_cells(lax.broadcasted_iota(jnp.int32, (1, cross), 1), edge, planes // 2, slab)
    cell = lax.broadcasted_iota(jnp.int32, (cells, cross), 0)
    one_hot = (cell == index).astype(jnp.float32).astype(jnp.bfloat16)
    fetches[1].wait()
    place_boxes(per_device, box_count, dest, box_table)

    def copy(shift, k, b):
        return pltpu.make_async_copy(
            boxes_ref.at[0, b], outs[shift].at[k, pl.ds(0, fields)], sems.at[shift, k]
        )

    for shift, k, slot in each_slot(box_count):
        b = box_table[slot]

        @pl.when(b >= 0)
        def _():
            copy(shift, k, b).start()

        @pl.when(b < 0)
        def _():
            outs[shift][k, :fields] = jnp.zeros((fields, planes, cross), jnp.float32)

    for slot in range(2 * box_count):
        face_table[slot] = -1
    fetches[2].wait()

    def place(b, carry):
        slot = 2 * dest[b]
        local = parent[b] - own * coarse_count

        @pl.when(jnp.logical_and(local >= 0, local < coarse_count))
        def _():
            face_table[jnp.where(face_table[slot] >= 0, slot + 1, slot)] = local

        return carry

    lax.fori_loop(0, dest.shape[0], place, 0)
    fetches[0].wait()
    high, middle, low = (
        jnp.dot(part, one_hot, preferred_element_type=jnp.float32)
        for part in split_three(shells[...].reshape(fields * coarse_count, cells))
    )
    chosen[...] = (high + (middle + low)).reshape(chosen.shape)
    for shift, k, slot in each_slot(box_count):
        local = face_table[slot]
        for row in range(ROWS):
            to = fields + row // planes
            if row < fields:
                values = chosen[row, pl.ds(jnp.maximum(local, 0), 1)]
                values = jnp.where(local >= 0, values, 0.0)
            else:
                values = jnp.zeros((1, cross), jnp.float32)
            outs[shift][k, to, row % planes : row % planes + 1] = values
    for shift, k, slot in each_slot(box_count):
        b = box_table[slot]

        @pl.when(b >= 0)
        def _():
            copy(shift, k, b).wait()


def pack_first(boxes, coarse, move_dest, parent, edge, box_count):
    per_device, fields, planes, cross = boxes.shape[1:]
    coarse = jnp.transpose(coarse, (1, 0, 2))
    hbm, vmem = pl.BlockSpec(memory_space=pltpu.HBM), pl.BlockSpec(memory_space=pltpu.VMEM)
    item = (2, fields + ROWS // planes, planes, cross)
    return pl.pallas_call(
        functools.partial(first_kernel, per_device, box_count, edge),
        out_shape=[jax.ShapeDtypeStruct(item, jnp.float32)] * box_count,
        in_specs=[hbm] * 4,
        out_specs=[vmem] * box_count,
        scratch_shapes=[
            pltpu.VMEM(coarse.shape, jnp.float32),
            pltpu.VMEM(coarse.shape[:2] + (cross,), jnp.float32),
            pltpu.SMEM(move_dest.shape, jnp.int32),
            pltpu.SMEM(parent.shape, jnp.int32),
            pltpu.SMEM((2 * box_count,), jnp.int32),
            pltpu.SMEM((2 * box_count,), jnp.int32),
            pltpu.SemaphoreType.DMA((box_count, 2)),
            pltpu.SemaphoreType.DMA((3,)),
        ],
        cost_estimate=pl.CostEstimate(
            flops=6 * coarse.size * cross, bytes_accessed=4 * (coarse.size + 2 * boxes.size), transcendentals=0
        ),
    )(move_dest, parent, boxes, coarse)


def later_kernel(turns, per_device, box_count, levels, dest_ref, boxes_ref, *refs):
    outs, (dest, table, sems, in_sem) = refs[: len(turns)], refs[len(turns) :]
    own = lax.axis_index("box")
    fetch = pltpu.make_async_copy(dest_ref, dest, in_sem)
    fetch.start()
    fetch.wait()
    place_boxes(per_device, box_count, dest, table)
    places = [(n, turn, k, 2 * partner(own, turn, box_count) + k) for n, turn in enumerate(turns) for k in range(2)]

    def copies(n, turn, k, b):
        skip = min(turn, 1)
        for level in range(skip, levels):
            yield pltpu.make_async_copy(boxes_ref.at[level, b], outs[n].at[level - skip, k], sems.at[n, level, k])

    for n, turn, k, slot in places:
        b = table[slot]

        @pl.when(b >= 0)
        def _():
            for copy in copies(n, turn, k, b):
                copy.start()

        @pl.when(b < 0)
        def _():
            for level in range(outs[n].shape[0]):
                outs[n][level, k] = jnp.zeros(outs[n].shape[2:], jnp.float32)

    for n, turn, k, slot in places:
        b = table[slot]

        @pl.when(b >= 0)
        def _():
            for copy in copies(n, turn, k, b):
                copy.wait()


def pack_later(turns, boxes, move_dest, box_count):
    levels, per_device = boxes.shape[:2]
    item = boxes.shape[2:]
    hbm, vmem = pl.BlockSpec(memory_space=pltpu.HBM), pl.BlockSpec(memory_space=pltpu.VMEM)
    size = int(np.prod(item)) * 4
    return pl.pallas_call(
        functools.partial(later_kernel, turns, per_device, box_count, levels),
        out_shape=[jax.ShapeDtypeStruct((levels - min(turn, 1), 2) + item, jnp.float32) for turn in turns],
        in_specs=[hbm] * 2,
        out_specs=[vmem] * len(turns),
        scratch_shapes=[
            pltpu.SMEM(move_dest.shape, jnp.int32),
            pltpu.SMEM((2 * box_count,), jnp.int32),
            pltpu.SemaphoreType.DMA((len(turns), levels, 2)),
            pltpu.SemaphoreType.DMA,
        ],
        cost_estimate=pl.CostEstimate(
            flops=0, bytes_accessed=4 * len(turns) * levels * size, transcendentals=0
        ),
    )(move_dest, boxes)


def settle_kernel(box_count, *refs):
    out_ref, sems = refs[-2:]
    own = lax.axis_index("box")
    levels = out_ref.shape[0]
    middle = jnp.logical_or(own == box_count // 2, own == box_count // 2 - 1)

    def copy(turn, piece):
        to = out_ref.at[pl.ds(1, levels - 1), pl.ds(2 * partner(own, turn, box_count), 2)]
        return pltpu.make_async_copy(piece, to, sems.at[turn])

    last = box_count - 1

    @pl.when(middle)
    def _():
        copy(last, refs[last]).start()

    @pl.when(jnp.logical_not(middle))
    def _():
        copy(last, refs[last - 1]).start()

    for turn in range(1, last):
        copy(turn, refs[turn - 1]).start()
    for turn in range(1, box_count):
        copy(turn, refs[turn - 1]).wait()


def settle(pieces, moved, after):
    count = len(pieces)
    vmem, hbm = pl.BlockSpec(memory_space=pltpu.VMEM), pl.BlockSpec(memory_space=pltpu.HBM)
    return pl.pallas_call(
        functools.partial(settle_kernel, count),
        out_shape=jax.ShapeDtypeStruct(moved.shape, jnp.float32),
        in_specs=[vmem] * count + [hbm, vmem],
        out_specs=hbm,
        scratch_shapes=[pltpu.SemaphoreType.DMA((count,))],
        input_output_aliases={count: 0},
        compiler_params=pltpu.CompilerParams(vmem_limit_bytes=48 * 2 ** 20),
        cost_estimate=pl.CostEstimate(
            flops=0, bytes_accessed=8 * count * pieces[0].size, transcendentals=0
        ),
    )(*pieces, moved, after)


def arrive_kernel(box_count, slabs, fields, *refs):
    pieces, stay = refs[:box_count], refs[box_count]
    now_ref, moved_ref, *edges, sems = refs[box_count + 1 :]
    own, slab = lax.axis_index("box"), lax.axis_index("slab")
    planes = now_ref.shape[2]
    mine = pltpu.make_async_copy(pieces[0], now_ref.at[pl.ds(2 * own, 2)], sems.at[0])
    mine.start()
    copies = [pltpu.make_async_copy(stay, moved_ref.at[:, pl.ds(2 * own, 2)], sems.at[box_count])]
    for turn in range(1, box_count):
        to = moved_ref.at[0, pl.ds(2 * partner(own, turn, box_count), 2)]
        copies.append(pltpu.make_async_copy(pieces[turn].at[:, pl.ds(0, fields)], to, sems.at[turn]))
    for copy in copies:
        copy.start()
    faced = [jnp.where(slab == 0, planes - 1, 0)] if slabs == 2 else [0, planes - 1]

    def cut(source):
        for k in range(2):
            for edge_ref, plane in zip(edges, faced):
                for f in range(fields):
                    edge_ref[2 * source + k, f : f + 1] = now_ref[2 * source + k, f, pl.ds(plane, 1)]

    for turn in range(1, box_count):
        source = partner(own, turn, box_count)
        for k in range(2):
            now_ref[2 * source + k] = pieces[turn][k]
        cut(source)
    mine.wait()
    cut(own)
    for copy in copies:
        copy.wait()


def arrive(pieces, stay, slabs):
    box_count = len(pieces)
    _, blocks, planes, cross = pieces[0].shape
    levels, _, fields = stay.shape[:3]
    slots = 2 * box_count
    sides = 1 if slabs == 2 else 2
    vmem, hbm = pl.BlockSpec(memory_space=pltpu.VMEM), pl.BlockSpec(memory_space=pltpu.HBM)
    shapes = [(slots, blocks, planes, cross), (levels, slots, fields, planes, cross)] + [(slots, fields, cross)] * sides
    return pl.pallas_call(
        functools.partial(arrive_kernel, box_count, slabs, fields),
        out_shape=[jax.ShapeDtypeStruct(shape, jnp.float32) for shape in shapes],
        in_specs=[hbm] + [vmem] * box_count,
        out_specs=[vmem, hbm] + [vmem] * sides,
        scratch_shapes=[pltpu.SemaphoreType.DMA((box_count + 1,))],
        compiler_params=pltpu.CompilerParams(vmem_limit_bytes=48 * 2 ** 20),
        cost_estimate=pl.CostEstimate(
            flops=0, bytes_accessed=12 * box_count * pieces[0].size, transcendentals=0
        ),
    )(*pieces, stay)


def face_cells(lane, edge, coarse_planes, slab):
    half, side = edge // 2, edge // 2 + 2
    plane, m = lane // (4 * half), lane % half + 1
    which = (lane // half) % 4
    rim = jnp.where(which == 0, m, jnp.where(which == 1, (side - 1) * side + m, m * side))
    rim = jnp.where(which == 3, rim + side - 1, rim) + (slab * coarse_planes + plane + 1) * side * side
    t = lane - 4 * half * coarse_planes
    x_rim = jnp.where(slab > 0, (side - 1) * side * side, 0) + (t // half + 1) * side + m
    return jnp.where(t < 0, rim, jnp.where(t < half * half, x_rim, -1))


def expand_table(coarse_planes, edge, lanes):
    half = edge // 2
    cross = edge * edge
    spread = np.zeros((lanes, (2 * coarse_planes + 1) * cross), np.float32)
    for c in range(coarse_planes):
        base = c * 4 * half
        forward, backward = 2 * c * cross, (2 * c + 1) * cross
        for m in range(edge):
            spread[base + m // 2, backward + m] += 1
            spread[base + half + m // 2, forward + (edge - 1) * edge + m] += 1
            spread[base + 2 * half + m // 2, backward + m * edge] += 1
            spread[base + 3 * half + m // 2, forward + m * edge + edge - 1] += 1
    base, to = coarse_planes * 4 * half, 2 * coarse_planes * cross
    for y in range(edge):
        for z in range(edge):
            spread[base + (y // 2) * half + z // 2, to + y * edge + z] = 1
    return spread


def slope_columns(fields, planes, coarse_planes):
    column_field, forward, backward, centre = [], [], [], []
    p = np.arange(planes)

    def add(field, f, b, c):
        column_field.append(field)
        forward.append(f * np.ones(planes))
        backward.append(b * np.ones(planes))
        centre.append(c * np.ones(planes))

    for f, b, c in ((1, 0, 0), (0, 1, 0), (0, 0, 1)):
        for g in range(2 * fields):
            for q in range(planes):
                here = p == q
                add(g, f * here + c * (p + 1 == q), b * here + c * (p - 1 == q), c * here)
    rows = [g if g < fields else -1 for g in range(ROWS)]
    rows += [fields + g if g < fields else -1 for g in range(ROWS)]
    for g in rows:
        add(g, 0, p == 0, 0)
    for g in rows:
        add(g, p == planes - 1, 0, 0)
    for c in range(coarse_planes):
        for g in rows:
            add(g, p // 2 == c, 0, 0)
        for g in rows:
            add(g, 0, p // 2 == c, 0)
    width = round_up(len(column_field), 128)
    select = np.zeros((2 * fields, width), np.float32)
    masks = np.zeros((3, planes, width), np.float32)
    for k, g in enumerate(column_field):
        if g >= 0:
            select[g, k] = 1
        masks[0, :, k], masks[1, :, k], masks[2, :, k] = forward[k], backward[k], centre[k]
    return select, masks


def slope_kernel(
    edge, planes, fields, coarse_planes, per_device, total, coarse_count, slots, slabs,
    dest_ref, parent_ref, own_ref, other_ref, own_low, other_low, own_high, other_high,
    spread_ref, weight_ref, out_ref, token_ref, stack, ghosts, table, count,
):
    step = pl.program_id(0)
    cross = edge * edge
    rows = fields * planes
    own, slab = lax.axis_index("box"), lax.axis_index("slab")

    @pl.when(step == 0)
    def _():
        token_ref[...] = jnp.zeros_like(token_ref)
        stack[...] = jnp.zeros_like(stack)
        for slot in range(slots):
            table[slot] = -1
            count[slot] = 0

        def place(b, carry):
            @pl.when(dest_ref[b] == own)
            def _():
                slot = 2 * (b // per_device)
                owner = parent_ref[b] // coarse_count
                table[jnp.where(table[slot] >= 0, slot + 1, slot)] = 2 * owner + count[owner]
                count[owner] = count[owner] + 1

            return carry

        lax.fori_loop(0, total, place, 0)
        for slot in range(slots):
            for n, ref in enumerate((own_ref, other_ref)):
                at = (2 * slot + n) * ROWS
                for block in range(ROWS // planes):
                    ghosts[at + block * planes : at + (block + 1) * planes, :cross] = ref[slot, fields + block]
        high, middle, low = (
            jnp.dot(part, spread_ref[...], preferred_element_type=jnp.float32)
            for part in split_three(ghosts[:, :cross])
        )
        ghosts[...] = high + (middle + low)

    face = table[step]

    @pl.when(face < 0)
    def _():
        out_ref[...] = jnp.zeros_like(out_ref)

    @pl.when(face >= 0)
    def _():
        lane = lax.broadcasted_iota(jnp.int32, (1, cross), 1)
        y, z = lane // edge, lane % edge
        for n, ref in enumerate((own_ref, other_ref)):
            at = (4 + n) * rows
            if planes % 8:
                for f in range(fields):
                    stack[at + f * planes : at + (f + 1) * planes] = ref[step, f]
            else:
                stack[at : at + rows] = ref[step, :fields].reshape(rows, cross)
        cells = stack[4 * rows : 6 * rows]
        stack[0 : 2 * rows] = jnp.where(y < edge - 1, pltpu.roll(cells, cross - edge, 1), 0.0) + jnp.where(
            z < edge - 1, pltpu.roll(cells, cross - 1, 1), 0.0
        )
        stack[2 * rows : 4 * rows] = jnp.where(y > 0, pltpu.roll(cells, edge, 1), 0.0) + jnp.where(
            z > 0, pltpu.roll(cells, 1, 1), 0.0
        )
        rim = ghosts[pl.ds(pl.multiple_of(2 * ROWS * face, 2 * ROWS), 2 * ROWS)]
        base = 6 * rows
        x_face = rim[:, 2 * coarse_planes * cross :]
        stack[base : base + 2 * ROWS] = x_face
        stack[base + 2 * ROWS : base + 4 * ROWS] = x_face

        @pl.when(slab > 0)
        def _():
            stack[base : base + fields] = own_low[step]
            stack[base + ROWS : base + ROWS + fields] = other_low[step]

        @pl.when(slab < slabs - 1)
        def _():
            stack[base + 2 * ROWS : base + 2 * ROWS + fields] = own_high[step]
            stack[base + 3 * ROWS : base + 3 * ROWS + fields] = other_high[step]

        base += 4 * ROWS
        for n in range(2 * coarse_planes):
            stack[base + 2 * ROWS * n : base + 2 * ROWS * (n + 1)] = rim[:, n * cross : (n + 1) * cross]
        mixed = jnp.dot(weight_ref[...], stack[...], precision=HIGHEST, preferred_element_type=jnp.float32)
        if planes % 8:
            for f in range(fields):
                out_ref[0, f] = mixed[f * planes : (f + 1) * planes]
        else:
            out_ref[0] = mixed.reshape(fields, planes, cross)


def mixing_weights(mixes, group, fields, planes, coarse_planes):
    lap_mix, grad_mix, damp_mix = mixes
    select, masks = slope_columns(fields, planes, coarse_planes)
    terms = jnp.stack([lap_mix + 0.5 * grad_mix, lap_mix - 0.5 * grad_mix, damp_mix - 6.0 * lap_mix])
    terms = lax.dynamic_slice_in_dim(terms, group * fields, fields, 1)
    terms = jnp.where(group == 0, terms, jnp.roll(terms, fields, axis=2))
    terms = jnp.einsum("tfg,gk->tfk", terms, jnp.asarray(select), precision=HIGHEST)
    return jnp.sum(terms[:, :, None, :] * jnp.asarray(masks)[:, None], axis=0).reshape(fields * planes, -1)


def body(boxes, move_dest, parent, coarse, lap_mix, grad_mix, damp_mix):
    box_count = lax.axis_size("box")
    slabs = lax.axis_size("slab")
    group = lax.axis_index("fld")
    levels, per_device, fields, planes, cross = boxes.shape
    edge = planes * slabs
    coarse_planes = planes // 2
    slots = 2 * box_count
    total = move_dest.shape[0]
    coarse_count = coarse.shape[0]

    def send(piece, turn, members=range(box_count)):
        return lax.ppermute(piece, "box", [(s, partner(s, turn, box_count)) for s in members])

    last = box_count - 1
    middle = (box_count // 2 - 1, box_count // 2)
    outer = [s for s in range(box_count) if s not in middle]
    fill = pack_later((1, last), boxes, move_dest, box_count)
    fillers = [send(fill[0], 1), send(fill[1], last, middle)]
    first = pack_first(boxes, coarse, move_dest, parent, edge, box_count)
    arrived = [first[0]] + [send(first[turn], turn) for turn in range(1, box_count)]
    stay, *rest = pack_later((0,) + tuple(range(2, last)), boxes, move_dest, box_count)
    held, *arrived[last - 1 :] = lax.optimization_barrier((rest + [fill[1]], *arrived[last - 1 :]))
    rest = [send(piece, n + 2) for n, piece in enumerate(held[:-1])] + [send(held[-1], last, outer)]
    now, moved, *facing = arrive(arrived, stay, slabs)
    now, *fillers = lax.optimization_barrier((now, *fillers))

    swap = [(0, 1), (1, 0)]
    now_other = lax.ppermute(now, "fld", swap)

    def shifted(values, up):
        pairs = [(s, s + 1) if up else (s + 1, s) for s in range(slabs - 1)]
        crossed = [(2 * a + f, 2 * b + 1 - f) for a, b in pairs for f in range(2)]
        return lax.ppermute(values, "slab", pairs), lax.ppermute(values, ("slab", "fld"), crossed)

    if slabs == 2:
        crossed = [(0, 3), (3, 0), (1, 2), (2, 1)]
        low = high = (lax.ppermute(facing[0], "slab", swap), lax.ppermute(facing[0], ("slab", "fld"), crossed))
    else:
        low, high = shifted(facing[1], True), shifted(facing[0], False)

    weight = mixing_weights((lap_mix, grad_mix, damp_mix), group, fields, planes, coarse_planes)
    spread = jnp.asarray(expand_table(coarse_planes, edge, cross)).astype(jnp.bfloat16)
    smem, vmem = pl.BlockSpec(memory_space=pltpu.SMEM), pl.BlockSpec(memory_space=pltpu.VMEM)
    slope, token = pl.pallas_call(
        functools.partial(
            slope_kernel, edge, planes, fields, coarse_planes, per_device, total, coarse_count, slots, slabs
        ),
        grid=(slots,),
        out_shape=[
            jax.ShapeDtypeStruct((slots, fields, planes, cross), jnp.float32),
            jax.ShapeDtypeStruct((8, 128), jnp.float32),
        ],
        in_specs=[smem, smem] + [vmem] * 8,
        out_specs=[pl.BlockSpec((1, fields, planes, cross), lambda n: (n, 0, 0, 0)), vmem],
        scratch_shapes=[
            pltpu.VMEM((weight.shape[1], cross), jnp.float32),
            pltpu.VMEM((2 * ROWS * slots, spread.shape[1]), jnp.float32),
            pltpu.SMEM((slots,), jnp.int32),
            pltpu.SMEM((slots,), jnp.int32),
        ],
        compiler_params=pltpu.CompilerParams(vmem_limit_bytes=48 * 2 ** 20),
        cost_estimate=pl.CostEstimate(
            flops=12 * slots * weight.size * cross, bytes_accessed=12 * now.size, transcendentals=0
        ),
    )(move_dest, parent, now, now_other, low[0], low[1], high[0], high[1], spread, weight)
    return settle([fillers[0]] + rest + [fillers[1]], moved, token), slope


def solution(mesh):
    placed = (
        P(None, ("runs", "box"), "fld", "slab", None),
        P("runs"),
        P("runs"),
        P(("runs", "box"), "fld", None),
        P(),
        P(),
        P(),
    )
    return jax.shard_map(
        body,
        mesh=mesh,
        in_specs=placed,
        out_specs=(
            P(None, ("runs", "box"), "fld", "slab", None),
            P(("runs", "box"), "fld", "slab", None),
        ),
        check_vma=False,
    )
```

```python
import functools

import jax
import jax.numpy as jnp
import numpy as np
from jax import lax
from jax.experimental import pallas as pl
from jax.experimental.pallas import tpu as pltpu
from jax.sharding import PartitionSpec as P

HIGHEST = lax.Precision.HIGHEST
ROWS = 16


def round_up(value, unit):
    return -(-value // unit) * unit


def split_three(values):
    high = values.astype(jnp.bfloat16)
    rest = values - high.astype(jnp.float32)
    middle = rest.astype(jnp.bfloat16)
    low = (rest - middle.astype(jnp.float32)).astype(jnp.bfloat16)
    return high, middle, low


def place_boxes(per_device, box_count, dest_ref, table):
    own = lax.axis_index("box")
    for slot in range(2 * box_count):
        table[slot] = -1

    def place(b, carry):
        slot = 2 * dest_ref[own * per_device + b]
        table[jnp.where(table[slot] >= 0, slot + 1, slot)] = b
        return carry

    lax.fori_loop(0, per_device, place, 0)


def target_of(own, turn, box_count):
    return lax.rem(own + turn, box_count)


def source_of(own, turn, box_count):
    return lax.rem(own - turn + box_count, box_count)


def each_slot(box_count):
    own = lax.axis_index("box")
    for turn in range(box_count):
        for k in range(2):
            yield turn, k, 2 * target_of(own, turn, box_count) + k


def first_kernel(per_device, box_count, edge, dest_ref, parent_ref, boxes_ref, coarse_ref, *refs):
    outs, (shells, chosen, dest, parent, box_table, face_table, sems, in_sems) = refs[:box_count], refs[box_count:]
    fields, coarse_count, cells = coarse_ref.shape
    planes, cross = outs[0].shape[2:]
    own, slab = lax.axis_index("box"), lax.axis_index("slab")
    fetches = [
        pltpu.make_async_copy(coarse_ref, shells, in_sems.at[0]),
        pltpu.make_async_copy(dest_ref, dest, in_sems.at[1]),
        pltpu.make_async_copy(parent_ref, parent, in_sems.at[2]),
    ]
    for fetch in fetches:
        fetch.start()
    index = face_cells(lax.broadcasted_iota(jnp.int32, (1, cross), 1), edge, planes // 2, slab)
    cell = lax.broadcasted_iota(jnp.int32, (cells, cross), 0)
    one_hot = (cell == index).astype(jnp.float32).astype(jnp.bfloat16)
    fetches[1].wait()
    place_boxes(per_device, box_count, dest, box_table)

    def copy(shift, k, b):
        return pltpu.make_async_copy(
            boxes_ref.at[0, b], outs[shift].at[k, pl.ds(0, fields)], sems.at[shift, k]
        )

    for shift, k, slot in each_slot(box_count):
        b = box_table[slot]

        @pl.when(b >= 0)
        def _():
            copy(shift, k, b).start()

        @pl.when(b < 0)
        def _():
            outs[shift][k, :fields] = jnp.zeros((fields, planes, cross), jnp.float32)

    for slot in range(2 * box_count):
        face_table[slot] = -1
    fetches[2].wait()

    def place(b, carry):
        slot = 2 * dest[b]
        local = parent[b] - own * coarse_count

        @pl.when(jnp.logical_and(local >= 0, local < coarse_count))
        def _():
            face_table[jnp.where(face_table[slot] >= 0, slot + 1, slot)] = local

        return carry

    lax.fori_loop(0, dest.shape[0], place, 0)
    fetches[0].wait()
    high, middle, low = (
        jnp.dot(part, one_hot, preferred_element_type=jnp.float32)
        for part in split_three(shells[...].reshape(fields * coarse_count, cells))
    )
    chosen[...] = (high + (middle + low)).reshape(chosen.shape)
    for shift, k, slot in each_slot(box_count):
        local = face_table[slot]
        for row in range(ROWS):
            to = fields + row // planes
            if row < fields:
                values = chosen[row, pl.ds(jnp.maximum(local, 0), 1)]
                values = jnp.where(local >= 0, values, 0.0)
            else:
                values = jnp.zeros((1, cross), jnp.float32)
            outs[shift][k, to, row % planes : row % planes + 1] = values
    for shift, k, slot in each_slot(box_count):
        b = box_table[slot]

        @pl.when(b >= 0)
        def _():
            copy(shift, k, b).wait()


def pack_first(boxes, coarse, move_dest, parent, edge, box_count):
    per_device, fields, planes, cross = boxes.shape[1:]
    coarse = jnp.transpose(coarse, (1, 0, 2))
    hbm, vmem = pl.BlockSpec(memory_space=pltpu.HBM), pl.BlockSpec(memory_space=pltpu.VMEM)
    item = (2, fields + ROWS // planes, planes, cross)
    return pl.pallas_call(
        functools.partial(first_kernel, per_device, box_count, edge),
        out_shape=[jax.ShapeDtypeStruct(item, jnp.float32)] * box_count,
        in_specs=[hbm] * 4,
        out_specs=[vmem] * box_count,
        scratch_shapes=[
            pltpu.VMEM(coarse.shape, jnp.float32),
            pltpu.VMEM(coarse.shape[:2] + (cross,), jnp.float32),
            pltpu.SMEM(move_dest.shape, jnp.int32),
            pltpu.SMEM(parent.shape, jnp.int32),
            pltpu.SMEM((2 * box_count,), jnp.int32),
            pltpu.SMEM((2 * box_count,), jnp.int32),
            pltpu.SemaphoreType.DMA((box_count, 2)),
            pltpu.SemaphoreType.DMA((3,)),
        ],
        cost_estimate=pl.CostEstimate(
            flops=6 * coarse.size * cross, bytes_accessed=4 * (coarse.size + 2 * boxes.size), transcendentals=0
        ),
    )(move_dest, parent, boxes, coarse)


def later_kernel(turns, per_device, box_count, levels, dest_ref, boxes_ref, *refs):
    outs, (dest, table, sems, in_sem, *stay) = refs[: len(turns)], refs[len(turns) :]
    own = lax.axis_index("box")
    fetch = pltpu.make_async_copy(dest_ref, dest, in_sem)
    fetch.start()
    fetch.wait()
    place_boxes(per_device, box_count, dest, table)
    places = [(n, k, 2 * target_of(own, turn, box_count) + k) for n, turn in enumerate(turns) for k in range(2)]
    held = [stay[0] if turn == 0 else out for turn, out in zip(turns, outs)]

    def copies(n, k, b):
        skip = levels - held[n].shape[0]
        for level in range(skip, levels):
            yield pltpu.make_async_copy(boxes_ref.at[level, b], held[n].at[level - skip, k], sems.at[n, level, k])

    for n, k, slot in places:
        b = table[slot]

        @pl.when(b >= 0)
        def _():
            for copy in copies(n, k, b):
                copy.start()

        @pl.when(b < 0)
        def _():
            for level in range(held[n].shape[0]):
                held[n][level, k] = jnp.zeros(held[n].shape[2:], jnp.float32)

    for n, k, slot in places:
        b = table[slot]

        @pl.when(b >= 0)
        def _():
            for copy in copies(n, k, b):
                copy.wait()

    for n, turn in enumerate(turns):
        if turn == 0:
            settled = pltpu.make_async_copy(held[n], outs[n].at[:, pl.ds(2 * own, 2)], in_sem)
            settled.start()
            settled.wait()


def pack_later(turns, boxes, move_dest, box_count):
    levels, per_device = boxes.shape[:2]
    item = boxes.shape[2:]
    hbm, vmem = pl.BlockSpec(memory_space=pltpu.HBM), pl.BlockSpec(memory_space=pltpu.VMEM)
    size = int(np.prod(item)) * 4
    shapes = [(levels - 1, 2) + item if turn else (levels, 2 * box_count) + item for turn in turns]
    return pl.pallas_call(
        functools.partial(later_kernel, turns, per_device, box_count, levels),
        out_shape=[jax.ShapeDtypeStruct(shape, jnp.float32) for shape in shapes],
        in_specs=[hbm] * 2,
        out_specs=[vmem if turn else hbm for turn in turns],
        scratch_shapes=[
            pltpu.SMEM(move_dest.shape, jnp.int32),
            pltpu.SMEM((2 * box_count,), jnp.int32),
            pltpu.SemaphoreType.DMA((len(turns), levels, 2)),
            pltpu.SemaphoreType.DMA,
        ]
        + [pltpu.VMEM((levels, 2) + item, jnp.float32) for turn in turns if turn == 0],
        cost_estimate=pl.CostEstimate(
            flops=0, bytes_accessed=4 * len(turns) * levels * size, transcendentals=0
        ),
    )(move_dest, boxes)


def settle_later(piece, turn, moved_ref, sem):
    source = source_of(lax.axis_index("box"), turn, moved_ref.shape[1] // 2)
    to = moved_ref.at[pl.ds(1, moved_ref.shape[0] - 1), pl.ds(2 * source, 2)]
    return pltpu.make_async_copy(piece, to, sem)


def settle_kernel(turns, *refs):
    out_ref, sems = refs[-2:]
    copies = [settle_later(refs[n], turn, out_ref, sems.at[n]) for n, turn in enumerate(turns)]
    for copy in copies:
        copy.start()
    for copy in copies:
        copy.wait()


def settle(turns, pieces, moved, after):
    count = len(pieces)
    vmem, hbm = pl.BlockSpec(memory_space=pltpu.VMEM), pl.BlockSpec(memory_space=pltpu.HBM)
    return pl.pallas_call(
        functools.partial(settle_kernel, turns),
        out_shape=jax.ShapeDtypeStruct(moved.shape, jnp.float32),
        in_specs=[vmem] * count + [hbm, vmem],
        out_specs=hbm,
        scratch_shapes=[pltpu.SemaphoreType.DMA((count,))],
        input_output_aliases={count: 0},
        compiler_params=pltpu.CompilerParams(vmem_limit_bytes=48 * 2 ** 20),
        cost_estimate=pl.CostEstimate(
            flops=0, bytes_accessed=8 * count * pieces[0].size, transcendentals=0
        ),
    )(*pieces, moved, after)


def arrive_kernel(box_count, slabs, early, fields, *refs):
    pieces, later = refs[:box_count], refs[box_count : box_count + len(early)]
    now_ref, moved_ref, *edges, sems = refs[box_count + len(early) + 1 :]
    own, slab = lax.axis_index("box"), lax.axis_index("slab")
    planes = now_ref.shape[2]
    mine = pltpu.make_async_copy(pieces[0], now_ref.at[pl.ds(2 * own, 2)], sems.at[0])
    mine.start()
    copies = []
    for turn in range(1, box_count):
        to = moved_ref.at[0, pl.ds(2 * source_of(own, turn, box_count), 2)]
        copies.append(pltpu.make_async_copy(pieces[turn].at[:, pl.ds(0, fields)], to, sems.at[turn]))
    for n, turn in enumerate(early):
        copies.append(settle_later(later[n], turn, moved_ref, sems.at[box_count + n]))
    for copy in copies:
        copy.start()
    faced = [jnp.where(slab == 0, planes - 1, 0)] if slabs == 2 else [0, planes - 1]

    def cut(source):
        for k in range(2):
            for edge_ref, plane in zip(edges, faced):
                for f in range(fields):
                    edge_ref[2 * source + k, f : f + 1] = now_ref[2 * source + k, f, pl.ds(plane, 1)]

    for turn in range(1, box_count):
        source = source_of(own, turn, box_count)
        for k in range(2):
            now_ref[2 * source + k] = pieces[turn][k]
        cut(source)
    mine.wait()
    cut(own)
    for copy in copies:
        copy.wait()


def arrive(pieces, early, later, moved, slabs):
    box_count = len(pieces)
    _, blocks, planes, cross = pieces[0].shape
    fields = moved.shape[2]
    slots = 2 * box_count
    sides = 1 if slabs == 2 else 2
    vmem, hbm = pl.BlockSpec(memory_space=pltpu.VMEM), pl.BlockSpec(memory_space=pltpu.HBM)
    shapes = [(slots, blocks, planes, cross), moved.shape] + [(slots, fields, cross)] * sides
    count = box_count + len(later)
    return pl.pallas_call(
        functools.partial(arrive_kernel, box_count, slabs, early, fields),
        out_shape=[jax.ShapeDtypeStruct(shape, jnp.float32) for shape in shapes],
        in_specs=[hbm] + [vmem] * (count - 1) + [hbm],
        out_specs=[vmem, hbm] + [vmem] * sides,
        scratch_shapes=[pltpu.SemaphoreType.DMA((count,))],
        input_output_aliases={count: 1},
        compiler_params=pltpu.CompilerParams(vmem_limit_bytes=48 * 2 ** 20),
        cost_estimate=pl.CostEstimate(
            flops=0, bytes_accessed=12 * box_count * pieces[0].size, transcendentals=0
        ),
    )(*pieces, *later, moved)


def face_cells(lane, edge, coarse_planes, slab):
    half, side = edge // 2, edge // 2 + 2
    plane, m = lane // (4 * half), lane % half + 1
    which = (lane // half) % 4
    rim = jnp.where(which == 0, m, jnp.where(which == 1, (side - 1) * side + m, m * side))
    rim = jnp.where(which == 3, rim + side - 1, rim) + (slab * coarse_planes + plane + 1) * side * side
    t = lane - 4 * half * coarse_planes
    x_rim = jnp.where(slab > 0, (side - 1) * side * side, 0) + (t // half + 1) * side + m
    return jnp.where(t < 0, rim, jnp.where(t < half * half, x_rim, -1))


def expand_table(coarse_planes, edge, lanes):
    half = edge // 2
    cross = edge * edge
    spread = np.zeros((lanes, (2 * coarse_planes + 1) * cross), np.float32)
    for c in range(coarse_planes):
        base = c * 4 * half
        forward, backward = 2 * c * cross, (2 * c + 1) * cross
        for m in range(edge):
            spread[base + m // 2, backward + m] += 1
            spread[base + half + m // 2, forward + (edge - 1) * edge + m] += 1
            spread[base + 2 * half + m // 2, backward + m * edge] += 1
            spread[base + 3 * half + m // 2, forward + m * edge + edge - 1] += 1
    base, to = coarse_planes * 4 * half, 2 * coarse_planes * cross
    for y in range(edge):
        for z in range(edge):
            spread[base + (y // 2) * half + z // 2, to + y * edge + z] = 1
    return spread


def slope_columns(fields, planes, coarse_planes):
    column_field, forward, backward, centre = [], [], [], []
    p = np.arange(planes)

    def add(field, f, b, c):
        column_field.append(field)
        forward.append(f * np.ones(planes))
        backward.append(b * np.ones(planes))
        centre.append(c * np.ones(planes))

    for f, b, c in ((1, 0, 0), (0, 1, 0), (0, 0, 1)):
        for g in range(2 * fields):
            for q in range(planes):
                here = p == q
                add(g, f * here + c * (p + 1 == q), b * here + c * (p - 1 == q), c * here)
    rows = [g if g < fields else -1 for g in range(ROWS)]
    rows += [fields + g if g < fields else -1 for g in range(ROWS)]
    for g in rows:
        add(g, 0, p == 0, 0)
    for g in rows:
        add(g, p == planes - 1, 0, 0)
    for c in range(coarse_planes):
        for g in rows:
            add(g, p // 2 == c, 0, 0)
        for g in rows:
            add(g, 0, p // 2 == c, 0)
    width = round_up(len(column_field), 128)
    select = np.zeros((2 * fields, width), np.float32)
    masks = np.zeros((3, planes, width), np.float32)
    for k, g in enumerate(column_field):
        if g >= 0:
            select[g, k] = 1
        masks[0, :, k], masks[1, :, k], masks[2, :, k] = forward[k], backward[k], centre[k]
    return select, masks


def slope_kernel(
    edge, planes, fields, coarse_planes, per_device, total, coarse_count, slots, slabs,
    dest_ref, parent_ref, own_ref, other_ref, own_low, other_low, own_high, other_high,
    spread_ref, weight_ref, out_ref, token_ref, stack, parts, ghosts, table, count,
):
    step = pl.program_id(0)
    cross = edge * edge
    rows = fields * planes
    own, slab = lax.axis_index("box"), lax.axis_index("slab")

    @pl.when(step == 0)
    def _():
        token_ref[...] = jnp.zeros_like(token_ref)
        stack[...] = jnp.zeros_like(stack)
        half = weight_ref.shape[0]
        weights = weight_ref[...]
        parts[:half] = weights.astype(jnp.bfloat16)
        parts[half:] = (weights - weights.astype(jnp.bfloat16).astype(jnp.float32)).astype(jnp.bfloat16)
        for slot in range(slots):
            table[slot] = -1
            count[slot] = 0

        def place(b, carry):
            @pl.when(dest_ref[b] == own)
            def _():
                slot = 2 * (b // per_device)
                owner = parent_ref[b] // coarse_count
                table[jnp.where(table[slot] >= 0, slot + 1, slot)] = 2 * owner + count[owner]
                count[owner] = count[owner] + 1

            return carry

        lax.fori_loop(0, total, place, 0)
        for slot in range(slots):
            for n, ref in enumerate((own_ref, other_ref)):
                at = (2 * slot + n) * ROWS
                for block in range(ROWS // planes):
                    ghosts[at + block * planes : at + (block + 1) * planes, :cross] = ref[slot, fields + block]
        high, middle, low = (
            jnp.dot(part, spread_ref[...], preferred_element_type=jnp.float32)
            for part in split_three(ghosts[:, :cross])
        )
        ghosts[...] = high + (middle + low)

    face = table[step]

    @pl.when(face < 0)
    def _():
        out_ref[...] = jnp.zeros_like(out_ref)

    @pl.when(face >= 0)
    def _():
        lane = lax.broadcasted_iota(jnp.int32, (1, cross), 1)
        y, z = lane // edge, lane % edge
        for n, ref in enumerate((own_ref, other_ref)):
            at = (4 + n) * rows
            if planes % 8:
                for f in range(fields):
                    stack[at + f * planes : at + (f + 1) * planes] = ref[step, f]
            else:
                stack[at : at + rows] = ref[step, :fields].reshape(rows, cross)
        cells = stack[4 * rows : 6 * rows]
        stack[0 : 2 * rows] = jnp.where(y < edge - 1, pltpu.roll(cells, cross - edge, 1), 0.0) + jnp.where(
            z < edge - 1, pltpu.roll(cells, cross - 1, 1), 0.0
        )
        stack[2 * rows : 4 * rows] = jnp.where(y > 0, pltpu.roll(cells, edge, 1), 0.0) + jnp.where(
            z > 0, pltpu.roll(cells, 1, 1), 0.0
        )
        rim = ghosts[pl.ds(pl.multiple_of(2 * ROWS * face, 2 * ROWS), 2 * ROWS)]
        base = 6 * rows
        x_face = rim[:, 2 * coarse_planes * cross :]
        stack[base : base + 2 * ROWS] = x_face
        stack[base + 2 * ROWS : base + 4 * ROWS] = x_face

        @pl.when(slab > 0)
        def _():
            stack[base : base + fields] = own_low[step]
            stack[base + ROWS : base + ROWS + fields] = other_low[step]

        @pl.when(slab < slabs - 1)
        def _():
            stack[base + 2 * ROWS : base + 2 * ROWS + fields] = own_high[step]
            stack[base + 3 * ROWS : base + 3 * ROWS + fields] = other_high[step]

        base += 4 * ROWS
        for n in range(2 * coarse_planes):
            stack[base + 2 * ROWS * n : base + 2 * ROWS * (n + 1)] = rim[:, n * cross : (n + 1) * cross]
        values = stack[...]
        high = values.astype(jnp.bfloat16)
        low = (values - high.astype(jnp.float32)).astype(jnp.bfloat16)
        half = weight_ref.shape[0]
        both = jnp.dot(parts[...], high, preferred_element_type=jnp.float32)
        mixed = jnp.dot(parts[:half], low, preferred_element_type=jnp.float32)
        mixed = both[:half] + (both[half:] + mixed)
        if planes % 8:
            for f in range(fields):
                out_ref[0, f] = mixed[f * planes : (f + 1) * planes]
        else:
            out_ref[0] = mixed[:rows].reshape(fields, planes, cross)


def mixing_weights(mixes, group, fields, planes, coarse_planes):
    lap_mix, grad_mix, damp_mix = mixes
    select, masks = slope_columns(fields, planes, coarse_planes)
    terms = jnp.stack([lap_mix + 0.5 * grad_mix, lap_mix - 0.5 * grad_mix, damp_mix - 6.0 * lap_mix])
    terms = lax.dynamic_slice_in_dim(terms, group * fields, fields, 1)
    terms = jnp.where(group == 0, terms, jnp.roll(terms, fields, axis=2))
    terms = jnp.einsum("tfg,gk->tfk", terms, jnp.asarray(select), precision=HIGHEST)
    weight = jnp.sum(terms[:, :, None, :] * jnp.asarray(masks)[:, None], axis=0).reshape(fields * planes, -1)
    return jnp.pad(weight, ((0, round_up(fields * planes, 16) - fields * planes), (0, 0)))


def body(boxes, move_dest, parent, coarse, lap_mix, grad_mix, damp_mix):
    box_count = lax.axis_size("box")
    slabs = lax.axis_size("slab")
    group = lax.axis_index("fld")
    levels, per_device, fields, planes, cross = boxes.shape
    edge = planes * slabs
    coarse_planes = planes // 2
    slots = 2 * box_count
    total = move_dest.shape[0]
    coarse_count = coarse.shape[0]

    def send(piece, turn):
        return lax.ppermute(piece, "box", [(s, (s + turn) % box_count) for s in range(box_count)])

    near = pack_later((1, box_count - 1), boxes, move_dest, box_count)
    near = [send(near[0], 1), send(near[1], box_count - 1)]
    first = pack_first(boxes, coarse, move_dest, parent, edge, box_count)
    arrived = [first[0]] + [send(first[turn], turn) for turn in range(1, box_count)]
    moved, *middle = pack_later((0,) + tuple(range(2, box_count - 1)), boxes, move_dest, box_count)
    middle, arrived[1:] = lax.optimization_barrier((middle, arrived[1:]))
    middle = [send(piece, n + 2) for n, piece in enumerate(middle)]
    later_arrived = [near[0]] + middle + [near[1]]
    now, moved, *facing = arrive(arrived, (), [], moved, slabs)

    swap = [(0, 1), (1, 0)]
    now_other = lax.ppermute(now, "fld", swap)

    def shifted(values, up):
        pairs = [(s, s + 1) if up else (s + 1, s) for s in range(slabs - 1)]
        own_group = lax.ppermute(values, "slab", swap if slabs == 2 else pairs)
        return own_group, lax.ppermute(own_group, "fld", swap)

    low = shifted(facing[-1], True)
    high = low if slabs == 2 else shifted(facing[0], False)

    weight = mixing_weights((lap_mix, grad_mix, damp_mix), group, fields, planes, coarse_planes)
    spread = jnp.asarray(expand_table(coarse_planes, edge, cross)).astype(jnp.bfloat16)
    smem, vmem = pl.BlockSpec(memory_space=pltpu.SMEM), pl.BlockSpec(memory_space=pltpu.VMEM)
    slope, token = pl.pallas_call(
        functools.partial(
            slope_kernel, edge, planes, fields, coarse_planes, per_device, total, coarse_count, slots, slabs
        ),
        grid=(slots,),
        out_shape=[
            jax.ShapeDtypeStruct((slots, fields, planes, cross), jnp.float32),
            jax.ShapeDtypeStruct((8, 128), jnp.float32),
        ],
        in_specs=[smem, smem] + [vmem] * 8,
        out_specs=[pl.BlockSpec((1, fields, planes, cross), lambda n: (n, 0, 0, 0)), vmem],
        scratch_shapes=[
            pltpu.VMEM((weight.shape[1], cross), jnp.float32),
            pltpu.VMEM((2 * weight.shape[0], weight.shape[1]), jnp.bfloat16),
            pltpu.VMEM((2 * ROWS * slots, spread.shape[1]), jnp.float32),
            pltpu.SMEM((slots,), jnp.int32),
            pltpu.SMEM((slots,), jnp.int32),
        ],
        compiler_params=pltpu.CompilerParams(vmem_limit_bytes=48 * 2 ** 20),
        cost_estimate=pl.CostEstimate(
            flops=3 * slots * weight.size * cross, bytes_accessed=12 * now.size, transcendentals=0
        ),
    )(move_dest, parent, now, now_other, low[0], low[1], high[0], high[1], spread, weight)
    return settle(tuple(range(1, box_count)), later_arrived, moved, token), slope


def solution(mesh):
    placed = (
        P(None, ("runs", "box"), "fld", "slab", None),
        P("runs"),
        P("runs"),
        P(("runs", "box"), "fld", None),
        P(),
        P(),
        P(),
    )
    return jax.shard_map(
        body,
        mesh=mesh,
        in_specs=placed,
        out_specs=(
            P(None, ("runs", "box"), "fld", "slab", None),
            P(("runs", "box"), "fld", "slab", None),
        ),
        check_vma=False,
    )
```

```python
import functools

import jax
import jax.numpy as jnp
import numpy as np
from jax import lax
from jax.experimental import pallas as pl
from jax.experimental.pallas import tpu as pltpu
from jax.sharding import PartitionSpec as P

HIGHEST = lax.Precision.HIGHEST
ROWS = 16


def round_up(value, unit):
    return -(-value // unit) * unit


def split_three(values):
    high = values.astype(jnp.bfloat16)
    rest = values - high.astype(jnp.float32)
    middle = rest.astype(jnp.bfloat16)
    low = (rest - middle.astype(jnp.float32)).astype(jnp.bfloat16)
    return high, middle, low


def place_boxes(per_device, box_count, dest_ref, table):
    own = lax.axis_index("box")
    for slot in range(2 * box_count):
        table[slot] = -1

    def place(b, carry):
        slot = 2 * dest_ref[own * per_device + b]
        table[jnp.where(table[slot] >= 0, slot + 1, slot)] = b
        return carry

    lax.fori_loop(0, per_device, place, 0)


def target_of(own, turn, box_count):
    return lax.rem(own + turn, box_count)


def source_of(own, turn, box_count):
    return lax.rem(own - turn + box_count, box_count)


def each_slot(box_count):
    own = lax.axis_index("box")
    for turn in range(box_count):
        for k in range(2):
            yield turn, k, 2 * target_of(own, turn, box_count) + k


def first_kernel(per_device, box_count, edge, dest_ref, parent_ref, boxes_ref, coarse_ref, *refs):
    outs, (shells, chosen, dest, parent, box_table, face_table, sems, in_sems) = refs[:box_count], refs[box_count:]
    fields, coarse_count, cells = coarse_ref.shape
    planes, cross = outs[0].shape[2:]
    own, slab = lax.axis_index("box"), lax.axis_index("slab")
    fetches = [
        pltpu.make_async_copy(coarse_ref, shells, in_sems.at[0]),
        pltpu.make_async_copy(dest_ref, dest, in_sems.at[1]),
        pltpu.make_async_copy(parent_ref, parent, in_sems.at[2]),
    ]
    for fetch in fetches:
        fetch.start()
    index = face_cells(lax.broadcasted_iota(jnp.int32, (1, cross), 1), edge, planes // 2, slab)
    cell = lax.broadcasted_iota(jnp.int32, (cells, cross), 0)
    one_hot = (cell == index).astype(jnp.float32).astype(jnp.bfloat16)
    fetches[1].wait()
    place_boxes(per_device, box_count, dest, box_table)

    def copy(shift, k, b):
        return pltpu.make_async_copy(
            boxes_ref.at[0, b], outs[shift].at[k, pl.ds(0, fields)], sems.at[shift, k]
        )

    for shift, k, slot in each_slot(box_count):
        b = box_table[slot]

        @pl.when(b >= 0)
        def _():
            copy(shift, k, b).start()

        @pl.when(b < 0)
        def _():
            outs[shift][k, :fields] = jnp.zeros((fields, planes, cross), jnp.float32)

    for slot in range(2 * box_count):
        face_table[slot] = -1
    fetches[2].wait()

    def place(b, carry):
        slot = 2 * dest[b]
        local = parent[b] - own * coarse_count

        @pl.when(jnp.logical_and(local >= 0, local < coarse_count))
        def _():
            face_table[jnp.where(face_table[slot] >= 0, slot + 1, slot)] = local

        return carry

    lax.fori_loop(0, dest.shape[0], place, 0)
    fetches[0].wait()
    high, middle, low = (
        jnp.dot(part, one_hot, preferred_element_type=jnp.float32)
        for part in split_three(shells[...].reshape(fields * coarse_count, cells))
    )
    chosen[...] = (high + (middle + low)).reshape(chosen.shape)
    for shift, k, slot in each_slot(box_count):
        local = face_table[slot]
        for row in range(ROWS):
            to = fields + row // planes
            if row < fields:
                values = chosen[row, pl.ds(jnp.maximum(local, 0), 1)]
                values = jnp.where(local >= 0, values, 0.0)
            else:
                values = jnp.zeros((1, cross), jnp.float32)
            outs[shift][k, to, row % planes : row % planes + 1] = values
    for shift, k, slot in each_slot(box_count):
        b = box_table[slot]

        @pl.when(b >= 0)
        def _():
            copy(shift, k, b).wait()


def pack_first(boxes, coarse, move_dest, parent, edge, box_count):
    per_device, fields, planes, cross = boxes.shape[1:]
    coarse = jnp.transpose(coarse, (1, 0, 2))
    hbm, vmem = pl.BlockSpec(memory_space=pltpu.HBM), pl.BlockSpec(memory_space=pltpu.VMEM)
    item = (2, fields + ROWS // planes, planes, cross)
    return pl.pallas_call(
        functools.partial(first_kernel, per_device, box_count, edge),
        out_shape=[jax.ShapeDtypeStruct(item, jnp.float32)] * box_count,
        in_specs=[hbm] * 4,
        out_specs=[vmem] * box_count,
        scratch_shapes=[
            pltpu.VMEM(coarse.shape, jnp.float32),
            pltpu.VMEM(coarse.shape[:2] + (cross,), jnp.float32),
            pltpu.SMEM(move_dest.shape, jnp.int32),
            pltpu.SMEM(parent.shape, jnp.int32),
            pltpu.SMEM((2 * box_count,), jnp.int32),
            pltpu.SMEM((2 * box_count,), jnp.int32),
            pltpu.SemaphoreType.DMA((box_count, 2)),
            pltpu.SemaphoreType.DMA((3,)),
        ],
        cost_estimate=pl.CostEstimate(
            flops=6 * coarse.size * cross, bytes_accessed=4 * (coarse.size + 2 * boxes.size), transcendentals=0
        ),
    )(move_dest, parent, boxes, coarse)


def later_kernel(turns, per_device, box_count, levels, dest_ref, boxes_ref, *refs):
    outs, (dest, table, sems, in_sem, *stay) = refs[: len(turns)], refs[len(turns) :]
    own = lax.axis_index("box")
    fetch = pltpu.make_async_copy(dest_ref, dest, in_sem)
    fetch.start()
    fetch.wait()
    place_boxes(per_device, box_count, dest, table)
    places = [(n, k, 2 * target_of(own, turn, box_count) + k) for n, turn in enumerate(turns) for k in range(2)]
    held = [stay[0] if turn == 0 else out for turn, out in zip(turns, outs)]

    def copies(n, k, b):
        skip = levels - held[n].shape[0]
        for level in range(skip, levels):
            yield pltpu.make_async_copy(boxes_ref.at[level, b], held[n].at[level - skip, k], sems.at[n, level, k])

    for n, k, slot in places:
        b = table[slot]

        @pl.when(b >= 0)
        def _():
            for copy in copies(n, k, b):
                copy.start()

        @pl.when(b < 0)
        def _():
            for level in range(held[n].shape[0]):
                held[n][level, k] = jnp.zeros(held[n].shape[2:], jnp.float32)

    for n, k, slot in places:
        b = table[slot]

        @pl.when(b >= 0)
        def _():
            for copy in copies(n, k, b):
                copy.wait()

    for n, turn in enumerate(turns):
        if turn == 0:
            settled = pltpu.make_async_copy(held[n], outs[n].at[:, pl.ds(2 * own, 2)], in_sem)
            settled.start()
            settled.wait()


def pack_later(turns, boxes, move_dest, box_count):
    levels, per_device = boxes.shape[:2]
    item = boxes.shape[2:]
    hbm, vmem = pl.BlockSpec(memory_space=pltpu.HBM), pl.BlockSpec(memory_space=pltpu.VMEM)
    size = int(np.prod(item)) * 4
    shapes = [(levels - 1, 2) + item if turn else (levels, 2 * box_count) + item for turn in turns]
    return pl.pallas_call(
        functools.partial(later_kernel, turns, per_device, box_count, levels),
        out_shape=[jax.ShapeDtypeStruct(shape, jnp.float32) for shape in shapes],
        in_specs=[hbm] * 2,
        out_specs=[vmem if turn else hbm for turn in turns],
        scratch_shapes=[
            pltpu.SMEM(move_dest.shape, jnp.int32),
            pltpu.SMEM((2 * box_count,), jnp.int32),
            pltpu.SemaphoreType.DMA((len(turns), levels, 2)),
            pltpu.SemaphoreType.DMA,
        ]
        + [pltpu.VMEM((levels, 2) + item, jnp.float32) for turn in turns if turn == 0],
        cost_estimate=pl.CostEstimate(
            flops=0, bytes_accessed=4 * len(turns) * levels * size, transcendentals=0
        ),
    )(move_dest, boxes)


def settle_later(piece, turn, moved_ref, sem):
    source = source_of(lax.axis_index("box"), turn, moved_ref.shape[1] // 2)
    to = moved_ref.at[pl.ds(1, moved_ref.shape[0] - 1), pl.ds(2 * source, 2)]
    return pltpu.make_async_copy(piece, to, sem)


def settle_kernel(turns, *refs):
    out_ref, sems = refs[-2:]
    copies = [settle_later(refs[n], turn, out_ref, sems.at[n]) for n, turn in enumerate(turns)]
    for copy in copies:
        copy.start()
    for copy in copies:
        copy.wait()


def settle(turns, pieces, moved, after):
    count = len(pieces)
    vmem, hbm = pl.BlockSpec(memory_space=pltpu.VMEM), pl.BlockSpec(memory_space=pltpu.HBM)
    return pl.pallas_call(
        functools.partial(settle_kernel, turns),
        out_shape=jax.ShapeDtypeStruct(moved.shape, jnp.float32),
        in_specs=[vmem] * count + [hbm, vmem],
        out_specs=hbm,
        scratch_shapes=[pltpu.SemaphoreType.DMA((count,))],
        input_output_aliases={count: 0},
        compiler_params=pltpu.CompilerParams(vmem_limit_bytes=48 * 2 ** 20),
        cost_estimate=pl.CostEstimate(
            flops=0, bytes_accessed=8 * count * pieces[0].size, transcendentals=0
        ),
    )(*pieces, moved, after)


def arrive_kernel(box_count, slabs, early, fields, *refs):
    pieces, later = refs[:box_count], refs[box_count : box_count + len(early)]
    now_ref, moved_ref, *edges, sems = refs[box_count + len(early) + 1 :]
    own, slab = lax.axis_index("box"), lax.axis_index("slab")
    planes = now_ref.shape[2]
    mine = pltpu.make_async_copy(pieces[0], now_ref.at[pl.ds(2 * own, 2)], sems.at[0])
    mine.start()
    copies = []
    for turn in range(1, box_count):
        to = moved_ref.at[0, pl.ds(2 * source_of(own, turn, box_count), 2)]
        copies.append(pltpu.make_async_copy(pieces[turn].at[:, pl.ds(0, fields)], to, sems.at[turn]))
    for n, turn in enumerate(early):
        copies.append(settle_later(later[n], turn, moved_ref, sems.at[box_count + n]))
    for copy in copies:
        copy.start()
    faced = [jnp.where(slab == 0, planes - 1, 0)] if slabs == 2 else [0, planes - 1]

    def cut(source):
        for k in range(2):
            for edge_ref, plane in zip(edges, faced):
                for f in range(fields):
                    edge_ref[2 * source + k, f : f + 1] = now_ref[2 * source + k, f, pl.ds(plane, 1)]

    for turn in range(1, box_count):
        source = source_of(own, turn, box_count)
        for k in range(2):
            now_ref[2 * source + k] = pieces[turn][k]
        cut(source)
    mine.wait()
    cut(own)
    for copy in copies:
        copy.wait()


def arrive(pieces, early, later, moved, slabs):
    box_count = len(pieces)
    _, blocks, planes, cross = pieces[0].shape
    fields = moved.shape[2]
    slots = 2 * box_count
    sides = 1 if slabs == 2 else 2
    vmem, hbm = pl.BlockSpec(memory_space=pltpu.VMEM), pl.BlockSpec(memory_space=pltpu.HBM)
    shapes = [(slots, blocks, planes, cross), moved.shape] + [(slots, fields, cross)] * sides
    count = box_count + len(later)
    return pl.pallas_call(
        functools.partial(arrive_kernel, box_count, slabs, early, fields),
        out_shape=[jax.ShapeDtypeStruct(shape, jnp.float32) for shape in shapes],
        in_specs=[hbm] + [vmem] * (count - 1) + [hbm],
        out_specs=[vmem, hbm] + [vmem] * sides,
        scratch_shapes=[pltpu.SemaphoreType.DMA((count,))],
        input_output_aliases={count: 1},
        compiler_params=pltpu.CompilerParams(vmem_limit_bytes=48 * 2 ** 20),
        cost_estimate=pl.CostEstimate(
            flops=0, bytes_accessed=12 * box_count * pieces[0].size, transcendentals=0
        ),
    )(*pieces, *later, moved)


def face_cells(lane, edge, coarse_planes, slab):
    half, side = edge // 2, edge // 2 + 2
    plane, m = lane // (4 * half), lane % half + 1
    which = (lane // half) % 4
    rim = jnp.where(which == 0, m, jnp.where(which == 1, (side - 1) * side + m, m * side))
    rim = jnp.where(which == 3, rim + side - 1, rim) + (slab * coarse_planes + plane + 1) * side * side
    t = lane - 4 * half * coarse_planes
    x_rim = jnp.where(slab > 0, (side - 1) * side * side, 0) + (t // half + 1) * side + m
    return jnp.where(t < 0, rim, jnp.where(t < half * half, x_rim, -1))


def expand_table(coarse_planes, edge, lanes):
    half = edge // 2
    cross = edge * edge
    spread = np.zeros((lanes, (2 * coarse_planes + 1) * cross), np.float32)
    for c in range(coarse_planes):
        base = c * 4 * half
        forward, backward = 2 * c * cross, (2 * c + 1) * cross
        for m in range(edge):
            spread[base + m // 2, backward + m] += 1
            spread[base + half + m // 2, forward + (edge - 1) * edge + m] += 1
            spread[base + 2 * half + m // 2, backward + m * edge] += 1
            spread[base + 3 * half + m // 2, forward + m * edge + edge - 1] += 1
    base, to = coarse_planes * 4 * half, 2 * coarse_planes * cross
    for y in range(edge):
        for z in range(edge):
            spread[base + (y // 2) * half + z // 2, to + y * edge + z] = 1
    return spread


def slope_columns(fields, planes, coarse_planes):
    column_field, forward, backward, centre = [], [], [], []
    p = np.arange(planes)

    def add(field, f, b, c):
        column_field.append(field)
        forward.append(f * np.ones(planes))
        backward.append(b * np.ones(planes))
        centre.append(c * np.ones(planes))

    for f, b, c in ((1, 0, 0), (0, 1, 0), (0, 0, 1)):
        for g in range(2 * fields):
            for q in range(planes):
                here = p == q
                add(g, f * here + c * (p + 1 == q), b * here + c * (p - 1 == q), c * here)
    rows = [g if g < fields else -1 for g in range(ROWS)]
    rows += [fields + g if g < fields else -1 for g in range(ROWS)]
    for g in rows:
        add(g, 0, p == 0, 0)
    for g in rows:
        add(g, p == planes - 1, 0, 0)
    for c in range(coarse_planes):
        for g in rows:
            add(g, p // 2 == c, 0, 0)
        for g in rows:
            add(g, 0, p // 2 == c, 0)
    width = round_up(len(column_field), 128)
    select = np.zeros((2 * fields, width), np.float32)
    masks = np.zeros((3, planes, width), np.float32)
    for k, g in enumerate(column_field):
        if g >= 0:
            select[g, k] = 1
        masks[0, :, k], masks[1, :, k], masks[2, :, k] = forward[k], backward[k], centre[k]
    return select, masks


def slope_kernel(
    edge, planes, fields, coarse_planes, per_device, total, coarse_count, slots, slabs,
    dest_ref, parent_ref, own_ref, other_ref, own_low, other_low, own_high, other_high,
    spread_ref, weight_ref, out_ref, token_ref, stack, parts, ghosts, table, count,
):
    step = pl.program_id(0)
    cross = edge * edge
    rows = fields * planes
    own, slab = lax.axis_index("box"), lax.axis_index("slab")

    @pl.when(step == 0)
    def _():
        token_ref[...] = jnp.zeros_like(token_ref)
        stack[...] = jnp.zeros_like(stack)
        half = weight_ref.shape[0]
        weights = weight_ref[...]
        parts[:half] = weights.astype(jnp.bfloat16)
        parts[half:] = (weights - weights.astype(jnp.bfloat16).astype(jnp.float32)).astype(jnp.bfloat16)
        for slot in range(slots):
            table[slot] = -1
            count[slot] = 0

        def place(b, carry):
            @pl.when(dest_ref[b] == own)
            def _():
                slot = 2 * (b // per_device)
                owner = parent_ref[b] // coarse_count
                table[jnp.where(table[slot] >= 0, slot + 1, slot)] = 2 * owner + count[owner]
                count[owner] = count[owner] + 1

            return carry

        lax.fori_loop(0, total, place, 0)
        for slot in range(slots):
            for n, ref in enumerate((own_ref, other_ref)):
                at = (2 * slot + n) * ROWS
                for block in range(ROWS // planes):
                    ghosts[at + block * planes : at + (block + 1) * planes, :cross] = ref[slot, fields + block]
        high, middle, low = (
            jnp.dot(part, spread_ref[...], preferred_element_type=jnp.float32)
            for part in split_three(ghosts[:, :cross])
        )
        ghosts[...] = high + (middle + low)

    face = table[step]

    @pl.when(face < 0)
    def _():
        out_ref[...] = jnp.zeros_like(out_ref)

    @pl.when(face >= 0)
    def _():
        lane = lax.broadcasted_iota(jnp.int32, (1, cross), 1)
        y, z = lane // edge, lane % edge
        for n, ref in enumerate((own_ref, other_ref)):
            at = (4 + n) * rows
            if planes % 8:
                for f in range(fields):
                    stack[at + f * planes : at + (f + 1) * planes] = ref[step, f]
            else:
                stack[at : at + rows] = ref[step, :fields].reshape(rows, cross)
        cells = stack[4 * rows : 6 * rows]
        stack[0 : 2 * rows] = jnp.where(y < edge - 1, pltpu.roll(cells, cross - edge, 1), 0.0) + jnp.where(
            z < edge - 1, pltpu.roll(cells, cross - 1, 1), 0.0
        )
        stack[2 * rows : 4 * rows] = jnp.where(y > 0, pltpu.roll(cells, edge, 1), 0.0) + jnp.where(
            z > 0, pltpu.roll(cells, 1, 1), 0.0
        )
        rim = ghosts[pl.ds(pl.multiple_of(2 * ROWS * face, 2 * ROWS), 2 * ROWS)]
        base = 6 * rows
        x_face = rim[:, 2 * coarse_planes * cross :]
        stack[base : base + 2 * ROWS] = x_face
        stack[base + 2 * ROWS : base + 4 * ROWS] = x_face

        @pl.when(slab > 0)
        def _():
            stack[base : base + fields] = own_low[step]
            stack[base + ROWS : base + ROWS + fields] = other_low[step]

        @pl.when(slab < slabs - 1)
        def _():
            stack[base + 2 * ROWS : base + 2 * ROWS + fields] = own_high[step]
            stack[base + 3 * ROWS : base + 3 * ROWS + fields] = other_high[step]

        base += 4 * ROWS
        for n in range(2 * coarse_planes):
            stack[base + 2 * ROWS * n : base + 2 * ROWS * (n + 1)] = rim[:, n * cross : (n + 1) * cross]
        values = stack[...]
        high = values.astype(jnp.bfloat16)
        low = (values - high.astype(jnp.float32)).astype(jnp.bfloat16)
        half = weight_ref.shape[0]
        both = jnp.dot(parts[...], high, preferred_element_type=jnp.float32)
        mixed = jnp.dot(parts[:half], low, preferred_element_type=jnp.float32)
        mixed = both[:half] + (both[half:] + mixed)
        if planes % 8:
            for f in range(fields):
                out_ref[0, f] = mixed[f * planes : (f + 1) * planes]
        else:
            out_ref[0] = mixed[:rows].reshape(fields, planes, cross)


def mixing_weights(mixes, group, fields, planes, coarse_planes):
    lap_mix, grad_mix, damp_mix = mixes
    select, masks = slope_columns(fields, planes, coarse_planes)
    terms = jnp.stack([lap_mix + 0.5 * grad_mix, lap_mix - 0.5 * grad_mix, damp_mix - 6.0 * lap_mix])
    terms = lax.dynamic_slice_in_dim(terms, group * fields, fields, 1)
    terms = jnp.where(group == 0, terms, jnp.roll(terms, fields, axis=2))
    terms = jnp.einsum("tfg,gk->tfk", terms, jnp.asarray(select), precision=HIGHEST)
    weight = jnp.sum(terms[:, :, None, :] * jnp.asarray(masks)[:, None], axis=0).reshape(fields * planes, -1)
    return jnp.pad(weight, ((0, round_up(fields * planes, 16) - fields * planes), (0, 0)))


def body(boxes, move_dest, parent, coarse, lap_mix, grad_mix, damp_mix):
    box_count = lax.axis_size("box")
    slabs = lax.axis_size("slab")
    group = lax.axis_index("fld")
    levels, per_device, fields, planes, cross = boxes.shape
    edge = planes * slabs
    coarse_planes = planes // 2
    slots = 2 * box_count
    total = move_dest.shape[0]
    coarse_count = coarse.shape[0]

    def send(piece, turn):
        return lax.ppermute(piece, "box", [(s, (s + turn) % box_count) for s in range(box_count)])

    near = pack_later((1, box_count - 1), boxes, move_dest, box_count)
    near = [send(near[0], 1), send(near[1], box_count - 1)]
    first = pack_first(boxes, coarse, move_dest, parent, edge, box_count)
    arrived = [first[0]] + [send(first[turn], turn) for turn in range(1, box_count)]
    moved, *middle = pack_later((0,) + tuple(range(2, box_count - 1)), boxes, move_dest, box_count)
    middle = [send(piece, n + 2) for n, piece in enumerate(middle)]
    later_arrived = [near[0]] + middle + [near[1]]
    now, moved, *facing = arrive(arrived, (), [], moved, slabs)

    swap = [(0, 1), (1, 0)]
    now_other = lax.ppermute(now, "fld", swap)

    def shifted(values, up):
        pairs = [(s, s + 1) if up else (s + 1, s) for s in range(slabs - 1)]
        own_group = lax.ppermute(values, "slab", swap if slabs == 2 else pairs)
        return own_group, lax.ppermute(own_group, "fld", swap)

    low = shifted(facing[-1], True)
    high = low if slabs == 2 else shifted(facing[0], False)

    weight = mixing_weights((lap_mix, grad_mix, damp_mix), group, fields, planes, coarse_planes)
    spread = jnp.asarray(expand_table(coarse_planes, edge, cross)).astype(jnp.bfloat16)
    smem, vmem = pl.BlockSpec(memory_space=pltpu.SMEM), pl.BlockSpec(memory_space=pltpu.VMEM)
    slope, token = pl.pallas_call(
        functools.partial(
            slope_kernel, edge, planes, fields, coarse_planes, per_device, total, coarse_count, slots, slabs
        ),
        grid=(slots,),
        out_shape=[
            jax.ShapeDtypeStruct((slots, fields, planes, cross), jnp.float32),
            jax.ShapeDtypeStruct((8, 128), jnp.float32),
        ],
        in_specs=[smem, smem] + [vmem] * 8,
        out_specs=[pl.BlockSpec((1, fields, planes, cross), lambda n: (n, 0, 0, 0)), vmem],
        scratch_shapes=[
            pltpu.VMEM((weight.shape[1], cross), jnp.float32),
            pltpu.VMEM((2 * weight.shape[0], weight.shape[1]), jnp.bfloat16),
            pltpu.VMEM((2 * ROWS * slots, spread.shape[1]), jnp.float32),
            pltpu.SMEM((slots,), jnp.int32),
            pltpu.SMEM((slots,), jnp.int32),
        ],
        compiler_params=pltpu.CompilerParams(vmem_limit_bytes=48 * 2 ** 20),
        cost_estimate=pl.CostEstimate(
            flops=3 * slots * weight.size * cross, bytes_accessed=12 * now.size, transcendentals=0
        ),
    )(move_dest, parent, now, now_other, low[0], low[1], high[0], high[1], spread, weight)
    return settle(tuple(range(1, box_count)), later_arrived, moved, token), slope


def solution(mesh):
    placed = (
        P(None, ("runs", "box"), "fld", "slab", None),
        P("runs"),
        P("runs"),
        P(("runs", "box"), "fld", None),
        P(),
        P(),
        P(),
    )
    return jax.shard_map(
        body,
        mesh=mesh,
        in_specs=placed,
        out_specs=(
            P(None, ("runs", "box"), "fld", "slab", None),
            P(("runs", "box"), "fld", "slab", None),
        ),
        check_vma=False,
    )
```

```python
import functools

import jax
import jax.numpy as jnp
import numpy as np
from jax import lax
from jax.experimental import pallas as pl
from jax.experimental.pallas import tpu as pltpu
from jax.sharding import PartitionSpec as P

HIGHEST = lax.Precision.HIGHEST
ROWS = 16


def round_up(value, unit):
    return -(-value // unit) * unit


def split_three(values):
    high = values.astype(jnp.bfloat16)
    rest = values - high.astype(jnp.float32)
    middle = rest.astype(jnp.bfloat16)
    low = (rest - middle.astype(jnp.float32)).astype(jnp.bfloat16)
    return high, middle, low


def place_boxes(per_device, box_count, dest_ref, table):
    own = lax.axis_index("box")
    for slot in range(2 * box_count):
        table[slot] = -1

    def place(b, carry):
        slot = 2 * dest_ref[own * per_device + b]
        table[jnp.where(table[slot] >= 0, slot + 1, slot)] = b
        return carry

    lax.fori_loop(0, per_device, place, 0)


def target_of(own, turn, box_count):
    return lax.rem(own + turn, box_count)


def source_of(own, turn, box_count):
    return lax.rem(own - turn + box_count, box_count)


def each_slot(box_count):
    own = lax.axis_index("box")
    for turn in range(box_count):
        for k in range(2):
            yield turn, k, 2 * target_of(own, turn, box_count) + k


def first_kernel(per_device, box_count, edge, dest_ref, parent_ref, boxes_ref, coarse_ref, *refs):
    outs, (shells, chosen, dest, parent, box_table, face_table, sems, in_sems) = refs[:box_count], refs[box_count:]
    fields, coarse_count, cells = coarse_ref.shape
    planes, cross = outs[0].shape[2:]
    own, slab = lax.axis_index("box"), lax.axis_index("slab")
    fetches = [
        pltpu.make_async_copy(coarse_ref, shells, in_sems.at[0]),
        pltpu.make_async_copy(dest_ref, dest, in_sems.at[1]),
        pltpu.make_async_copy(parent_ref, parent, in_sems.at[2]),
    ]
    for fetch in fetches:
        fetch.start()
    index = face_cells(lax.broadcasted_iota(jnp.int32, (1, cross), 1), edge, planes // 2, slab)
    cell = lax.broadcasted_iota(jnp.int32, (cells, cross), 0)
    one_hot = (cell == index).astype(jnp.float32).astype(jnp.bfloat16)
    fetches[1].wait()
    place_boxes(per_device, box_count, dest, box_table)

    def copy(shift, k, b):
        return pltpu.make_async_copy(
            boxes_ref.at[0, b], outs[shift].at[k, pl.ds(0, fields)], sems.at[shift, k]
        )

    for shift, k, slot in each_slot(box_count):
        b = box_table[slot]

        @pl.when(b >= 0)
        def _():
            copy(shift, k, b).start()

        @pl.when(b < 0)
        def _():
            outs[shift][k, :fields] = jnp.zeros((fields, planes, cross), jnp.float32)

    for slot in range(2 * box_count):
        face_table[slot] = -1
    fetches[2].wait()

    def place(b, carry):
        slot = 2 * dest[b]
        local = parent[b] - own * coarse_count

        @pl.when(jnp.logical_and(local >= 0, local < coarse_count))
        def _():
            face_table[jnp.where(face_table[slot] >= 0, slot + 1, slot)] = local

        return carry

    lax.fori_loop(0, dest.shape[0], place, 0)
    fetches[0].wait()
    high, middle, low = (
        jnp.dot(part, one_hot, preferred_element_type=jnp.float32)
        for part in split_three(shells[...].reshape(fields * coarse_count, cells))
    )
    chosen[...] = (high + (middle + low)).reshape(chosen.shape)
    for shift, k, slot in each_slot(box_count):
        local = face_table[slot]
        for row in range(ROWS):
            to = fields + row // planes
            if row < fields:
                values = chosen[row, pl.ds(jnp.maximum(local, 0), 1)]
                values = jnp.where(local >= 0, values, 0.0)
            else:
                values = jnp.zeros((1, cross), jnp.float32)
            outs[shift][k, to, row % planes : row % planes + 1] = values
    for shift, k, slot in each_slot(box_count):
        b = box_table[slot]

        @pl.when(b >= 0)
        def _():
            copy(shift, k, b).wait()


def pack_first(boxes, coarse, move_dest, parent, edge, box_count):
    per_device, fields, planes, cross = boxes.shape[1:]
    coarse = jnp.transpose(coarse, (1, 0, 2))
    hbm, vmem = pl.BlockSpec(memory_space=pltpu.HBM), pl.BlockSpec(memory_space=pltpu.VMEM)
    item = (2, fields + ROWS // planes, planes, cross)
    return pl.pallas_call(
        functools.partial(first_kernel, per_device, box_count, edge),
        out_shape=[jax.ShapeDtypeStruct(item, jnp.float32)] * box_count,
        in_specs=[hbm] * 4,
        out_specs=[vmem] * box_count,
        scratch_shapes=[
            pltpu.VMEM(coarse.shape, jnp.float32),
            pltpu.VMEM(coarse.shape[:2] + (cross,), jnp.float32),
            pltpu.SMEM(move_dest.shape, jnp.int32),
            pltpu.SMEM(parent.shape, jnp.int32),
            pltpu.SMEM((2 * box_count,), jnp.int32),
            pltpu.SMEM((2 * box_count,), jnp.int32),
            pltpu.SemaphoreType.DMA((box_count, 2)),
            pltpu.SemaphoreType.DMA((3,)),
        ],
        cost_estimate=pl.CostEstimate(
            flops=6 * coarse.size * cross, bytes_accessed=4 * (coarse.size + 2 * boxes.size), transcendentals=0
        ),
    )(move_dest, parent, boxes, coarse)


def later_kernel(turns, per_device, box_count, levels, dest_ref, boxes_ref, *refs):
    outs, (dest, table, sems, in_sem, *stay) = refs[: len(turns)], refs[len(turns) :]
    own = lax.axis_index("box")
    fetch = pltpu.make_async_copy(dest_ref, dest, in_sem)
    fetch.start()
    fetch.wait()
    place_boxes(per_device, box_count, dest, table)
    places = [(n, k, 2 * target_of(own, turn, box_count) + k) for n, turn in enumerate(turns) for k in range(2)]
    held = [stay[0] if turn == 0 else out for turn, out in zip(turns, outs)]

    def copies(n, k, b):
        skip = levels - held[n].shape[0]
        for level in range(skip, levels):
            yield pltpu.make_async_copy(boxes_ref.at[level, b], held[n].at[level - skip, k], sems.at[n, level, k])

    for n, k, slot in places:
        b = table[slot]

        @pl.when(b >= 0)
        def _():
            for copy in copies(n, k, b):
                copy.start()

        @pl.when(b < 0)
        def _():
            for level in range(held[n].shape[0]):
                held[n][level, k] = jnp.zeros(held[n].shape[2:], jnp.float32)

    for n, k, slot in places:
        b = table[slot]

        @pl.when(b >= 0)
        def _():
            for copy in copies(n, k, b):
                copy.wait()

    for n, turn in enumerate(turns):
        if turn == 0:
            settled = pltpu.make_async_copy(held[n], outs[n].at[:, pl.ds(2 * own, 2)], in_sem)
            settled.start()
            settled.wait()


def pack_later(turns, boxes, move_dest, box_count):
    levels, per_device = boxes.shape[:2]
    item = boxes.shape[2:]
    hbm, vmem = pl.BlockSpec(memory_space=pltpu.HBM), pl.BlockSpec(memory_space=pltpu.VMEM)
    size = int(np.prod(item)) * 4
    shapes = [(levels - 1, 2) + item if turn else (levels, 2 * box_count) + item for turn in turns]
    return pl.pallas_call(
        functools.partial(later_kernel, turns, per_device, box_count, levels),
        out_shape=[jax.ShapeDtypeStruct(shape, jnp.float32) for shape in shapes],
        in_specs=[hbm] * 2,
        out_specs=[vmem if turn else hbm for turn in turns],
        scratch_shapes=[
            pltpu.SMEM(move_dest.shape, jnp.int32),
            pltpu.SMEM((2 * box_count,), jnp.int32),
            pltpu.SemaphoreType.DMA((len(turns), levels, 2)),
            pltpu.SemaphoreType.DMA,
        ]
        + [pltpu.VMEM((levels, 2) + item, jnp.float32) for turn in turns if turn == 0],
        cost_estimate=pl.CostEstimate(
            flops=0, bytes_accessed=4 * len(turns) * levels * size, transcendentals=0
        ),
    )(move_dest, boxes)


def settle_later(piece, turn, moved_ref, sem):
    source = source_of(lax.axis_index("box"), turn, moved_ref.shape[1] // 2)
    to = moved_ref.at[pl.ds(1, moved_ref.shape[0] - 1), pl.ds(2 * source, 2)]
    return pltpu.make_async_copy(piece, to, sem)


def settle_kernel(turns, *refs):
    out_ref, sems = refs[-2:]
    copies = [settle_later(refs[n], turn, out_ref, sems.at[n]) for n, turn in enumerate(turns)]
    for copy in copies:
        copy.start()
    for copy in copies:
        copy.wait()


def settle(turns, pieces, moved, after):
    count = len(pieces)
    vmem, hbm = pl.BlockSpec(memory_space=pltpu.VMEM), pl.BlockSpec(memory_space=pltpu.HBM)
    return pl.pallas_call(
        functools.partial(settle_kernel, turns),
        out_shape=jax.ShapeDtypeStruct(moved.shape, jnp.float32),
        in_specs=[vmem] * count + [hbm, vmem],
        out_specs=hbm,
        scratch_shapes=[pltpu.SemaphoreType.DMA((count,))],
        input_output_aliases={count: 0},
        compiler_params=pltpu.CompilerParams(vmem_limit_bytes=48 * 2 ** 20),
        cost_estimate=pl.CostEstimate(
            flops=0, bytes_accessed=8 * count * pieces[0].size, transcendentals=0
        ),
    )(*pieces, moved, after)


def arrive_kernel(box_count, slabs, early, fields, *refs):
    pieces, later = refs[:box_count], refs[box_count : box_count + len(early)]
    now_ref, moved_ref, *edges, sems = refs[box_count + len(early) + 1 :]
    own, slab = lax.axis_index("box"), lax.axis_index("slab")
    planes = now_ref.shape[2]
    mine = pltpu.make_async_copy(pieces[0], now_ref.at[pl.ds(2 * own, 2)], sems.at[0])
    mine.start()
    copies = []
    for turn in range(1, box_count):
        to = moved_ref.at[0, pl.ds(2 * source_of(own, turn, box_count), 2)]
        copies.append(pltpu.make_async_copy(pieces[turn].at[:, pl.ds(0, fields)], to, sems.at[turn]))
    for n, turn in enumerate(early):
        copies.append(settle_later(later[n], turn, moved_ref, sems.at[box_count + n]))
    for copy in copies:
        copy.start()
    faced = [jnp.where(slab == 0, planes - 1, 0)] if slabs == 2 else [0, planes - 1]

    def cut(source):
        for k in range(2):
            for edge_ref, plane in zip(edges, faced):
                for f in range(fields):
                    edge_ref[2 * source + k, f : f + 1] = now_ref[2 * source + k, f, pl.ds(plane, 1)]

    for turn in range(1, box_count):
        source = source_of(own, turn, box_count)
        for k in range(2):
            now_ref[2 * source + k] = pieces[turn][k]
        cut(source)
    mine.wait()
    cut(own)
    for copy in copies:
        copy.wait()


def arrive(pieces, early, later, moved, slabs):
    box_count = len(pieces)
    _, blocks, planes, cross = pieces[0].shape
    fields = moved.shape[2]
    slots = 2 * box_count
    sides = 1 if slabs == 2 else 2
    vmem, hbm = pl.BlockSpec(memory_space=pltpu.VMEM), pl.BlockSpec(memory_space=pltpu.HBM)
    shapes = [(slots, blocks, planes, cross), moved.shape] + [(slots, fields, cross)] * sides
    count = box_count + len(later)
    return pl.pallas_call(
        functools.partial(arrive_kernel, box_count, slabs, early, fields),
        out_shape=[jax.ShapeDtypeStruct(shape, jnp.float32) for shape in shapes],
        in_specs=[hbm] + [vmem] * (count - 1) + [hbm],
        out_specs=[vmem, hbm] + [vmem] * sides,
        scratch_shapes=[pltpu.SemaphoreType.DMA((count,))],
        input_output_aliases={count: 1},
        compiler_params=pltpu.CompilerParams(vmem_limit_bytes=48 * 2 ** 20),
        cost_estimate=pl.CostEstimate(
            flops=0, bytes_accessed=12 * box_count * pieces[0].size, transcendentals=0
        ),
    )(*pieces, *later, moved)


def face_cells(lane, edge, coarse_planes, slab):
    half, side = edge // 2, edge // 2 + 2
    plane, m = lane // (4 * half), lane % half + 1
    which = (lane // half) % 4
    rim = jnp.where(which == 0, m, jnp.where(which == 1, (side - 1) * side + m, m * side))
    rim = jnp.where(which == 3, rim + side - 1, rim) + (slab * coarse_planes + plane + 1) * side * side
    t = lane - 4 * half * coarse_planes
    x_rim = jnp.where(slab > 0, (side - 1) * side * side, 0) + (t // half + 1) * side + m
    return jnp.where(t < 0, rim, jnp.where(t < half * half, x_rim, -1))


def expand_table(coarse_planes, edge, lanes):
    half = edge // 2
    cross = edge * edge
    spread = np.zeros((lanes, (2 * coarse_planes + 1) * cross), np.float32)
    for c in range(coarse_planes):
        base = c * 4 * half
        forward, backward = 2 * c * cross, (2 * c + 1) * cross
        for m in range(edge):
            spread[base + m // 2, backward + m] += 1
            spread[base + half + m // 2, forward + (edge - 1) * edge + m] += 1
            spread[base + 2 * half + m // 2, backward + m * edge] += 1
            spread[base + 3 * half + m // 2, forward + m * edge + edge - 1] += 1
    base, to = coarse_planes * 4 * half, 2 * coarse_planes * cross
    for y in range(edge):
        for z in range(edge):
            spread[base + (y // 2) * half + z // 2, to + y * edge + z] = 1
    return spread


def slope_columns(fields, planes, coarse_planes):
    column_field, forward, backward, centre = [], [], [], []
    p = np.arange(planes)

    def add(field, f, b, c):
        column_field.append(field)
        forward.append(f * np.ones(planes))
        backward.append(b * np.ones(planes))
        centre.append(c * np.ones(planes))

    for f, b, c in ((1, 0, 0), (0, 1, 0), (0, 0, 1)):
        for g in range(2 * fields):
            for q in range(planes):
                here = p == q
                add(g, f * here + c * (p + 1 == q), b * here + c * (p - 1 == q), c * here)
    rows = [g if g < fields else -1 for g in range(ROWS)]
    rows += [fields + g if g < fields else -1 for g in range(ROWS)]
    for g in rows:
        add(g, 0, p == 0, 0)
    for g in rows:
        add(g, p == planes - 1, 0, 0)
    for c in range(coarse_planes):
        for g in rows:
            add(g, p // 2 == c, 0, 0)
        for g in rows:
            add(g, 0, p // 2 == c, 0)
    width = round_up(len(column_field), 128)
    select = np.zeros((2 * fields, width), np.float32)
    masks = np.zeros((3, planes, width), np.float32)
    for k, g in enumerate(column_field):
        if g >= 0:
            select[g, k] = 1
        masks[0, :, k], masks[1, :, k], masks[2, :, k] = forward[k], backward[k], centre[k]
    return select, masks


def expand_faces(slots_ref, fields, spread_ref, out_ref):
    slots, _, planes, cross = slots_ref.shape
    for slot in range(slots):
        for block in range(ROWS // planes):
            at = slot * ROWS + block * planes
            out_ref[at : at + planes, :cross] = slots_ref[slot, fields + block]
    cells = out_ref[:, :cross]
    high = cells.astype(jnp.bfloat16)
    low = (cells - high.astype(jnp.float32)).astype(jnp.bfloat16)
    both = jnp.dot(jnp.concatenate([high, low], axis=0), spread_ref[...], preferred_element_type=jnp.float32)
    out_ref[...] = both[: slots * ROWS] + both[slots * ROWS :]


def own_ghosts(now, fields, spread):
    vmem = pl.BlockSpec(memory_space=pltpu.VMEM)
    shape = (now.shape[0] * ROWS, spread.shape[1])

    def kernel(now_ref, spread_ref, out_ref):
        expand_faces(now_ref, fields, spread_ref, out_ref)

    return pl.pallas_call(
        kernel,
        out_shape=jax.ShapeDtypeStruct(shape, jnp.float32),
        in_specs=[vmem] * 2,
        out_specs=vmem,
        compiler_params=pltpu.CompilerParams(vmem_limit_bytes=48 * 2 ** 20),
        cost_estimate=pl.CostEstimate(
            flops=4 * shape[0] * spread.size, bytes_accessed=4 * shape[0] * shape[1], transcendentals=0
        ),
    )(now, spread)


def slope_kernel(
    edge, planes, fields, coarse_planes, per_device, total, coarse_count, slots, slabs,
    dest_ref, parent_ref, own_ref, other_ref, own_low, other_low, own_high, other_high,
    own_rim, spread_ref, weight_ref, out_ref, token_ref, stack, parts, other_rim, table, count,
):
    step = pl.program_id(0)
    cross = edge * edge
    rows = fields * planes
    own, slab = lax.axis_index("box"), lax.axis_index("slab")

    @pl.when(step == 0)
    def _():
        token_ref[...] = jnp.zeros_like(token_ref)
        stack[...] = jnp.zeros_like(stack)
        half = weight_ref.shape[0]
        weights = weight_ref[...]
        parts[:half] = weights.astype(jnp.bfloat16)
        parts[half:] = (weights - weights.astype(jnp.bfloat16).astype(jnp.float32)).astype(jnp.bfloat16)
        for slot in range(slots):
            table[slot] = -1
            count[slot] = 0

        def place(b, carry):
            @pl.when(dest_ref[b] == own)
            def _():
                slot = 2 * (b // per_device)
                owner = parent_ref[b] // coarse_count
                table[jnp.where(table[slot] >= 0, slot + 1, slot)] = 2 * owner + count[owner]
                count[owner] = count[owner] + 1

            return carry

        lax.fori_loop(0, total, place, 0)
        expand_faces(other_ref, fields, spread_ref, other_rim)

    face = table[step]

    @pl.when(face < 0)
    def _():
        out_ref[...] = jnp.zeros_like(out_ref)

    @pl.when(face >= 0)
    def _():
        lane = lax.broadcasted_iota(jnp.int32, (1, cross), 1)
        y, z = lane // edge, lane % edge
        for n, ref in enumerate((own_ref, other_ref)):
            at = (4 + n) * rows
            if planes % 8:
                for f in range(fields):
                    stack[at + f * planes : at + (f + 1) * planes] = ref[step, f]
            else:
                stack[at : at + rows] = ref[step, :fields].reshape(rows, cross)
        cells = stack[4 * rows : 6 * rows]
        stack[0 : 2 * rows] = jnp.where(y < edge - 1, pltpu.roll(cells, cross - edge, 1), 0.0) + jnp.where(
            z < edge - 1, pltpu.roll(cells, cross - 1, 1), 0.0
        )
        stack[2 * rows : 4 * rows] = jnp.where(y > 0, pltpu.roll(cells, edge, 1), 0.0) + jnp.where(
            z > 0, pltpu.roll(cells, 1, 1), 0.0
        )
        here = pl.ds(pl.multiple_of(ROWS * face, ROWS), ROWS)
        rim = jnp.concatenate([own_rim[here], other_rim[here]], axis=0)
        base = 6 * rows
        x_face = rim[:, 2 * coarse_planes * cross :]
        stack[base : base + 2 * ROWS] = x_face
        stack[base + 2 * ROWS : base + 4 * ROWS] = x_face

        @pl.when(slab > 0)
        def _():
            stack[base : base + fields] = own_low[step]
            stack[base + ROWS : base + ROWS + fields] = other_low[step]

        @pl.when(slab < slabs - 1)
        def _():
            stack[base + 2 * ROWS : base + 2 * ROWS + fields] = own_high[step]
            stack[base + 3 * ROWS : base + 3 * ROWS + fields] = other_high[step]

        base += 4 * ROWS
        for n in range(2 * coarse_planes):
            stack[base + 2 * ROWS * n : base + 2 * ROWS * (n + 1)] = rim[:, n * cross : (n + 1) * cross]
        values = stack[...]
        high = values.astype(jnp.bfloat16)
        low = (values - high.astype(jnp.float32)).astype(jnp.bfloat16)
        half = weight_ref.shape[0]
        both = jnp.dot(parts[...], high, preferred_element_type=jnp.float32)
        mixed = jnp.dot(parts[:half], low, preferred_element_type=jnp.float32)
        mixed = both[:half] + (both[half:] + mixed)
        if planes % 8:
            for f in range(fields):
                out_ref[0, f] = mixed[f * planes : (f + 1) * planes]
        else:
            out_ref[0] = mixed[:rows].reshape(fields, planes, cross)


def mixing_weights(mixes, group, fields, planes, coarse_planes):
    lap_mix, grad_mix, damp_mix = mixes
    select, masks = slope_columns(fields, planes, coarse_planes)
    terms = jnp.stack([lap_mix + 0.5 * grad_mix, lap_mix - 0.5 * grad_mix, damp_mix - 6.0 * lap_mix])
    terms = lax.dynamic_slice_in_dim(terms, group * fields, fields, 1)
    terms = jnp.where(group == 0, terms, jnp.roll(terms, fields, axis=2))
    terms = jnp.einsum("tfg,gk->tfk", terms, jnp.asarray(select), precision=HIGHEST)
    weight = jnp.sum(terms[:, :, None, :] * jnp.asarray(masks)[:, None], axis=0).reshape(fields * planes, -1)
    return jnp.pad(weight, ((0, round_up(fields * planes, 16) - fields * planes), (0, 0)))


def body(boxes, move_dest, parent, coarse, lap_mix, grad_mix, damp_mix):
    box_count = lax.axis_size("box")
    slabs = lax.axis_size("slab")
    group = lax.axis_index("fld")
    levels, per_device, fields, planes, cross = boxes.shape
    edge = planes * slabs
    coarse_planes = planes // 2
    slots = 2 * box_count
    total = move_dest.shape[0]
    coarse_count = coarse.shape[0]

    def send(piece, turn):
        return lax.ppermute(piece, "box", [(s, (s + turn) % box_count) for s in range(box_count)])

    near = pack_later((1, box_count - 1), boxes, move_dest, box_count)
    near = [send(near[0], 1), send(near[1], box_count - 1)]
    first = pack_first(boxes, coarse, move_dest, parent, edge, box_count)
    arrived = [first[0]] + [send(first[turn], turn) for turn in range(1, box_count)]
    moved, *middle = pack_later((0,) + tuple(range(2, box_count - 1)), boxes, move_dest, box_count)
    middle = [send(piece, n + 2) for n, piece in enumerate(middle)]
    now, moved, *facing = arrive(arrived, (), [], moved, slabs)

    swap = [(0, 1), (1, 0)]
    now_other = lax.ppermute(now, "fld", swap)

    spread = jnp.asarray(expand_table(coarse_planes, edge, cross)).astype(jnp.bfloat16)
    rim = own_ghosts(now, fields, spread)

    def shifted(values, up):
        pairs = [(s, s + 1) if up else (s + 1, s) for s in range(slabs - 1)]
        return lax.ppermute(values, "slab", swap if slabs == 2 else pairs)

    low = shifted(facing[-1], True)
    low, rim = lax.optimization_barrier((low, rim))
    low = low, lax.ppermute(low, "fld", swap)
    high = low
    if slabs != 2:
        high = shifted(facing[0], False)
        high = high, lax.ppermute(high, "fld", swap)

    weight = mixing_weights((lap_mix, grad_mix, damp_mix), group, fields, planes, coarse_planes)
    smem, vmem = pl.BlockSpec(memory_space=pltpu.SMEM), pl.BlockSpec(memory_space=pltpu.VMEM)
    slope, token = pl.pallas_call(
        functools.partial(
            slope_kernel, edge, planes, fields, coarse_planes, per_device, total, coarse_count, slots, slabs
        ),
        grid=(slots,),
        out_shape=[
            jax.ShapeDtypeStruct((slots, fields, planes, cross), jnp.float32),
            jax.ShapeDtypeStruct((8, 128), jnp.float32),
        ],
        in_specs=[smem, smem] + [vmem] * 9,
        out_specs=[pl.BlockSpec((1, fields, planes, cross), lambda n: (n, 0, 0, 0)), vmem],
        scratch_shapes=[
            pltpu.VMEM((weight.shape[1], cross), jnp.float32),
            pltpu.VMEM((2 * weight.shape[0], weight.shape[1]), jnp.bfloat16),
            pltpu.VMEM((ROWS * slots, spread.shape[1]), jnp.float32),
            pltpu.SMEM((slots,), jnp.int32),
            pltpu.SMEM((slots,), jnp.int32),
        ],
        compiler_params=pltpu.CompilerParams(vmem_limit_bytes=48 * 2 ** 20),
        cost_estimate=pl.CostEstimate(
            flops=3 * slots * weight.size * cross, bytes_accessed=12 * now.size, transcendentals=0
        ),
    )(move_dest, parent, now, now_other, low[0], low[1], high[0], high[1], rim, spread, weight)
    moved = settle(tuple(range(2, box_count - 1)), middle, moved, token)
    return settle((1, box_count - 1), near, moved, token), slope


def solution(mesh):
    placed = (
        P(None, ("runs", "box"), "fld", "slab", None),
        P("runs"),
        P("runs"),
        P(("runs", "box"), "fld", None),
        P(),
        P(),
        P(),
    )
    return jax.shard_map(
        body,
        mesh=mesh,
        in_specs=placed,
        out_specs=(
            P(None, ("runs", "box"), "fld", "slab", None),
            P(("runs", "box"), "fld", "slab", None),
        ),
        check_vma=False,
    )
```

```python
import functools

import jax
import jax.numpy as jnp
import numpy as np
from jax import lax
from jax.experimental import pallas as pl
from jax.experimental.pallas import tpu as pltpu
from jax.sharding import PartitionSpec as P

HIGHEST = lax.Precision.HIGHEST
ROWS = 16


def round_up(value, unit):
    return -(-value // unit) * unit


def split_three(values):
    high = values.astype(jnp.bfloat16)
    rest = values - high.astype(jnp.float32)
    middle = rest.astype(jnp.bfloat16)
    low = (rest - middle.astype(jnp.float32)).astype(jnp.bfloat16)
    return high, middle, low


def place_boxes(per_device, box_count, dest_ref, table):
    own = lax.axis_index("box")
    for slot in range(2 * box_count):
        table[slot] = -1

    def place(b, carry):
        slot = 2 * dest_ref[own * per_device + b]
        table[jnp.where(table[slot] >= 0, slot + 1, slot)] = b
        return carry

    lax.fori_loop(0, per_device, place, 0)


def target_of(own, turn, box_count):
    return lax.rem(own + turn, box_count)


def source_of(own, turn, box_count):
    return lax.rem(own - turn + box_count, box_count)


def each_slot(box_count):
    own = lax.axis_index("box")
    for turn in range(box_count):
        for k in range(2):
            yield turn, k, 2 * target_of(own, turn, box_count) + k


def first_kernel(per_device, box_count, edge, dest_ref, parent_ref, boxes_ref, coarse_ref, *refs):
    outs, (shells, chosen, dest, parent, box_table, face_table, sems, in_sems) = refs[:box_count], refs[box_count:]
    fields, coarse_count, cells = coarse_ref.shape
    planes, cross = outs[0].shape[1:]
    own, slab = lax.axis_index("box"), lax.axis_index("slab")
    fetches = [
        pltpu.make_async_copy(coarse_ref, shells, in_sems.at[0]),
        pltpu.make_async_copy(dest_ref, dest, in_sems.at[1]),
        pltpu.make_async_copy(parent_ref, parent, in_sems.at[2]),
    ]
    for fetch in fetches:
        fetch.start()
    index = face_cells(lax.broadcasted_iota(jnp.int32, (1, cross), 1), edge, planes // 2, slab)
    cell = lax.broadcasted_iota(jnp.int32, (cells, cross), 0)
    one_hot = (cell == index).astype(jnp.float32).astype(jnp.bfloat16)
    fetches[1].wait()
    place_boxes(per_device, box_count, dest, box_table)

    def copy(shift, k, b):
        return pltpu.make_async_copy(
            boxes_ref.at[0, b], outs[shift].at[pl.ds(k * fields, fields)], sems.at[shift, k]
        )

    for shift, k, slot in each_slot(box_count):
        b = box_table[slot]

        @pl.when(b >= 0)
        def _():
            copy(shift, k, b).start()

        @pl.when(b < 0)
        def _():
            outs[shift][k * fields : (k + 1) * fields] = jnp.zeros((fields, planes, cross), jnp.float32)

    for slot in range(2 * box_count):
        face_table[slot] = -1
    fetches[2].wait()

    def place(b, carry):
        slot = 2 * dest[b]
        local = parent[b] - own * coarse_count

        @pl.when(jnp.logical_and(local >= 0, local < coarse_count))
        def _():
            face_table[jnp.where(face_table[slot] >= 0, slot + 1, slot)] = local

        return carry

    lax.fori_loop(0, dest.shape[0], place, 0)
    fetches[0].wait()
    high, middle, low = (
        jnp.dot(part, one_hot, preferred_element_type=jnp.float32)
        for part in split_three(shells[...].reshape(fields * coarse_count, cells))
    )
    chosen[...] = (high + (middle + low)).reshape(chosen.shape)
    for shift, k, slot in each_slot(box_count):
        local = face_table[slot]
        for f in range(fields):
            values = chosen[f, pl.ds(jnp.maximum(local, 0), 1)]
            block, row = divmod(k * fields + f, planes)
            outs[shift][2 * fields + block, row : row + 1] = jnp.where(local >= 0, values, 0.0)
    for shift, k, slot in each_slot(box_count):
        b = box_table[slot]

        @pl.when(b >= 0)
        def _():
            copy(shift, k, b).wait()


def pack_first(boxes, coarse, move_dest, parent, edge, box_count):
    per_device, fields, planes, cross = boxes.shape[1:]
    coarse = jnp.transpose(coarse, (1, 0, 2))
    hbm, vmem = pl.BlockSpec(memory_space=pltpu.HBM), pl.BlockSpec(memory_space=pltpu.VMEM)
    item = (2 * fields + 2 * fields // planes, planes, cross)
    return pl.pallas_call(
        functools.partial(first_kernel, per_device, box_count, edge),
        out_shape=[jax.ShapeDtypeStruct(item, jnp.float32)] * box_count,
        in_specs=[hbm] * 4,
        out_specs=[vmem] * box_count,
        scratch_shapes=[
            pltpu.VMEM(coarse.shape, jnp.float32),
            pltpu.VMEM(coarse.shape[:2] + (cross,), jnp.float32),
            pltpu.SMEM(move_dest.shape, jnp.int32),
            pltpu.SMEM(parent.shape, jnp.int32),
            pltpu.SMEM((2 * box_count,), jnp.int32),
            pltpu.SMEM((2 * box_count,), jnp.int32),
            pltpu.SemaphoreType.DMA((box_count, 2)),
            pltpu.SemaphoreType.DMA((3,)),
        ],
        cost_estimate=pl.CostEstimate(
            flops=6 * coarse.size * cross, bytes_accessed=4 * (coarse.size + 2 * boxes.size), transcendentals=0
        ),
    )(move_dest, parent, boxes, coarse)


def later_kernel(turns, per_device, box_count, levels, dest_ref, boxes_ref, *refs):
    outs, (dest, table, sems, in_sem, *stay) = refs[: len(turns)], refs[len(turns) :]
    own = lax.axis_index("box")
    fetch = pltpu.make_async_copy(dest_ref, dest, in_sem)
    fetch.start()
    fetch.wait()
    place_boxes(per_device, box_count, dest, table)
    places = [(n, k, 2 * target_of(own, turn, box_count) + k) for n, turn in enumerate(turns) for k in range(2)]
    held = [stay[0] if turn == 0 else out for turn, out in zip(turns, outs)]

    def copies(n, k, b):
        skip = levels - held[n].shape[0]
        for level in range(skip, levels):
            yield pltpu.make_async_copy(boxes_ref.at[level, b], held[n].at[level - skip, k], sems.at[n, level, k])

    for n, k, slot in places:
        b = table[slot]

        @pl.when(b >= 0)
        def _():
            for copy in copies(n, k, b):
                copy.start()

        @pl.when(b < 0)
        def _():
            for level in range(held[n].shape[0]):
                held[n][level, k] = jnp.zeros(held[n].shape[2:], jnp.float32)

    for n, k, slot in places:
        b = table[slot]

        @pl.when(b >= 0)
        def _():
            for copy in copies(n, k, b):
                copy.wait()

    for n, turn in enumerate(turns):
        if turn == 0:
            settled = pltpu.make_async_copy(held[n], outs[n].at[:, pl.ds(2 * own, 2)], in_sem)
            settled.start()
            settled.wait()


def pack_later(turns, boxes, move_dest, box_count):
    levels, per_device = boxes.shape[:2]
    item = boxes.shape[2:]
    hbm, vmem = pl.BlockSpec(memory_space=pltpu.HBM), pl.BlockSpec(memory_space=pltpu.VMEM)
    size = int(np.prod(item)) * 4
    shapes = [(levels - 1, 2) + item if turn else (levels, 2 * box_count) + item for turn in turns]
    return pl.pallas_call(
        functools.partial(later_kernel, turns, per_device, box_count, levels),
        out_shape=[jax.ShapeDtypeStruct(shape, jnp.float32) for shape in shapes],
        in_specs=[hbm] * 2,
        out_specs=[vmem if turn else hbm for turn in turns],
        scratch_shapes=[
            pltpu.SMEM(move_dest.shape, jnp.int32),
            pltpu.SMEM((2 * box_count,), jnp.int32),
            pltpu.SemaphoreType.DMA((len(turns), levels, 2)),
            pltpu.SemaphoreType.DMA,
        ]
        + [pltpu.VMEM((levels, 2) + item, jnp.float32) for turn in turns if turn == 0],
        cost_estimate=pl.CostEstimate(
            flops=0, bytes_accessed=4 * len(turns) * levels * size, transcendentals=0
        ),
    )(move_dest, boxes)


def settle_later(piece, turn, moved_ref, sem):
    source = source_of(lax.axis_index("box"), turn, moved_ref.shape[1] // 2)
    to = moved_ref.at[pl.ds(1, moved_ref.shape[0] - 1), pl.ds(2 * source, 2)]
    return pltpu.make_async_copy(piece, to, sem)


def settle_kernel(turns, *refs):
    out_ref, sems = refs[-2:]
    copies = [settle_later(refs[n], turn, out_ref, sems.at[n]) for n, turn in enumerate(turns)]
    for copy in copies:
        copy.start()
    for copy in copies:
        copy.wait()


def settle(turns, pieces, moved, after):
    count = len(pieces)
    vmem, hbm = pl.BlockSpec(memory_space=pltpu.VMEM), pl.BlockSpec(memory_space=pltpu.HBM)
    return pl.pallas_call(
        functools.partial(settle_kernel, turns),
        out_shape=jax.ShapeDtypeStruct(moved.shape, jnp.float32),
        in_specs=[vmem] * count + [hbm, vmem],
        out_specs=hbm,
        scratch_shapes=[pltpu.SemaphoreType.DMA((count,))],
        input_output_aliases={count: 0},
        compiler_params=pltpu.CompilerParams(vmem_limit_bytes=48 * 2 ** 20),
        cost_estimate=pl.CostEstimate(
            flops=0, bytes_accessed=8 * count * pieces[0].size, transcendentals=0
        ),
    )(*pieces, moved, after)


def arrive_kernel(box_count, slabs, fields, *refs):
    pieces = refs[:box_count]
    now_ref, moved_ref, *edges, own_rows, sems, own_sem = refs[box_count + 1 :]
    own, slab = lax.axis_index("box"), lax.axis_index("slab")
    planes, cross = now_ref.shape[2:]
    faces = pl.ds(2 * fields, own_rows.shape[0])
    mine = [pltpu.make_async_copy(pieces[0].at[faces], own_rows, own_sem)]
    copies = []
    for turn in range(box_count):
        source = source_of(own, turn, box_count)
        for k in range(2):
            box = pieces[turn].at[pl.ds(k * fields, fields)]
            if turn:
                copies.append(pltpu.make_async_copy(box, moved_ref.at[0, 2 * source + k], sems.at[turn, k]))
            else:
                mine.append(pltpu.make_async_copy(box, now_ref.at[2 * own + k, pl.ds(0, fields)], sems.at[0, k]))
    for copy in mine + copies:
        copy.start()
    faced = [jnp.where(slab == 0, planes - 1, 0)] if slabs == 2 else [0, planes - 1]

    def place_rows(rows_ref, first_block, source):
        for k in range(2):
            for f in range(ROWS):
                values = jnp.zeros((1, cross), jnp.float32)
                if f < fields:
                    block, row = divmod(k * fields + f, planes)
                    values = rows_ref[first_block + block, row : row + 1]
                now_ref[2 * source + k, fields + f // planes, f % planes : f % planes + 1] = values
            for edge_ref, plane in zip(edges, faced):
                for f in range(fields):
                    edge_ref[2 * source + k, f : f + 1] = now_ref[2 * source + k, f, pl.ds(plane, 1)]

    for turn in range(1, box_count):
        source = source_of(own, turn, box_count)
        for k in range(2):
            now_ref[2 * source + k, :fields] = pieces[turn][k * fields : (k + 1) * fields]
        place_rows(pieces[turn], 2 * fields, source)
    for copy in mine:
        copy.wait()
    place_rows(own_rows, 0, own)
    for copy in copies:
        copy.wait()


def arrive(pieces, moved, slabs):
    box_count = len(pieces)
    _, planes, cross = pieces[0].shape
    fields = moved.shape[2]
    slots = 2 * box_count
    sides = 1 if slabs == 2 else 2
    vmem, hbm = pl.BlockSpec(memory_space=pltpu.VMEM), pl.BlockSpec(memory_space=pltpu.HBM)
    shapes = [(slots, fields + ROWS // planes, planes, cross), moved.shape] + [(slots, fields, cross)] * sides
    return pl.pallas_call(
        functools.partial(arrive_kernel, box_count, slabs, fields),
        out_shape=[jax.ShapeDtypeStruct(shape, jnp.float32) for shape in shapes],
        in_specs=[hbm] + [vmem] * (box_count - 1) + [hbm],
        out_specs=[vmem, hbm] + [vmem] * sides,
        scratch_shapes=[
            pltpu.VMEM((2 * fields // planes, planes, cross), jnp.float32),
            pltpu.SemaphoreType.DMA((box_count, 2)),
            pltpu.SemaphoreType.DMA,
        ],
        input_output_aliases={box_count: 1},
        compiler_params=pltpu.CompilerParams(vmem_limit_bytes=48 * 2 ** 20),
        cost_estimate=pl.CostEstimate(
            flops=0, bytes_accessed=12 * box_count * pieces[0].size, transcendentals=0
        ),
    )(*pieces, moved)


def face_cells(lane, edge, coarse_planes, slab):
    half, side = edge // 2, edge // 2 + 2
    plane, m = lane // (4 * half), lane % half + 1
    which = (lane // half) % 4
    rim = jnp.where(which == 0, m, jnp.where(which == 1, (side - 1) * side + m, m * side))
    rim = jnp.where(which == 3, rim + side - 1, rim) + (slab * coarse_planes + plane + 1) * side * side
    t = lane - 4 * half * coarse_planes
    x_rim = jnp.where(slab > 0, (side - 1) * side * side, 0) + (t // half + 1) * side + m
    return jnp.where(t < 0, rim, jnp.where(t < half * half, x_rim, -1))


def expand_table(coarse_planes, edge, lanes):
    half = edge // 2
    cross = edge * edge
    spread = np.zeros((lanes, (2 * coarse_planes + 1) * cross), np.float32)
    for c in range(coarse_planes):
        base = c * 4 * half
        forward, backward = 2 * c * cross, (2 * c + 1) * cross
        for m in range(edge):
            spread[base + m // 2, backward + m] += 1
            spread[base + half + m // 2, forward + (edge - 1) * edge + m] += 1
            spread[base + 2 * half + m // 2, backward + m * edge] += 1
            spread[base + 3 * half + m // 2, forward + m * edge + edge - 1] += 1
    base, to = coarse_planes * 4 * half, 2 * coarse_planes * cross
    for y in range(edge):
        for z in range(edge):
            spread[base + (y // 2) * half + z // 2, to + y * edge + z] = 1
    return spread


def slope_columns(fields, planes, coarse_planes):
    column_field, forward, backward, centre = [], [], [], []
    p = np.arange(planes)

    def add(field, f, b, c):
        column_field.append(field)
        forward.append(f * np.ones(planes))
        backward.append(b * np.ones(planes))
        centre.append(c * np.ones(planes))

    for f, b, c in ((1, 0, 0), (0, 1, 0), (0, 0, 1)):
        for g in range(2 * fields):
            for q in range(planes):
                here = p == q
                add(g, f * here + c * (p + 1 == q), b * here + c * (p - 1 == q), c * here)
    rows = [g if g < fields else -1 for g in range(ROWS)]
    rows += [fields + g if g < fields else -1 for g in range(ROWS)]
    for g in rows:
        add(g, 0, p == 0, 0)
    for g in rows:
        add(g, p == planes - 1, 0, 0)
    for c in range(coarse_planes):
        for g in rows:
            add(g, p // 2 == c, 0, 0)
        for g in rows:
            add(g, 0, p // 2 == c, 0)
    width = round_up(len(column_field), 128)
    select = np.zeros((2 * fields, width), np.float32)
    masks = np.zeros((3, planes, width), np.float32)
    for k, g in enumerate(column_field):
        if g >= 0:
            select[g, k] = 1
        masks[0, :, k], masks[1, :, k], masks[2, :, k] = forward[k], backward[k], centre[k]
    return select, masks


def expand_faces(slots_ref, fields, spread_ref, out_ref):
    slots, _, planes, cross = slots_ref.shape
    for slot in range(slots):
        for block in range(ROWS // planes):
            at = slot * ROWS + block * planes
            out_ref[at : at + planes, :cross] = slots_ref[slot, fields + block]
    cells = out_ref[:, :cross]
    high = cells.astype(jnp.bfloat16)
    low = (cells - high.astype(jnp.float32)).astype(jnp.bfloat16)
    both = jnp.dot(jnp.concatenate([high, low], axis=0), spread_ref[...], preferred_element_type=jnp.float32)
    out_ref[...] = both[: slots * ROWS] + both[slots * ROWS :]


def own_ghosts(now, fields, spread):
    vmem = pl.BlockSpec(memory_space=pltpu.VMEM)
    shape = (now.shape[0] * ROWS, spread.shape[1])

    def kernel(now_ref, spread_ref, out_ref):
        expand_faces(now_ref, fields, spread_ref, out_ref)

    return pl.pallas_call(
        kernel,
        out_shape=jax.ShapeDtypeStruct(shape, jnp.float32),
        in_specs=[vmem] * 2,
        out_specs=vmem,
        compiler_params=pltpu.CompilerParams(vmem_limit_bytes=48 * 2 ** 20),
        cost_estimate=pl.CostEstimate(
            flops=4 * shape[0] * spread.size, bytes_accessed=4 * shape[0] * shape[1], transcendentals=0
        ),
    )(now, spread)


def slope_kernel(
    edge, planes, fields, coarse_planes, per_device, total, coarse_count, slots, slabs,
    dest_ref, parent_ref, own_ref, other_ref, own_low, other_low, own_high, other_high,
    own_rim, spread_ref, weight_ref, out_ref, token_ref, stack, parts, other_rim, table, count,
):
    step = pl.program_id(0)
    cross = edge * edge
    rows = fields * planes
    own, slab = lax.axis_index("box"), lax.axis_index("slab")

    @pl.when(step == 0)
    def _():
        token_ref[...] = jnp.zeros_like(token_ref)
        stack[...] = jnp.zeros_like(stack)
        half = weight_ref.shape[0]
        weights = weight_ref[...]
        parts[:half] = weights.astype(jnp.bfloat16)
        parts[half:] = (weights - weights.astype(jnp.bfloat16).astype(jnp.float32)).astype(jnp.bfloat16)
        for slot in range(slots):
            table[slot] = -1
            count[slot] = 0

        def place(b, carry):
            @pl.when(dest_ref[b] == own)
            def _():
                slot = 2 * (b // per_device)
                owner = parent_ref[b] // coarse_count
                table[jnp.where(table[slot] >= 0, slot + 1, slot)] = 2 * owner + count[owner]
                count[owner] = count[owner] + 1

            return carry

        lax.fori_loop(0, total, place, 0)
        expand_faces(other_ref, fields, spread_ref, other_rim)

    face = table[step]

    @pl.when(face < 0)
    def _():
        out_ref[...] = jnp.zeros_like(out_ref)

    @pl.when(face >= 0)
    def _():
        lane = lax.broadcasted_iota(jnp.int32, (1, cross), 1)
        y, z = lane // edge, lane % edge
        for n, ref in enumerate((own_ref, other_ref)):
            at = (4 + n) * rows
            if planes % 8:
                for f in range(fields):
                    stack[at + f * planes : at + (f + 1) * planes] = ref[step, f]
            else:
                stack[at : at + rows] = ref[step, :fields].reshape(rows, cross)
        cells = stack[4 * rows : 6 * rows]
        stack[0 : 2 * rows] = jnp.where(y < edge - 1, pltpu.roll(cells, cross - edge, 1), 0.0) + jnp.where(
            z < edge - 1, pltpu.roll(cells, cross - 1, 1), 0.0
        )
        stack[2 * rows : 4 * rows] = jnp.where(y > 0, pltpu.roll(cells, edge, 1), 0.0) + jnp.where(
            z > 0, pltpu.roll(cells, 1, 1), 0.0
        )
        here = pl.ds(pl.multiple_of(ROWS * face, ROWS), ROWS)
        rim = jnp.concatenate([own_rim[here], other_rim[here]], axis=0)
        base = 6 * rows
        x_face = rim[:, 2 * coarse_planes * cross :]
        stack[base : base + 2 * ROWS] = x_face
        stack[base + 2 * ROWS : base + 4 * ROWS] = x_face

        @pl.when(slab > 0)
        def _():
            stack[base : base + fields] = own_low[step]
            stack[base + ROWS : base + ROWS + fields] = other_low[step]

        @pl.when(slab < slabs - 1)
        def _():
            stack[base + 2 * ROWS : base + 2 * ROWS + fields] = own_high[step]
            stack[base + 3 * ROWS : base + 3 * ROWS + fields] = other_high[step]

        base += 4 * ROWS
        for n in range(2 * coarse_planes):
            stack[base + 2 * ROWS * n : base + 2 * ROWS * (n + 1)] = rim[:, n * cross : (n + 1) * cross]
        values = stack[...]
        high = values.astype(jnp.bfloat16)
        low = (values - high.astype(jnp.float32)).astype(jnp.bfloat16)
        half = weight_ref.shape[0]
        both = jnp.dot(parts[...], high, preferred_element_type=jnp.float32)
        mixed = jnp.dot(parts[:half], low, preferred_element_type=jnp.float32)
        mixed = both[:half] + (both[half:] + mixed)
        if planes % 8:
            for f in range(fields):
                out_ref[0, f] = mixed[f * planes : (f + 1) * planes]
        else:
            out_ref[0] = mixed[:rows].reshape(fields, planes, cross)


def mixing_weights(mixes, group, fields, planes, coarse_planes):
    lap_mix, grad_mix, damp_mix = mixes
    select, masks = slope_columns(fields, planes, coarse_planes)
    terms = jnp.stack([lap_mix + 0.5 * grad_mix, lap_mix - 0.5 * grad_mix, damp_mix - 6.0 * lap_mix])
    terms = lax.dynamic_slice_in_dim(terms, group * fields, fields, 1)
    terms = jnp.where(group == 0, terms, jnp.roll(terms, fields, axis=2))
    terms = jnp.einsum("tfg,gk->tfk", terms, jnp.asarray(select), precision=HIGHEST)
    weight = jnp.sum(terms[:, :, None, :] * jnp.asarray(masks)[:, None], axis=0).reshape(fields * planes, -1)
    return jnp.pad(weight, ((0, round_up(fields * planes, 16) - fields * planes), (0, 0)))


def body(boxes, move_dest, parent, coarse, lap_mix, grad_mix, damp_mix):
    box_count = lax.axis_size("box")
    slabs = lax.axis_size("slab")
    group = lax.axis_index("fld")
    levels, per_device, fields, planes, cross = boxes.shape
    edge = planes * slabs
    coarse_planes = planes // 2
    slots = 2 * box_count
    total = move_dest.shape[0]
    coarse_count = coarse.shape[0]

    def send(piece, turn):
        return lax.ppermute(piece, "box", [(s, (s + turn) % box_count) for s in range(box_count)])

    near = pack_later((1, box_count - 1), boxes, move_dest, box_count)
    near = [send(near[0], 1), send(near[1], box_count - 1)]
    first = pack_first(boxes, coarse, move_dest, parent, edge, box_count)
    arrived = [first[0]] + [send(first[turn], turn) for turn in range(1, box_count)]
    moved, *middle = pack_later((0,) + tuple(range(2, box_count - 1)), boxes, move_dest, box_count)
    middle = [send(piece, n + 2) for n, piece in enumerate(middle)]
    now, moved, *facing = arrive(arrived, moved, slabs)

    swap = [(0, 1), (1, 0)]
    now_other = lax.ppermute(now, "fld", swap)

    spread = jnp.asarray(expand_table(coarse_planes, edge, cross)).astype(jnp.bfloat16)
    rim = own_ghosts(now, fields, spread)

    def shifted(values, up):
        pairs = [(s, s + 1) if up else (s + 1, s) for s in range(slabs - 1)]
        return lax.ppermute(values, "slab", swap if slabs == 2 else pairs)

    low = shifted(facing[-1], True)
    low, rim = lax.optimization_barrier((low, rim))
    low = low, lax.ppermute(low, "fld", swap)
    high = low
    if slabs != 2:
        high = shifted(facing[0], False)
        high = high, lax.ppermute(high, "fld", swap)

    weight = mixing_weights((lap_mix, grad_mix, damp_mix), group, fields, planes, coarse_planes)
    smem, vmem = pl.BlockSpec(memory_space=pltpu.SMEM), pl.BlockSpec(memory_space=pltpu.VMEM)
    slope, token = pl.pallas_call(
        functools.partial(
            slope_kernel, edge, planes, fields, coarse_planes, per_device, total, coarse_count, slots, slabs
        ),
        grid=(slots,),
        out_shape=[
            jax.ShapeDtypeStruct((slots, fields, planes, cross), jnp.float32),
            jax.ShapeDtypeStruct((8, 128), jnp.float32),
        ],
        in_specs=[smem, smem] + [vmem] * 9,
        out_specs=[pl.BlockSpec((1, fields, planes, cross), lambda n: (n, 0, 0, 0)), vmem],
        scratch_shapes=[
            pltpu.VMEM((weight.shape[1], cross), jnp.float32),
            pltpu.VMEM((2 * weight.shape[0], weight.shape[1]), jnp.bfloat16),
            pltpu.VMEM((ROWS * slots, spread.shape[1]), jnp.float32),
            pltpu.SMEM((slots,), jnp.int32),
            pltpu.SMEM((slots,), jnp.int32),
        ],
        compiler_params=pltpu.CompilerParams(vmem_limit_bytes=48 * 2 ** 20),
        cost_estimate=pl.CostEstimate(
            flops=3 * slots * weight.size * cross, bytes_accessed=12 * now.size, transcendentals=0
        ),
    )(move_dest, parent, now, now_other, low[0], low[1], high[0], high[1], rim, spread, weight)
    moved = settle(tuple(range(2, box_count - 1)), middle, moved, token)
    return settle((1, box_count - 1), near, moved, token), slope


def solution(mesh):
    placed = (
        P(None, ("runs", "box"), "fld", "slab", None),
        P("runs"),
        P("runs"),
        P(("runs", "box"), "fld", None),
        P(),
        P(),
        P(),
    )
    return jax.shard_map(
        body,
        mesh=mesh,
        in_specs=placed,
        out_specs=(
            P(None, ("runs", "box"), "fld", "slab", None),
            P(("runs", "box"), "fld", "slab", None),
        ),
        check_vma=False,
    )
```

```python
import functools

import jax
import jax.numpy as jnp
import numpy as np
from jax import lax
from jax.experimental import pallas as pl
from jax.experimental.pallas import tpu as pltpu
from jax.sharding import PartitionSpec as P

HIGHEST = lax.Precision.HIGHEST
ROWS = 16


def round_up(value, unit):
    return -(-value // unit) * unit


def split_two(values):
    high = values.astype(jnp.bfloat16)
    low = (values - high.astype(jnp.float32)).astype(jnp.bfloat16)
    return jnp.concatenate([high, low], axis=0)


def place_boxes(per_device, box_count, dest_ref, table):
    own = lax.axis_index("box")
    for slot in range(2 * box_count):
        table[slot] = -1

    def place(b, carry):
        slot = 2 * dest_ref[own * per_device + b]
        table[jnp.where(table[slot] >= 0, slot + 1, slot)] = b
        return carry

    lax.fori_loop(0, per_device, place, 0)


def target_of(own, turn, box_count):
    return lax.rem(own + turn, box_count)


def source_of(own, turn, box_count):
    return lax.rem(own - turn + box_count, box_count)


def each_slot(box_count):
    own = lax.axis_index("box")
    for turn in range(box_count):
        for k in range(2):
            yield turn, k, 2 * target_of(own, turn, box_count) + k


def first_kernel(per_device, box_count, edge, dest_ref, parent_ref, boxes_ref, coarse_ref, *refs):
    outs, (shells, chosen, dest, parent, box_table, face_table, sems, in_sems) = refs[:box_count], refs[box_count:]
    fields, coarse_count, cells = coarse_ref.shape
    planes, cross = outs[0].shape[1:]
    own, slab = lax.axis_index("box"), lax.axis_index("slab")
    fetches = [
        pltpu.make_async_copy(coarse_ref, shells, in_sems.at[0]),
        pltpu.make_async_copy(dest_ref, dest, in_sems.at[1]),
        pltpu.make_async_copy(parent_ref, parent, in_sems.at[2]),
    ]
    for fetch in fetches:
        fetch.start()
    index = face_cells(lax.broadcasted_iota(jnp.int32, (1, cross), 1), edge, planes // 2, slab)
    cell = lax.broadcasted_iota(jnp.int32, (cells, cross), 0)
    one_hot = (cell == index).astype(jnp.float32).astype(jnp.bfloat16)
    fetches[1].wait()
    place_boxes(per_device, box_count, dest, box_table)

    def copy(shift, k, b):
        return pltpu.make_async_copy(
            boxes_ref.at[0, b], outs[shift].at[pl.ds(k * fields, fields)], sems.at[shift, k]
        )

    for shift, k, slot in each_slot(box_count):
        b = box_table[slot]

        @pl.when(b >= 0)
        def _():
            copy(shift, k, b).start()

        @pl.when(b < 0)
        def _():
            outs[shift][k * fields : (k + 1) * fields] = jnp.zeros((fields, planes, cross), jnp.float32)

    for slot in range(2 * box_count):
        face_table[slot] = -1
    fetches[2].wait()

    def place(b, carry):
        slot = 2 * dest[b]
        local = parent[b] - own * coarse_count

        @pl.when(jnp.logical_and(local >= 0, local < coarse_count))
        def _():
            face_table[jnp.where(face_table[slot] >= 0, slot + 1, slot)] = local

        return carry

    lax.fori_loop(0, dest.shape[0], place, 0)
    fetches[0].wait()
    count = fields * coarse_count
    both = jnp.dot(split_two(shells[...].reshape(count, cells)), one_hot, preferred_element_type=jnp.float32)
    chosen[...] = (both[:count] + both[count:]).reshape(chosen.shape)
    for shift, k, slot in each_slot(box_count):
        local = face_table[slot]
        for f in range(fields):
            values = chosen[f, pl.ds(jnp.maximum(local, 0), 1)]
            block, row = divmod(k * fields + f, planes)
            outs[shift][2 * fields + block, row : row + 1] = jnp.where(local >= 0, values, 0.0)
    for shift, k, slot in each_slot(box_count):
        b = box_table[slot]

        @pl.when(b >= 0)
        def _():
            copy(shift, k, b).wait()


def pack_first(boxes, coarse, move_dest, parent, edge, box_count):
    per_device, fields, planes, cross = boxes.shape[1:]
    coarse = jnp.transpose(coarse, (1, 0, 2))
    hbm, vmem = pl.BlockSpec(memory_space=pltpu.HBM), pl.BlockSpec(memory_space=pltpu.VMEM)
    item = (2 * fields + 2 * fields // planes, planes, cross)
    return pl.pallas_call(
        functools.partial(first_kernel, per_device, box_count, edge),
        out_shape=[jax.ShapeDtypeStruct(item, jnp.float32)] * box_count,
        in_specs=[hbm] * 4,
        out_specs=[vmem] * box_count,
        scratch_shapes=[
            pltpu.VMEM(coarse.shape, jnp.float32),
            pltpu.VMEM(coarse.shape[:2] + (cross,), jnp.float32),
            pltpu.SMEM(move_dest.shape, jnp.int32),
            pltpu.SMEM(parent.shape, jnp.int32),
            pltpu.SMEM((2 * box_count,), jnp.int32),
            pltpu.SMEM((2 * box_count,), jnp.int32),
            pltpu.SemaphoreType.DMA((box_count, 2)),
            pltpu.SemaphoreType.DMA((3,)),
        ],
        cost_estimate=pl.CostEstimate(
            flops=6 * coarse.size * cross, bytes_accessed=4 * (coarse.size + 2 * boxes.size), transcendentals=0
        ),
    )(move_dest, parent, boxes, coarse)


def later_kernel(turns, per_device, box_count, levels, dest_ref, boxes_ref, *refs):
    outs, (dest, table, sems, in_sem, *stay) = refs[: len(turns)], refs[len(turns) :]
    own = lax.axis_index("box")
    fetch = pltpu.make_async_copy(dest_ref, dest, in_sem)
    fetch.start()
    fetch.wait()
    place_boxes(per_device, box_count, dest, table)
    places = [(n, k, 2 * target_of(own, turn, box_count) + k) for n, turn in enumerate(turns) for k in range(2)]
    held = [stay[0] if turn == 0 else out for turn, out in zip(turns, outs)]

    def copies(n, k, b):
        skip = levels - held[n].shape[0]
        for level in range(skip, levels):
            yield pltpu.make_async_copy(boxes_ref.at[level, b], held[n].at[level - skip, k], sems.at[n, level, k])

    for n, k, slot in places:
        b = table[slot]

        @pl.when(b >= 0)
        def _():
            for copy in copies(n, k, b):
                copy.start()

        @pl.when(b < 0)
        def _():
            for level in range(held[n].shape[0]):
                held[n][level, k] = jnp.zeros(held[n].shape[2:], jnp.float32)

    for n, k, slot in places:
        b = table[slot]

        @pl.when(b >= 0)
        def _():
            for copy in copies(n, k, b):
                copy.wait()

    for n, turn in enumerate(turns):
        if turn == 0:
            settled = pltpu.make_async_copy(held[n], outs[n].at[:, pl.ds(2 * own, 2)], in_sem)
            settled.start()
            settled.wait()


def pack_later(turns, boxes, move_dest, box_count):
    levels, per_device = boxes.shape[:2]
    item = boxes.shape[2:]
    hbm, vmem = pl.BlockSpec(memory_space=pltpu.HBM), pl.BlockSpec(memory_space=pltpu.VMEM)
    size = int(np.prod(item)) * 4
    shapes = [(levels - 1, 2) + item if turn else (levels, 2 * box_count) + item for turn in turns]
    return pl.pallas_call(
        functools.partial(later_kernel, turns, per_device, box_count, levels),
        out_shape=[jax.ShapeDtypeStruct(shape, jnp.float32) for shape in shapes],
        in_specs=[hbm] * 2,
        out_specs=[vmem if turn else hbm for turn in turns],
        scratch_shapes=[
            pltpu.SMEM(move_dest.shape, jnp.int32),
            pltpu.SMEM((2 * box_count,), jnp.int32),
            pltpu.SemaphoreType.DMA((len(turns), levels, 2)),
            pltpu.SemaphoreType.DMA,
        ]
        + [pltpu.VMEM((levels, 2) + item, jnp.float32) for turn in turns if turn == 0],
        cost_estimate=pl.CostEstimate(
            flops=0, bytes_accessed=4 * len(turns) * levels * size, transcendentals=0
        ),
    )(move_dest, boxes)


def settle_later(piece, turn, moved_ref, sem):
    source = source_of(lax.axis_index("box"), turn, moved_ref.shape[1] // 2)
    to = moved_ref.at[pl.ds(1, moved_ref.shape[0] - 1), pl.ds(2 * source, 2)]
    return pltpu.make_async_copy(piece, to, sem)


def settle_kernel(turns, *refs):
    out_ref, sems = refs[-2:]
    copies = [settle_later(refs[n], turn, out_ref, sems.at[n]) for n, turn in enumerate(turns)]
    for copy in copies:
        copy.start()
    for copy in copies:
        copy.wait()


def settle(turns, pieces, moved, after):
    count = len(pieces)
    vmem, hbm = pl.BlockSpec(memory_space=pltpu.VMEM), pl.BlockSpec(memory_space=pltpu.HBM)
    return pl.pallas_call(
        functools.partial(settle_kernel, turns),
        out_shape=jax.ShapeDtypeStruct(moved.shape, jnp.float32),
        in_specs=[vmem] * count + [hbm, vmem],
        out_specs=hbm,
        scratch_shapes=[pltpu.SemaphoreType.DMA((count,))],
        input_output_aliases={count: 0},
        compiler_params=pltpu.CompilerParams(vmem_limit_bytes=48 * 2 ** 20),
        cost_estimate=pl.CostEstimate(
            flops=0, bytes_accessed=8 * count * pieces[0].size, transcendentals=0
        ),
    )(*pieces, moved, after)


def arrive_kernel(box_count, slabs, fields, *refs):
    pieces = refs[:box_count]
    now_ref, moved_ref, *edges, own_rows, sems, own_sem = refs[box_count + 1 :]
    own, slab = lax.axis_index("box"), lax.axis_index("slab")
    planes, cross = now_ref.shape[2:]
    faces = pl.ds(2 * fields, own_rows.shape[0])
    mine = [pltpu.make_async_copy(pieces[0].at[faces], own_rows, own_sem)]
    copies = []
    for turn in range(box_count):
        source = source_of(own, turn, box_count)
        for k in range(2):
            box = pieces[turn].at[pl.ds(k * fields, fields)]
            if turn:
                copies.append(pltpu.make_async_copy(box, moved_ref.at[0, 2 * source + k], sems.at[turn, k]))
            else:
                mine.append(pltpu.make_async_copy(box, now_ref.at[2 * own + k, pl.ds(0, fields)], sems.at[0, k]))
    for copy in mine + copies:
        copy.start()
    faced = [jnp.where(slab == 0, planes - 1, 0)] if slabs == 2 else [0, planes - 1]

    def place_rows(rows_ref, first_block, source):
        for k in range(2):
            for f in range(ROWS):
                values = jnp.zeros((1, cross), jnp.float32)
                if f < fields:
                    block, row = divmod(k * fields + f, planes)
                    values = rows_ref[first_block + block, row : row + 1]
                now_ref[2 * source + k, fields + f // planes, f % planes : f % planes + 1] = values
            for edge_ref, plane in zip(edges, faced):
                for f in range(fields):
                    edge_ref[2 * source + k, f : f + 1] = now_ref[2 * source + k, f, pl.ds(plane, 1)]

    for turn in range(1, box_count):
        source = source_of(own, turn, box_count)
        for k in range(2):
            now_ref[2 * source + k, :fields] = pieces[turn][k * fields : (k + 1) * fields]
        place_rows(pieces[turn], 2 * fields, source)
    for copy in mine:
        copy.wait()
    place_rows(own_rows, 0, own)
    for copy in copies:
        copy.wait()


def arrive(pieces, moved, slabs):
    box_count = len(pieces)
    _, planes, cross = pieces[0].shape
    fields = moved.shape[2]
    slots = 2 * box_count
    sides = 1 if slabs == 2 else 2
    vmem, hbm = pl.BlockSpec(memory_space=pltpu.VMEM), pl.BlockSpec(memory_space=pltpu.HBM)
    shapes = [(slots, fields + ROWS // planes, planes, cross), moved.shape] + [(slots, fields, cross)] * sides
    return pl.pallas_call(
        functools.partial(arrive_kernel, box_count, slabs, fields),
        out_shape=[jax.ShapeDtypeStruct(shape, jnp.float32) for shape in shapes],
        in_specs=[hbm] + [vmem] * (box_count - 1) + [hbm],
        out_specs=[vmem, hbm] + [vmem] * sides,
        scratch_shapes=[
            pltpu.VMEM((2 * fields // planes, planes, cross), jnp.float32),
            pltpu.SemaphoreType.DMA((box_count, 2)),
            pltpu.SemaphoreType.DMA,
        ],
        input_output_aliases={box_count: 1},
        compiler_params=pltpu.CompilerParams(vmem_limit_bytes=48 * 2 ** 20),
        cost_estimate=pl.CostEstimate(
            flops=0, bytes_accessed=12 * box_count * pieces[0].size, transcendentals=0
        ),
    )(*pieces, moved)


def face_cells(lane, edge, coarse_planes, slab):
    half, side = edge // 2, edge // 2 + 2
    plane, m = lane // (4 * half), lane % half + 1
    which = (lane // half) % 4
    rim = jnp.where(which == 0, m, jnp.where(which == 1, (side - 1) * side + m, m * side))
    rim = jnp.where(which == 3, rim + side - 1, rim) + (slab * coarse_planes + plane + 1) * side * side
    t = lane - 4 * half * coarse_planes
    x_rim = jnp.where(slab > 0, (side - 1) * side * side, 0) + (t // half + 1) * side + m
    return jnp.where(t < 0, rim, jnp.where(t < half * half, x_rim, -1))


def expand_table(coarse_planes, edge, lanes):
    half = edge // 2
    cross = edge * edge
    spread = np.zeros((lanes, (2 * coarse_planes + 1) * cross), np.float32)
    for c in range(coarse_planes):
        base = c * 4 * half
        forward, backward = 2 * c * cross, (2 * c + 1) * cross
        for m in range(edge):
            spread[base + m // 2, backward + m] += 1
            spread[base + half + m // 2, forward + (edge - 1) * edge + m] += 1
            spread[base + 2 * half + m // 2, backward + m * edge] += 1
            spread[base + 3 * half + m // 2, forward + m * edge + edge - 1] += 1
    base, to = coarse_planes * 4 * half, 2 * coarse_planes * cross
    for y in range(edge):
        for z in range(edge):
            spread[base + (y // 2) * half + z // 2, to + y * edge + z] = 1
    return spread


def slope_columns(fields, planes, coarse_planes):
    column_field, forward, backward, centre = [], [], [], []
    p = np.arange(planes)

    def add(field, f, b, c):
        column_field.append(field)
        forward.append(f * np.ones(planes))
        backward.append(b * np.ones(planes))
        centre.append(c * np.ones(planes))

    for f, b, c in ((1, 0, 0), (0, 1, 0), (0, 0, 1)):
        for g in range(2 * fields):
            for q in range(planes):
                here = p == q
                add(g, f * here + c * (p + 1 == q), b * here + c * (p - 1 == q), c * here)
    rows = [g if g < fields else -1 for g in range(ROWS)]
    rows += [fields + g if g < fields else -1 for g in range(ROWS)]
    for g in rows:
        add(g, 0, p == 0, 0)
    for g in rows:
        add(g, p == planes - 1, 0, 0)
    for c in range(coarse_planes):
        for g in rows:
            add(g, p // 2 == c, 0, 0)
        for g in rows:
            add(g, 0, p // 2 == c, 0)
    width = round_up(len(column_field), 128)
    select = np.zeros((2 * fields, width), np.float32)
    masks = np.zeros((3, planes, width), np.float32)
    for k, g in enumerate(column_field):
        if g >= 0:
            select[g, k] = 1
        masks[0, :, k], masks[1, :, k], masks[2, :, k] = forward[k], backward[k], centre[k]
    return select, masks


def expand_faces(slots_ref, fields, spread_ref, out_ref):
    slots, _, planes, cross = slots_ref.shape
    for slot in range(slots):
        for block in range(ROWS // planes):
            at = slot * ROWS + block * planes
            out_ref[at : at + planes, :cross] = slots_ref[slot, fields + block]
    both = jnp.dot(split_two(out_ref[:, :cross]), spread_ref[...], preferred_element_type=jnp.float32)
    out_ref[...] = both[: slots * ROWS] + both[slots * ROWS :]


def own_ghosts(now, fields, spread):
    vmem = pl.BlockSpec(memory_space=pltpu.VMEM)
    shape = (now.shape[0] * ROWS, spread.shape[1])

    def kernel(now_ref, spread_ref, out_ref):
        expand_faces(now_ref, fields, spread_ref, out_ref)

    return pl.pallas_call(
        kernel,
        out_shape=jax.ShapeDtypeStruct(shape, jnp.float32),
        in_specs=[vmem] * 2,
        out_specs=vmem,
        compiler_params=pltpu.CompilerParams(vmem_limit_bytes=48 * 2 ** 20),
        cost_estimate=pl.CostEstimate(
            flops=4 * shape[0] * spread.size, bytes_accessed=4 * shape[0] * shape[1], transcendentals=0
        ),
    )(now, spread)


def slope_kernel(
    edge, planes, fields, coarse_planes, per_device, total, coarse_count, slots, slabs,
    dest_ref, parent_ref, own_ref, other_ref, own_low, other_low, own_high, other_high,
    own_rim, spread_ref, weight_ref, out_ref, token_ref, stack, parts, other_rim, table, count,
):
    step = pl.program_id(0)
    cross = edge * edge
    rows = fields * planes
    own, slab = lax.axis_index("box"), lax.axis_index("slab")

    @pl.when(step == 0)
    def _():
        token_ref[...] = jnp.zeros_like(token_ref)
        stack[...] = jnp.zeros_like(stack)
        half = weight_ref.shape[0]
        weights = weight_ref[...]
        parts[:half] = weights.astype(jnp.bfloat16)
        parts[half:] = (weights - weights.astype(jnp.bfloat16).astype(jnp.float32)).astype(jnp.bfloat16)
        for slot in range(slots):
            table[slot] = -1
            count[slot] = 0

        def place(b, carry):
            @pl.when(dest_ref[b] == own)
            def _():
                slot = 2 * (b // per_device)
                owner = parent_ref[b] // coarse_count
                table[jnp.where(table[slot] >= 0, slot + 1, slot)] = 2 * owner + count[owner]
                count[owner] = count[owner] + 1

            return carry

        lax.fori_loop(0, total, place, 0)
        expand_faces(other_ref, fields, spread_ref, other_rim)

    face = table[step]

    @pl.when(face < 0)
    def _():
        out_ref[...] = jnp.zeros_like(out_ref)

    @pl.when(face >= 0)
    def _():
        lane = lax.broadcasted_iota(jnp.int32, (1, cross), 1)
        y, z = lane // edge, lane % edge
        for n, ref in enumerate((own_ref, other_ref)):
            at = (4 + n) * rows
            if planes % 8:
                for f in range(fields):
                    stack[at + f * planes : at + (f + 1) * planes] = ref[step, f]
            else:
                stack[at : at + rows] = ref[step, :fields].reshape(rows, cross)
        cells = stack[4 * rows : 6 * rows]
        stack[0 : 2 * rows] = jnp.where(y < edge - 1, pltpu.roll(cells, cross - edge, 1), 0.0) + jnp.where(
            z < edge - 1, pltpu.roll(cells, cross - 1, 1), 0.0
        )
        stack[2 * rows : 4 * rows] = jnp.where(y > 0, pltpu.roll(cells, edge, 1), 0.0) + jnp.where(
            z > 0, pltpu.roll(cells, 1, 1), 0.0
        )
        here = pl.ds(pl.multiple_of(ROWS * face, ROWS), ROWS)
        rim = jnp.concatenate([own_rim[here], other_rim[here]], axis=0)
        base = 6 * rows
        x_face = rim[:, 2 * coarse_planes * cross :]
        stack[base : base + 2 * ROWS] = x_face
        stack[base + 2 * ROWS : base + 4 * ROWS] = x_face

        @pl.when(slab > 0)
        def _():
            stack[base : base + fields] = own_low[step]
            stack[base + ROWS : base + ROWS + fields] = other_low[step]

        @pl.when(slab < slabs - 1)
        def _():
            stack[base + 2 * ROWS : base + 2 * ROWS + fields] = own_high[step]
            stack[base + 3 * ROWS : base + 3 * ROWS + fields] = other_high[step]

        base += 4 * ROWS
        for n in range(2 * coarse_planes):
            stack[base + 2 * ROWS * n : base + 2 * ROWS * (n + 1)] = rim[:, n * cross : (n + 1) * cross]
        values = stack[...]
        high = values.astype(jnp.bfloat16)
        low = (values - high.astype(jnp.float32)).astype(jnp.bfloat16)
        half = weight_ref.shape[0]
        both = jnp.dot(parts[...], high, preferred_element_type=jnp.float32)
        mixed = jnp.dot(parts[:half], low, preferred_element_type=jnp.float32)
        mixed = both[:half] + (both[half:] + mixed)
        if planes % 8:
            for f in range(fields):
                out_ref[0, f] = mixed[f * planes : (f + 1) * planes]
        else:
            out_ref[0] = mixed[:rows].reshape(fields, planes, cross)


def mixing_weights(mixes, group, fields, planes, coarse_planes):
    lap_mix, grad_mix, damp_mix = mixes
    select, masks = slope_columns(fields, planes, coarse_planes)
    terms = jnp.stack([lap_mix + 0.5 * grad_mix, lap_mix - 0.5 * grad_mix, damp_mix - 6.0 * lap_mix])
    terms = lax.dynamic_slice_in_dim(terms, group * fields, fields, 1)
    terms = jnp.where(group == 0, terms, jnp.roll(terms, fields, axis=2))
    terms = jnp.einsum("tfg,gk->tfk", terms, jnp.asarray(select), precision=HIGHEST)
    weight = jnp.sum(terms[:, :, None, :] * jnp.asarray(masks)[:, None], axis=0).reshape(fields * planes, -1)
    return jnp.pad(weight, ((0, round_up(fields * planes, 16) - fields * planes), (0, 0)))


def body(boxes, move_dest, parent, coarse, lap_mix, grad_mix, damp_mix):
    box_count = lax.axis_size("box")
    slabs = lax.axis_size("slab")
    group = lax.axis_index("fld")
    levels, per_device, fields, planes, cross = boxes.shape
    edge = planes * slabs
    coarse_planes = planes // 2
    slots = 2 * box_count
    total = move_dest.shape[0]
    coarse_count = coarse.shape[0]

    def send(piece, turn):
        return lax.ppermute(piece, "box", [(s, (s + turn) % box_count) for s in range(box_count)])

    near = pack_later((1, box_count - 1), boxes, move_dest, box_count)
    near = [send(near[0], 1), send(near[1], box_count - 1)]
    first = pack_first(boxes, coarse, move_dest, parent, edge, box_count)
    arrived = [first[0]] + [send(first[turn], turn) for turn in range(1, box_count)]
    moved, *middle = pack_later((0,) + tuple(range(2, box_count - 1)), boxes, move_dest, box_count)
    middle = [send(piece, n + 2) for n, piece in enumerate(middle)]
    now, moved, *facing = arrive(arrived, moved, slabs)

    swap = [(0, 1), (1, 0)]
    now_other = lax.ppermute(now, "fld", swap)

    spread = jnp.asarray(expand_table(coarse_planes, edge, cross)).astype(jnp.bfloat16)
    rim = own_ghosts(now, fields, spread)

    def shifted(values, up):
        pairs = [(s, s + 1) if up else (s + 1, s) for s in range(slabs - 1)]
        return lax.ppermute(values, "slab", swap if slabs == 2 else pairs)

    low = shifted(facing[-1], True)
    low, rim = lax.optimization_barrier((low, rim))
    low = low, lax.ppermute(low, "fld", swap)
    high = low
    if slabs != 2:
        high = shifted(facing[0], False)
        high = high, lax.ppermute(high, "fld", swap)

    weight = mixing_weights((lap_mix, grad_mix, damp_mix), group, fields, planes, coarse_planes)
    smem, vmem = pl.BlockSpec(memory_space=pltpu.SMEM), pl.BlockSpec(memory_space=pltpu.VMEM)
    slope, token = pl.pallas_call(
        functools.partial(
            slope_kernel, edge, planes, fields, coarse_planes, per_device, total, coarse_count, slots, slabs
        ),
        grid=(slots,),
        out_shape=[
            jax.ShapeDtypeStruct((slots, fields, planes, cross), jnp.float32),
            jax.ShapeDtypeStruct((8, 128), jnp.float32),
        ],
        in_specs=[smem, smem] + [vmem] * 9,
        out_specs=[pl.BlockSpec((1, fields, planes, cross), lambda n: (n, 0, 0, 0)), vmem],
        scratch_shapes=[
            pltpu.VMEM((weight.shape[1], cross), jnp.float32),
            pltpu.VMEM((2 * weight.shape[0], weight.shape[1]), jnp.bfloat16),
            pltpu.VMEM((ROWS * slots, spread.shape[1]), jnp.float32),
            pltpu.SMEM((slots,), jnp.int32),
            pltpu.SMEM((slots,), jnp.int32),
        ],
        compiler_params=pltpu.CompilerParams(vmem_limit_bytes=48 * 2 ** 20),
        cost_estimate=pl.CostEstimate(
            flops=3 * slots * weight.size * cross, bytes_accessed=12 * now.size, transcendentals=0
        ),
    )(move_dest, parent, now, now_other, low[0], low[1], high[0], high[1], rim, spread, weight)
    moved = settle(tuple(range(2, box_count - 1)), middle, moved, token)
    return settle((1, box_count - 1), near, moved, token), slope


def solution(mesh):
    placed = (
        P(None, ("runs", "box"), "fld", "slab", None),
        P("runs"),
        P("runs"),
        P(("runs", "box"), "fld", None),
        P(),
        P(),
        P(),
    )
    return jax.shard_map(
        body,
        mesh=mesh,
        in_specs=placed,
        out_specs=(
            P(None, ("runs", "box"), "fld", "slab", None),
            P(("runs", "box"), "fld", "slab", None),
        ),
        check_vma=False,
    )
```

```python
import functools

import jax
import jax.numpy as jnp
import numpy as np
from jax import lax
from jax.experimental import pallas as pl
from jax.experimental.pallas import tpu as pltpu
from jax.sharding import PartitionSpec as P

HIGHEST = lax.Precision.HIGHEST
ROWS = 16


def round_up(value, unit):
    return -(-value // unit) * unit


def split_two(values):
    high = values.astype(jnp.bfloat16)
    low = (values - high.astype(jnp.float32)).astype(jnp.bfloat16)
    return jnp.concatenate([high, low], axis=0)


def place_boxes(per_device, box_count, dest_ref, table):
    own = lax.axis_index("box")
    for slot in range(2 * box_count):
        table[slot] = -1

    def place(b, carry):
        slot = 2 * dest_ref[own * per_device + b]
        table[jnp.where(table[slot] >= 0, slot + 1, slot)] = b
        return carry

    lax.fori_loop(0, per_device, place, 0)


def target_of(own, turn, box_count):
    return lax.rem(own + turn, box_count)


def source_of(own, turn, box_count):
    return lax.rem(own - turn + box_count, box_count)


def each_slot(box_count):
    own = lax.axis_index("box")
    for turn in range(box_count):
        for k in range(2):
            yield turn, k, 2 * target_of(own, turn, box_count) + k


def first_kernel(per_device, box_count, edge, dest_ref, parent_ref, boxes_ref, coarse_ref, *refs):
    outs, (boxes, zeros, shells, chosen, rows, dest, parent, box_table, face_table, sems, row_sems, in_sems) = (
        refs[:box_count], refs[box_count:]
    )
    fields, coarse_count, cells = coarse_ref.shape
    planes, cross = outs[0].shape[1:]
    own, slab = lax.axis_index("box"), lax.axis_index("slab")
    fetches = [
        pltpu.make_async_copy(dest_ref, dest, in_sems.at[0]),
        pltpu.make_async_copy(boxes_ref.at[0], boxes, in_sems.at[1]),
        pltpu.make_async_copy(parent_ref, parent, in_sems.at[2]),
        pltpu.make_async_copy(coarse_ref, shells, in_sems.at[3]),
    ]
    for fetch in fetches:
        fetch.start()
    zeros[...] = jnp.zeros_like(zeros)
    index = face_cells(lax.broadcasted_iota(jnp.int32, (1, cross), 1), edge, planes // 2, slab)
    cell = lax.broadcasted_iota(jnp.int32, (cells, cross), 0)
    one_hot = (cell == index).astype(jnp.float32).astype(jnp.bfloat16)
    fetches[0].wait()
    place_boxes(per_device, box_count, dest, box_table)
    fetches[1].wait()

    def copy(shift, k, values):
        return pltpu.make_async_copy(values, outs[shift].at[pl.ds(k * fields, fields)], sems.at[shift, k])

    for shift, k, slot in each_slot(box_count):
        b = box_table[slot]

        @pl.when(b >= 0)
        def _():
            copy(shift, k, boxes.at[b]).start()

        @pl.when(b < 0)
        def _():
            copy(shift, k, zeros).start()

    for slot in range(2 * box_count):
        face_table[slot] = -1
    fetches[2].wait()

    def place(b, carry):
        slot = 2 * dest[b]
        local = parent[b] - own * coarse_count

        @pl.when(jnp.logical_and(local >= 0, local < coarse_count))
        def _():
            face_table[jnp.where(face_table[slot] >= 0, slot + 1, slot)] = local

        return carry

    lax.fori_loop(0, dest.shape[0], place, 0)
    fetches[3].wait()
    count = fields * coarse_count
    both = jnp.dot(split_two(shells[...].reshape(count, cells)), one_hot, preferred_element_type=jnp.float32)
    chosen[...] = (both[:count] + both[count:]).reshape(chosen.shape)
    sent = []
    for shift, k, slot in each_slot(box_count):
        local = face_table[slot]
        for f in range(fields):
            values = chosen[f, pl.ds(jnp.maximum(local, 0), 1)]
            block, row = divmod(k * fields + f, planes)
            rows[shift, block, row : row + 1] = jnp.where(local >= 0, values, 0.0)
        if k == 1:
            to = outs[shift].at[pl.ds(2 * fields, rows.shape[1])]
            sent.append(pltpu.make_async_copy(rows.at[shift], to, row_sems.at[shift]))
            sent[-1].start()
    for shift, k, slot in each_slot(box_count):
        copy(shift, k, zeros).wait()
    for rows_copy in sent:
        rows_copy.wait()


def pack_first(boxes, coarse, move_dest, parent, edge, box_count):
    per_device, fields, planes, cross = boxes.shape[1:]
    coarse = jnp.transpose(coarse, (1, 0, 2))
    hbm = pl.BlockSpec(memory_space=pltpu.HBM)
    face_blocks = 2 * fields // planes
    item = (2 * fields + face_blocks, planes, cross)
    return pl.pallas_call(
        functools.partial(first_kernel, per_device, box_count, edge),
        out_shape=[jax.ShapeDtypeStruct(item, jnp.float32)] * box_count,
        in_specs=[hbm] * 4,
        out_specs=[hbm] * box_count,
        scratch_shapes=[
            pltpu.VMEM(boxes.shape[1:], jnp.float32),
            pltpu.VMEM(boxes.shape[2:], jnp.float32),
            pltpu.VMEM(coarse.shape, jnp.float32),
            pltpu.VMEM(coarse.shape[:2] + (cross,), jnp.float32),
            pltpu.VMEM((box_count, face_blocks, planes, cross), jnp.float32),
            pltpu.SMEM(move_dest.shape, jnp.int32),
            pltpu.SMEM(parent.shape, jnp.int32),
            pltpu.SMEM((2 * box_count,), jnp.int32),
            pltpu.SMEM((2 * box_count,), jnp.int32),
            pltpu.SemaphoreType.DMA((box_count, 2)),
            pltpu.SemaphoreType.DMA((box_count,)),
            pltpu.SemaphoreType.DMA((4,)),
        ],
        cost_estimate=pl.CostEstimate(
            flops=6 * coarse.size * cross, bytes_accessed=4 * (coarse.size + 2 * boxes.size), transcendentals=0
        ),
    )(move_dest, parent, boxes, coarse)


def later_kernel(turns, per_device, box_count, levels, dest_ref, boxes_ref, *refs):
    outs, (dest, table, sems, in_sem, *stay) = refs[: len(turns)], refs[len(turns) :]
    own = lax.axis_index("box")
    fetch = pltpu.make_async_copy(dest_ref, dest, in_sem)
    fetch.start()
    fetch.wait()
    place_boxes(per_device, box_count, dest, table)
    places = [(n, k, 2 * target_of(own, turn, box_count) + k) for n, turn in enumerate(turns) for k in range(2)]
    held = [stay[0] if turn == 0 else out for turn, out in zip(turns, outs)]

    def copies(n, k, b):
        skip = levels - held[n].shape[0]
        for level in range(skip, levels):
            yield pltpu.make_async_copy(boxes_ref.at[level, b], held[n].at[level - skip, k], sems.at[n, level, k])

    for n, k, slot in places:
        b = table[slot]

        @pl.when(b >= 0)
        def _():
            for copy in copies(n, k, b):
                copy.start()

        @pl.when(b < 0)
        def _():
            for level in range(held[n].shape[0]):
                held[n][level, k] = jnp.zeros(held[n].shape[2:], jnp.float32)

    for n, k, slot in places:
        b = table[slot]

        @pl.when(b >= 0)
        def _():
            for copy in copies(n, k, b):
                copy.wait()

    for n, turn in enumerate(turns):
        if turn == 0:
            settled = pltpu.make_async_copy(held[n], outs[n].at[:, pl.ds(2 * own, 2)], in_sem)
            settled.start()
            settled.wait()


def pack_later(turns, boxes, move_dest, box_count):
    levels, per_device = boxes.shape[:2]
    item = boxes.shape[2:]
    hbm, vmem = pl.BlockSpec(memory_space=pltpu.HBM), pl.BlockSpec(memory_space=pltpu.VMEM)
    size = int(np.prod(item)) * 4
    shapes = [(levels - 1, 2) + item if turn else (levels, 2 * box_count) + item for turn in turns]
    return pl.pallas_call(
        functools.partial(later_kernel, turns, per_device, box_count, levels),
        out_shape=[jax.ShapeDtypeStruct(shape, jnp.float32) for shape in shapes],
        in_specs=[hbm] * 2,
        out_specs=[vmem if turn else hbm for turn in turns],
        scratch_shapes=[
            pltpu.SMEM(move_dest.shape, jnp.int32),
            pltpu.SMEM((2 * box_count,), jnp.int32),
            pltpu.SemaphoreType.DMA((len(turns), levels, 2)),
            pltpu.SemaphoreType.DMA,
        ]
        + [pltpu.VMEM((levels, 2) + item, jnp.float32) for turn in turns if turn == 0],
        cost_estimate=pl.CostEstimate(
            flops=0, bytes_accessed=4 * len(turns) * levels * size, transcendentals=0
        ),
    )(move_dest, boxes)


def settle_later(piece, turn, moved_ref, sem):
    source = source_of(lax.axis_index("box"), turn, moved_ref.shape[1] // 2)
    to = moved_ref.at[pl.ds(1, moved_ref.shape[0] - 1), pl.ds(2 * source, 2)]
    return pltpu.make_async_copy(piece, to, sem)


def settle_kernel(turns, *refs):
    out_ref, sems = refs[-2:]
    copies = [settle_later(refs[n], turn, out_ref, sems.at[n]) for n, turn in enumerate(turns)]
    for copy in copies:
        copy.start()
    for copy in copies:
        copy.wait()


def settle(turns, pieces, moved, after):
    count = len(pieces)
    vmem, hbm = pl.BlockSpec(memory_space=pltpu.VMEM), pl.BlockSpec(memory_space=pltpu.HBM)
    return pl.pallas_call(
        functools.partial(settle_kernel, turns),
        out_shape=jax.ShapeDtypeStruct(moved.shape, jnp.float32),
        in_specs=[vmem] * count + [hbm, vmem],
        out_specs=hbm,
        scratch_shapes=[pltpu.SemaphoreType.DMA((count,))],
        input_output_aliases={count: 0},
        compiler_params=pltpu.CompilerParams(vmem_limit_bytes=48 * 2 ** 20),
        cost_estimate=pl.CostEstimate(
            flops=0, bytes_accessed=8 * count * pieces[0].size, transcendentals=0
        ),
    )(*pieces, moved, after)


def arrive_kernel(box_count, slabs, fields, *refs):
    pieces = refs[:box_count]
    now_ref, moved_ref, *edges, own_rows, sems, own_sem = refs[box_count + 1 :]
    own, slab = lax.axis_index("box"), lax.axis_index("slab")
    planes, cross = now_ref.shape[2:]
    faces = pl.ds(2 * fields, own_rows.shape[0])
    mine = [pltpu.make_async_copy(pieces[0].at[faces], own_rows, own_sem)]
    copies = []
    for turn in range(box_count):
        source = source_of(own, turn, box_count)
        for k in range(2):
            box = pieces[turn].at[pl.ds(k * fields, fields)]
            if turn:
                copies.append(pltpu.make_async_copy(box, moved_ref.at[0, 2 * source + k], sems.at[turn, k]))
            else:
                mine.append(pltpu.make_async_copy(box, now_ref.at[2 * own + k, pl.ds(0, fields)], sems.at[0, k]))
    for copy in mine + copies:
        copy.start()
    faced = [jnp.where(slab == 0, planes - 1, 0)] if slabs == 2 else [0, planes - 1]

    def place_rows(rows_ref, first_block, source):
        for k in range(2):
            for f in range(ROWS):
                values = jnp.zeros((1, cross), jnp.float32)
                if f < fields:
                    block, row = divmod(k * fields + f, planes)
                    values = rows_ref[first_block + block, row : row + 1]
                now_ref[2 * source + k, fields + f // planes, f % planes : f % planes + 1] = values
            for edge_ref, plane in zip(edges, faced):
                for f in range(fields):
                    edge_ref[2 * source + k, f : f + 1] = now_ref[2 * source + k, f, pl.ds(plane, 1)]

    for turn in range(1, box_count):
        source = source_of(own, turn, box_count)
        for k in range(2):
            now_ref[2 * source + k, :fields] = pieces[turn][k * fields : (k + 1) * fields]
        place_rows(pieces[turn], 2 * fields, source)
    for copy in mine:
        copy.wait()
    place_rows(own_rows, 0, own)
    for copy in copies:
        copy.wait()


def arrive(pieces, moved, slabs):
    box_count = len(pieces)
    _, planes, cross = pieces[0].shape
    fields = moved.shape[2]
    slots = 2 * box_count
    sides = 1 if slabs == 2 else 2
    vmem, hbm = pl.BlockSpec(memory_space=pltpu.VMEM), pl.BlockSpec(memory_space=pltpu.HBM)
    shapes = [(slots, fields + ROWS // planes, planes, cross), moved.shape] + [(slots, fields, cross)] * sides
    return pl.pallas_call(
        functools.partial(arrive_kernel, box_count, slabs, fields),
        out_shape=[jax.ShapeDtypeStruct(shape, jnp.float32) for shape in shapes],
        in_specs=[hbm] + [vmem] * (box_count - 1) + [hbm],
        out_specs=[vmem, hbm] + [vmem] * sides,
        scratch_shapes=[
            pltpu.VMEM((2 * fields // planes, planes, cross), jnp.float32),
            pltpu.SemaphoreType.DMA((box_count, 2)),
            pltpu.SemaphoreType.DMA,
        ],
        input_output_aliases={box_count: 1},
        compiler_params=pltpu.CompilerParams(vmem_limit_bytes=48 * 2 ** 20),
        cost_estimate=pl.CostEstimate(
            flops=0, bytes_accessed=12 * box_count * pieces[0].size, transcendentals=0
        ),
    )(*pieces, moved)


def face_cells(lane, edge, coarse_planes, slab):
    half, side = edge // 2, edge // 2 + 2
    plane, m = lane // (4 * half), lane % half + 1
    which = (lane // half) % 4
    rim = jnp.where(which == 0, m, jnp.where(which == 1, (side - 1) * side + m, m * side))
    rim = jnp.where(which == 3, rim + side - 1, rim) + (slab * coarse_planes + plane + 1) * side * side
    t = lane - 4 * half * coarse_planes
    x_rim = jnp.where(slab > 0, (side - 1) * side * side, 0) + (t // half + 1) * side + m
    return jnp.where(t < 0, rim, jnp.where(t < half * half, x_rim, -1))


def expand_table(coarse_planes, edge, lanes):
    half = edge // 2
    cross = edge * edge
    spread = np.zeros((lanes, (2 * coarse_planes + 1) * cross), np.float32)
    for c in range(coarse_planes):
        base = c * 4 * half
        forward, backward = 2 * c * cross, (2 * c + 1) * cross
        for m in range(edge):
            spread[base + m // 2, backward + m] += 1
            spread[base + half + m // 2, forward + (edge - 1) * edge + m] += 1
            spread[base + 2 * half + m // 2, backward + m * edge] += 1
            spread[base + 3 * half + m // 2, forward + m * edge + edge - 1] += 1
    base, to = coarse_planes * 4 * half, 2 * coarse_planes * cross
    for y in range(edge):
        for z in range(edge):
            spread[base + (y // 2) * half + z // 2, to + y * edge + z] = 1
    return spread


def slope_columns(fields, planes, coarse_planes):
    column_field, forward, backward, centre = [], [], [], []
    p = np.arange(planes)

    def add(field, f, b, c):
        column_field.append(field)
        forward.append(f * np.ones(planes))
        backward.append(b * np.ones(planes))
        centre.append(c * np.ones(planes))

    for f, b, c in ((1, 0, 0), (0, 1, 0), (0, 0, 1)):
        for g in range(2 * fields):
            for q in range(planes):
                here = p == q
                add(g, f * here + c * (p + 1 == q), b * here + c * (p - 1 == q), c * here)
    rows = [g if g < fields else -1 for g in range(ROWS)]
    rows += [fields + g if g < fields else -1 for g in range(ROWS)]
    for g in rows:
        add(g, 0, p == 0, 0)
    for g in rows:
        add(g, p == planes - 1, 0, 0)
    for c in range(coarse_planes):
        for g in rows:
            add(g, p // 2 == c, 0, 0)
        for g in rows:
            add(g, 0, p // 2 == c, 0)
    width = round_up(len(column_field), 128)
    select = np.zeros((2 * fields, width), np.float32)
    masks = np.zeros((3, planes, width), np.float32)
    for k, g in enumerate(column_field):
        if g >= 0:
            select[g, k] = 1
        masks[0, :, k], masks[1, :, k], masks[2, :, k] = forward[k], backward[k], centre[k]
    return select, masks


def expand_faces(slots_ref, fields, spread_ref, out_ref):
    slots, _, planes, cross = slots_ref.shape
    for slot in range(slots):
        for block in range(ROWS // planes):
            at = slot * ROWS + block * planes
            out_ref[at : at + planes, :cross] = slots_ref[slot, fields + block]
    both = jnp.dot(split_two(out_ref[:, :cross]), spread_ref[...], preferred_element_type=jnp.float32)
    out_ref[...] = both[: slots * ROWS] + both[slots * ROWS :]


def own_ghosts(now, fields, spread):
    vmem = pl.BlockSpec(memory_space=pltpu.VMEM)
    shape = (now.shape[0] * ROWS, spread.shape[1])

    def kernel(now_ref, spread_ref, out_ref):
        expand_faces(now_ref, fields, spread_ref, out_ref)

    return pl.pallas_call(
        kernel,
        out_shape=jax.ShapeDtypeStruct(shape, jnp.float32),
        in_specs=[vmem] * 2,
        out_specs=vmem,
        compiler_params=pltpu.CompilerParams(vmem_limit_bytes=48 * 2 ** 20),
        cost_estimate=pl.CostEstimate(
            flops=4 * shape[0] * spread.size, bytes_accessed=4 * shape[0] * shape[1], transcendentals=0
        ),
    )(now, spread)


def slope_kernel(
    edge, planes, fields, coarse_planes, per_device, total, coarse_count, slots, slabs,
    dest_ref, parent_ref, own_ref, other_ref, own_low, other_low, own_high, other_high,
    own_rim, spread_ref, weight_ref, out_ref, token_ref, stack, parts, other_rim, staged, table, count, sems,
):
    cross = edge * edge
    rows = fields * planes
    own, slab = lax.axis_index("box"), lax.axis_index("slab")

    token_ref[...] = jnp.zeros_like(token_ref)
    stack[...] = jnp.zeros_like(stack)
    half = weight_ref.shape[0]
    weights = weight_ref[...]
    parts[:half] = weights.astype(jnp.bfloat16)
    parts[half:] = (weights - weights.astype(jnp.bfloat16).astype(jnp.float32)).astype(jnp.bfloat16)
    for slot in range(slots):
        table[slot] = -1
        count[slot] = 0

    def place(b, carry):
        @pl.when(dest_ref[b] == own)
        def _():
            slot = 2 * (b // per_device)
            owner = parent_ref[b] // coarse_count
            table[jnp.where(table[slot] >= 0, slot + 1, slot)] = 2 * owner + count[owner]
            count[owner] = count[owner] + 1

        return carry

    lax.fori_loop(0, total, place, 0)
    expand_faces(other_ref, fields, spread_ref, other_rim)

    def write(step):
        return pltpu.make_async_copy(staged.at[step], out_ref.at[step], sems.at[step])

    def one_slot(step, carry):
        face = table[step]

        @pl.when(face < 0)
        def _():
            staged[step] = jnp.zeros(staged.shape[1:], jnp.float32)

        @pl.when(face >= 0)
        def _():
            lane = lax.broadcasted_iota(jnp.int32, (1, cross), 1)
            y, z = lane // edge, lane % edge
            for n, ref in enumerate((own_ref, other_ref)):
                at = (4 + n) * rows
                if planes % 8:
                    for f in range(fields):
                        stack[at + f * planes : at + (f + 1) * planes] = ref[step, f]
                else:
                    stack[at : at + rows] = ref[step, :fields].reshape(rows, cross)
            cells = stack[4 * rows : 6 * rows]
            stack[0 : 2 * rows] = jnp.where(y < edge - 1, pltpu.roll(cells, cross - edge, 1), 0.0) + jnp.where(
                z < edge - 1, pltpu.roll(cells, cross - 1, 1), 0.0
            )
            stack[2 * rows : 4 * rows] = jnp.where(y > 0, pltpu.roll(cells, edge, 1), 0.0) + jnp.where(
                z > 0, pltpu.roll(cells, 1, 1), 0.0
            )
            here = pl.ds(pl.multiple_of(ROWS * face, ROWS), ROWS)
            rim = jnp.concatenate([own_rim[here], other_rim[here]], axis=0)
            base = 6 * rows
            x_face = rim[:, 2 * coarse_planes * cross :]
            stack[base : base + 2 * ROWS] = x_face
            stack[base + 2 * ROWS : base + 4 * ROWS] = x_face

            @pl.when(slab > 0)
            def _():
                stack[base : base + fields] = own_low[step]
                stack[base + ROWS : base + ROWS + fields] = other_low[step]

            @pl.when(slab < slabs - 1)
            def _():
                stack[base + 2 * ROWS : base + 2 * ROWS + fields] = own_high[step]
                stack[base + 3 * ROWS : base + 3 * ROWS + fields] = other_high[step]

            base += 4 * ROWS
            for n in range(2 * coarse_planes):
                stack[base + 2 * ROWS * n : base + 2 * ROWS * (n + 1)] = rim[:, n * cross : (n + 1) * cross]
            values = stack[...]
            high = values.astype(jnp.bfloat16)
            low = (values - high.astype(jnp.float32)).astype(jnp.bfloat16)
            half = weight_ref.shape[0]
            both = jnp.dot(parts[...], high, preferred_element_type=jnp.float32)
            mixed = jnp.dot(parts[:half], low, preferred_element_type=jnp.float32)
            mixed = both[:half] + (both[half:] + mixed)
            if planes % 8:
                for f in range(fields):
                    staged[step, f] = mixed[f * planes : (f + 1) * planes]
            else:
                staged[step] = mixed[:rows].reshape(fields, planes, cross)

        write(step).start()
        return carry

    lax.fori_loop(0, slots, one_slot, 0)
    for step in range(slots):
        write(step).wait()


def mixing_weights(mixes, group, fields, planes, coarse_planes):
    lap_mix, grad_mix, damp_mix = mixes
    select, masks = slope_columns(fields, planes, coarse_planes)
    terms = jnp.stack([lap_mix + 0.5 * grad_mix, lap_mix - 0.5 * grad_mix, damp_mix - 6.0 * lap_mix])
    terms = lax.dynamic_slice_in_dim(terms, group * fields, fields, 1)
    terms = jnp.where(group == 0, terms, jnp.roll(terms, fields, axis=2))
    terms = jnp.einsum("tfg,gk->tfk", terms, jnp.asarray(select), precision=HIGHEST)
    weight = jnp.sum(terms[:, :, None, :] * jnp.asarray(masks)[:, None], axis=0).reshape(fields * planes, -1)
    return jnp.pad(weight, ((0, round_up(fields * planes, 16) - fields * planes), (0, 0)))


def body(boxes, move_dest, parent, coarse, lap_mix, grad_mix, damp_mix):
    box_count = lax.axis_size("box")
    slabs = lax.axis_size("slab")
    group = lax.axis_index("fld")
    levels, per_device, fields, planes, cross = boxes.shape
    edge = planes * slabs
    coarse_planes = planes // 2
    slots = 2 * box_count
    total = move_dest.shape[0]
    coarse_count = coarse.shape[0]

    def send(piece, turn):
        return lax.ppermute(piece, "box", [(s, (s + turn) % box_count) for s in range(box_count)])

    near = pack_later((1, box_count - 1), boxes, move_dest, box_count)
    near = [send(near[0], 1), send(near[1], box_count - 1)]
    first = pack_first(boxes, coarse, move_dest, parent, edge, box_count)
    arrived = [first[0]] + [send(first[turn], turn) for turn in range(1, box_count)]
    moved, *middle = pack_later((0,) + tuple(range(2, box_count - 1)), boxes, move_dest, box_count)
    middle = [send(piece, n + 2) for n, piece in enumerate(middle)]
    now, moved, *facing = arrive(arrived, moved, slabs)

    swap = [(0, 1), (1, 0)]
    now_other = lax.ppermute(now, "fld", swap)

    spread = jnp.asarray(expand_table(coarse_planes, edge, cross)).astype(jnp.bfloat16)
    rim = own_ghosts(now, fields, spread)

    def shifted(values, up):
        pairs = [(s, s + 1) if up else (s + 1, s) for s in range(slabs - 1)]
        return lax.ppermute(values, "slab", swap if slabs == 2 else pairs)

    low = shifted(facing[-1], True)
    low, rim = lax.optimization_barrier((low, rim))
    low = low, lax.ppermute(low, "fld", swap)
    high = low
    if slabs != 2:
        high = shifted(facing[0], False)
        high = high, lax.ppermute(high, "fld", swap)

    weight = mixing_weights((lap_mix, grad_mix, damp_mix), group, fields, planes, coarse_planes)
    smem, vmem = pl.BlockSpec(memory_space=pltpu.SMEM), pl.BlockSpec(memory_space=pltpu.VMEM)
    slope, token = pl.pallas_call(
        functools.partial(
            slope_kernel, edge, planes, fields, coarse_planes, per_device, total, coarse_count, slots, slabs
        ),
        out_shape=[
            jax.ShapeDtypeStruct((slots, fields, planes, cross), jnp.float32),
            jax.ShapeDtypeStruct((8, 128), jnp.float32),
        ],
        in_specs=[smem, smem] + [vmem] * 9,
        out_specs=[pl.BlockSpec(memory_space=pltpu.HBM), vmem],
        scratch_shapes=[
            pltpu.VMEM((weight.shape[1], cross), jnp.float32),
            pltpu.VMEM((2 * weight.shape[0], weight.shape[1]), jnp.bfloat16),
            pltpu.VMEM((ROWS * slots, spread.shape[1]), jnp.float32),
            pltpu.VMEM((slots, fields, planes, cross), jnp.float32),
            pltpu.SMEM((slots,), jnp.int32),
            pltpu.SMEM((slots,), jnp.int32),
            pltpu.SemaphoreType.DMA((slots,)),
        ],
        compiler_params=pltpu.CompilerParams(vmem_limit_bytes=48 * 2 ** 20),
        cost_estimate=pl.CostEstimate(
            flops=3 * slots * weight.size * cross, bytes_accessed=12 * now.size, transcendentals=0
        ),
    )(move_dest, parent, now, now_other, low[0], low[1], high[0], high[1], rim, spread, weight)
    moved = settle(tuple(range(2, box_count - 1)), middle, moved, token)
    return settle((1, box_count - 1), near, moved, token), slope


def solution(mesh):
    placed = (
        P(None, ("runs", "box"), "fld", "slab", None),
        P("runs"),
        P("runs"),
        P(("runs", "box"), "fld", None),
        P(),
        P(),
        P(),
    )
    return jax.shard_map(
        body,
        mesh=mesh,
        in_specs=placed,
        out_specs=(
            P(None, ("runs", "box"), "fld", "slab", None),
            P(("runs", "box"), "fld", "slab", None),
        ),
        check_vma=False,
    )
```

```python
import functools

import jax
import jax.numpy as jnp
import numpy as np
from jax import lax
from jax.experimental import pallas as pl
from jax.experimental.pallas import tpu as pltpu
from jax.sharding import PartitionSpec as P

HIGHEST = lax.Precision.HIGHEST
ROWS = 16


def round_up(value, unit):
    return -(-value // unit) * unit


def split_two(values):
    high = values.astype(jnp.bfloat16)
    low = (values - high.astype(jnp.float32)).astype(jnp.bfloat16)
    return jnp.concatenate([high, low], axis=0)


def place_boxes(per_device, box_count, dest_ref, table):
    own = lax.axis_index("box")
    for slot in range(2 * box_count):
        table[slot] = -1

    def place(b, carry):
        slot = 2 * dest_ref[own * per_device + b]
        table[jnp.where(table[slot] >= 0, slot + 1, slot)] = b
        return carry

    lax.fori_loop(0, per_device, place, 0)


def target_of(own, turn, box_count):
    return lax.rem(own + turn, box_count)


def source_of(own, turn, box_count):
    return lax.rem(own - turn + box_count, box_count)


def each_slot(box_count):
    own = lax.axis_index("box")
    for turn in range(box_count):
        for k in range(2):
            yield turn, k, 2 * target_of(own, turn, box_count) + k


def first_kernel(per_device, box_count, edge, dest_ref, parent_ref, boxes_ref, coarse_ref, *refs):
    outs, (boxes, zeros, shells, chosen, rows, dest, parent, box_table, face_table, sems, row_sems, in_sems) = (
        refs[:box_count], refs[box_count:]
    )
    fields, coarse_count, cells = coarse_ref.shape
    planes, cross = outs[0].shape[1:]
    own, slab = lax.axis_index("box"), lax.axis_index("slab")
    fetches = [
        pltpu.make_async_copy(dest_ref, dest, in_sems.at[0]),
        pltpu.make_async_copy(boxes_ref.at[0], boxes, in_sems.at[1]),
        pltpu.make_async_copy(parent_ref, parent, in_sems.at[2]),
        pltpu.make_async_copy(coarse_ref, shells, in_sems.at[3]),
    ]
    for fetch in fetches:
        fetch.start()
    zeros[...] = jnp.zeros_like(zeros)
    index = face_cells(lax.broadcasted_iota(jnp.int32, (1, cross), 1), edge, planes // 2, slab)
    cell = lax.broadcasted_iota(jnp.int32, (cells, cross), 0)
    one_hot = (cell == index).astype(jnp.float32).astype(jnp.bfloat16)
    fetches[0].wait()
    place_boxes(per_device, box_count, dest, box_table)
    fetches[1].wait()

    def copy(shift, k, values):
        return pltpu.make_async_copy(values, outs[shift].at[pl.ds(k * fields, fields)], sems.at[shift, k])

    for shift, k, slot in each_slot(box_count):
        b = box_table[slot]

        @pl.when(b >= 0)
        def _():
            copy(shift, k, boxes.at[b]).start()

        @pl.when(b < 0)
        def _():
            copy(shift, k, zeros).start()

    for slot in range(2 * box_count):
        face_table[slot] = -1
    fetches[2].wait()

    def place(b, carry):
        slot = 2 * dest[b]
        local = parent[b] - own * coarse_count

        @pl.when(jnp.logical_and(local >= 0, local < coarse_count))
        def _():
            face_table[jnp.where(face_table[slot] >= 0, slot + 1, slot)] = local

        return carry

    lax.fori_loop(0, dest.shape[0], place, 0)
    fetches[3].wait()
    count = fields * coarse_count
    both = jnp.dot(split_two(shells[...].reshape(count, cells)), one_hot, preferred_element_type=jnp.float32)
    chosen[...] = (both[:count] + both[count:]).reshape(chosen.shape)
    sent = []
    for shift, k, slot in each_slot(box_count):
        local = face_table[slot]
        for f in range(fields):
            values = chosen[f, pl.ds(jnp.maximum(local, 0), 1)]
            block, row = divmod(k * fields + f, planes)
            rows[shift, block, row : row + 1] = jnp.where(local >= 0, values, 0.0)
        if k == 1:
            to = outs[shift].at[pl.ds(2 * fields, rows.shape[1])]
            sent.append(pltpu.make_async_copy(rows.at[shift], to, row_sems.at[shift]))
            sent[-1].start()
    for shift, k, slot in each_slot(box_count):
        copy(shift, k, zeros).wait()
    for rows_copy in sent:
        rows_copy.wait()


def pack_first(boxes, coarse, move_dest, parent, edge, box_count):
    per_device, fields, planes, cross = boxes.shape[1:]
    coarse = jnp.transpose(coarse, (1, 0, 2))
    hbm = pl.BlockSpec(memory_space=pltpu.HBM)
    face_blocks = 2 * fields // planes
    item = (2 * fields + face_blocks, planes, cross)
    return pl.pallas_call(
        functools.partial(first_kernel, per_device, box_count, edge),
        out_shape=[jax.ShapeDtypeStruct(item, jnp.float32)] * box_count,
        in_specs=[hbm] * 4,
        out_specs=[hbm] * box_count,
        scratch_shapes=[
            pltpu.VMEM(boxes.shape[1:], jnp.float32),
            pltpu.VMEM(boxes.shape[2:], jnp.float32),
            pltpu.VMEM(coarse.shape, jnp.float32),
            pltpu.VMEM(coarse.shape[:2] + (cross,), jnp.float32),
            pltpu.VMEM((box_count, face_blocks, planes, cross), jnp.float32),
            pltpu.SMEM(move_dest.shape, jnp.int32),
            pltpu.SMEM(parent.shape, jnp.int32),
            pltpu.SMEM((2 * box_count,), jnp.int32),
            pltpu.SMEM((2 * box_count,), jnp.int32),
            pltpu.SemaphoreType.DMA((box_count, 2)),
            pltpu.SemaphoreType.DMA((box_count,)),
            pltpu.SemaphoreType.DMA((4,)),
        ],
        cost_estimate=pl.CostEstimate(
            flops=6 * coarse.size * cross, bytes_accessed=4 * (coarse.size + 2 * boxes.size), transcendentals=0
        ),
    )(move_dest, parent, boxes, coarse)


def later_kernel(turns, per_device, box_count, levels, dest_ref, boxes_ref, *refs):
    outs, (dest, table, sems, in_sem, *stay) = refs[: len(turns)], refs[len(turns) :]
    own = lax.axis_index("box")
    fetch = pltpu.make_async_copy(dest_ref, dest, in_sem)
    fetch.start()
    fetch.wait()
    place_boxes(per_device, box_count, dest, table)
    places = [(n, k, 2 * target_of(own, turn, box_count) + k) for n, turn in enumerate(turns) for k in range(2)]
    held = [stay[0] if turn == 0 else out for turn, out in zip(turns, outs)]

    def copies(n, k, b):
        skip = levels - held[n].shape[0]
        for level in range(skip, levels):
            yield pltpu.make_async_copy(boxes_ref.at[level, b], held[n].at[level - skip, k], sems.at[n, level, k])

    for n, k, slot in places:
        b = table[slot]

        @pl.when(b >= 0)
        def _():
            for copy in copies(n, k, b):
                copy.start()

        @pl.when(b < 0)
        def _():
            for level in range(held[n].shape[0]):
                held[n][level, k] = jnp.zeros(held[n].shape[2:], jnp.float32)

    for n, k, slot in places:
        b = table[slot]

        @pl.when(b >= 0)
        def _():
            for copy in copies(n, k, b):
                copy.wait()

    for n, turn in enumerate(turns):
        if turn == 0:
            settled = pltpu.make_async_copy(held[n], outs[n].at[:, pl.ds(2 * own, 2)], in_sem)
            settled.start()
            settled.wait()


def pack_later(turns, boxes, move_dest, box_count):
    levels, per_device = boxes.shape[:2]
    item = boxes.shape[2:]
    hbm, vmem = pl.BlockSpec(memory_space=pltpu.HBM), pl.BlockSpec(memory_space=pltpu.VMEM)
    size = int(np.prod(item)) * 4
    shapes = [(levels - 1, 2) + item if turn else (levels, 2 * box_count) + item for turn in turns]
    return pl.pallas_call(
        functools.partial(later_kernel, turns, per_device, box_count, levels),
        out_shape=[jax.ShapeDtypeStruct(shape, jnp.float32) for shape in shapes],
        in_specs=[hbm] * 2,
        out_specs=[vmem if turn else hbm for turn in turns],
        scratch_shapes=[
            pltpu.SMEM(move_dest.shape, jnp.int32),
            pltpu.SMEM((2 * box_count,), jnp.int32),
            pltpu.SemaphoreType.DMA((len(turns), levels, 2)),
            pltpu.SemaphoreType.DMA,
        ]
        + [pltpu.VMEM((levels, 2) + item, jnp.float32) for turn in turns if turn == 0],
        cost_estimate=pl.CostEstimate(
            flops=0, bytes_accessed=4 * len(turns) * levels * size, transcendentals=0
        ),
    )(move_dest, boxes)


def settle_later(piece, turn, moved_ref, sem):
    source = source_of(lax.axis_index("box"), turn, moved_ref.shape[1] // 2)
    to = moved_ref.at[pl.ds(1, moved_ref.shape[0] - 1), pl.ds(2 * source, 2)]
    return pltpu.make_async_copy(piece, to, sem)


def settle_kernel(turns, *refs):
    out_ref, sems = refs[-2:]
    copies = [settle_later(refs[n], turn, out_ref, sems.at[n]) for n, turn in enumerate(turns)]
    for copy in copies:
        copy.start()
    for copy in copies:
        copy.wait()


def settle(turns, pieces, moved, after):
    count = len(pieces)
    vmem, hbm = pl.BlockSpec(memory_space=pltpu.VMEM), pl.BlockSpec(memory_space=pltpu.HBM)
    return pl.pallas_call(
        functools.partial(settle_kernel, turns),
        out_shape=jax.ShapeDtypeStruct(moved.shape, jnp.float32),
        in_specs=[vmem] * count + [hbm, vmem],
        out_specs=hbm,
        scratch_shapes=[pltpu.SemaphoreType.DMA((count,))],
        input_output_aliases={count: 0},
        compiler_params=pltpu.CompilerParams(vmem_limit_bytes=48 * 2 ** 20),
        cost_estimate=pl.CostEstimate(
            flops=0, bytes_accessed=8 * count * pieces[0].size, transcendentals=0
        ),
    )(*pieces, moved, after)


def arrive_kernel(box_count, slabs, fields, *refs):
    pieces = refs[:box_count]
    now_ref, moved_ref, *edges, own_rows, sems, own_sem = refs[box_count + 1 :]
    own, slab = lax.axis_index("box"), lax.axis_index("slab")
    planes, cross = now_ref.shape[2:]
    faces = pl.ds(2 * fields, own_rows.shape[0])
    mine = [pltpu.make_async_copy(pieces[0].at[faces], own_rows, own_sem)]
    copies = []
    for turn in range(box_count):
        source = source_of(own, turn, box_count)
        for k in range(2):
            box = pieces[turn].at[pl.ds(k * fields, fields)]
            if turn:
                copies.append(pltpu.make_async_copy(box, moved_ref.at[0, 2 * source + k], sems.at[turn, k]))
            else:
                mine.append(pltpu.make_async_copy(box, now_ref.at[2 * own + k, pl.ds(0, fields)], sems.at[0, k]))
    for copy in mine + copies:
        copy.start()
    faced = [jnp.where(slab == 0, planes - 1, 0)] if slabs == 2 else [0, planes - 1]

    def place_rows(rows_ref, first_block, source):
        for k in range(2):
            for f in range(ROWS):
                values = jnp.zeros((1, cross), jnp.float32)
                if f < fields:
                    block, row = divmod(k * fields + f, planes)
                    values = rows_ref[first_block + block, row : row + 1]
                now_ref[2 * source + k, fields + f // planes, f % planes : f % planes + 1] = values
            for edge_ref, plane in zip(edges, faced):
                for f in range(fields):
                    edge_ref[pl.ds((2 * source + k) * fields + f, 1)] = now_ref[2 * source + k, f, pl.ds(plane, 1)]

    for turn in range(1, box_count):
        source = source_of(own, turn, box_count)
        for k in range(2):
            now_ref[2 * source + k, :fields] = pieces[turn][k * fields : (k + 1) * fields]
        place_rows(pieces[turn], 2 * fields, source)
    for copy in mine:
        copy.wait()
    place_rows(own_rows, 0, own)
    for copy in copies:
        copy.wait()


def arrive(pieces, moved, slabs):
    box_count = len(pieces)
    _, planes, cross = pieces[0].shape
    fields = moved.shape[2]
    slots = 2 * box_count
    sides = 1 if slabs == 2 else 2
    vmem, hbm = pl.BlockSpec(memory_space=pltpu.VMEM), pl.BlockSpec(memory_space=pltpu.HBM)
    shapes = [(slots, fields + ROWS // planes, planes, cross), moved.shape] + [(slots * fields, cross)] * sides
    return pl.pallas_call(
        functools.partial(arrive_kernel, box_count, slabs, fields),
        out_shape=[jax.ShapeDtypeStruct(shape, jnp.float32) for shape in shapes],
        in_specs=[hbm] + [vmem] * (box_count - 1) + [hbm],
        out_specs=[vmem, hbm] + [vmem] * sides,
        scratch_shapes=[
            pltpu.VMEM((2 * fields // planes, planes, cross), jnp.float32),
            pltpu.SemaphoreType.DMA((box_count, 2)),
            pltpu.SemaphoreType.DMA,
        ],
        input_output_aliases={box_count: 1},
        compiler_params=pltpu.CompilerParams(vmem_limit_bytes=48 * 2 ** 20),
        cost_estimate=pl.CostEstimate(
            flops=0, bytes_accessed=12 * box_count * pieces[0].size, transcendentals=0
        ),
    )(*pieces, moved)


def face_cells(lane, edge, coarse_planes, slab):
    half, side = edge // 2, edge // 2 + 2
    plane, m = lane // (4 * half), lane % half + 1
    which = (lane // half) % 4
    rim = jnp.where(which == 0, m, jnp.where(which == 1, (side - 1) * side + m, m * side))
    rim = jnp.where(which == 3, rim + side - 1, rim) + (slab * coarse_planes + plane + 1) * side * side
    t = lane - 4 * half * coarse_planes
    x_rim = jnp.where(slab > 0, (side - 1) * side * side, 0) + (t // half + 1) * side + m
    return jnp.where(t < 0, rim, jnp.where(t < half * half, x_rim, -1))


def expand_table(coarse_planes, edge, lanes):
    half = edge // 2
    cross = edge * edge
    spread = np.zeros((lanes, (2 * coarse_planes + 1) * cross), np.float32)
    for c in range(coarse_planes):
        base = c * 4 * half
        forward, backward = 2 * c * cross, (2 * c + 1) * cross
        for m in range(edge):
            spread[base + m // 2, backward + m] += 1
            spread[base + half + m // 2, forward + (edge - 1) * edge + m] += 1
            spread[base + 2 * half + m // 2, backward + m * edge] += 1
            spread[base + 3 * half + m // 2, forward + m * edge + edge - 1] += 1
    base, to = coarse_planes * 4 * half, 2 * coarse_planes * cross
    for y in range(edge):
        for z in range(edge):
            spread[base + (y // 2) * half + z // 2, to + y * edge + z] = 1
    return spread


def slope_columns(fields, planes, coarse_planes):
    column_field, forward, backward, centre = [], [], [], []
    p = np.arange(planes)

    def add(field, f, b, c):
        column_field.append(field)
        forward.append(f * np.ones(planes))
        backward.append(b * np.ones(planes))
        centre.append(c * np.ones(planes))

    for f, b, c in ((1, 0, 0), (0, 1, 0), (0, 0, 1)):
        for g in range(2 * fields):
            for q in range(planes):
                here = p == q
                add(g, f * here + c * (p + 1 == q), b * here + c * (p - 1 == q), c * here)
    rows = [g if g < fields else -1 for g in range(ROWS)]
    rows += [fields + g if g < fields else -1 for g in range(ROWS)]
    for g in rows:
        add(g, 0, p == 0, 0)
    for g in rows:
        add(g, p == planes - 1, 0, 0)
    for c in range(coarse_planes):
        for g in rows:
            add(g, p // 2 == c, 0, 0)
        for g in rows:
            add(g, 0, p // 2 == c, 0)
    width = round_up(len(column_field), 128)
    select = np.zeros((2 * fields, width), np.float32)
    masks = np.zeros((3, planes, width), np.float32)
    for k, g in enumerate(column_field):
        if g >= 0:
            select[g, k] = 1
        masks[0, :, k], masks[1, :, k], masks[2, :, k] = forward[k], backward[k], centre[k]
    return select, masks


def expand_faces(slots_ref, fields, spread_ref, out_ref):
    slots, _, planes, cross = slots_ref.shape
    for slot in range(slots):
        for block in range(ROWS // planes):
            at = slot * ROWS + block * planes
            out_ref[at : at + planes, :cross] = slots_ref[slot, fields + block]
    both = jnp.dot(split_two(out_ref[:, :cross]), spread_ref[...], preferred_element_type=jnp.float32)
    out_ref[...] = both[: slots * ROWS] + both[slots * ROWS :]


def own_ghosts(now, fields, spread):
    vmem = pl.BlockSpec(memory_space=pltpu.VMEM)
    shape = (now.shape[0] * ROWS, spread.shape[1])

    def kernel(now_ref, spread_ref, out_ref):
        expand_faces(now_ref, fields, spread_ref, out_ref)

    return pl.pallas_call(
        kernel,
        out_shape=jax.ShapeDtypeStruct(shape, jnp.float32),
        in_specs=[vmem] * 2,
        out_specs=vmem,
        compiler_params=pltpu.CompilerParams(vmem_limit_bytes=48 * 2 ** 20),
        cost_estimate=pl.CostEstimate(
            flops=4 * shape[0] * spread.size, bytes_accessed=4 * shape[0] * shape[1], transcendentals=0
        ),
    )(now, spread)


def slope_kernel(
    edge, planes, fields, coarse_planes, per_device, total, coarse_count, slots, slabs,
    dest_ref, parent_ref, own_ref, other_ref, own_low, other_low, own_high, other_high,
    own_rim, spread_ref, weight_ref, out_ref, token_ref, stack, parts, other_rim, staged, table, count, sems,
):
    cross = edge * edge
    rows = fields * planes
    own, slab = lax.axis_index("box"), lax.axis_index("slab")

    token_ref[...] = jnp.zeros_like(token_ref)
    stack[...] = jnp.zeros_like(stack)
    half = weight_ref.shape[0]
    weights = weight_ref[...]
    parts[:half] = weights.astype(jnp.bfloat16)
    parts[half:] = (weights - weights.astype(jnp.bfloat16).astype(jnp.float32)).astype(jnp.bfloat16)
    for slot in range(slots):
        table[slot] = -1
        count[slot] = 0

    def place(b, carry):
        @pl.when(dest_ref[b] == own)
        def _():
            slot = 2 * (b // per_device)
            owner = parent_ref[b] // coarse_count
            table[jnp.where(table[slot] >= 0, slot + 1, slot)] = 2 * owner + count[owner]
            count[owner] = count[owner] + 1

        return carry

    lax.fori_loop(0, total, place, 0)
    expand_faces(other_ref, fields, spread_ref, other_rim)

    def write(step):
        return pltpu.make_async_copy(staged.at[step], out_ref.at[step], sems.at[step])

    def one_slot(step, carry):
        face = table[step]

        @pl.when(face < 0)
        def _():
            staged[step] = jnp.zeros(staged.shape[1:], jnp.float32)

        @pl.when(face >= 0)
        def _():
            lane = lax.broadcasted_iota(jnp.int32, (1, cross), 1)
            y, z = lane // edge, lane % edge
            for n, ref in enumerate((own_ref, other_ref)):
                at = (4 + n) * rows
                if planes % 8:
                    for f in range(fields):
                        stack[at + f * planes : at + (f + 1) * planes] = ref[step, f]
                else:
                    stack[at : at + rows] = ref[step, :fields].reshape(rows, cross)
            cells = stack[4 * rows : 6 * rows]
            stack[0 : 2 * rows] = jnp.where(y < edge - 1, pltpu.roll(cells, cross - edge, 1), 0.0) + jnp.where(
                z < edge - 1, pltpu.roll(cells, cross - 1, 1), 0.0
            )
            stack[2 * rows : 4 * rows] = jnp.where(y > 0, pltpu.roll(cells, edge, 1), 0.0) + jnp.where(
                z > 0, pltpu.roll(cells, 1, 1), 0.0
            )
            here = pl.ds(pl.multiple_of(ROWS * face, ROWS), ROWS)
            rim = jnp.concatenate([own_rim[here], other_rim[here]], axis=0)
            base = 6 * rows
            x_face = rim[:, 2 * coarse_planes * cross :]
            stack[base : base + 2 * ROWS] = x_face
            stack[base + 2 * ROWS : base + 4 * ROWS] = x_face

            def set_halo(at, refs):
                for n, ref in enumerate(refs):
                    for f in range(fields):
                        row = at + n * ROWS + f
                        stack[row : row + 1] = ref[pl.ds(step * fields + f, 1)]

            @pl.when(slab > 0)
            def _():
                set_halo(6 * rows, (own_low, other_low))

            @pl.when(slab < slabs - 1)
            def _():
                set_halo(6 * rows + 2 * ROWS, (own_high, other_high))

            base += 4 * ROWS
            for n in range(2 * coarse_planes):
                stack[base + 2 * ROWS * n : base + 2 * ROWS * (n + 1)] = rim[:, n * cross : (n + 1) * cross]
            values = stack[...]
            high = values.astype(jnp.bfloat16)
            low = (values - high.astype(jnp.float32)).astype(jnp.bfloat16)
            half = weight_ref.shape[0]
            both = jnp.dot(parts[...], high, preferred_element_type=jnp.float32)
            mixed = jnp.dot(parts[:half], low, preferred_element_type=jnp.float32)
            mixed = both[:half] + (both[half:] + mixed)
            if planes % 8:
                for f in range(fields):
                    staged[step, f] = mixed[f * planes : (f + 1) * planes]
            else:
                staged[step] = mixed[:rows].reshape(fields, planes, cross)

        write(step).start()
        return carry

    lax.fori_loop(0, slots, one_slot, 0)
    for step in range(slots):
        write(step).wait()


def mixing_weights(mixes, group, fields, planes, coarse_planes):
    lap_mix, grad_mix, damp_mix = mixes
    select, masks = slope_columns(fields, planes, coarse_planes)
    terms = jnp.stack([lap_mix + 0.5 * grad_mix, lap_mix - 0.5 * grad_mix, damp_mix - 6.0 * lap_mix])
    terms = lax.dynamic_slice_in_dim(terms, group * fields, fields, 1)
    terms = jnp.where(group == 0, terms, jnp.roll(terms, fields, axis=2))
    terms = jnp.einsum("tfg,gk->tfk", terms, jnp.asarray(select), precision=HIGHEST)
    weight = jnp.sum(terms[:, :, None, :] * jnp.asarray(masks)[:, None], axis=0).reshape(fields * planes, -1)
    return jnp.pad(weight, ((0, round_up(fields * planes, 16) - fields * planes), (0, 0)))


def body(boxes, move_dest, parent, coarse, lap_mix, grad_mix, damp_mix):
    box_count = lax.axis_size("box")
    slabs = lax.axis_size("slab")
    group = lax.axis_index("fld")
    levels, per_device, fields, planes, cross = boxes.shape
    edge = planes * slabs
    coarse_planes = planes // 2
    slots = 2 * box_count
    total = move_dest.shape[0]
    coarse_count = coarse.shape[0]

    def send(piece, turn):
        return lax.ppermute(piece, "box", [(s, (s + turn) % box_count) for s in range(box_count)])

    near = pack_later((1, box_count - 1), boxes, move_dest, box_count)
    near = [send(near[0], 1), send(near[1], box_count - 1)]
    first = pack_first(boxes, coarse, move_dest, parent, edge, box_count)
    arrived = [first[0]] + [send(first[turn], turn) for turn in range(1, box_count)]
    moved, *middle = pack_later((0,) + tuple(range(2, box_count - 1)), boxes, move_dest, box_count)
    middle = [send(piece, n + 2) for n, piece in enumerate(middle)]
    now, moved, *facing = arrive(arrived, moved, slabs)

    swap = [(0, 1), (1, 0)]
    now_other = lax.ppermute(now, "fld", swap)

    spread = jnp.asarray(expand_table(coarse_planes, edge, cross)).astype(jnp.bfloat16)
    rim = own_ghosts(now, fields, spread)

    def shifted(values, up):
        pairs = [(s, s + 1) if up else (s + 1, s) for s in range(slabs - 1)]
        return lax.ppermute(values, "slab", swap if slabs == 2 else pairs)

    low = shifted(facing[-1], True)
    low, rim = lax.optimization_barrier((low, rim))
    low = low, lax.ppermute(low, "fld", swap)
    high = low
    if slabs != 2:
        high = shifted(facing[0], False)
        high = high, lax.ppermute(high, "fld", swap)

    weight = mixing_weights((lap_mix, grad_mix, damp_mix), group, fields, planes, coarse_planes)
    smem, vmem = pl.BlockSpec(memory_space=pltpu.SMEM), pl.BlockSpec(memory_space=pltpu.VMEM)
    slope, token = pl.pallas_call(
        functools.partial(
            slope_kernel, edge, planes, fields, coarse_planes, per_device, total, coarse_count, slots, slabs
        ),
        out_shape=[
            jax.ShapeDtypeStruct((slots, fields, planes, cross), jnp.float32),
            jax.ShapeDtypeStruct((8, 128), jnp.float32),
        ],
        in_specs=[smem, smem] + [vmem] * 9,
        out_specs=[pl.BlockSpec(memory_space=pltpu.HBM), vmem],
        scratch_shapes=[
            pltpu.VMEM((weight.shape[1], cross), jnp.float32),
            pltpu.VMEM((2 * weight.shape[0], weight.shape[1]), jnp.bfloat16),
            pltpu.VMEM((ROWS * slots, spread.shape[1]), jnp.float32),
            pltpu.VMEM((slots, fields, planes, cross), jnp.float32),
            pltpu.SMEM((slots,), jnp.int32),
            pltpu.SMEM((slots,), jnp.int32),
            pltpu.SemaphoreType.DMA((slots,)),
        ],
        compiler_params=pltpu.CompilerParams(vmem_limit_bytes=48 * 2 ** 20),
        cost_estimate=pl.CostEstimate(
            flops=3 * slots * weight.size * cross, bytes_accessed=12 * now.size, transcendentals=0
        ),
    )(move_dest, parent, now, now_other, low[0], low[1], high[0], high[1], rim, spread, weight)
    later_arrived = [near[0]] + middle + [near[1]]
    return settle(tuple(range(1, box_count)), later_arrived, moved, token), slope


def solution(mesh):
    placed = (
        P(None, ("runs", "box"), "fld", "slab", None),
        P("runs"),
        P("runs"),
        P(("runs", "box"), "fld", None),
        P(),
        P(),
        P(),
    )
    return jax.shard_map(
        body,
        mesh=mesh,
        in_specs=placed,
        out_specs=(
            P(None, ("runs", "box"), "fld", "slab", None),
            P(("runs", "box"), "fld", "slab", None),
        ),
        check_vma=False,
    )
```

```python
import functools

import jax
import jax.numpy as jnp
import numpy as np
from jax import lax
from jax.experimental import pallas as pl
from jax.experimental.pallas import tpu as pltpu
from jax.sharding import PartitionSpec as P

HIGHEST = lax.Precision.HIGHEST
ROWS = 16


def round_up(value, unit):
    return -(-value // unit) * unit


def split_two(values):
    high = values.astype(jnp.bfloat16)
    low = (values - high.astype(jnp.float32)).astype(jnp.bfloat16)
    return jnp.concatenate([high, low], axis=0)


def place_boxes(per_device, box_count, dest_ref, table):
    own = lax.axis_index("box")
    for slot in range(2 * box_count):
        table[slot] = -1

    def place(b, carry):
        slot = 2 * dest_ref[own * per_device + b]
        table[jnp.where(table[slot] >= 0, slot + 1, slot)] = b
        return carry

    lax.fori_loop(0, per_device, place, 0)


def target_of(own, turn, box_count):
    return lax.rem(own + turn, box_count)


def source_of(own, turn, box_count):
    return lax.rem(own - turn + box_count, box_count)


def each_slot(box_count):
    own = lax.axis_index("box")
    for turn in range(box_count):
        for k in range(2):
            yield turn, k, 2 * target_of(own, turn, box_count) + k


def first_kernel(per_device, box_count, edge, dest_ref, parent_ref, boxes_ref, coarse_ref, *refs):
    outs, (boxes, zeros, shells, chosen, rows, dest, parent, box_table, face_table, sems, row_sems, in_sems) = (
        refs[:box_count], refs[box_count:]
    )
    fields, coarse_count, cells = coarse_ref.shape
    planes, cross = outs[0].shape[1:]
    own, slab = lax.axis_index("box"), lax.axis_index("slab")
    fetches = [
        pltpu.make_async_copy(dest_ref, dest, in_sems.at[0]),
        pltpu.make_async_copy(boxes_ref.at[0], boxes, in_sems.at[1]),
        pltpu.make_async_copy(parent_ref, parent, in_sems.at[2]),
        pltpu.make_async_copy(coarse_ref, shells, in_sems.at[3]),
    ]
    for fetch in fetches:
        fetch.start()
    zeros[...] = jnp.zeros_like(zeros)
    index = face_cells(lax.broadcasted_iota(jnp.int32, (1, cross), 1), edge, planes // 2, slab)
    cell = lax.broadcasted_iota(jnp.int32, (cells, cross), 0)
    one_hot = (cell == index).astype(jnp.float32).astype(jnp.bfloat16)
    fetches[0].wait()
    place_boxes(per_device, box_count, dest, box_table)
    fetches[1].wait()

    def copy(shift, k, values):
        return pltpu.make_async_copy(values, outs[shift].at[pl.ds(k * fields, fields)], sems.at[shift, k])

    for shift, k, slot in each_slot(box_count):
        b = box_table[slot]

        @pl.when(b >= 0)
        def _():
            copy(shift, k, boxes.at[b]).start()

        @pl.when(b < 0)
        def _():
            copy(shift, k, zeros).start()

    for slot in range(2 * box_count):
        face_table[slot] = -1
    fetches[2].wait()

    def place(b, carry):
        slot = 2 * dest[b]
        local = parent[b] - own * coarse_count

        @pl.when(jnp.logical_and(local >= 0, local < coarse_count))
        def _():
            face_table[jnp.where(face_table[slot] >= 0, slot + 1, slot)] = local

        return carry

    lax.fori_loop(0, dest.shape[0], place, 0)
    fetches[3].wait()
    count = fields * coarse_count
    both = jnp.dot(split_two(shells[...].reshape(count, cells)), one_hot, preferred_element_type=jnp.float32)
    chosen[...] = (both[:count] + both[count:]).reshape(chosen.shape)
    sent = []
    for shift, k, slot in each_slot(box_count):
        local = face_table[slot]
        for f in range(fields):
            values = chosen[f, pl.ds(jnp.maximum(local, 0), 1)]
            block, row = divmod(k * fields + f, planes)
            rows[shift, block, row : row + 1] = jnp.where(local >= 0, values, 0.0)
        if k == 1:
            to = outs[shift].at[pl.ds(2 * fields, rows.shape[1])]
            sent.append(pltpu.make_async_copy(rows.at[shift], to, row_sems.at[shift]))
            sent[-1].start()
    for shift, k, slot in each_slot(box_count):
        copy(shift, k, zeros).wait()
    for rows_copy in sent:
        rows_copy.wait()


def pack_first(boxes, coarse, move_dest, parent, edge, box_count):
    per_device, fields, planes, cross = boxes.shape[1:]
    coarse = jnp.transpose(coarse, (1, 0, 2))
    hbm = pl.BlockSpec(memory_space=pltpu.HBM)
    face_blocks = 2 * fields // planes
    item = (2 * fields + face_blocks, planes, cross)
    return pl.pallas_call(
        functools.partial(first_kernel, per_device, box_count, edge),
        out_shape=[jax.ShapeDtypeStruct(item, jnp.float32)] * box_count,
        in_specs=[hbm] * 4,
        out_specs=[hbm] * box_count,
        scratch_shapes=[
            pltpu.VMEM(boxes.shape[1:], jnp.float32),
            pltpu.VMEM(boxes.shape[2:], jnp.float32),
            pltpu.VMEM(coarse.shape, jnp.float32),
            pltpu.VMEM(coarse.shape[:2] + (cross,), jnp.float32),
            pltpu.VMEM((box_count, face_blocks, planes, cross), jnp.float32),
            pltpu.SMEM(move_dest.shape, jnp.int32),
            pltpu.SMEM(parent.shape, jnp.int32),
            pltpu.SMEM((2 * box_count,), jnp.int32),
            pltpu.SMEM((2 * box_count,), jnp.int32),
            pltpu.SemaphoreType.DMA((box_count, 2)),
            pltpu.SemaphoreType.DMA((box_count,)),
            pltpu.SemaphoreType.DMA((4,)),
        ],
        cost_estimate=pl.CostEstimate(
            flops=6 * coarse.size * cross, bytes_accessed=4 * (coarse.size + 2 * boxes.size), transcendentals=0
        ),
    )(move_dest, parent, boxes, coarse)


def later_kernel(turns, per_device, box_count, levels, dest_ref, boxes_ref, *refs):
    outs, (dest, table, sems, in_sem, *stay) = refs[: len(turns)], refs[len(turns) :]
    own = lax.axis_index("box")
    fetch = pltpu.make_async_copy(dest_ref, dest, in_sem)
    fetch.start()
    fetch.wait()
    place_boxes(per_device, box_count, dest, table)
    places = [(n, k, 2 * target_of(own, turn, box_count) + k) for n, turn in enumerate(turns) for k in range(2)]
    held = [stay[0] if turn == 0 else out for turn, out in zip(turns, outs)]

    def copies(n, k, b):
        skip = levels - held[n].shape[0]
        for level in range(skip, levels):
            yield pltpu.make_async_copy(boxes_ref.at[level, b], held[n].at[level - skip, k], sems.at[n, level, k])

    for n, k, slot in places:
        b = table[slot]

        @pl.when(b >= 0)
        def _():
            for copy in copies(n, k, b):
                copy.start()

        @pl.when(b < 0)
        def _():
            for level in range(held[n].shape[0]):
                held[n][level, k] = jnp.zeros(held[n].shape[2:], jnp.float32)

    for n, k, slot in places:
        b = table[slot]

        @pl.when(b >= 0)
        def _():
            for copy in copies(n, k, b):
                copy.wait()

    for n, turn in enumerate(turns):
        if turn == 0:
            settled = pltpu.make_async_copy(held[n], outs[n].at[:, pl.ds(2 * own, 2)], in_sem)
            settled.start()
            settled.wait()


def pack_later(turns, boxes, move_dest, box_count):
    levels, per_device = boxes.shape[:2]
    item = boxes.shape[2:]
    hbm, vmem = pl.BlockSpec(memory_space=pltpu.HBM), pl.BlockSpec(memory_space=pltpu.VMEM)
    size = int(np.prod(item)) * 4
    shapes = [(levels - 1, 2) + item if turn else (levels, 2 * box_count) + item for turn in turns]
    return pl.pallas_call(
        functools.partial(later_kernel, turns, per_device, box_count, levels),
        out_shape=[jax.ShapeDtypeStruct(shape, jnp.float32) for shape in shapes],
        in_specs=[hbm] * 2,
        out_specs=[vmem if turn else hbm for turn in turns],
        scratch_shapes=[
            pltpu.SMEM(move_dest.shape, jnp.int32),
            pltpu.SMEM((2 * box_count,), jnp.int32),
            pltpu.SemaphoreType.DMA((len(turns), levels, 2)),
            pltpu.SemaphoreType.DMA,
        ]
        + [pltpu.VMEM((levels, 2) + item, jnp.float32) for turn in turns if turn == 0],
        cost_estimate=pl.CostEstimate(
            flops=0, bytes_accessed=4 * len(turns) * levels * size, transcendentals=0
        ),
    )(move_dest, boxes)


def settle_later(piece, turn, moved_ref, sem):
    source = source_of(lax.axis_index("box"), turn, moved_ref.shape[1] // 2)
    to = moved_ref.at[pl.ds(1, moved_ref.shape[0] - 1), pl.ds(2 * source, 2)]
    return pltpu.make_async_copy(piece, to, sem)


def settle_kernel(turns, *refs):
    out_ref, sems = refs[-2:]
    copies = [settle_later(refs[n], turn, out_ref, sems.at[n]) for n, turn in enumerate(turns)]
    for copy in copies:
        copy.start()
    for copy in copies:
        copy.wait()


def settle(turns, pieces, moved, after):
    count = len(pieces)
    vmem, hbm = pl.BlockSpec(memory_space=pltpu.VMEM), pl.BlockSpec(memory_space=pltpu.HBM)
    return pl.pallas_call(
        functools.partial(settle_kernel, turns),
        out_shape=jax.ShapeDtypeStruct(moved.shape, jnp.float32),
        in_specs=[vmem] * count + [hbm, vmem],
        out_specs=hbm,
        scratch_shapes=[pltpu.SemaphoreType.DMA((count,))],
        input_output_aliases={count: 0},
        compiler_params=pltpu.CompilerParams(vmem_limit_bytes=48 * 2 ** 20),
        cost_estimate=pl.CostEstimate(
            flops=0, bytes_accessed=8 * count * pieces[0].size, transcendentals=0
        ),
    )(*pieces, moved, after)


def arrive_kernel(box_count, slabs, fields, *refs):
    pieces = refs[:box_count]
    now_ref, moved_ref, *edges, own_rows, sems, own_sem = refs[box_count + 1 :]
    own, slab = lax.axis_index("box"), lax.axis_index("slab")
    planes, cross = now_ref.shape[2:]
    faces = pl.ds(2 * fields, own_rows.shape[0])
    mine = [pltpu.make_async_copy(pieces[0].at[faces], own_rows, own_sem)]
    copies = []
    for turn in range(box_count):
        source = source_of(own, turn, box_count)
        for k in range(2):
            box = pieces[turn].at[pl.ds(k * fields, fields)]
            if turn:
                copies.append(pltpu.make_async_copy(box, moved_ref.at[0, 2 * source + k], sems.at[turn, k]))
            else:
                mine.append(pltpu.make_async_copy(box, now_ref.at[2 * own + k, pl.ds(0, fields)], sems.at[0, k]))
    for copy in mine + copies:
        copy.start()
    faced = [jnp.where(slab == 0, planes - 1, 0)] if slabs == 2 else [0, planes - 1]

    def place_rows(rows_ref, first_block, source):
        for k in range(2):
            for f in range(ROWS):
                values = jnp.zeros((1, cross), jnp.float32)
                if f < fields:
                    block, row = divmod(k * fields + f, planes)
                    values = rows_ref[first_block + block, row : row + 1]
                now_ref[2 * source + k, fields + f // planes, f % planes : f % planes + 1] = values
            for edge_ref, plane in zip(edges, faced):
                for f in range(fields):
                    edge_ref[pl.ds((2 * source + k) * fields + f, 1)] = now_ref[2 * source + k, f, pl.ds(plane, 1)]

    for turn in range(1, box_count):
        source = source_of(own, turn, box_count)
        for k in range(2):
            now_ref[2 * source + k, :fields] = pieces[turn][k * fields : (k + 1) * fields]
        place_rows(pieces[turn], 2 * fields, source)
    for copy in mine:
        copy.wait()
    place_rows(own_rows, 0, own)
    for copy in copies:
        copy.wait()


def arrive(pieces, moved, slabs):
    box_count = len(pieces)
    _, planes, cross = pieces[0].shape
    fields = moved.shape[2]
    slots = 2 * box_count
    sides = 1 if slabs == 2 else 2
    vmem, hbm = pl.BlockSpec(memory_space=pltpu.VMEM), pl.BlockSpec(memory_space=pltpu.HBM)
    shapes = [(slots, fields + ROWS // planes, planes, cross), moved.shape] + [(slots * fields, cross)] * sides
    return pl.pallas_call(
        functools.partial(arrive_kernel, box_count, slabs, fields),
        out_shape=[jax.ShapeDtypeStruct(shape, jnp.float32) for shape in shapes],
        in_specs=[hbm] + [vmem] * (box_count - 1) + [hbm],
        out_specs=[vmem, hbm] + [vmem] * sides,
        scratch_shapes=[
            pltpu.VMEM((2 * fields // planes, planes, cross), jnp.float32),
            pltpu.SemaphoreType.DMA((box_count, 2)),
            pltpu.SemaphoreType.DMA,
        ],
        input_output_aliases={box_count: 1},
        compiler_params=pltpu.CompilerParams(vmem_limit_bytes=48 * 2 ** 20),
        cost_estimate=pl.CostEstimate(
            flops=0, bytes_accessed=12 * box_count * pieces[0].size, transcendentals=0
        ),
    )(*pieces, moved)


def face_cells(lane, edge, coarse_planes, slab):
    half, side = edge // 2, edge // 2 + 2
    plane, m = lane // (4 * half), lane % half + 1
    which = (lane // half) % 4
    rim = jnp.where(which == 0, m, jnp.where(which == 1, (side - 1) * side + m, m * side))
    rim = jnp.where(which == 3, rim + side - 1, rim) + (slab * coarse_planes + plane + 1) * side * side
    t = lane - 4 * half * coarse_planes
    x_rim = jnp.where(slab > 0, (side - 1) * side * side, 0) + (t // half + 1) * side + m
    return jnp.where(t < 0, rim, jnp.where(t < half * half, x_rim, -1))


def expand_table(coarse_planes, edge, lanes):
    half = edge // 2
    cross = edge * edge
    spread = np.zeros((lanes, (2 * coarse_planes + 1) * cross), np.float32)
    for c in range(coarse_planes):
        base = c * 4 * half
        forward, backward = 2 * c * cross, (2 * c + 1) * cross
        for m in range(edge):
            spread[base + m // 2, backward + m] += 1
            spread[base + half + m // 2, forward + (edge - 1) * edge + m] += 1
            spread[base + 2 * half + m // 2, backward + m * edge] += 1
            spread[base + 3 * half + m // 2, forward + m * edge + edge - 1] += 1
    base, to = coarse_planes * 4 * half, 2 * coarse_planes * cross
    for y in range(edge):
        for z in range(edge):
            spread[base + (y // 2) * half + z // 2, to + y * edge + z] = 1
    return spread


def slope_columns(fields, planes, coarse_planes):
    column_field, forward, backward, centre = [], [], [], []
    p = np.arange(planes)

    def add(field, f, b, c):
        column_field.append(field)
        forward.append(f * np.ones(planes))
        backward.append(b * np.ones(planes))
        centre.append(c * np.ones(planes))

    for f, b, c in ((1, 0, 0), (0, 1, 0), (0, 0, 1)):
        for g in range(2 * fields):
            for q in range(planes):
                here = p == q
                add(g, f * here + c * (p + 1 == q), b * here + c * (p - 1 == q), c * here)
    rows = [g if g < fields else -1 for g in range(ROWS)]
    rows += [fields + g if g < fields else -1 for g in range(ROWS)]
    for g in rows:
        add(g, 0, p == 0, 0)
    for g in rows:
        add(g, p == planes - 1, 0, 0)
    for c in range(coarse_planes):
        for g in rows:
            add(g, p // 2 == c, 0, 0)
        for g in rows:
            add(g, 0, p // 2 == c, 0)
    width = round_up(len(column_field), 128)
    select = np.zeros((2 * fields, width), np.float32)
    masks = np.zeros((3, planes, width), np.float32)
    for k, g in enumerate(column_field):
        if g >= 0:
            select[g, k] = 1
        masks[0, :, k], masks[1, :, k], masks[2, :, k] = forward[k], backward[k], centre[k]
    return select, masks


def expand_faces(slots_ref, fields, spread_ref, out_ref):
    slots, _, planes, cross = slots_ref.shape
    for slot in range(slots):
        for block in range(ROWS // planes):
            at = slot * ROWS + block * planes
            out_ref[at : at + planes, :cross] = slots_ref[slot, fields + block]
    both = jnp.dot(split_two(out_ref[:, :cross]), spread_ref[...], preferred_element_type=jnp.float32)
    out_ref[...] = both[: slots * ROWS] + both[slots * ROWS :]


def own_ghosts(now, fields, spread):
    vmem = pl.BlockSpec(memory_space=pltpu.VMEM)
    shape = (now.shape[0] * ROWS, spread.shape[1])

    def kernel(now_ref, spread_ref, out_ref):
        expand_faces(now_ref, fields, spread_ref, out_ref)

    return pl.pallas_call(
        kernel,
        out_shape=jax.ShapeDtypeStruct(shape, jnp.float32),
        in_specs=[vmem] * 2,
        out_specs=vmem,
        compiler_params=pltpu.CompilerParams(vmem_limit_bytes=48 * 2 ** 20),
        cost_estimate=pl.CostEstimate(
            flops=4 * shape[0] * spread.size, bytes_accessed=4 * shape[0] * shape[1], transcendentals=0
        ),
    )(now, spread)


def slope_kernel(
    edge, planes, fields, coarse_planes, per_device, total, coarse_count, slots, slabs,
    dest_ref, parent_ref, own_ref, other_ref, own_low, other_low, own_high, other_high,
    own_rim, spread_ref, weight_ref, out_ref, token_ref, stack, parts, other_rim, staged, table, count, sems,
):
    cross = edge * edge
    rows = fields * planes
    own, slab = lax.axis_index("box"), lax.axis_index("slab")

    token_ref[...] = jnp.zeros_like(token_ref)
    stack[...] = jnp.zeros_like(stack)
    half = weight_ref.shape[0]
    weights = weight_ref[...]
    parts[:half] = weights.astype(jnp.bfloat16)
    parts[half:] = (weights - weights.astype(jnp.bfloat16).astype(jnp.float32)).astype(jnp.bfloat16)
    for slot in range(slots):
        table[slot] = -1
        count[slot] = 0

    def place(b, carry):
        @pl.when(dest_ref[b] == own)
        def _():
            slot = 2 * (b // per_device)
            owner = parent_ref[b] // coarse_count
            table[jnp.where(table[slot] >= 0, slot + 1, slot)] = 2 * owner + count[owner]
            count[owner] = count[owner] + 1

        return carry

    lax.fori_loop(0, total, place, 0)
    expand_faces(other_ref, fields, spread_ref, other_rim)

    def write(step):
        return pltpu.make_async_copy(staged.at[step], out_ref.at[step], sems.at[step])

    def one_slot(step, carry):
        face = table[step]

        @pl.when(face < 0)
        def _():
            staged[step] = jnp.zeros(staged.shape[1:], jnp.float32)

        @pl.when(face >= 0)
        def _():
            lane = lax.broadcasted_iota(jnp.int32, (1, cross), 1)
            y, z = lane // edge, lane % edge
            for n, ref in enumerate((own_ref, other_ref)):
                at = (4 + n) * rows
                if planes % 8:
                    for f in range(fields):
                        stack[at + f * planes : at + (f + 1) * planes] = ref[step, f]
                else:
                    stack[at : at + rows] = ref[step, :fields].reshape(rows, cross)
            cells = stack[4 * rows : 6 * rows]
            stack[0 : 2 * rows] = jnp.where(y < edge - 1, pltpu.roll(cells, cross - edge, 1), 0.0) + jnp.where(
                z < edge - 1, pltpu.roll(cells, cross - 1, 1), 0.0
            )
            stack[2 * rows : 4 * rows] = jnp.where(y > 0, pltpu.roll(cells, edge, 1), 0.0) + jnp.where(
                z > 0, pltpu.roll(cells, 1, 1), 0.0
            )
            here = pl.ds(pl.multiple_of(ROWS * face, ROWS), ROWS)
            rim = jnp.concatenate([own_rim[here], other_rim[here]], axis=0)
            base = 6 * rows
            x_face = rim[:, 2 * coarse_planes * cross :]
            stack[base : base + 2 * ROWS] = x_face
            stack[base + 2 * ROWS : base + 4 * ROWS] = x_face

            def set_halo(at, refs):
                for n, ref in enumerate(refs):
                    for f in range(fields):
                        row = at + n * ROWS + f
                        stack[row : row + 1] = ref[pl.ds(step * fields + f, 1)]

            @pl.when(slab > 0)
            def _():
                set_halo(6 * rows, (own_low, other_low))

            @pl.when(slab < slabs - 1)
            def _():
                set_halo(6 * rows + 2 * ROWS, (own_high, other_high))

            base += 4 * ROWS
            for n in range(2 * coarse_planes):
                stack[base + 2 * ROWS * n : base + 2 * ROWS * (n + 1)] = rim[:, n * cross : (n + 1) * cross]
            values = stack[...]
            high = values.astype(jnp.bfloat16)
            low = (values - high.astype(jnp.float32)).astype(jnp.bfloat16)
            half = weight_ref.shape[0]
            both = jnp.dot(parts[...], high, preferred_element_type=jnp.float32)
            mixed = jnp.dot(parts[:half], low, preferred_element_type=jnp.float32)
            mixed = both[:half] + (both[half:] + mixed)
            if planes % 8:
                for f in range(fields):
                    staged[step, f] = mixed[f * planes : (f + 1) * planes]
            else:
                staged[step] = mixed[:rows].reshape(fields, planes, cross)

        write(step).start()
        return carry

    lax.fori_loop(0, slots, one_slot, 0)
    for step in range(slots):
        write(step).wait()


def mixing_weights(mixes, group, fields, planes, coarse_planes):
    lap_mix, grad_mix, damp_mix = mixes
    select, masks = slope_columns(fields, planes, coarse_planes)
    terms = jnp.stack([lap_mix + 0.5 * grad_mix, lap_mix - 0.5 * grad_mix, damp_mix - 6.0 * lap_mix])
    terms = lax.dynamic_slice_in_dim(terms, group * fields, fields, 1)
    terms = jnp.where(group == 0, terms, jnp.roll(terms, fields, axis=2))
    terms = jnp.einsum("tfg,gk->tfk", terms, jnp.asarray(select), precision=HIGHEST)
    weight = jnp.sum(terms[:, :, None, :] * jnp.asarray(masks)[:, None], axis=0).reshape(fields * planes, -1)
    return jnp.pad(weight, ((0, round_up(fields * planes, 16) - fields * planes), (0, 0)))


def body(boxes, move_dest, parent, coarse, lap_mix, grad_mix, damp_mix):
    box_count = lax.axis_size("box")
    slabs = lax.axis_size("slab")
    group = lax.axis_index("fld")
    levels, per_device, fields, planes, cross = boxes.shape
    edge = planes * slabs
    coarse_planes = planes // 2
    slots = 2 * box_count
    total = move_dest.shape[0]
    coarse_count = coarse.shape[0]

    def send(piece, turn):
        return lax.ppermute(piece, "box", [(s, (s + turn) % box_count) for s in range(box_count)])

    near = pack_later((1, box_count - 1), boxes, move_dest, box_count)
    near = [send(near[0], 1), send(near[1], box_count - 1)]
    first = pack_first(boxes, coarse, move_dest, parent, edge, box_count)
    arrived = [first[0]] + [send(first[turn], turn) for turn in range(1, box_count)]
    moved, *middle = pack_later((0,) + tuple(range(2, box_count - 1)), boxes, move_dest, box_count)
    middle = [send(piece, n + 2) for n, piece in enumerate(middle)]
    now, moved, *facing = arrive(arrived, moved, slabs)

    swap = [(0, 1), (1, 0)]
    now_other = lax.ppermute(now, "fld", swap)

    spread = jnp.asarray(expand_table(coarse_planes, edge, cross)).astype(jnp.bfloat16)
    rim = own_ghosts(now, fields, spread)

    def shifted(values, up):
        pairs = [(s, s + 1) if up else (s + 1, s) for s in range(slabs - 1)]
        return lax.ppermute(values, "slab", swap if slabs == 2 else pairs)

    low = shifted(facing[-1], True)
    low, rim = lax.optimization_barrier((low, rim))
    low = low, lax.ppermute(low, "fld", swap)
    high = low
    if slabs != 2:
        high = shifted(facing[0], False)
        high = high, lax.ppermute(high, "fld", swap)

    weight = mixing_weights((lap_mix, grad_mix, damp_mix), group, fields, planes, coarse_planes)
    smem, vmem = pl.BlockSpec(memory_space=pltpu.SMEM), pl.BlockSpec(memory_space=pltpu.VMEM)
    slope, token = pl.pallas_call(
        functools.partial(
            slope_kernel, edge, planes, fields, coarse_planes, per_device, total, coarse_count, slots, slabs
        ),
        out_shape=[
            jax.ShapeDtypeStruct((slots, fields, planes, cross), jnp.float32),
            jax.ShapeDtypeStruct((8, 128), jnp.float32),
        ],
        in_specs=[smem, smem] + [vmem] * 9,
        out_specs=[pl.BlockSpec(memory_space=pltpu.HBM), vmem],
        scratch_shapes=[
            pltpu.VMEM((weight.shape[1], cross), jnp.float32),
            pltpu.VMEM((2 * weight.shape[0], weight.shape[1]), jnp.bfloat16),
            pltpu.VMEM((ROWS * slots, spread.shape[1]), jnp.float32),
            pltpu.VMEM((slots, fields, planes, cross), jnp.float32),
            pltpu.SMEM((slots,), jnp.int32),
            pltpu.SMEM((slots,), jnp.int32),
            pltpu.SemaphoreType.DMA((slots,)),
        ],
        compiler_params=pltpu.CompilerParams(vmem_limit_bytes=48 * 2 ** 20),
        cost_estimate=pl.CostEstimate(
            flops=3 * slots * weight.size * cross, bytes_accessed=12 * now.size, transcendentals=0
        ),
    )(move_dest, parent, now, now_other, low[0], low[1], high[0], high[1], rim, spread, weight)
    moved = settle(tuple(range(2, box_count - 1)), middle, moved, token)
    return settle((1, box_count - 1), near, moved, token), slope


def solution(mesh):
    placed = (
        P(None, ("runs", "box"), "fld", "slab", None),
        P("runs"),
        P("runs"),
        P(("runs", "box"), "fld", None),
        P(),
        P(),
        P(),
    )
    return jax.shard_map(
        body,
        mesh=mesh,
        in_specs=placed,
        out_specs=(
            P(None, ("runs", "box"), "fld", "slab", None),
            P(("runs", "box"), "fld", "slab", None),
        ),
        check_vma=False,
    )
```

```python
import functools

import jax
import jax.numpy as jnp
import numpy as np
from jax import lax
from jax.experimental import pallas as pl
from jax.experimental.pallas import tpu as pltpu
from jax.sharding import PartitionSpec as P

HIGHEST = lax.Precision.HIGHEST
ROWS = 16


def round_up(value, unit):
    return -(-value // unit) * unit


def split_two(values):
    high = values.astype(jnp.bfloat16)
    low = (values - high.astype(jnp.float32)).astype(jnp.bfloat16)
    return jnp.concatenate([high, low], axis=0)


def place_boxes(per_device, box_count, dest_ref, table):
    own = lax.axis_index("box")
    for slot in range(2 * box_count):
        table[slot] = -1

    def place(b, carry):
        slot = 2 * dest_ref[own * per_device + b]
        table[jnp.where(table[slot] >= 0, slot + 1, slot)] = b
        return carry

    lax.fori_loop(0, per_device, place, 0)


def target_of(own, turn, box_count):
    return lax.rem(own + turn, box_count)


def source_of(own, turn, box_count):
    return lax.rem(own - turn + box_count, box_count)


def each_slot(box_count):
    own = lax.axis_index("box")
    for turn in range(box_count):
        for k in range(2):
            yield turn, k, 2 * target_of(own, turn, box_count) + k


def first_kernel(per_device, box_count, edge, dest_ref, parent_ref, boxes_ref, coarse_ref, *refs):
    outs, (boxes, zeros, shells, chosen, rows, dest, parent, box_table, face_table, sems, row_sems, in_sems) = (
        refs[:box_count], refs[box_count:]
    )
    fields, coarse_count, cells = coarse_ref.shape
    planes, cross = outs[0].shape[1:]
    own, slab = lax.axis_index("box"), lax.axis_index("slab")
    fetches = [
        pltpu.make_async_copy(dest_ref, dest, in_sems.at[0]),
        pltpu.make_async_copy(boxes_ref.at[0], boxes, in_sems.at[1]),
        pltpu.make_async_copy(parent_ref, parent, in_sems.at[2]),
        pltpu.make_async_copy(coarse_ref, shells, in_sems.at[3]),
    ]
    for fetch in fetches:
        fetch.start()
    zeros[...] = jnp.zeros_like(zeros)
    index = face_cells(lax.broadcasted_iota(jnp.int32, (1, cross), 1), edge, planes // 2, slab)
    cell = lax.broadcasted_iota(jnp.int32, (cells, cross), 0)
    one_hot = (cell == index).astype(jnp.float32).astype(jnp.bfloat16)
    fetches[0].wait()
    place_boxes(per_device, box_count, dest, box_table)
    fetches[1].wait()

    def copy(shift, k, values):
        return pltpu.make_async_copy(values, outs[shift].at[pl.ds(k * fields, fields)], sems.at[shift, k])

    for shift, k, slot in each_slot(box_count):
        b = box_table[slot]

        @pl.when(b >= 0)
        def _():
            copy(shift, k, boxes.at[b]).start()

        @pl.when(b < 0)
        def _():
            copy(shift, k, zeros).start()

    for slot in range(2 * box_count):
        face_table[slot] = -1
    fetches[2].wait()

    def place(b, carry):
        slot = 2 * dest[b]
        local = parent[b] - own * coarse_count

        @pl.when(jnp.logical_and(local >= 0, local < coarse_count))
        def _():
            face_table[jnp.where(face_table[slot] >= 0, slot + 1, slot)] = local

        return carry

    lax.fori_loop(0, dest.shape[0], place, 0)
    fetches[3].wait()
    count = fields * coarse_count
    both = jnp.dot(split_two(shells[...].reshape(count, cells)), one_hot, preferred_element_type=jnp.float32)
    chosen[...] = (both[:count] + both[count:]).reshape(chosen.shape)
    sent = []
    for shift, k, slot in each_slot(box_count):
        local = face_table[slot]
        for f in range(fields):
            values = chosen[f, pl.ds(jnp.maximum(local, 0), 1)]
            block, row = divmod(k * fields + f, planes)
            rows[shift, block, row : row + 1] = jnp.where(local >= 0, values, 0.0)
        if k == 1:
            to = outs[shift].at[pl.ds(2 * fields, rows.shape[1])]
            sent.append(pltpu.make_async_copy(rows.at[shift], to, row_sems.at[shift]))
            sent[-1].start()
    for shift, k, slot in each_slot(box_count):
        copy(shift, k, zeros).wait()
    for rows_copy in sent:
        rows_copy.wait()


def pack_first(boxes, coarse, move_dest, parent, edge, box_count):
    per_device, fields, planes, cross = boxes.shape[1:]
    coarse = jnp.transpose(coarse, (1, 0, 2))
    hbm = pl.BlockSpec(memory_space=pltpu.HBM)
    face_blocks = 2 * fields // planes
    item = (2 * fields + face_blocks, planes, cross)
    return pl.pallas_call(
        functools.partial(first_kernel, per_device, box_count, edge),
        out_shape=[jax.ShapeDtypeStruct(item, jnp.float32)] * box_count,
        in_specs=[hbm] * 4,
        out_specs=[hbm] * box_count,
        scratch_shapes=[
            pltpu.VMEM(boxes.shape[1:], jnp.float32),
            pltpu.VMEM(boxes.shape[2:], jnp.float32),
            pltpu.VMEM(coarse.shape, jnp.float32),
            pltpu.VMEM(coarse.shape[:2] + (cross,), jnp.float32),
            pltpu.VMEM((box_count, face_blocks, planes, cross), jnp.float32),
            pltpu.SMEM(move_dest.shape, jnp.int32),
            pltpu.SMEM(parent.shape, jnp.int32),
            pltpu.SMEM((2 * box_count,), jnp.int32),
            pltpu.SMEM((2 * box_count,), jnp.int32),
            pltpu.SemaphoreType.DMA((box_count, 2)),
            pltpu.SemaphoreType.DMA((box_count,)),
            pltpu.SemaphoreType.DMA((4,)),
        ],
        cost_estimate=pl.CostEstimate(
            flops=6 * coarse.size * cross, bytes_accessed=4 * (coarse.size + 2 * boxes.size), transcendentals=0
        ),
    )(move_dest, parent, boxes, coarse)


def later_kernel(turns, per_device, box_count, levels, dest_ref, boxes_ref, *refs):
    outs, (dest, table, sems, in_sem, *stay) = refs[: len(turns)], refs[len(turns) :]
    own = lax.axis_index("box")
    fetch = pltpu.make_async_copy(dest_ref, dest, in_sem)
    fetch.start()
    fetch.wait()
    place_boxes(per_device, box_count, dest, table)
    places = [(n, k, 2 * target_of(own, turn, box_count) + k) for n, turn in enumerate(turns) for k in range(2)]
    held = [stay[0] if turn == 0 else out for turn, out in zip(turns, outs)]

    def copies(n, k, b):
        skip = levels - held[n].shape[0]
        for level in range(skip, levels):
            yield pltpu.make_async_copy(boxes_ref.at[level, b], held[n].at[level - skip, k], sems.at[n, level, k])

    for n, k, slot in places:
        b = table[slot]

        @pl.when(b >= 0)
        def _():
            for copy in copies(n, k, b):
                copy.start()

        @pl.when(b < 0)
        def _():
            for level in range(held[n].shape[0]):
                held[n][level, k] = jnp.zeros(held[n].shape[2:], jnp.float32)

    for n, k, slot in places:
        b = table[slot]

        @pl.when(b >= 0)
        def _():
            for copy in copies(n, k, b):
                copy.wait()

    for n, turn in enumerate(turns):
        if turn == 0:
            settled = pltpu.make_async_copy(held[n], outs[n].at[:, pl.ds(2 * own, 2)], in_sem)
            settled.start()
            settled.wait()


def pack_later(turns, boxes, move_dest, box_count):
    levels, per_device = boxes.shape[:2]
    item = boxes.shape[2:]
    hbm, vmem = pl.BlockSpec(memory_space=pltpu.HBM), pl.BlockSpec(memory_space=pltpu.VMEM)
    size = int(np.prod(item)) * 4
    shapes = [(levels - 1, 2) + item if turn else (levels, 2 * box_count) + item for turn in turns]
    return pl.pallas_call(
        functools.partial(later_kernel, turns, per_device, box_count, levels),
        out_shape=[jax.ShapeDtypeStruct(shape, jnp.float32) for shape in shapes],
        in_specs=[hbm] * 2,
        out_specs=[vmem if turn else hbm for turn in turns],
        scratch_shapes=[
            pltpu.SMEM(move_dest.shape, jnp.int32),
            pltpu.SMEM((2 * box_count,), jnp.int32),
            pltpu.SemaphoreType.DMA((len(turns), levels, 2)),
            pltpu.SemaphoreType.DMA,
        ]
        + [pltpu.VMEM((levels, 2) + item, jnp.float32) for turn in turns if turn == 0],
        cost_estimate=pl.CostEstimate(
            flops=0, bytes_accessed=4 * len(turns) * levels * size, transcendentals=0
        ),
    )(move_dest, boxes)


def settle_later(piece, turn, moved_ref, sem):
    source = source_of(lax.axis_index("box"), turn, moved_ref.shape[1] // 2)
    to = moved_ref.at[pl.ds(1, moved_ref.shape[0] - 1), pl.ds(2 * source, 2)]
    return pltpu.make_async_copy(piece, to, sem)


def settle_kernel(turns, *refs):
    out_ref, sems = refs[-2:]
    copies = [settle_later(refs[n], turn, out_ref, sems.at[n]) for n, turn in enumerate(turns)]
    for copy in copies:
        copy.start()
    for copy in copies:
        copy.wait()


def settle(turns, pieces, moved, after):
    count = len(pieces)
    vmem, hbm = pl.BlockSpec(memory_space=pltpu.VMEM), pl.BlockSpec(memory_space=pltpu.HBM)
    return pl.pallas_call(
        functools.partial(settle_kernel, turns),
        out_shape=jax.ShapeDtypeStruct(moved.shape, jnp.float32),
        in_specs=[vmem] * count + [hbm, vmem],
        out_specs=hbm,
        scratch_shapes=[pltpu.SemaphoreType.DMA((count,))],
        input_output_aliases={count: 0},
        compiler_params=pltpu.CompilerParams(vmem_limit_bytes=48 * 2 ** 20),
        cost_estimate=pl.CostEstimate(
            flops=0, bytes_accessed=8 * count * pieces[0].size, transcendentals=0
        ),
    )(*pieces, moved, after)


def arrive_kernel(box_count, slabs, fields, *refs):
    pieces = refs[:box_count]
    now_ref, moved_ref, *edges, own_rows, sems, own_sem = refs[box_count + 1 :]
    own, slab = lax.axis_index("box"), lax.axis_index("slab")
    planes, cross = now_ref.shape[2:]
    faces = pl.ds(2 * fields, own_rows.shape[0])
    mine = [pltpu.make_async_copy(pieces[0].at[faces], own_rows, own_sem)]
    copies = []
    for turn in range(box_count):
        source = source_of(own, turn, box_count)
        for k in range(2):
            box = pieces[turn].at[pl.ds(k * fields, fields)]
            if turn:
                copies.append(pltpu.make_async_copy(box, moved_ref.at[0, 2 * source + k], sems.at[turn, k]))
            else:
                mine.append(pltpu.make_async_copy(box, now_ref.at[2 * own + k, pl.ds(0, fields)], sems.at[0, k]))
    for copy in mine + copies:
        copy.start()
    faced = [jnp.where(slab == 0, planes - 1, 0)] if slabs == 2 else [0, planes - 1]

    def place_rows(rows_ref, first_block, source):
        for k in range(2):
            for f in range(ROWS):
                values = jnp.zeros((1, cross), jnp.float32)
                if f < fields:
                    block, row = divmod(k * fields + f, planes)
                    values = rows_ref[first_block + block, row : row + 1]
                now_ref[2 * source + k, fields + f // planes, f % planes : f % planes + 1] = values
            for edge_ref, plane in zip(edges, faced):
                for f in range(fields):
                    edge_ref[pl.ds((2 * source + k) * fields + f, 1)] = now_ref[2 * source + k, f, pl.ds(plane, 1)]

    for turn in range(1, box_count):
        source = source_of(own, turn, box_count)
        for k in range(2):
            now_ref[2 * source + k, :fields] = pieces[turn][k * fields : (k + 1) * fields]
        place_rows(pieces[turn], 2 * fields, source)
    for copy in mine:
        copy.wait()
    place_rows(own_rows, 0, own)
    for copy in copies:
        copy.wait()


def arrive(pieces, moved, slabs):
    box_count = len(pieces)
    _, planes, cross = pieces[0].shape
    fields = moved.shape[2]
    slots = 2 * box_count
    sides = 1 if slabs == 2 else 2
    vmem, hbm = pl.BlockSpec(memory_space=pltpu.VMEM), pl.BlockSpec(memory_space=pltpu.HBM)
    shapes = [(slots, fields + ROWS // planes, planes, cross), moved.shape] + [(slots * fields, cross)] * sides
    return pl.pallas_call(
        functools.partial(arrive_kernel, box_count, slabs, fields),
        out_shape=[jax.ShapeDtypeStruct(shape, jnp.float32) for shape in shapes],
        in_specs=[hbm] + [vmem] * (box_count - 1) + [hbm],
        out_specs=[vmem, hbm] + [vmem] * sides,
        scratch_shapes=[
            pltpu.VMEM((2 * fields // planes, planes, cross), jnp.float32),
            pltpu.SemaphoreType.DMA((box_count, 2)),
            pltpu.SemaphoreType.DMA,
        ],
        input_output_aliases={box_count: 1},
        compiler_params=pltpu.CompilerParams(vmem_limit_bytes=48 * 2 ** 20),
        cost_estimate=pl.CostEstimate(
            flops=0, bytes_accessed=12 * box_count * pieces[0].size, transcendentals=0
        ),
    )(*pieces, moved)


def face_cells(lane, edge, coarse_planes, slab):
    half, side = edge // 2, edge // 2 + 2
    plane, m = lane // (4 * half), lane % half + 1
    which = (lane // half) % 4
    rim = jnp.where(which == 0, m, jnp.where(which == 1, (side - 1) * side + m, m * side))
    rim = jnp.where(which == 3, rim + side - 1, rim) + (slab * coarse_planes + plane + 1) * side * side
    t = lane - 4 * half * coarse_planes
    x_rim = jnp.where(slab > 0, (side - 1) * side * side, 0) + (t // half + 1) * side + m
    return jnp.where(t < 0, rim, jnp.where(t < half * half, x_rim, -1))


def expand_table(coarse_planes, edge, lanes):
    half = edge // 2
    cross = edge * edge
    spread = np.zeros((lanes, (2 * coarse_planes + 1) * cross), np.float32)
    for c in range(coarse_planes):
        base = c * 4 * half
        forward, backward = 2 * c * cross, (2 * c + 1) * cross
        for m in range(edge):
            spread[base + m // 2, backward + m] += 1
            spread[base + half + m // 2, forward + (edge - 1) * edge + m] += 1
            spread[base + 2 * half + m // 2, backward + m * edge] += 1
            spread[base + 3 * half + m // 2, forward + m * edge + edge - 1] += 1
    base, to = coarse_planes * 4 * half, 2 * coarse_planes * cross
    for y in range(edge):
        for z in range(edge):
            spread[base + (y // 2) * half + z // 2, to + y * edge + z] = 1
    return spread


def slope_columns(fields, planes, coarse_planes):
    column_field, forward, backward, centre = [], [], [], []
    p = np.arange(planes)

    def add(field, f, b, c):
        column_field.append(field)
        forward.append(f * np.ones(planes))
        backward.append(b * np.ones(planes))
        centre.append(c * np.ones(planes))

    for f, b, c in ((1, 0, 0), (0, 1, 0), (0, 0, 1)):
        for g in range(2 * fields):
            for q in range(planes):
                here = p == q
                add(g, f * here + c * (p + 1 == q), b * here + c * (p - 1 == q), c * here)
    rows = [g if g < fields else -1 for g in range(ROWS)]
    rows += [fields + g if g < fields else -1 for g in range(ROWS)]
    for g in rows:
        add(g, 0, p == 0, 0)
    for g in rows:
        add(g, p == planes - 1, 0, 0)
    for c in range(coarse_planes):
        for g in rows:
            add(g, p // 2 == c, 0, 0)
        for g in rows:
            add(g, 0, p // 2 == c, 0)
    width = round_up(len(column_field), 128)
    select = np.zeros((2 * fields, width), np.float32)
    masks = np.zeros((3, planes, width), np.float32)
    for k, g in enumerate(column_field):
        if g >= 0:
            select[g, k] = 1
        masks[0, :, k], masks[1, :, k], masks[2, :, k] = forward[k], backward[k], centre[k]
    return select, masks


def expand_faces(slots_ref, fields, spread_ref, out_ref):
    slots, _, planes, cross = slots_ref.shape
    for slot in range(slots):
        for block in range(ROWS // planes):
            at = slot * ROWS + block * planes
            out_ref[at : at + planes, :cross] = slots_ref[slot, fields + block]
    both = jnp.dot(split_two(out_ref[:, :cross]), spread_ref[...], preferred_element_type=jnp.float32)
    out_ref[...] = both[: slots * ROWS] + both[slots * ROWS :]


def own_ghosts(now, fields, spread):
    vmem = pl.BlockSpec(memory_space=pltpu.VMEM)
    shape = (now.shape[0] * ROWS, spread.shape[1])

    def kernel(now_ref, spread_ref, out_ref):
        expand_faces(now_ref, fields, spread_ref, out_ref)

    return pl.pallas_call(
        kernel,
        out_shape=jax.ShapeDtypeStruct(shape, jnp.float32),
        in_specs=[vmem] * 2,
        out_specs=vmem,
        compiler_params=pltpu.CompilerParams(vmem_limit_bytes=48 * 2 ** 20),
        cost_estimate=pl.CostEstimate(
            flops=4 * shape[0] * spread.size, bytes_accessed=4 * shape[0] * shape[1], transcendentals=0
        ),
    )(now, spread)


def slope_kernel(
    edge, planes, fields, coarse_planes, per_device, total, coarse_count, slots, slabs,
    dest_ref, parent_ref, own_ref, other_ref, own_low, other_low, own_high, other_high,
    own_rim, spread_ref, weight_ref, out_ref, token_ref, stack, parts, other_rim, staged, table, count, sems,
):
    cross = edge * edge
    rows = fields * planes
    own, slab = lax.axis_index("box"), lax.axis_index("slab")

    token_ref[...] = jnp.zeros_like(token_ref)
    stack[...] = jnp.zeros_like(stack)
    half = weight_ref.shape[0]
    weights = weight_ref[...]
    parts[:half] = weights.astype(jnp.bfloat16)
    parts[half:] = (weights - weights.astype(jnp.bfloat16).astype(jnp.float32)).astype(jnp.bfloat16)
    for slot in range(slots):
        table[slot] = -1
        count[slot] = 0

    def place(b, carry):
        @pl.when(dest_ref[b] == own)
        def _():
            slot = 2 * (b // per_device)
            owner = parent_ref[b] // coarse_count
            table[jnp.where(table[slot] >= 0, slot + 1, slot)] = 2 * owner + count[owner]
            count[owner] = count[owner] + 1

        return carry

    lax.fori_loop(0, total, place, 0)
    expand_faces(other_ref, fields, spread_ref, other_rim)

    def write(step):
        return pltpu.make_async_copy(staged.at[step], out_ref.at[step], sems.at[step])

    def one_slot(step, carry):
        face = table[step]

        @pl.when(face < 0)
        def _():
            staged[step] = jnp.zeros(staged.shape[1:], jnp.float32)

        @pl.when(face >= 0)
        def _():
            lane = lax.broadcasted_iota(jnp.int32, (1, cross), 1)
            y, z = lane // edge, lane % edge
            for n, ref in enumerate((own_ref, other_ref)):
                at = (4 + n) * rows
                if planes % 8:
                    for f in range(fields):
                        stack[at + f * planes : at + (f + 1) * planes] = ref[step, f]
                else:
                    stack[at : at + rows] = ref[step, :fields].reshape(rows, cross)
            cells = stack[4 * rows : 6 * rows]
            stack[0 : 2 * rows] = jnp.where(y < edge - 1, pltpu.roll(cells, cross - edge, 1), 0.0) + jnp.where(
                z < edge - 1, pltpu.roll(cells, cross - 1, 1), 0.0
            )
            stack[2 * rows : 4 * rows] = jnp.where(y > 0, pltpu.roll(cells, edge, 1), 0.0) + jnp.where(
                z > 0, pltpu.roll(cells, 1, 1), 0.0
            )
            here = pl.ds(pl.multiple_of(ROWS * face, ROWS), ROWS)
            rim = jnp.concatenate([own_rim[here], other_rim[here]], axis=0)
            base = 6 * rows
            x_face = rim[:, 2 * coarse_planes * cross :]
            stack[base : base + 2 * ROWS] = x_face
            stack[base + 2 * ROWS : base + 4 * ROWS] = x_face

            def set_halo(at, refs):
                for n, ref in enumerate(refs):
                    for f in range(fields):
                        row = at + n * ROWS + f
                        stack[row : row + 1] = ref[pl.ds(step * fields + f, 1)]

            @pl.when(slab > 0)
            def _():
                set_halo(6 * rows, (own_low, other_low))

            @pl.when(slab < slabs - 1)
            def _():
                set_halo(6 * rows + 2 * ROWS, (own_high, other_high))

            base += 4 * ROWS
            for n in range(2 * coarse_planes):
                stack[base + 2 * ROWS * n : base + 2 * ROWS * (n + 1)] = rim[:, n * cross : (n + 1) * cross]
            values = stack[...]
            high = values.astype(jnp.bfloat16)
            low = (values - high.astype(jnp.float32)).astype(jnp.bfloat16)
            half = weight_ref.shape[0]
            both = jnp.dot(parts[...], high, preferred_element_type=jnp.float32)
            mixed = jnp.dot(parts[:half], low, preferred_element_type=jnp.float32)
            mixed = both[:half] + (both[half:] + mixed)
            if planes % 8:
                for f in range(fields):
                    staged[step, f] = mixed[f * planes : (f + 1) * planes]
            else:
                staged[step] = mixed[:rows].reshape(fields, planes, cross)

        write(step).start()
        return carry

    lax.fori_loop(0, slots, one_slot, 0)
    for step in range(slots):
        write(step).wait()


def mixing_weights(mixes, group, fields, planes, coarse_planes):
    lap_mix, grad_mix, damp_mix = mixes
    select, masks = slope_columns(fields, planes, coarse_planes)
    terms = jnp.stack([lap_mix + 0.5 * grad_mix, lap_mix - 0.5 * grad_mix, damp_mix - 6.0 * lap_mix])
    terms = lax.dynamic_slice_in_dim(terms, group * fields, fields, 1)
    terms = jnp.where(group == 0, terms, jnp.roll(terms, fields, axis=2))
    terms = jnp.einsum("tfg,gk->tfk", terms, jnp.asarray(select), precision=HIGHEST)
    weight = jnp.sum(terms[:, :, None, :] * jnp.asarray(masks)[:, None], axis=0).reshape(fields * planes, -1)
    return jnp.pad(weight, ((0, round_up(fields * planes, 16) - fields * planes), (0, 0)))


def body(boxes, move_dest, parent, coarse, lap_mix, grad_mix, damp_mix):
    box_count = lax.axis_size("box")
    slabs = lax.axis_size("slab")
    group = lax.axis_index("fld")
    levels, per_device, fields, planes, cross = boxes.shape
    edge = planes * slabs
    coarse_planes = planes // 2
    slots = 2 * box_count
    total = move_dest.shape[0]
    coarse_count = coarse.shape[0]

    def send(piece, turn):
        return lax.ppermute(piece, "box", [(s, (s + turn) % box_count) for s in range(box_count)])

    last = box_count - 1
    first = pack_first(boxes, coarse, move_dest, parent, edge, box_count)
    arrived = [first[0]] + [send(first[turn], turn) for turn in range(1, box_count)]
    moved, *later = pack_later((0, 1), boxes, move_dest, box_count)
    later += pack_later((last,) + tuple(range(2, last)), boxes, move_dest, box_count)
    next_one, last_one, *middle = [send(piece, turn) for piece, turn in zip(later, [1, last, *range(2, last)])]
    now, moved, *facing = arrive(arrived, moved, slabs)

    swap = [(0, 1), (1, 0)]
    now_other = lax.ppermute(now, "fld", swap)

    spread = jnp.asarray(expand_table(coarse_planes, edge, cross)).astype(jnp.bfloat16)
    rim = own_ghosts(now, fields, spread)

    def shifted(values, up):
        pairs = [(s, s + 1) if up else (s + 1, s) for s in range(slabs - 1)]
        return lax.ppermute(values, "slab", swap if slabs == 2 else pairs)

    low = shifted(facing[-1], True)
    low, rim = lax.optimization_barrier((low, rim))
    low = low, lax.ppermute(low, "fld", swap)
    high = low
    if slabs != 2:
        high = shifted(facing[0], False)
        high = high, lax.ppermute(high, "fld", swap)

    weight = mixing_weights((lap_mix, grad_mix, damp_mix), group, fields, planes, coarse_planes)
    smem, vmem = pl.BlockSpec(memory_space=pltpu.SMEM), pl.BlockSpec(memory_space=pltpu.VMEM)
    slope, token = pl.pallas_call(
        functools.partial(
            slope_kernel, edge, planes, fields, coarse_planes, per_device, total, coarse_count, slots, slabs
        ),
        out_shape=[
            jax.ShapeDtypeStruct((slots, fields, planes, cross), jnp.float32),
            jax.ShapeDtypeStruct((8, 128), jnp.float32),
        ],
        in_specs=[smem, smem] + [vmem] * 9,
        out_specs=[pl.BlockSpec(memory_space=pltpu.HBM), vmem],
        scratch_shapes=[
            pltpu.VMEM((weight.shape[1], cross), jnp.float32),
            pltpu.VMEM((2 * weight.shape[0], weight.shape[1]), jnp.bfloat16),
            pltpu.VMEM((ROWS * slots, spread.shape[1]), jnp.float32),
            pltpu.VMEM((slots, fields, planes, cross), jnp.float32),
            pltpu.SMEM((slots,), jnp.int32),
            pltpu.SMEM((slots,), jnp.int32),
            pltpu.SemaphoreType.DMA((slots,)),
        ],
        compiler_params=pltpu.CompilerParams(vmem_limit_bytes=48 * 2 ** 20),
        cost_estimate=pl.CostEstimate(
            flops=3 * slots * weight.size * cross, bytes_accessed=12 * now.size, transcendentals=0
        ),
    )(move_dest, parent, now, now_other, low[0], low[1], high[0], high[1], rim, spread, weight)
    moved = settle((1, last), [next_one, last_one], moved, token)
    return settle(tuple(range(2, last)), middle, moved, token), slope


def solution(mesh):
    placed = (
        P(None, ("runs", "box"), "fld", "slab", None),
        P("runs"),
        P("runs"),
        P(("runs", "box"), "fld", None),
        P(),
        P(),
        P(),
    )
    return jax.shard_map(
        body,
        mesh=mesh,
        in_specs=placed,
        out_specs=(
            P(None, ("runs", "box"), "fld", "slab", None),
            P(("runs", "box"), "fld", "slab", None),
        ),
        check_vma=False,
    )
```

```python
import functools

import jax
import jax.numpy as jnp
import numpy as np
from jax import lax
from jax.experimental import pallas as pl
from jax.experimental.pallas import tpu as pltpu
from jax.sharding import PartitionSpec as P

HIGHEST = lax.Precision.HIGHEST
ROWS = 16


def round_up(value, unit):
    return -(-value // unit) * unit


def split_two(values):
    high = values.astype(jnp.bfloat16)
    low = (values - high.astype(jnp.float32)).astype(jnp.bfloat16)
    return jnp.concatenate([high, low], axis=0)


def place_boxes(per_device, box_count, dest_ref, table):
    own = lax.axis_index("box")
    for slot in range(2 * box_count):
        table[slot] = -1

    def place(b, carry):
        slot = 2 * dest_ref[own * per_device + b]
        table[jnp.where(table[slot] >= 0, slot + 1, slot)] = b
        return carry

    lax.fori_loop(0, per_device, place, 0)


def target_of(own, turn, box_count):
    return lax.rem(own + turn, box_count)


def source_of(own, turn, box_count):
    return lax.rem(own - turn + box_count, box_count)


def each_slot(box_count):
    own = lax.axis_index("box")
    for turn in range(box_count):
        for k in range(2):
            yield turn, k, 2 * target_of(own, turn, box_count) + k


def first_kernel(per_device, box_count, edge, dest_ref, parent_ref, boxes_ref, coarse_ref, *refs):
    outs, (boxes, zeros, shells, chosen, rows, dest, parent, box_table, face_table, sems, row_sems, in_sems) = (
        refs[:box_count], refs[box_count:]
    )
    fields, coarse_count, cells = coarse_ref.shape
    planes, cross = outs[0].shape[1:]
    own, slab = lax.axis_index("box"), lax.axis_index("slab")
    fetches = [
        pltpu.make_async_copy(dest_ref, dest, in_sems.at[0]),
        pltpu.make_async_copy(boxes_ref.at[0], boxes, in_sems.at[1]),
        pltpu.make_async_copy(parent_ref, parent, in_sems.at[2]),
        pltpu.make_async_copy(coarse_ref, shells, in_sems.at[3]),
    ]
    for fetch in fetches:
        fetch.start()
    zeros[...] = jnp.zeros_like(zeros)
    index = face_cells(lax.broadcasted_iota(jnp.int32, (1, cross), 1), edge, planes // 2, slab)
    cell = lax.broadcasted_iota(jnp.int32, (cells, cross), 0)
    one_hot = (cell == index).astype(jnp.float32).astype(jnp.bfloat16)
    fetches[0].wait()
    place_boxes(per_device, box_count, dest, box_table)
    fetches[1].wait()

    def copy(shift, k, values):
        return pltpu.make_async_copy(values, outs[shift].at[pl.ds(k * fields, fields)], sems.at[shift, k])

    for shift, k, slot in each_slot(box_count):
        b = box_table[slot]

        @pl.when(b >= 0)
        def _():
            copy(shift, k, boxes.at[b]).start()

        @pl.when(b < 0)
        def _():
            copy(shift, k, zeros).start()

    for slot in range(2 * box_count):
        face_table[slot] = -1
    fetches[2].wait()

    def place(b, carry):
        slot = 2 * dest[b]
        local = parent[b] - own * coarse_count

        @pl.when(jnp.logical_and(local >= 0, local < coarse_count))
        def _():
            face_table[jnp.where(face_table[slot] >= 0, slot + 1, slot)] = local

        return carry

    lax.fori_loop(0, dest.shape[0], place, 0)
    fetches[3].wait()
    count = fields * coarse_count
    both = jnp.dot(split_two(shells[...].reshape(count, cells)), one_hot, preferred_element_type=jnp.float32)
    chosen[...] = (both[:count] + both[count:]).reshape(chosen.shape)
    sent = []
    for shift, k, slot in each_slot(box_count):
        local = face_table[slot]
        for f in range(fields):
            values = chosen[f, pl.ds(jnp.maximum(local, 0), 1)]
            block, row = divmod(k * fields + f, planes)
            rows[shift, block, row : row + 1] = jnp.where(local >= 0, values, 0.0)
        if k == 1:
            to = outs[shift].at[pl.ds(2 * fields, rows.shape[1])]
            sent.append(pltpu.make_async_copy(rows.at[shift], to, row_sems.at[shift]))
            sent[-1].start()
    for shift, k, slot in each_slot(box_count):
        copy(shift, k, zeros).wait()
    for rows_copy in sent:
        rows_copy.wait()


def pack_first(boxes, coarse, move_dest, parent, edge, box_count):
    per_device, fields, planes, cross = boxes.shape[1:]
    coarse = jnp.transpose(coarse, (1, 0, 2))
    hbm = pl.BlockSpec(memory_space=pltpu.HBM)
    face_blocks = 2 * fields // planes
    item = (2 * fields + face_blocks, planes, cross)
    return pl.pallas_call(
        functools.partial(first_kernel, per_device, box_count, edge),
        out_shape=[jax.ShapeDtypeStruct(item, jnp.float32)] * box_count,
        in_specs=[hbm] * 4,
        out_specs=[hbm] * box_count,
        scratch_shapes=[
            pltpu.VMEM(boxes.shape[1:], jnp.float32),
            pltpu.VMEM(boxes.shape[2:], jnp.float32),
            pltpu.VMEM(coarse.shape, jnp.float32),
            pltpu.VMEM(coarse.shape[:2] + (cross,), jnp.float32),
            pltpu.VMEM((box_count, face_blocks, planes, cross), jnp.float32),
            pltpu.SMEM(move_dest.shape, jnp.int32),
            pltpu.SMEM(parent.shape, jnp.int32),
            pltpu.SMEM((2 * box_count,), jnp.int32),
            pltpu.SMEM((2 * box_count,), jnp.int32),
            pltpu.SemaphoreType.DMA((box_count, 2)),
            pltpu.SemaphoreType.DMA((box_count,)),
            pltpu.SemaphoreType.DMA((4,)),
        ],
        cost_estimate=pl.CostEstimate(
            flops=6 * coarse.size * cross, bytes_accessed=4 * (coarse.size + 2 * boxes.size), transcendentals=0
        ),
    )(move_dest, parent, boxes, coarse)


def later_kernel(turns, per_device, box_count, levels, dest_ref, boxes_ref, *refs):
    outs, (dest, table, sems, in_sem, *stay) = refs[: len(turns)], refs[len(turns) :]
    own = lax.axis_index("box")
    fetch = pltpu.make_async_copy(dest_ref, dest, in_sem)
    fetch.start()
    fetch.wait()
    place_boxes(per_device, box_count, dest, table)
    places = [(n, k, 2 * target_of(own, turn, box_count) + k) for n, turn in enumerate(turns) for k in range(2)]
    held = [stay[0] if turn == 0 else out for turn, out in zip(turns, outs)]

    def copies(n, k, b):
        skip = levels - held[n].shape[0]
        for level in range(skip, levels):
            yield pltpu.make_async_copy(boxes_ref.at[level, b], held[n].at[level - skip, k], sems.at[n, level, k])

    for n, k, slot in places:
        b = table[slot]

        @pl.when(b >= 0)
        def _():
            for copy in copies(n, k, b):
                copy.start()

        @pl.when(b < 0)
        def _():
            for level in range(held[n].shape[0]):
                held[n][level, k] = jnp.zeros(held[n].shape[2:], jnp.float32)

    for n, k, slot in places:
        b = table[slot]

        @pl.when(b >= 0)
        def _():
            for copy in copies(n, k, b):
                copy.wait()

    for n, turn in enumerate(turns):
        if turn == 0:
            settled = pltpu.make_async_copy(held[n], outs[n].at[:, pl.ds(2 * own, 2)], in_sem)
            settled.start()
            settled.wait()


def pack_later(turns, boxes, move_dest, box_count):
    levels, per_device = boxes.shape[:2]
    item = boxes.shape[2:]
    hbm, vmem = pl.BlockSpec(memory_space=pltpu.HBM), pl.BlockSpec(memory_space=pltpu.VMEM)
    size = int(np.prod(item)) * 4
    shapes = [(levels - 1, 2) + item if turn else (levels, 2 * box_count) + item for turn in turns]
    return pl.pallas_call(
        functools.partial(later_kernel, turns, per_device, box_count, levels),
        out_shape=[jax.ShapeDtypeStruct(shape, jnp.float32) for shape in shapes],
        in_specs=[hbm] * 2,
        out_specs=[vmem if turn else hbm for turn in turns],
        scratch_shapes=[
            pltpu.SMEM(move_dest.shape, jnp.int32),
            pltpu.SMEM((2 * box_count,), jnp.int32),
            pltpu.SemaphoreType.DMA((len(turns), levels, 2)),
            pltpu.SemaphoreType.DMA,
        ]
        + [pltpu.VMEM((levels, 2) + item, jnp.float32) for turn in turns if turn == 0],
        cost_estimate=pl.CostEstimate(
            flops=0, bytes_accessed=4 * len(turns) * levels * size, transcendentals=0
        ),
    )(move_dest, boxes)


def settle_later(piece, turn, moved_ref, sem):
    source = source_of(lax.axis_index("box"), turn, moved_ref.shape[1] // 2)
    to = moved_ref.at[pl.ds(1, moved_ref.shape[0] - 1), pl.ds(2 * source, 2)]
    return pltpu.make_async_copy(piece, to, sem)


def settle_kernel(turns, *refs):
    out_ref, sems = refs[-2:]
    copies = [settle_later(refs[n], turn, out_ref, sems.at[n]) for n, turn in enumerate(turns)]
    for copy in copies:
        copy.start()
    for copy in copies:
        copy.wait()


def settle(turns, pieces, moved, after):
    count = len(pieces)
    vmem, hbm = pl.BlockSpec(memory_space=pltpu.VMEM), pl.BlockSpec(memory_space=pltpu.HBM)
    return pl.pallas_call(
        functools.partial(settle_kernel, turns),
        out_shape=jax.ShapeDtypeStruct(moved.shape, jnp.float32),
        in_specs=[vmem] * count + [hbm, vmem],
        out_specs=hbm,
        scratch_shapes=[pltpu.SemaphoreType.DMA((count,))],
        input_output_aliases={count: 0},
        compiler_params=pltpu.CompilerParams(vmem_limit_bytes=48 * 2 ** 20),
        cost_estimate=pl.CostEstimate(
            flops=0, bytes_accessed=8 * count * pieces[0].size, transcendentals=0
        ),
    )(*pieces, moved, after)


def arrive_kernel(box_count, slabs, fields, *refs):
    pieces = refs[:box_count]
    now_ref, moved_ref, *edges, own_rows, sems, own_sem = refs[box_count + 1 :]
    own, slab = lax.axis_index("box"), lax.axis_index("slab")
    planes, cross = now_ref.shape[2:]
    faces = pl.ds(2 * fields, own_rows.shape[0])
    mine = [pltpu.make_async_copy(pieces[0].at[faces], own_rows, own_sem)]
    copies = []
    for turn in range(box_count):
        source = source_of(own, turn, box_count)
        for k in range(2):
            box = pieces[turn].at[pl.ds(k * fields, fields)]
            if turn:
                copies.append(pltpu.make_async_copy(box, moved_ref.at[0, 2 * source + k], sems.at[turn, k]))
            else:
                mine.append(pltpu.make_async_copy(box, now_ref.at[2 * own + k, pl.ds(0, fields)], sems.at[0, k]))
    for copy in mine + copies:
        copy.start()
    faced = [jnp.where(slab == 0, planes - 1, 0)] if slabs == 2 else [0, planes - 1]

    def place_rows(rows_ref, first_block, source):
        for k in range(2):
            for f in range(ROWS):
                values = jnp.zeros((1, cross), jnp.float32)
                if f < fields:
                    block, row = divmod(k * fields + f, planes)
                    values = rows_ref[first_block + block, row : row + 1]
                now_ref[2 * source + k, fields + f // planes, f % planes : f % planes + 1] = values
            for edge_ref, plane in zip(edges, faced):
                for f in range(fields):
                    edge_ref[pl.ds((2 * source + k) * fields + f, 1)] = now_ref[2 * source + k, f, pl.ds(plane, 1)]

    for turn in range(1, box_count):
        source = source_of(own, turn, box_count)
        for k in range(2):
            now_ref[2 * source + k, :fields] = pieces[turn][k * fields : (k + 1) * fields]
        place_rows(pieces[turn], 2 * fields, source)
    for copy in mine:
        copy.wait()
    place_rows(own_rows, 0, own)
    for copy in copies:
        copy.wait()


def arrive(pieces, moved, slabs):
    box_count = len(pieces)
    _, planes, cross = pieces[0].shape
    fields = moved.shape[2]
    slots = 2 * box_count
    sides = 1 if slabs == 2 else 2
    vmem, hbm = pl.BlockSpec(memory_space=pltpu.VMEM), pl.BlockSpec(memory_space=pltpu.HBM)
    shapes = [(slots, fields + ROWS // planes, planes, cross), moved.shape] + [(slots * fields, cross)] * sides
    return pl.pallas_call(
        functools.partial(arrive_kernel, box_count, slabs, fields),
        out_shape=[jax.ShapeDtypeStruct(shape, jnp.float32) for shape in shapes],
        in_specs=[hbm] + [vmem] * (box_count - 1) + [hbm],
        out_specs=[vmem, hbm] + [vmem] * sides,
        scratch_shapes=[
            pltpu.VMEM((2 * fields // planes, planes, cross), jnp.float32),
            pltpu.SemaphoreType.DMA((box_count, 2)),
            pltpu.SemaphoreType.DMA,
        ],
        input_output_aliases={box_count: 1},
        compiler_params=pltpu.CompilerParams(vmem_limit_bytes=48 * 2 ** 20),
        cost_estimate=pl.CostEstimate(
            flops=0, bytes_accessed=12 * box_count * pieces[0].size, transcendentals=0
        ),
    )(*pieces, moved)


def face_cells(lane, edge, coarse_planes, slab):
    half, side = edge // 2, edge // 2 + 2
    plane, m = lane // (4 * half), lane % half + 1
    which = (lane // half) % 4
    rim = jnp.where(which == 0, m, jnp.where(which == 1, (side - 1) * side + m, m * side))
    rim = jnp.where(which == 3, rim + side - 1, rim) + (slab * coarse_planes + plane + 1) * side * side
    t = lane - 4 * half * coarse_planes
    x_rim = jnp.where(slab > 0, (side - 1) * side * side, 0) + (t // half + 1) * side + m
    return jnp.where(t < 0, rim, jnp.where(t < half * half, x_rim, -1))


def expand_table(coarse_planes, edge, lanes):
    half = edge // 2
    cross = edge * edge
    spread = np.zeros((lanes, (2 * coarse_planes + 1) * cross), np.float32)
    for c in range(coarse_planes):
        base = c * 4 * half
        forward, backward = 2 * c * cross, (2 * c + 1) * cross
        for m in range(edge):
            spread[base + m // 2, backward + m] += 1
            spread[base + half + m // 2, forward + (edge - 1) * edge + m] += 1
            spread[base + 2 * half + m // 2, backward + m * edge] += 1
            spread[base + 3 * half + m // 2, forward + m * edge + edge - 1] += 1
    base, to = coarse_planes * 4 * half, 2 * coarse_planes * cross
    for y in range(edge):
        for z in range(edge):
            spread[base + (y // 2) * half + z // 2, to + y * edge + z] = 1
    return spread


def slope_columns(fields, planes, coarse_planes):
    column_field, forward, backward, centre = [], [], [], []
    p = np.arange(planes)

    def add(field, f, b, c):
        column_field.append(field)
        forward.append(f * np.ones(planes))
        backward.append(b * np.ones(planes))
        centre.append(c * np.ones(planes))

    for f, b, c in ((1, 0, 0), (0, 1, 0), (0, 0, 1)):
        for g in range(2 * fields):
            for q in range(planes):
                here = p == q
                add(g, f * here + c * (p + 1 == q), b * here + c * (p - 1 == q), c * here)
    rows = [g if g < fields else -1 for g in range(ROWS)]
    rows += [fields + g if g < fields else -1 for g in range(ROWS)]
    for g in rows:
        add(g, 0, p == 0, 0)
    for g in rows:
        add(g, p == planes - 1, 0, 0)
    for c in range(coarse_planes):
        for g in rows:
            add(g, p // 2 == c, 0, 0)
        for g in rows:
            add(g, 0, p // 2 == c, 0)
    width = round_up(len(column_field), 128)
    select = np.zeros((2 * fields, width), np.float32)
    masks = np.zeros((3, planes, width), np.float32)
    for k, g in enumerate(column_field):
        if g >= 0:
            select[g, k] = 1
        masks[0, :, k], masks[1, :, k], masks[2, :, k] = forward[k], backward[k], centre[k]
    return select, masks


def expand_faces(slots_ref, fields, spread_ref, out_ref):
    slots, _, planes, cross = slots_ref.shape
    for slot in range(slots):
        for block in range(ROWS // planes):
            at = slot * ROWS + block * planes
            out_ref[at : at + planes, :cross] = slots_ref[slot, fields + block]
    both = jnp.dot(split_two(out_ref[:, :cross]), spread_ref[...], preferred_element_type=jnp.float32)
    out_ref[...] = both[: slots * ROWS] + both[slots * ROWS :]


def own_ghosts(now, fields, spread):
    vmem = pl.BlockSpec(memory_space=pltpu.VMEM)
    shape = (now.shape[0] * ROWS, spread.shape[1])

    def kernel(now_ref, spread_ref, out_ref):
        expand_faces(now_ref, fields, spread_ref, out_ref)

    return pl.pallas_call(
        kernel,
        out_shape=jax.ShapeDtypeStruct(shape, jnp.float32),
        in_specs=[vmem] * 2,
        out_specs=vmem,
        compiler_params=pltpu.CompilerParams(vmem_limit_bytes=48 * 2 ** 20),
        cost_estimate=pl.CostEstimate(
            flops=4 * shape[0] * spread.size, bytes_accessed=4 * shape[0] * shape[1], transcendentals=0
        ),
    )(now, spread)


def slope_kernel(
    edge, planes, fields, coarse_planes, per_device, total, coarse_count, slots, slabs,
    dest_ref, parent_ref, own_ref, other_ref, own_low, other_low, own_high, other_high,
    own_rim, spread_ref, weight_ref, out_ref, token_ref, stack, parts, other_rim, staged, table, count, sems,
):
    cross = edge * edge
    rows = fields * planes
    own, slab = lax.axis_index("box"), lax.axis_index("slab")

    token_ref[...] = jnp.zeros_like(token_ref)
    stack[...] = jnp.zeros_like(stack)
    half = weight_ref.shape[0]
    weights = weight_ref[...]
    parts[:half] = weights.astype(jnp.bfloat16)
    parts[half:] = (weights - weights.astype(jnp.bfloat16).astype(jnp.float32)).astype(jnp.bfloat16)
    for slot in range(slots):
        table[slot] = -1
        count[slot] = 0

    def place(b, carry):
        @pl.when(dest_ref[b] == own)
        def _():
            slot = 2 * (b // per_device)
            owner = parent_ref[b] // coarse_count
            table[jnp.where(table[slot] >= 0, slot + 1, slot)] = 2 * owner + count[owner]
            count[owner] = count[owner] + 1

        return carry

    lax.fori_loop(0, total, place, 0)
    expand_faces(other_ref, fields, spread_ref, other_rim)

    def write(step):
        return pltpu.make_async_copy(staged.at[step], out_ref.at[step], sems.at[step])

    def one_slot(step, carry):
        face = table[step]

        @pl.when(face < 0)
        def _():
            staged[step] = jnp.zeros(staged.shape[1:], jnp.float32)

        @pl.when(face >= 0)
        def _():
            lane = lax.broadcasted_iota(jnp.int32, (1, cross), 1)
            y, z = lane // edge, lane % edge
            for n, ref in enumerate((own_ref, other_ref)):
                at = (4 + n) * rows
                if planes % 8:
                    for f in range(fields):
                        stack[at + f * planes : at + (f + 1) * planes] = ref[step, f]
                else:
                    stack[at : at + rows] = ref[step, :fields].reshape(rows, cross)
            cells = stack[4 * rows : 6 * rows]
            stack[0 : 2 * rows] = jnp.where(y < edge - 1, pltpu.roll(cells, cross - edge, 1), 0.0) + jnp.where(
                z < edge - 1, pltpu.roll(cells, cross - 1, 1), 0.0
            )
            stack[2 * rows : 4 * rows] = jnp.where(y > 0, pltpu.roll(cells, edge, 1), 0.0) + jnp.where(
                z > 0, pltpu.roll(cells, 1, 1), 0.0
            )
            here = pl.ds(pl.multiple_of(ROWS * face, ROWS), ROWS)
            rim = jnp.concatenate([own_rim[here], other_rim[here]], axis=0)
            base = 6 * rows
            x_face = rim[:, 2 * coarse_planes * cross :]
            stack[base : base + 2 * ROWS] = x_face
            stack[base + 2 * ROWS : base + 4 * ROWS] = x_face

            def set_halo(at, refs):
                for n, ref in enumerate(refs):
                    for f in range(fields):
                        row = at + n * ROWS + f
                        stack[row : row + 1] = ref[pl.ds(step * fields + f, 1)]

            @pl.when(slab > 0)
            def _():
                set_halo(6 * rows, (own_low, other_low))

            @pl.when(slab < slabs - 1)
            def _():
                set_halo(6 * rows + 2 * ROWS, (own_high, other_high))

            base += 4 * ROWS
            for n in range(2 * coarse_planes):
                stack[base + 2 * ROWS * n : base + 2 * ROWS * (n + 1)] = rim[:, n * cross : (n + 1) * cross]
            values = stack[...]
            high = values.astype(jnp.bfloat16)
            low = (values - high.astype(jnp.float32)).astype(jnp.bfloat16)
            half = weight_ref.shape[0]
            both = jnp.dot(parts[...], high, preferred_element_type=jnp.float32)
            mixed = jnp.dot(parts[:half], low, preferred_element_type=jnp.float32)
            mixed = both[:half] + (both[half:] + mixed)
            if planes % 8:
                for f in range(fields):
                    staged[step, f] = mixed[f * planes : (f + 1) * planes]
            else:
                staged[step] = mixed[:rows].reshape(fields, planes, cross)

        write(step).start()
        return carry

    lax.fori_loop(0, slots, one_slot, 0)
    for step in range(slots):
        write(step).wait()


def mixing_weights(mixes, group, fields, planes, coarse_planes):
    lap_mix, grad_mix, damp_mix = mixes
    select, masks = slope_columns(fields, planes, coarse_planes)
    terms = jnp.stack([lap_mix + 0.5 * grad_mix, lap_mix - 0.5 * grad_mix, damp_mix - 6.0 * lap_mix])
    terms = lax.dynamic_slice_in_dim(terms, group * fields, fields, 1)
    terms = jnp.where(group == 0, terms, jnp.roll(terms, fields, axis=2))
    terms = jnp.einsum("tfg,gk->tfk", terms, jnp.asarray(select), precision=HIGHEST)
    weight = jnp.sum(terms[:, :, None, :] * jnp.asarray(masks)[:, None], axis=0).reshape(fields * planes, -1)
    return jnp.pad(weight, ((0, round_up(fields * planes, 16) - fields * planes), (0, 0)))


def body(boxes, move_dest, parent, coarse, lap_mix, grad_mix, damp_mix):
    box_count = lax.axis_size("box")
    slabs = lax.axis_size("slab")
    group = lax.axis_index("fld")
    levels, per_device, fields, planes, cross = boxes.shape
    edge = planes * slabs
    coarse_planes = planes // 2
    slots = 2 * box_count
    total = move_dest.shape[0]
    coarse_count = coarse.shape[0]

    def send(piece, turn):
        return lax.ppermute(piece, "box", [(s, (s + turn) % box_count) for s in range(box_count)])

    first = pack_first(boxes, coarse, move_dest, parent, edge, box_count)
    arrived = [first[0]] + [send(first[turn], turn) for turn in range(1, box_count)]
    moved, *later = pack_later((0, 1), boxes, move_dest, box_count)
    later += pack_later(tuple(range(2, box_count)), boxes, move_dest, box_count)
    next_one, *middle, last_one = [send(piece, n + 1) for n, piece in enumerate(later)]
    now, moved, *facing = arrive(arrived, moved, slabs)

    swap = [(0, 1), (1, 0)]
    now_other = lax.ppermute(now, "fld", swap)

    spread = jnp.asarray(expand_table(coarse_planes, edge, cross)).astype(jnp.bfloat16)
    rim = own_ghosts(now, fields, spread)

    def shifted(values, up):
        pairs = [(s, s + 1) if up else (s + 1, s) for s in range(slabs - 1)]
        return lax.ppermute(values, "slab", swap if slabs == 2 else pairs)

    low = shifted(facing[-1], True)
    low, rim = lax.optimization_barrier((low, rim))
    low = low, lax.ppermute(low, "fld", swap)
    high = low
    if slabs != 2:
        high = shifted(facing[0], False)
        high = high, lax.ppermute(high, "fld", swap)

    weight = mixing_weights((lap_mix, grad_mix, damp_mix), group, fields, planes, coarse_planes)
    smem, vmem = pl.BlockSpec(memory_space=pltpu.SMEM), pl.BlockSpec(memory_space=pltpu.VMEM)
    slope, token = pl.pallas_call(
        functools.partial(
            slope_kernel, edge, planes, fields, coarse_planes, per_device, total, coarse_count, slots, slabs
        ),
        out_shape=[
            jax.ShapeDtypeStruct((slots, fields, planes, cross), jnp.float32),
            jax.ShapeDtypeStruct((8, 128), jnp.float32),
        ],
        in_specs=[smem, smem] + [vmem] * 9,
        out_specs=[pl.BlockSpec(memory_space=pltpu.HBM), vmem],
        scratch_shapes=[
            pltpu.VMEM((weight.shape[1], cross), jnp.float32),
            pltpu.VMEM((2 * weight.shape[0], weight.shape[1]), jnp.bfloat16),
            pltpu.VMEM((ROWS * slots, spread.shape[1]), jnp.float32),
            pltpu.VMEM((slots, fields, planes, cross), jnp.float32),
            pltpu.SMEM((slots,), jnp.int32),
            pltpu.SMEM((slots,), jnp.int32),
            pltpu.SemaphoreType.DMA((slots,)),
        ],
        compiler_params=pltpu.CompilerParams(vmem_limit_bytes=48 * 2 ** 20),
        cost_estimate=pl.CostEstimate(
            flops=3 * slots * weight.size * cross, bytes_accessed=12 * now.size, transcendentals=0
        ),
    )(move_dest, parent, now, now_other, low[0], low[1], high[0], high[1], rim, spread, weight)
    moved = settle(tuple(range(2, box_count - 1)), middle, moved, token)
    return settle((1, box_count - 1), [next_one, last_one], moved, token), slope


def solution(mesh):
    placed = (
        P(None, ("runs", "box"), "fld", "slab", None),
        P("runs"),
        P("runs"),
        P(("runs", "box"), "fld", None),
        P(),
        P(),
        P(),
    )
    return jax.shard_map(
        body,
        mesh=mesh,
        in_specs=placed,
        out_specs=(
            P(None, ("runs", "box"), "fld", "slab", None),
            P(("runs", "box"), "fld", "slab", None),
        ),
        check_vma=False,
    )
```

```python
import functools

import jax
import jax.numpy as jnp
import numpy as np
from jax import lax
from jax.experimental import pallas as pl
from jax.experimental.pallas import tpu as pltpu
from jax.sharding import PartitionSpec as P

HIGHEST = lax.Precision.HIGHEST
ROWS = 16


def round_up(value, unit):
    return -(-value // unit) * unit


def split_two(values):
    high = values.astype(jnp.bfloat16)
    low = (values - high.astype(jnp.float32)).astype(jnp.bfloat16)
    return jnp.concatenate([high, low], axis=0)


def place_boxes(per_device, box_count, dest_ref, table):
    own = lax.axis_index("box")
    for slot in range(2 * box_count):
        table[slot] = -1

    def place(b, carry):
        slot = 2 * dest_ref[own * per_device + b]
        table[jnp.where(table[slot] >= 0, slot + 1, slot)] = b
        return carry

    lax.fori_loop(0, per_device, place, 0)


def target_of(own, turn, box_count):
    return lax.rem(own + turn, box_count)


def source_of(own, turn, box_count):
    return lax.rem(own - turn + box_count, box_count)


def each_slot(box_count):
    own = lax.axis_index("box")
    for turn in range(box_count):
        for k in range(2):
            yield turn, k, 2 * target_of(own, turn, box_count) + k


def first_kernel(per_device, box_count, edge, dest_ref, parent_ref, boxes_ref, coarse_ref, *refs):
    outs, (boxes, zeros, shells, chosen, rows, dest, parent, box_table, face_table, sems, row_sems, in_sems) = (
        refs[:box_count], refs[box_count:]
    )
    fields, coarse_count, cells = coarse_ref.shape
    planes, cross = outs[0].shape[1:]
    own, slab = lax.axis_index("box"), lax.axis_index("slab")
    fetches = [
        pltpu.make_async_copy(dest_ref, dest, in_sems.at[0]),
        pltpu.make_async_copy(boxes_ref.at[0], boxes, in_sems.at[1]),
        pltpu.make_async_copy(parent_ref, parent, in_sems.at[2]),
        pltpu.make_async_copy(coarse_ref, shells, in_sems.at[3]),
    ]
    for fetch in fetches:
        fetch.start()
    zeros[...] = jnp.zeros_like(zeros)
    index = face_cells(lax.broadcasted_iota(jnp.int32, (1, cross), 1), edge, planes // 2, slab)
    cell = lax.broadcasted_iota(jnp.int32, (cells, cross), 0)
    one_hot = (cell == index).astype(jnp.float32).astype(jnp.bfloat16)
    fetches[0].wait()
    place_boxes(per_device, box_count, dest, box_table)
    fetches[1].wait()

    def copy(shift, k, values):
        return pltpu.make_async_copy(values, outs[shift].at[pl.ds(k * fields, fields)], sems.at[shift, k])

    for shift, k, slot in each_slot(box_count):
        b = box_table[slot]

        @pl.when(b >= 0)
        def _():
            copy(shift, k, boxes.at[b]).start()

        @pl.when(b < 0)
        def _():
            copy(shift, k, zeros).start()

    for slot in range(2 * box_count):
        face_table[slot] = -1
    fetches[2].wait()

    def place(b, carry):
        slot = 2 * dest[b]
        local = parent[b] - own * coarse_count

        @pl.when(jnp.logical_and(local >= 0, local < coarse_count))
        def _():
            face_table[jnp.where(face_table[slot] >= 0, slot + 1, slot)] = local

        return carry

    lax.fori_loop(0, dest.shape[0], place, 0)
    fetches[3].wait()
    count = fields * coarse_count
    both = jnp.dot(split_two(shells[...].reshape(count, cells)), one_hot, preferred_element_type=jnp.float32)
    chosen[...] = (both[:count] + both[count:]).reshape(chosen.shape)
    sent = []
    for shift, k, slot in each_slot(box_count):
        local = face_table[slot]
        for f in range(fields):
            values = chosen[f, pl.ds(jnp.maximum(local, 0), 1)]
            block, row = divmod(k * fields + f, planes)
            rows[shift, block, row : row + 1] = jnp.where(local >= 0, values, 0.0)
        if k == 1:
            to = outs[shift].at[pl.ds(2 * fields, rows.shape[1])]
            sent.append(pltpu.make_async_copy(rows.at[shift], to, row_sems.at[shift]))
            sent[-1].start()
    for shift, k, slot in each_slot(box_count):
        copy(shift, k, zeros).wait()
    for rows_copy in sent:
        rows_copy.wait()


def pack_first(boxes, coarse, move_dest, parent, edge, box_count):
    per_device, fields, planes, cross = boxes.shape[1:]
    coarse = jnp.transpose(coarse, (1, 0, 2))
    hbm = pl.BlockSpec(memory_space=pltpu.HBM)
    face_blocks = 2 * fields // planes
    item = (2 * fields + face_blocks, planes, cross)
    return pl.pallas_call(
        functools.partial(first_kernel, per_device, box_count, edge),
        out_shape=[jax.ShapeDtypeStruct(item, jnp.float32)] * box_count,
        in_specs=[hbm] * 4,
        out_specs=[hbm] * box_count,
        scratch_shapes=[
            pltpu.VMEM(boxes.shape[1:], jnp.float32),
            pltpu.VMEM(boxes.shape[2:], jnp.float32),
            pltpu.VMEM(coarse.shape, jnp.float32),
            pltpu.VMEM(coarse.shape[:2] + (cross,), jnp.float32),
            pltpu.VMEM((box_count, face_blocks, planes, cross), jnp.float32),
            pltpu.SMEM(move_dest.shape, jnp.int32),
            pltpu.SMEM(parent.shape, jnp.int32),
            pltpu.SMEM((2 * box_count,), jnp.int32),
            pltpu.SMEM((2 * box_count,), jnp.int32),
            pltpu.SemaphoreType.DMA((box_count, 2)),
            pltpu.SemaphoreType.DMA((box_count,)),
            pltpu.SemaphoreType.DMA((4,)),
        ],
        cost_estimate=pl.CostEstimate(
            flops=6 * coarse.size * cross, bytes_accessed=4 * (coarse.size + 2 * boxes.size), transcendentals=0
        ),
    )(move_dest, parent, boxes, coarse)


def later_kernel(turns, per_device, box_count, levels, dest_ref, boxes_ref, *refs):
    outs, (dest, table, sems, in_sem, *stay) = refs[: len(turns)], refs[len(turns) :]
    own = lax.axis_index("box")
    fetch = pltpu.make_async_copy(dest_ref, dest, in_sem)
    fetch.start()
    fetch.wait()
    place_boxes(per_device, box_count, dest, table)
    places = [(n, k, 2 * target_of(own, turn, box_count) + k) for n, turn in enumerate(turns) for k in range(2)]
    held = [stay[0] if turn == 0 else out for turn, out in zip(turns, outs)]

    def copies(n, k, b):
        skip = levels - held[n].shape[0]
        for level in range(skip, levels):
            yield pltpu.make_async_copy(boxes_ref.at[level, b], held[n].at[level - skip, k], sems.at[n, level, k])

    for n, k, slot in places:
        b = table[slot]

        @pl.when(b >= 0)
        def _():
            for copy in copies(n, k, b):
                copy.start()

        @pl.when(b < 0)
        def _():
            for level in range(held[n].shape[0]):
                held[n][level, k] = jnp.zeros(held[n].shape[2:], jnp.float32)

    for n, k, slot in places:
        b = table[slot]

        @pl.when(b >= 0)
        def _():
            for copy in copies(n, k, b):
                copy.wait()

    for n, turn in enumerate(turns):
        if turn == 0:
            settled = pltpu.make_async_copy(held[n], outs[n].at[:, pl.ds(2 * own, 2)], in_sem)
            settled.start()
            settled.wait()


def pack_later(turns, boxes, move_dest, box_count):
    levels, per_device = boxes.shape[:2]
    item = boxes.shape[2:]
    hbm, vmem = pl.BlockSpec(memory_space=pltpu.HBM), pl.BlockSpec(memory_space=pltpu.VMEM)
    size = int(np.prod(item)) * 4
    shapes = [(levels - 1, 2) + item if turn else (levels, 2 * box_count) + item for turn in turns]
    return pl.pallas_call(
        functools.partial(later_kernel, turns, per_device, box_count, levels),
        out_shape=[jax.ShapeDtypeStruct(shape, jnp.float32) for shape in shapes],
        in_specs=[hbm] * 2,
        out_specs=[vmem if turn else hbm for turn in turns],
        scratch_shapes=[
            pltpu.SMEM(move_dest.shape, jnp.int32),
            pltpu.SMEM((2 * box_count,), jnp.int32),
            pltpu.SemaphoreType.DMA((len(turns), levels, 2)),
            pltpu.SemaphoreType.DMA,
        ]
        + [pltpu.VMEM((levels, 2) + item, jnp.float32) for turn in turns if turn == 0],
        cost_estimate=pl.CostEstimate(
            flops=0, bytes_accessed=4 * len(turns) * levels * size, transcendentals=0
        ),
    )(move_dest, boxes)


def settle_kernel(turns, *refs):
    out_ref, sems = refs[-2:]
    own = lax.axis_index("box")
    levels, slots = out_ref.shape[:2]
    copies = []
    for n, turn in enumerate(turns):
        source = source_of(own, turn, slots // 2)
        for level in range(levels - 1):
            for k in range(2):
                to = out_ref.at[level + 1, 2 * source + k]
                copies.append(pltpu.make_async_copy(refs[n].at[level, k], to, sems.at[n, level, k]))
    for copy in copies:
        copy.start()
    for copy in copies:
        copy.wait()


def settle(turns, pieces, moved, after):
    count = len(pieces)
    vmem, hbm = pl.BlockSpec(memory_space=pltpu.VMEM), pl.BlockSpec(memory_space=pltpu.HBM)
    return pl.pallas_call(
        functools.partial(settle_kernel, turns),
        out_shape=jax.ShapeDtypeStruct(moved.shape, jnp.float32),
        in_specs=[vmem] * count + [hbm, vmem],
        out_specs=hbm,
        scratch_shapes=[pltpu.SemaphoreType.DMA((count, moved.shape[0] - 1, 2))],
        input_output_aliases={count: 0},
        compiler_params=pltpu.CompilerParams(vmem_limit_bytes=48 * 2 ** 20),
        cost_estimate=pl.CostEstimate(
            flops=0, bytes_accessed=8 * count * pieces[0].size, transcendentals=0
        ),
    )(*pieces, moved, after)


def arrive_kernel(box_count, slabs, fields, *refs):
    pieces = refs[:box_count]
    now_ref, moved_ref, *edges, own_rows, sems, own_sem = refs[box_count + 1 :]
    own, slab = lax.axis_index("box"), lax.axis_index("slab")
    planes, cross = now_ref.shape[2:]
    faces = pl.ds(2 * fields, own_rows.shape[0])
    mine = [pltpu.make_async_copy(pieces[0].at[faces], own_rows, own_sem)]
    copies = []
    for turn in range(box_count):
        source = source_of(own, turn, box_count)
        for k in range(2):
            box = pieces[turn].at[pl.ds(k * fields, fields)]
            if turn:
                copies.append(pltpu.make_async_copy(box, moved_ref.at[0, 2 * source + k], sems.at[turn, k]))
            else:
                mine.append(pltpu.make_async_copy(box, now_ref.at[2 * own + k, pl.ds(0, fields)], sems.at[0, k]))
    for copy in mine + copies:
        copy.start()
    faced = [jnp.where(slab == 0, planes - 1, 0)] if slabs == 2 else [0, planes - 1]

    def place_rows(rows_ref, first_block, source):
        for k in range(2):
            for f in range(ROWS):
                values = jnp.zeros((1, cross), jnp.float32)
                if f < fields:
                    block, row = divmod(k * fields + f, planes)
                    values = rows_ref[first_block + block, row : row + 1]
                now_ref[2 * source + k, fields + f // planes, f % planes : f % planes + 1] = values
            for edge_ref, plane in zip(edges, faced):
                for f in range(fields):
                    edge_ref[pl.ds((2 * source + k) * fields + f, 1)] = now_ref[2 * source + k, f, pl.ds(plane, 1)]

    for turn in range(1, box_count):
        source = source_of(own, turn, box_count)
        for k in range(2):
            now_ref[2 * source + k, :fields] = pieces[turn][k * fields : (k + 1) * fields]
        place_rows(pieces[turn], 2 * fields, source)
    for copy in mine:
        copy.wait()
    place_rows(own_rows, 0, own)
    for copy in copies:
        copy.wait()


def arrive(pieces, moved, slabs):
    box_count = len(pieces)
    _, planes, cross = pieces[0].shape
    fields = moved.shape[2]
    slots = 2 * box_count
    sides = 1 if slabs == 2 else 2
    vmem, hbm = pl.BlockSpec(memory_space=pltpu.VMEM), pl.BlockSpec(memory_space=pltpu.HBM)
    shapes = [(slots, fields + ROWS // planes, planes, cross), moved.shape] + [(slots * fields, cross)] * sides
    return pl.pallas_call(
        functools.partial(arrive_kernel, box_count, slabs, fields),
        out_shape=[jax.ShapeDtypeStruct(shape, jnp.float32) for shape in shapes],
        in_specs=[hbm] + [vmem] * (box_count - 1) + [hbm],
        out_specs=[vmem, hbm] + [vmem] * sides,
        scratch_shapes=[
            pltpu.VMEM((2 * fields // planes, planes, cross), jnp.float32),
            pltpu.SemaphoreType.DMA((box_count, 2)),
            pltpu.SemaphoreType.DMA,
        ],
        input_output_aliases={box_count: 1},
        compiler_params=pltpu.CompilerParams(vmem_limit_bytes=48 * 2 ** 20),
        cost_estimate=pl.CostEstimate(
            flops=0, bytes_accessed=12 * box_count * pieces[0].size, transcendentals=0
        ),
    )(*pieces, moved)


def face_cells(lane, edge, coarse_planes, slab):
    half, side = edge // 2, edge // 2 + 2
    plane, m = lane // (4 * half), lane % half + 1
    which = (lane // half) % 4
    rim = jnp.where(which == 0, m, jnp.where(which == 1, (side - 1) * side + m, m * side))
    rim = jnp.where(which == 3, rim + side - 1, rim) + (slab * coarse_planes + plane + 1) * side * side
    t = lane - 4 * half * coarse_planes
    x_rim = jnp.where(slab > 0, (side - 1) * side * side, 0) + (t // half + 1) * side + m
    return jnp.where(t < 0, rim, jnp.where(t < half * half, x_rim, -1))


def expand_table(coarse_planes, edge, lanes):
    half = edge // 2
    cross = edge * edge
    spread = np.zeros((lanes, (2 * coarse_planes + 1) * cross), np.float32)
    for c in range(coarse_planes):
        base = c * 4 * half
        forward, backward = 2 * c * cross, (2 * c + 1) * cross
        for m in range(edge):
            spread[base + m // 2, backward + m] += 1
            spread[base + half + m // 2, forward + (edge - 1) * edge + m] += 1
            spread[base + 2 * half + m // 2, backward + m * edge] += 1
            spread[base + 3 * half + m // 2, forward + m * edge + edge - 1] += 1
    base, to = coarse_planes * 4 * half, 2 * coarse_planes * cross
    for y in range(edge):
        for z in range(edge):
            spread[base + (y // 2) * half + z // 2, to + y * edge + z] = 1
    return spread


def slope_columns(fields, planes, coarse_planes):
    column_field, forward, backward, centre = [], [], [], []
    p = np.arange(planes)

    def add(field, f, b, c):
        column_field.append(field)
        forward.append(f * np.ones(planes))
        backward.append(b * np.ones(planes))
        centre.append(c * np.ones(planes))

    for f, b, c in ((1, 0, 0), (0, 1, 0), (0, 0, 1)):
        for g in range(2 * fields):
            for q in range(planes):
                here = p == q
                add(g, f * here + c * (p + 1 == q), b * here + c * (p - 1 == q), c * here)
    rows = [g if g < fields else -1 for g in range(ROWS)]
    rows += [fields + g if g < fields else -1 for g in range(ROWS)]
    for g in rows:
        add(g, 0, p == 0, 0)
    for g in rows:
        add(g, p == planes - 1, 0, 0)
    for c in range(coarse_planes):
        for g in rows:
            add(g, p // 2 == c, 0, 0)
        for g in rows:
            add(g, 0, p // 2 == c, 0)
    width = round_up(len(column_field), 128)
    select = np.zeros((2 * fields, width), np.float32)
    masks = np.zeros((3, planes, width), np.float32)
    for k, g in enumerate(column_field):
        if g >= 0:
            select[g, k] = 1
        masks[0, :, k], masks[1, :, k], masks[2, :, k] = forward[k], backward[k], centre[k]
    return select, masks


def expand_faces(slots_ref, fields, spread_ref, out_ref):
    slots, _, planes, cross = slots_ref.shape
    for slot in range(slots):
        for block in range(ROWS // planes):
            at = slot * ROWS + block * planes
            out_ref[at : at + planes, :cross] = slots_ref[slot, fields + block]
    both = jnp.dot(split_two(out_ref[:, :cross]), spread_ref[...], preferred_element_type=jnp.float32)
    out_ref[...] = both[: slots * ROWS] + both[slots * ROWS :]


def own_ghosts(now, fields, spread):
    vmem = pl.BlockSpec(memory_space=pltpu.VMEM)
    shape = (now.shape[0] * ROWS, spread.shape[1])

    def kernel(now_ref, spread_ref, out_ref):
        expand_faces(now_ref, fields, spread_ref, out_ref)

    return pl.pallas_call(
        kernel,
        out_shape=jax.ShapeDtypeStruct(shape, jnp.float32),
        in_specs=[vmem] * 2,
        out_specs=vmem,
        compiler_params=pltpu.CompilerParams(vmem_limit_bytes=48 * 2 ** 20),
        cost_estimate=pl.CostEstimate(
            flops=4 * shape[0] * spread.size, bytes_accessed=4 * shape[0] * shape[1], transcendentals=0
        ),
    )(now, spread)


def slope_kernel(
    edge, planes, fields, coarse_planes, per_device, total, coarse_count, slots, slabs,
    dest_ref, parent_ref, own_ref, other_ref, own_low, other_low, own_high, other_high,
    own_rim, spread_ref, weight_ref, out_ref, token_ref, stack, parts, other_rim, staged, table, count, sems,
):
    cross = edge * edge
    rows = fields * planes
    own, slab = lax.axis_index("box"), lax.axis_index("slab")

    token_ref[...] = jnp.zeros_like(token_ref)
    stack[...] = jnp.zeros_like(stack)
    half = weight_ref.shape[0]
    weights = weight_ref[...]
    parts[:half] = weights.astype(jnp.bfloat16)
    parts[half:] = (weights - weights.astype(jnp.bfloat16).astype(jnp.float32)).astype(jnp.bfloat16)
    for slot in range(slots):
        table[slot] = -1
        count[slot] = 0

    def place(b, carry):
        @pl.when(dest_ref[b] == own)
        def _():
            slot = 2 * (b // per_device)
            owner = parent_ref[b] // coarse_count
            table[jnp.where(table[slot] >= 0, slot + 1, slot)] = 2 * owner + count[owner]
            count[owner] = count[owner] + 1

        return carry

    lax.fori_loop(0, total, place, 0)
    expand_faces(other_ref, fields, spread_ref, other_rim)

    def write(step):
        return pltpu.make_async_copy(staged.at[step], out_ref.at[step], sems.at[step])

    def one_slot(step, carry):
        face = table[step]

        @pl.when(face < 0)
        def _():
            staged[step] = jnp.zeros(staged.shape[1:], jnp.float32)

        @pl.when(face >= 0)
        def _():
            lane = lax.broadcasted_iota(jnp.int32, (1, cross), 1)
            y, z = lane // edge, lane % edge
            for n, ref in enumerate((own_ref, other_ref)):
                at = (4 + n) * rows
                if planes % 8:
                    for f in range(fields):
                        stack[at + f * planes : at + (f + 1) * planes] = ref[step, f]
                else:
                    stack[at : at + rows] = ref[step, :fields].reshape(rows, cross)
            cells = stack[4 * rows : 6 * rows]
            stack[0 : 2 * rows] = jnp.where(y < edge - 1, pltpu.roll(cells, cross - edge, 1), 0.0) + jnp.where(
                z < edge - 1, pltpu.roll(cells, cross - 1, 1), 0.0
            )
            stack[2 * rows : 4 * rows] = jnp.where(y > 0, pltpu.roll(cells, edge, 1), 0.0) + jnp.where(
                z > 0, pltpu.roll(cells, 1, 1), 0.0
            )
            here = pl.ds(pl.multiple_of(ROWS * face, ROWS), ROWS)
            rim = jnp.concatenate([own_rim[here], other_rim[here]], axis=0)
            base = 6 * rows
            x_face = rim[:, 2 * coarse_planes * cross :]
            stack[base : base + 2 * ROWS] = x_face
            stack[base + 2 * ROWS : base + 4 * ROWS] = x_face

            def set_halo(at, refs):
                for n, ref in enumerate(refs):
                    for f in range(fields):
                        row = at + n * ROWS + f
                        stack[row : row + 1] = ref[pl.ds(step * fields + f, 1)]

            @pl.when(slab > 0)
            def _():
                set_halo(6 * rows, (own_low, other_low))

            @pl.when(slab < slabs - 1)
            def _():
                set_halo(6 * rows + 2 * ROWS, (own_high, other_high))

            base += 4 * ROWS
            for n in range(2 * coarse_planes):
                stack[base + 2 * ROWS * n : base + 2 * ROWS * (n + 1)] = rim[:, n * cross : (n + 1) * cross]
            values = stack[...]
            high = values.astype(jnp.bfloat16)
            low = (values - high.astype(jnp.float32)).astype(jnp.bfloat16)
            half = weight_ref.shape[0]
            both = jnp.dot(parts[...], high, preferred_element_type=jnp.float32)
            mixed = jnp.dot(parts[:half], low, preferred_element_type=jnp.float32)
            mixed = both[:half] + (both[half:] + mixed)
            if planes % 8:
                for f in range(fields):
                    staged[step, f] = mixed[f * planes : (f + 1) * planes]
            else:
                staged[step] = mixed[:rows].reshape(fields, planes, cross)

        write(step).start()
        return carry

    lax.fori_loop(0, slots, one_slot, 0)
    for step in range(slots):
        write(step).wait()


def mixing_weights(mixes, group, fields, planes, coarse_planes):
    lap_mix, grad_mix, damp_mix = mixes
    select, masks = slope_columns(fields, planes, coarse_planes)
    terms = jnp.stack([lap_mix + 0.5 * grad_mix, lap_mix - 0.5 * grad_mix, damp_mix - 6.0 * lap_mix])
    terms = lax.dynamic_slice_in_dim(terms, group * fields, fields, 1)
    terms = jnp.where(group == 0, terms, jnp.roll(terms, fields, axis=2))
    terms = jnp.einsum("tfg,gk->tfk", terms, jnp.asarray(select), precision=HIGHEST)
    weight = jnp.sum(terms[:, :, None, :] * jnp.asarray(masks)[:, None], axis=0).reshape(fields * planes, -1)
    return jnp.pad(weight, ((0, round_up(fields * planes, 16) - fields * planes), (0, 0)))


def body(boxes, move_dest, parent, coarse, lap_mix, grad_mix, damp_mix):
    box_count = lax.axis_size("box")
    slabs = lax.axis_size("slab")
    group = lax.axis_index("fld")
    levels, per_device, fields, planes, cross = boxes.shape
    edge = planes * slabs
    coarse_planes = planes // 2
    slots = 2 * box_count
    total = move_dest.shape[0]
    coarse_count = coarse.shape[0]

    def send(piece, turn):
        return lax.ppermute(piece, "box", [(s, (s + turn) % box_count) for s in range(box_count)])

    first = pack_first(boxes, coarse, move_dest, parent, edge, box_count)
    arrived = [first[0]] + [send(first[turn], turn) for turn in range(1, box_count)]
    moved, *later = pack_later((0, 1), boxes, move_dest, box_count)
    later += pack_later(tuple(range(2, box_count)), boxes, move_dest, box_count)
    next_one, *middle, last_one = [send(piece, n + 1) for n, piece in enumerate(later)]
    now, moved, *facing = arrive(arrived, moved, slabs)

    swap = [(0, 1), (1, 0)]
    now_other = lax.ppermute(now, "fld", swap)

    spread = jnp.asarray(expand_table(coarse_planes, edge, cross)).astype(jnp.bfloat16)
    rim = own_ghosts(now, fields, spread)

    def shifted(values, up):
        pairs = [(s, s + 1) if up else (s + 1, s) for s in range(slabs - 1)]
        return lax.ppermute(values, "slab", swap if slabs == 2 else pairs)

    low = shifted(facing[-1], True)
    low, rim = lax.optimization_barrier((low, rim))
    low = low, lax.ppermute(low, "fld", swap)
    high = low
    if slabs != 2:
        high = shifted(facing[0], False)
        high = high, lax.ppermute(high, "fld", swap)

    weight = mixing_weights((lap_mix, grad_mix, damp_mix), group, fields, planes, coarse_planes)
    smem, vmem = pl.BlockSpec(memory_space=pltpu.SMEM), pl.BlockSpec(memory_space=pltpu.VMEM)
    slope, token = pl.pallas_call(
        functools.partial(
            slope_kernel, edge, planes, fields, coarse_planes, per_device, total, coarse_count, slots, slabs
        ),
        out_shape=[
            jax.ShapeDtypeStruct((slots, fields, planes, cross), jnp.float32),
            jax.ShapeDtypeStruct((8, 128), jnp.float32),
        ],
        in_specs=[smem, smem] + [vmem] * 9,
        out_specs=[pl.BlockSpec(memory_space=pltpu.HBM), vmem],
        scratch_shapes=[
            pltpu.VMEM((weight.shape[1], cross), jnp.float32),
            pltpu.VMEM((2 * weight.shape[0], weight.shape[1]), jnp.bfloat16),
            pltpu.VMEM((ROWS * slots, spread.shape[1]), jnp.float32),
            pltpu.VMEM((slots, fields, planes, cross), jnp.float32),
            pltpu.SMEM((slots,), jnp.int32),
            pltpu.SMEM((slots,), jnp.int32),
            pltpu.SemaphoreType.DMA((slots,)),
        ],
        compiler_params=pltpu.CompilerParams(vmem_limit_bytes=48 * 2 ** 20),
        cost_estimate=pl.CostEstimate(
            flops=3 * slots * weight.size * cross, bytes_accessed=12 * now.size, transcendentals=0
        ),
    )(move_dest, parent, now, now_other, low[0], low[1], high[0], high[1], rim, spread, weight)
    moved = settle(tuple(range(2, box_count - 1)), middle, moved, token)
    return settle((1, box_count - 1), [next_one, last_one], moved, token), slope


def solution(mesh):
    placed = (
        P(None, ("runs", "box"), "fld", "slab", None),
        P("runs"),
        P("runs"),
        P(("runs", "box"), "fld", None),
        P(),
        P(),
        P(),
    )
    return jax.shard_map(
        body,
        mesh=mesh,
        in_specs=placed,
        out_specs=(
            P(None, ("runs", "box"), "fld", "slab", None),
            P(("runs", "box"), "fld", "slab", None),
        ),
        check_vma=False,
    )
```
